32 devices in a mesh: blk: 8 (over z, y), grp: 4 (over x, core).
Axes of the slice: x: 2, y: 2, z: 4, core: 2. Of those that a mesh axis runs over, the one named last changes fastest.
Arguments:
- tiles: bfloat16 [128, 20, 128, 128], P(('blk', 'grp')), may hold values from -1 to 3.5
- columns: int32 [128, 20], P(('blk', 'grp')), may hold values from -1 to 127, as said below
Outputs:
- square: bfloat16 [128, 20, 128, 128], P(('blk', 'grp'))
- trace_mean: float32 [], replicated
The draws below stay inside these ranges and needn't reach their ends.
Inputs may be any that keep to these rules, and one draw needn't show every extreme that they name: Slot 0 of row i holds i. The filled slots of a row come first, then -1. The filled columns of a row are distinct and lie within 12 block rows of i, counted periodically modulo 128. Every device has a row with all 20 slots filled that reaches i - 12 and one that reaches i + 12.
All inputs are finite; a program needn't handle non-finite values.
Results may differ from the reference program's by a relative error of at most 0.001.
Values may be sent and summed in bfloat16 or wider, within the bound.
No kernel may reach another device: no remote copies, remote signals or barrier semaphores. Data moves between devices by JAX's collectives and lax.ppermute only.
A program may use at most 192 MiB of HBM per device.

```python
import jax
import jax.numpy as jnp
from jax import lax

BS = 128
NNZ = 20
REACH = 12
R_DEV = 4
NB = 128


def draw_tiles(key, part):
    entry_key, gain_key = jax.random.split(jax.random.fold_in(key, 11))
    entries = jnp.clip(0.14 * jax.random.normal(entry_key, (NB, NNZ, BS, BS), jnp.float32), -0.8, 0.8)
    row_ramp = 1.0 + 0.7 * jnp.arange(NB, dtype=jnp.float32) / NB
    spread = jnp.exp(jax.random.uniform(gain_key, (NB, BS), jnp.float32, -0.3, 0.3))
    diagonal_gain = row_ramp[:, None] * spread
    identity = jnp.eye(BS, dtype=jnp.float32)
    entries = entries.at[:, 0].add(diagonal_gain[:, :, None] * identity[None])
    return entries.astype(jnp.bfloat16)


def draw_columns(key, part):
    count_key, score_key = jax.random.split(jax.random.fold_in(key, 23))
    row_index = jnp.arange(NB, dtype=jnp.int32)
    full_rows = (row_index % R_DEV == 0) | (row_index % R_DEV == R_DEV - 1)
    counts = jax.random.randint(count_key, (NB,), NNZ // 2, NNZ + 1, dtype=jnp.int32)
    counts = jnp.where(full_rows, NNZ, counts)
    candidates = jnp.concatenate([jnp.arange(-REACH, 0, dtype=jnp.int32), jnp.arange(1, REACH + 1, dtype=jnp.int32)])
    width_count = 2 * REACH
    scores = jax.random.randint(score_key, (NB, width_count), 0, 1 << 20, dtype=jnp.int32) * width_count + jnp.arange(width_count, dtype=jnp.int32)[None, :]
    forced = scores.at[:, 0].set(-2).at[:, width_count - 1].set(-1)
    scores = jnp.where(full_rows[:, None], forced, scores)
    order = jnp.argsort(scores, axis=1, stable=True)
    chosen = candidates[order][:, :NNZ - 1]
    others = jnp.mod(row_index[:, None] + chosen, NB).astype(jnp.int32)
    slot_ids = jnp.arange(1, NNZ, dtype=jnp.int32)
    others = jnp.where(slot_ids[None, :] < counts[:, None], others, -1)
    return jnp.concatenate([row_index[:, None], others], axis=1).astype(jnp.int32)


def setup_inputs(seed: int = 0) -> dict:
    splits = jax.random.split(jax.random.key(seed), 3)
    return {
        "tiles": draw_tiles(jax.random.fold_in(splits[2], 71), 0),
        "columns": draw_columns(jax.random.fold_in(splits[2], 71), 0),
    }


def reference(tiles, columns):
    all_rows = tiles.shape[0]
    slots_count = tiles.shape[1]
    block_size = tiles.shape[2]
    flat_tiles = tiles.reshape(all_rows * slots_count, block_size, block_size)
    slot_ids = jnp.arange(slots_count, dtype=jnp.int32)

    def one_row(inputs):
        own_tiles, row_cols = inputs
        filled = row_cols >= 0
        position = jnp.where(filled, row_cols, 0).astype(jnp.int32)
        far_cols = columns[position]
        matches = (far_cols[:, None, :] == row_cols[None, :, None]) & filled[:, None, None] & filled[None, :, None]
        found = jnp.any(matches, axis=2)
        which_slot = jnp.sum(jnp.where(matches, slot_ids[None, None, :], 0), axis=2).astype(jnp.int32)
        flat_index = (position[:, None] * slots_count + which_slot).astype(jnp.int32)
        panel = jnp.where(found[:, :, None, None], flat_tiles[flat_index], jnp.zeros((), tiles.dtype))
        product = jnp.einsum("tab,tsbc->sac", own_tiles.astype(jnp.float32), panel.astype(jnp.float32))
        return product.astype(jnp.bfloat16), jnp.trace(product[0])

    square, traces = lax.map(one_row, (tiles, columns))
    trace_mean = jnp.sum(traces) / (all_rows * block_size)
    return square, trace_mean
```

```python
import functools

import jax
import jax.numpy as jnp
from jax import lax
from jax.experimental import pallas as pl
from jax.experimental.pallas import tpu as pltpu
from jax.sharding import PartitionSpec as P

REACH = 12
AXES = ("blk", "grp")

FIRST = (2, 3, -3, -2)
SECOND = (-3, 2, -2, 3)
RELAY_FROM = (2, -5, 5, -2)
PARTNER = (1, -1, 1, -1)


def receive(shard, offsets):
    size = lax.axis_size(AXES)
    pairs = [((d + offsets[d % 4]) % size, d) for d in range(size)]
    return lax.ppermute(shard, AXES, pairs)


def body(rows, slots, block, window, piece_ids, final, has_prev, info, pos, *refs):
    refs = list(refs)
    take = lambda count: [refs.pop(0) for _ in range(count)]
    (own,) = take(1)
    sources = []
    for piece in piece_ids:
        sources.append(take({0: 0, 4: 2}.get(piece, 1)))
    prev = take(1)[0] if has_prev else None
    out = take(1)[0]
    trace_out = take(1)[0] if final else None
    own_stage, left, stage, right, total, out_stage = take(6)
    prev_stage = take(1)[0] if has_prev else None
    in_sem, own_sem, prev_sem, out_sem = take(4)
    span = rows * block
    chunks = window // rows

    def fetch(index, start):
        piece = piece_ids[index]
        source = sources[index]
        slot = index % 2
        if piece == 0:
            return
        if piece == 4:
            @pl.when(info[7] == 0)
            def _():
                copy = pltpu.make_async_copy(source[0], stage.at[slot], in_sem.at[slot])
                copy.start() if start else copy.wait()

            @pl.when(info[7] != 0)
            def _():
                copy = pltpu.make_async_copy(source[1], stage.at[slot], in_sem.at[slot])
                copy.start() if start else copy.wait()
        else:
            copy = pltpu.make_async_copy(source[0], stage.at[slot], in_sem.at[slot])
            copy.start() if start else copy.wait()

    own_copy = pltpu.make_async_copy(own, own_stage, own_sem)
    own_copy.start()
    fetch(0, True)
    if len(piece_ids) > 1:
        fetch(1, True)
    if has_prev:
        prev_copy = pltpu.make_async_copy(prev, prev_stage, prev_sem)
        prev_copy.start()

    def scatter(dense, source, place):
        dense[...] = jnp.zeros_like(dense)
        for r in range(rows):
            def one(u, carry):
                column = pl.multiple_of(pos[place * rows + r, u] * block, block)
                dense[r * block:(r + 1) * block, pl.ds(column, block)] = source[r, u]
                return carry
            lax.fori_loop(0, slots, one, 0, unroll=4)

    total[...] = jnp.zeros_like(total)
    own_copy.wait()
    scatter(left, own_stage, chunks // 2)

    for index, piece in enumerate(piece_ids):
        place = info[piece]
        fetch(index, False)
        if piece == 0:
            dense = left
        else:
            dense = right
            scatter(right, stage.at[index % 2], place)
            if index + 2 < len(piece_ids):
                fetch(index + 2, True)

        def multiply(n, carry):
            columns = pl.ds(pl.multiple_of(n * span, span), span)
            inner = pl.ds(pl.multiple_of(place * span, span), span)
            total[:, columns] += jnp.dot(
                left[:, inner], dense[:, columns], preferred_element_type=jnp.float32
            )
            return carry

        half = chunks // 2
        lax.fori_loop(jnp.maximum(0, place - half), jnp.minimum(chunks, place + half + 1), multiply, 0)

    if has_prev:
        prev_copy.wait()
    diagonal = jnp.zeros((block, block), jnp.float32)
    for r in range(rows):
        def emit(s, carry):
            column = pl.multiple_of(pos[rows * (chunks // 2) + r, s] * block, block)
            value = total[r * block:(r + 1) * block, pl.ds(column, block)]
            if has_prev:
                value = value + prev_stage[r, s]
            out_stage[r, s] = value.astype(out_stage.dtype)
            return carry
        lax.fori_loop(0, slots, emit, 0, unroll=2)
        copy = pltpu.make_async_copy(out_stage.at[r], out.at[r], out_sem.at[r])
        copy.start()
        if final:
            column = pl.multiple_of(pos[rows * (chunks // 2) + r, 0] * block, block)
            value = total[r * block:(r + 1) * block, pl.ds(column, block)]
            if has_prev:
                value = value + prev_stage[r, 0]
            diagonal = diagonal + value
    if final:
        on = lax.broadcasted_iota(jnp.int32, (block, block), 0) == lax.broadcasted_iota(
            jnp.int32, (block, block), 1
        )
        trace_out[...] = jnp.sum(jnp.where(on, diagonal, 0.0), axis=0, keepdims=True)
    for r in range(rows):
        pltpu.make_async_copy(out_stage.at[r], out.at[r], out_sem.at[r]).wait()


def partial_square(info, pos, own, pieces, prev, final):
    rows, slots, block, _ = own.shape
    window = pos.shape[0]
    span = rows * block
    piece_ids = tuple(p[0] for p in pieces)
    operands = [own]
    for _, arrays in pieces:
        operands.extend(arrays)
    if prev is not None:
        operands.append(prev)
    wide = (window + 1) * block
    scratch = [
        pltpu.VMEM(own.shape, own.dtype),
        pltpu.VMEM((span, wide), own.dtype),
        pltpu.VMEM((2,) + own.shape, own.dtype),
        pltpu.VMEM((span, wide), own.dtype),
        pltpu.VMEM((span, wide), jnp.float32),
        pltpu.VMEM(own.shape, own.dtype if final else jnp.float32),
    ]
    if prev is not None:
        scratch.append(pltpu.VMEM(own.shape, jnp.float32))
    scratch += [
        pltpu.SemaphoreType.DMA((2,)),
        pltpu.SemaphoreType.DMA,
        pltpu.SemaphoreType.DMA,
        pltpu.SemaphoreType.DMA((rows,)),
    ]
    any_spec = pl.BlockSpec(memory_space=pl.ANY)
    out_shape = [jax.ShapeDtypeStruct(own.shape, own.dtype if final else jnp.float32)]
    out_specs = [any_spec]
    if final:
        out_shape.append(jax.ShapeDtypeStruct((1, block), jnp.float32))
        out_specs.append(pl.BlockSpec(memory_space=pltpu.VMEM))
    count = len(piece_ids)
    return pl.pallas_call(
        functools.partial(body, rows, slots, block, window, piece_ids, final, prev is not None),
        out_shape=out_shape,
        grid_spec=pltpu.PrefetchScalarGridSpec(
            num_scalar_prefetch=2,
            grid=(),
            in_specs=[any_spec] * len(operands),
            out_specs=out_specs,
            scratch_shapes=scratch,
        ),
        compiler_params=pltpu.CompilerParams(vmem_limit_bytes=48 * 1024 * 1024),
        cost_estimate=pl.CostEstimate(
            flops=2 * span * span * window * block * count,
            bytes_accessed=own.size * 2 * (count + 2),
            transcendentals=0,
        ),
    )(info, pos, *operands)


def shards(tiles, columns):
    rows = tiles.shape[0]
    block = tiles.shape[2]
    devices = lax.axis_size(AXES)
    all_rows = rows * devices
    device = lax.axis_index(AXES)
    hops = (REACH + rows - 1) // rows
    assert hops == 3 and devices % 4 == 0 and devices > 8
    window = (2 * hops + 1) * rows

    first = receive(tiles, FIRST)
    second = receive(tiles, SECOND)
    beside = receive(tiles, PARTNER)
    all_cols = lax.all_gather(columns, AXES, tiled=True)
    start = jnp.mod((device - hops) * rows, all_rows)
    window_cols = lax.dynamic_slice_in_dim(jnp.concatenate([all_cols, all_cols]), start, window)
    pos = jnp.where(window_cols >= 0, jnp.mod(window_cols - start, all_rows), window)
    pos = jnp.minimum(pos, window).astype(jnp.int32)

    kind = device % 4
    other = kind ^ 1
    pick = lambda table: jnp.asarray(table, jnp.int32)
    first_off, second_off = pick(FIRST), pick(SECOND)
    relay_off = pick(tuple(RELAY_FROM[m] + FIRST[(m + RELAY_FROM[m]) % 4] for m in range(4)))
    beside_off = pick(PARTNER)[kind]
    use_second = jnp.abs(beside_off + first_off[other]) > hops
    beside_one = beside_off + jnp.where(use_second, second_off[other], first_off[other])
    info = jnp.stack([
        jnp.int32(0),
        beside_off,
        first_off[kind],
        second_off[kind],
        beside_one,
        relay_off[kind],
        beside_off + relay_off[other],
        use_second.astype(jnp.int32) - hops,
    ]) + hops

    acc = partial_square(info, pos, tiles, [(0, []), (1, [beside])], None, False)[0]
    relay = receive(first, RELAY_FROM)
    beside_first = receive(first, PARTNER)
    beside_second = receive(second, PARTNER)
    acc = partial_square(
        info, pos, tiles,
        [(2, [first]), (3, [second]), (4, [beside_first, beside_second])], acc, False,
    )[0]
    beside_relay = receive(relay, PARTNER)
    square, traces = partial_square(
        info, pos, tiles, [(5, [relay]), (6, [beside_relay])], acc, True
    )
    total_trace = lax.psum(jnp.sum(traces), AXES)
    return square, total_trace / (all_rows * block)


def solution(mesh):
    return jax.shard_map(
        shards,
        mesh=mesh,
        in_specs=(P(AXES, None, None, None), P(AXES, None)),
        out_specs=(P(AXES, None, None, None), P()),
        check_vma=False,
    )
```

```python
import functools

import jax
import jax.numpy as jnp
from jax import lax
from jax.experimental import pallas as pl
from jax.experimental.pallas import tpu as pltpu
from jax.sharding import PartitionSpec as P

REACH = 12
AXES = ("blk", "grp")
EMPTY = 64
VMEM_LIMIT = 48 * 1024 * 1024

FIRST = (2, 3, -3, -2)
SECOND = (-3, 2, -2, 3)
RELAY_FROM = (2, -5, 5, -2)
PARTNER = (1, -1, 1, -1)
RELAY = tuple(RELAY_FROM[m] + FIRST[(m + RELAY_FROM[m]) % 4] for m in range(4))


def across(table):
    return tuple(PARTNER[m] + table[m ^ 1] for m in range(4))


USE_SECOND = tuple(int(abs(offset) > 3) for offset in across(FIRST))
MIXED = tuple(
    second if use else first
    for first, second, use in zip(across(FIRST), across(SECOND), USE_SECOND)
)
OFFSETS = {
    "own": (0, 0, 0, 0),
    "beside": PARTNER,
    "first": FIRST,
    "second": SECOND,
    "mixed": MIXED,
    "relay": RELAY,
    "relay_beside": across(RELAY),
}


def receive(shard, offsets):
    size = lax.axis_size(AXES)
    pairs = [((d + offsets[d % 4]) % size, d) for d in range(size)]
    return lax.ppermute(shard, AXES, pairs)


def total_over_devices(value):
    size = lax.axis_size(AXES)
    assert size & (size - 1) == 0
    step = 1
    while step < size:
        value = value + lax.ppermute(value, AXES, [(d, d ^ step) for d in range(size)])
        step *= 2
    return value


def pick(table, kind):
    value = jnp.int32(table[3])
    for m in range(3):
        value = jnp.where(kind == m, jnp.int32(table[m]), value)
    return value


def swapped(kind):
    return kind // 2


def pack_body(rows, slots, devices, tiles, columns, out, meta, sems):
    device = lax.axis_index(AXES)
    swap = swapped(device % 4)
    half = rows // 2
    copies = []
    for h in range(2):
        for r in range(half):
            source = tiles.at[half * (h ^ swap) + r]
            copies.append(pltpu.make_async_copy(
                source, out.at[h, pl.ds(r * slots, slots)], sems.at[h * half + r]
            ))
    for copy in copies:
        copy.start()
    cols = columns[...]
    row = device * rows + lax.broadcasted_iota(jnp.int32, cols.shape, 0)
    offset = cols - row
    size = rows * devices
    offset = jnp.where(offset > size // 2, offset - size, offset)
    offset = jnp.where(offset < -(size // 2), offset + size, offset)
    offset = jnp.where(cols < 0, EMPTY, offset)
    meta[...] = jnp.zeros_like(meta)
    meta[0:16, :] = offset.astype(jnp.float32).astype(meta.dtype)
    for h in range(2):
        copy = pltpu.make_async_copy(meta, out.at[h, half * slots], sems.at[rows + h])
        copy.start()
        copies.append(copy)
    for copy in copies:
        copy.wait()


def pack(tiles, columns, devices):
    rows, slots, block, _ = tiles.shape
    columns = jnp.pad(columns, ((0, 16 - rows), (0, block - slots)), constant_values=-1)
    return pl.pallas_call(
        functools.partial(pack_body, rows, slots, devices),
        out_shape=jax.ShapeDtypeStruct((2, rows // 2 * slots + 1, block, block), tiles.dtype),
        in_specs=[pl.BlockSpec(memory_space=pl.ANY), pl.BlockSpec(memory_space=pltpu.VMEM)],
        out_specs=pl.BlockSpec(memory_space=pl.ANY),
        scratch_shapes=[
            pltpu.VMEM((block, block), tiles.dtype),
            pltpu.SemaphoreType.DMA((rows + 2,)),
        ],
        cost_estimate=pl.CostEstimate(flops=0, bytes_accessed=4 * tiles.size, transcendentals=0),
    )(tiles, columns)


def body(rows, slots, block, window, names, half_index, begin, final, *refs):
    refs = list(refs)
    take = lambda count: [refs.pop(0) for _ in range(count)]
    if begin:
        own = take(1)[0]
    else:
        left_in, own_pos, prev = take(3)
    sources = {name: take(2 if name == "mixed" else 1) for name in names}
    out = take(1)[0]
    if begin:
        left_out, own_pos = take(2)
    if final:
        trace_out = take(1)[0]
    left, stage, right, total, out_stage, pos_vmem, pos = take(7)
    if not begin:
        prev_stage = take(1)[0]
    in_sem, left_sem, prev_sem, pos_sem, out_sem = take(5)

    device = lax.axis_index(AXES)
    kind = device % 4
    half = rows // 2
    span = rows * block
    part = half * block
    chunks = window // rows
    middle = chunks // 2
    whole = half_index is None
    place = {name: pick(OFFSETS[name], kind) + middle for name in names}
    base = {
        name: half * swapped((kind + pick(OFFSETS[name], kind) + 8) % 4)
        for name in names
    }

    def fetch(index, start):
        name = names[index]
        refs_in = sources[name]
        target = stage.at[index % 2]
        def go(source):
            copy = pltpu.make_async_copy(source, target, in_sem.at[index % 2])
            copy.start() if start else copy.wait()
        if len(refs_in) == 1:
            go(refs_in[0])
        else:
            use_second = pick(USE_SECOND, kind)
            pl.when(use_second == 0)(lambda: go(refs_in[0]))
            pl.when(use_second != 0)(lambda: go(refs_in[1]))

    def start_decode(offsets, spot, where):
        value = offsets.astype(jnp.float32).astype(jnp.int32)
        value = value + spot * rows + lax.broadcasted_iota(jnp.int32, value.shape, 0)
        value = jnp.where((value < 0) | (value > window), window, value)
        pos_vmem[where] = value
        copy = pltpu.make_async_copy(pos_vmem.at[where], pos.at[where], pos_sem.at[where])
        copy.start()
        return copy

    def scatter(dense, source, where, first_row):
        for r in range(half):
            def one(u, carry):
                column = pl.multiple_of(pos[where, first_row + r, u] * block, block)
                dense[r * block:(r + 1) * block, pl.ds(column, block)] = source[r * slots + u]
                return carry
            lax.fori_loop(0, slots, one, 0, unroll=4)

    if begin:
        own_copy = pltpu.make_async_copy(own, stage.at[1], left_sem)
        own_copy.start()
        fetch(0, True)
        total[...] = jnp.zeros_like(total)
        left[...] = jnp.zeros_like(left)
        own_copy.wait()
        start_decode(stage[1, 0, half * slots, 0:16, :], jnp.int32(middle), 2).wait()
        own_base = half * swapped(kind)
        for h in range(2):
            first_row = half - own_base if h else own_base
            top = pl.multiple_of(first_row * block, block)
            for r in range(half):
                def one(u, carry):
                    column = pl.multiple_of(pos[2, first_row + r, u] * block, block)
                    left[pl.ds(top + r * block, block), pl.ds(column, block)] = stage[1, h, r * slots + u]
                    return carry
                lax.fori_loop(0, slots, one, 0, unroll=4)
        left_copy = pltpu.make_async_copy(left, left_out, left_sem)
        left_copy.start()
        def save(index, carry):
            r, s = index // slots, index % slots
            own_pos[r, s] = pos[2, r, s]
            return carry
        lax.fori_loop(0, rows * slots, save, 0)
    else:
        left_copy = pltpu.make_async_copy(left_in, left, left_sem)
        left_copy.start()
        for index in range(min(2, len(names))):
            fetch(index, True)
        prev_copy = pltpu.make_async_copy(prev, prev_stage, prev_sem)
        prev_copy.start()
        total[...] = jnp.zeros_like(total)
        left_copy.wait()

    def multiply(spot, parts):
        def one(n, carry):
            columns = pl.ds(pl.multiple_of(n * span, span), span)
            value = total[:, columns]
            for first_row, dense in parts:
                inner = pl.ds(pl.multiple_of(first_row * block, part), part)
                value = value + jnp.dot(
                    left[:, inner], dense[:, columns], preferred_element_type=jnp.float32
                )
            total[:, columns] = value
            return carry
        lax.fori_loop(
            jnp.maximum(0, spot - middle), jnp.minimum(chunks, spot + middle + 1), one, 0
        )

    if begin:
        def own_product(n, carry):
            columns = pl.ds(pl.multiple_of(n * span, span), span)
            total[:, columns] += jnp.dot(
                left[:, middle * span:(middle + 1) * span], left[:, columns],
                preferred_element_type=jnp.float32,
            )
            return carry
        lax.fori_loop(0, chunks, own_product, 0)

    for index, name in enumerate(names):
        slot = index % 2
        spot = place[name]
        first_base = base[name]
        if whole:
            right[...] = jnp.zeros_like(right)
            fetch(index, False)
            start_decode(stage[slot, 0, half * slots, 0:16, :], spot, slot).wait()
            parts = []
            for h in range(2):
                first_row = half - first_base if h else first_base
                scatter(right.at[h], stage.at[slot, h], slot, first_row)
                parts.append((spot * rows + first_row, right.at[h]))
            if index + 2 < len(names):
                fetch(index + 2, True)
            multiply(spot, parts)
        else:
            dense = right.at[slot]
            dense[...] = jnp.zeros_like(dense)
            fetch(index, False)
            start_decode(stage[slot, half * slots, 0:16, :], spot, slot).wait()
            first_row = half - first_base if half_index else first_base
            scatter(dense, stage.at[slot], slot, first_row)
            multiply(spot, [(spot * rows + first_row, dense)])

    if not begin:
        prev_copy.wait()
    diagonal = jnp.zeros((block, block), jnp.float32)
    for r in range(rows):
        def block_at(s):
            column = pl.multiple_of(own_pos[r, s] * block, block)
            value = total[r * block:(r + 1) * block, pl.ds(column, block)]
            return value if begin else value + prev_stage[r, s]
        def emit(s, carry):
            out_stage[r, s] = block_at(s).astype(out_stage.dtype)
            return carry
        lax.fori_loop(0, slots, emit, 0, unroll=2)
        pltpu.make_async_copy(out_stage.at[r], out.at[r], out_sem.at[r]).start()
        if final:
            diagonal = diagonal + block_at(0)
    if final:
        on = lax.broadcasted_iota(jnp.int32, (block, block), 0) == lax.broadcasted_iota(
            jnp.int32, (block, block), 1
        )
        trace_out[...] = jnp.sum(jnp.where(on, diagonal, 0.0), axis=0, keepdims=True)
    if begin:
        left_copy.wait()
    for r in range(rows):
        pltpu.make_async_copy(out_stage.at[r], out.at[r], out_sem.at[r]).wait()


def product(shape, dtype, window, names, arrays, carried=None, own=None, half_index=None, final=False):
    rows, slots, block = shape
    span = rows * block
    begin = carried is None
    wide = (window + 1) * block
    any_spec = pl.BlockSpec(memory_space=pl.ANY)
    smem_spec = pl.BlockSpec(memory_space=pltpu.SMEM)
    if begin:
        operands, in_specs = [own], [any_spec]
    else:
        operands, in_specs = list(carried), [any_spec, smem_spec, any_spec]
    operands += arrays
    in_specs += [any_spec] * len(arrays)
    tile_shape = (rows, slots, block, block)
    out_shape = [jax.ShapeDtypeStruct(tile_shape, dtype if final else jnp.float32)]
    out_specs = [any_spec]
    if begin:
        out_shape += [
            jax.ShapeDtypeStruct((span, wide), dtype),
            jax.ShapeDtypeStruct((rows, slots), jnp.int32),
        ]
        out_specs += [any_spec, smem_spec]
    if final:
        out_shape.append(jax.ShapeDtypeStruct((1, block), jnp.float32))
        out_specs.append(pl.BlockSpec(memory_space=pltpu.VMEM))
    half_shape = (rows // 2 * slots + 1, block, block)
    scratch = [
        pltpu.VMEM((span, wide), dtype),
        pltpu.VMEM((2, 2) + half_shape if half_index is None else (2,) + half_shape, dtype),
        pltpu.VMEM((2, span // 2, wide), dtype),
        pltpu.VMEM((span, wide), jnp.float32),
        pltpu.VMEM(tile_shape, dtype if final else jnp.float32),
        pltpu.VMEM((3, 16, block), jnp.int32),
        pltpu.SMEM((3, 16, block), jnp.int32),
    ]
    if not begin:
        scratch.append(pltpu.VMEM(tile_shape, jnp.float32))
    scratch += [
        pltpu.SemaphoreType.DMA((2,)),
        pltpu.SemaphoreType.DMA,
        pltpu.SemaphoreType.DMA,
        pltpu.SemaphoreType.DMA((3,)),
        pltpu.SemaphoreType.DMA((rows,)),
    ]
    count = len(names) * (1 if half_index is None else 0.5) + begin
    return pl.pallas_call(
        functools.partial(body, rows, slots, block, window, names, half_index, begin, final),
        out_shape=out_shape,
        in_specs=in_specs,
        out_specs=out_specs,
        scratch_shapes=scratch,
        compiler_params=pltpu.CompilerParams(vmem_limit_bytes=VMEM_LIMIT),
        cost_estimate=pl.CostEstimate(
            flops=int(2 * span * span * window * block * count),
            bytes_accessed=int(2 * span * slots * block * (count + 4)),
            transcendentals=0,
        ),
    )(*operands)


def shards(tiles, columns):
    rows, slots, block, _ = tiles.shape
    devices = lax.axis_size(AXES)
    hops = (REACH + rows - 1) // rows
    assert hops == 3 and rows == 4 and devices % 4 == 0 and devices > 8
    window = (2 * hops + 1) * rows
    multiply = functools.partial(product, (rows, slots, block), tiles.dtype, window)

    payload = pack(tiles, columns, devices)
    first = receive(payload, FIRST)
    beside = receive(payload, PARTNER)
    later, beside = lax.optimization_barrier((payload, beside))
    second = receive(later, SECOND)
    total, left, own_pos = multiply(("beside",), [beside], own=payload)
    relays = [receive(first[h], RELAY_FROM) for h in range(2)]
    first_beside = receive(first, PARTNER)
    second_beside = receive(second, PARTNER)
    total = multiply(
        ("first", "second", "mixed"), [first, second, first_beside, second_beside],
        (left, own_pos, total),
    )[0]
    for h in range(2):
        relay_beside = receive(relays[h], PARTNER)
        result = multiply(
            ("relay", "relay_beside"), [relays[h], relay_beside], (left, own_pos, total),
            half_index=h, final=h == 1,
        )
        total = result[0]
    trace = jnp.sum(total_over_devices(result[1]))
    return total, trace / (rows * devices * block)


def solution(mesh):
    return jax.shard_map(
        shards,
        mesh=mesh,
        in_specs=(P(AXES, None, None, None), P(AXES, None)),
        out_specs=(P(AXES, None, None, None), P()),
        check_vma=False,
    )
```

```python
import functools

import jax
import jax.numpy as jnp
from jax import lax
from jax.experimental import pallas as pl
from jax.experimental.pallas import tpu as pltpu
from jax.sharding import PartitionSpec as P

REACH = 12
AXES = ("blk", "grp")
VMEM_LIMIT = 48 * 1024 * 1024

FIRST = (2, 3, -3, -2)
SECOND = (-3, 2, -2, 3)
RELAY_FROM = (2, -5, 5, -2)
PARTNER = (1, -1, 1, -1)
RELAY = tuple(RELAY_FROM[m] + FIRST[(m + RELAY_FROM[m]) % 4] for m in range(4))


def across(table):
    return tuple(PARTNER[m] + table[m ^ 1] for m in range(4))


USE_SECOND = tuple(int(abs(offset) > 3) for offset in across(FIRST))
MIXED = tuple(
    second if use else first
    for first, second, use in zip(across(FIRST), across(SECOND), USE_SECOND)
)
OFFSETS = {
    "beside": PARTNER,
    "first": FIRST,
    "second": SECOND,
    "mixed": MIXED,
    "relay": RELAY,
    "relay_beside": across(RELAY),
}
COUNTS = {"beside": (2, 0, 2, 0), "first": (2, 0, 2, 0), "second": (2, 2, 0, 0), "mixed": (2, 2, 0, 0)}
OUTSIDE = {("first", "mixed"): (0, 2, 2, 0), ("first", "second"): (0, 2, 0, 0)}
CORNER = {1: -3, 2: 3}


def receive(shard, offsets, kinds=range(4)):
    size = lax.axis_size(AXES)
    pairs = [((d + offsets[d % 4]) % size, d) for d in range(size) if d % 4 in kinds]
    return lax.ppermute(shard, AXES, pairs)


def total_over_devices(value):
    size = lax.axis_size(AXES)
    assert size & (size - 1) == 0
    step = 1
    while step < size:
        value = value + lax.ppermute(value, AXES, [(d, d ^ step) for d in range(size)])
        step *= 2
    return value


def pick(table, kind):
    value = jnp.int32(table[3])
    for m in range(3):
        value = jnp.where(kind == m, jnp.int32(table[m]), value)
    return value


def aligned(index, unit):
    return pl.multiple_of(index * unit, unit)


class Sizes:
    def __init__(self, shape, devices):
        self.rows, self.slots, self.block, _ = shape
        self.hops = (REACH + self.rows - 1) // self.rows
        self.chunks = 2 * self.hops + 1
        self.window = self.chunks * self.rows
        self.span = self.rows * self.block
        self.wide = (self.window + 1) * self.block
        self.all_rows = self.rows * devices

    def start(self, device):
        start = (device - self.hops) * self.rows
        return jnp.where(start < 0, start + self.all_rows, start)

    def position(self, column, start):
        place = column - start
        place = jnp.where(place < 0, place + self.all_rows, place)
        place = jnp.where(column < 0, self.window, place)
        return jnp.minimum(place, self.window)


def scatter(z, dense, top, source, columns, start, save=None):
    for r in range(z.rows):
        def one(u, carry):
            place = z.position(columns[r, u], start)
            if save is not None:
                save[r, u] = place
            dense[top + r * z.block:top + (r + 1) * z.block, pl.ds(aligned(place, z.block), z.block)] = source[r, u]
            return carry
        lax.fori_loop(0, z.slots, one, 0, unroll=4)


def emit(z, total, positions, stage, out, sems, prev=None):
    for r in range(z.rows):
        def one(s, carry):
            value = total[r * z.block:(r + 1) * z.block, pl.ds(aligned(positions[r, s], z.block), z.block)]
            if prev is not None:
                value = value + prev[r, s]
            stage[r, s] = value.astype(stage.dtype)
            return carry
        lax.fori_loop(0, z.slots, one, 0, unroll=4)
        pltpu.make_async_copy(stage.at[r], out.at[r], sems.at[r]).start()
    for r in range(z.rows):
        pltpu.make_async_copy(stage.at[r], out.at[r], sems.at[r]).wait()


def add_trace(trace, weight, one, other):
    value = jnp.dot(one, other, preferred_element_type=jnp.float32)
    on = lax.broadcasted_iota(jnp.int32, value.shape, 0) == lax.broadcasted_iota(jnp.int32, value.shape, 1)
    diagonal = jnp.sum(jnp.where(on, value, 0.0), axis=0, keepdims=True)
    trace[:, :value.shape[1]] += weight.astype(jnp.float32) * diagonal


def own_body(z, own, columns, out, left_out, corner_out, positions, trace, stage, left, total, out_stage,
             in_sem, left_sem, corner_sem, out_sems):
    device = lax.axis_index(AXES)
    kind = device % 4
    copy = pltpu.make_async_copy(own, stage, in_sem)
    copy.start()
    left[...] = jnp.zeros_like(left)
    total[:, z.window * z.block:] = jnp.zeros((z.span, z.block), jnp.float32)
    copy.wait()
    scatter(z, left, 0, stage, columns, z.start(device), positions)
    left_copy = pltpu.make_async_copy(left, left_out, left_sem)
    left_copy.start()
    half = z.span // 2

    def corner(start):
        def go(rows, cols):
            copy = pltpu.make_async_copy(left.at[rows, cols], corner_out, corner_sem)
            copy.start() if start else copy.wait()
        pl.when(kind == 1)(lambda: go(pl.ds(0, half), pl.ds(0, z.span)))
        pl.when(kind != 1)(
            lambda: go(pl.ds(half, half), pl.ds((z.chunks - 1) * z.span, z.span))
        )

    corner(True)
    middle = slice(z.hops * z.span, (z.hops + 1) * z.span)

    def multiply(n, carry):
        cols = pl.ds(aligned(n, z.span), z.span)
        total[:, cols] = jnp.dot(left[:, middle], left[:, cols], preferred_element_type=jnp.float32)
        return carry

    lax.fori_loop(0, z.chunks, multiply, 0)
    trace[...] = jnp.zeros_like(trace)
    add_trace(trace, jnp.float32(1), left[:, middle], left[:, middle])
    emit(z, total, positions, out_stage, out, out_sems)
    corner(False)
    left_copy.wait()


def near_body(z, names, left_in, positions, prev, trace_in, corner, *refs):
    refs = list(refs)
    take = lambda count: [refs.pop(0) for _ in range(count)]
    columns = dict(zip(names, take(len(names))))
    sources = {name: take(2 if name == "mixed" else 1) for name in names}
    out, relay_left, trace = take(3)
    left, stage, right, total, out_stage, prev_stage = take(6)
    left_sem, in_sem, prev_sem, relay_sem, out_sems = take(5)
    device = lax.axis_index(AXES)
    kind = device % 4
    start = z.start(device)
    place = {name: pick(table, kind) + z.hops for name, table in OFFSETS.items()}

    def chunk(n):
        return pl.ds(aligned(n, z.span), z.span)

    def fetch(index, begin):
        def go(source):
            copy = pltpu.make_async_copy(source, stage.at[index % 2], in_sem.at[index % 2])
            copy.start() if begin else copy.wait()
        source = sources[names[index]]
        if len(source) == 1:
            go(source[0])
        else:
            use_second = pick(USE_SECOND, kind)
            pl.when(use_second == 0)(lambda: go(source[0]))
            pl.when(use_second != 0)(lambda: go(source[1]))

    left_copy = pltpu.make_async_copy(left_in, left, left_sem)
    left_copy.start()
    fetch(0, True)
    fetch(1, True)
    prev_copy = pltpu.make_async_copy(prev, prev_stage, prev_sem)
    prev_copy.start()
    total[...] = jnp.zeros_like(total)
    trace[...] = trace_in[...]
    left_copy.wait()
    relay_copies = []
    for index, name in enumerate(("relay", "relay_beside")):
        copy = pltpu.make_async_copy(
            left.at[:, chunk(place[name])], relay_left.at[:, pl.ds(index * z.span, z.span)], relay_sem.at[index]
        )
        copy.start()
        relay_copies.append(copy)
    dense_of = {}
    for index, name in enumerate(names):
        dense = right.at[index]
        dense_of[name] = dense
        spot = place[name]
        dense[...] = jnp.zeros_like(dense)
        fetch(index, False)
        scatter(z, dense, 0, stage.at[index % 2], columns[name], start)
        if index + 2 < len(names):
            fetch(index + 2, True)

        def multiply(n, carry):
            total[:, chunk(n)] += jnp.dot(
                left[:, chunk(spot)], dense[:, chunk(n)], preferred_element_type=jnp.float32
            )
            return carry

        lax.fori_loop(jnp.maximum(0, spot - z.hops), jnp.minimum(z.chunks, spot + z.hops + 1), multiply, 0)
        weight = pick(COUNTS[name], kind)
        pl.when(weight != 0)(
            lambda: add_trace(trace, weight, left[:, chunk(spot)], dense[:, chunk(z.hops)])
        )
    for (one, other), table in OUTSIDE.items():
        weight = pick(table, kind)
        pl.when(weight != 0)(lambda: add_trace(
            trace, weight, dense_of[one][:, chunk(place[other])], dense_of[other][:, chunk(place[one])]
        ))
    half = z.span // 2
    last = (z.chunks - 1) * z.span
    pl.when(kind == 1)(lambda: add_trace(trace, jnp.float32(2), left[:, half:z.span], corner[...]))
    pl.when(kind == 2)(
        lambda: add_trace(trace, jnp.float32(2), left[:half, last:last + half], corner[:, :half])
    )
    prev_copy.wait()
    emit(z, total, positions, out_stage, out, out_sems, prev_stage)
    for copy in relay_copies:
        copy.wait()


def last_body(z, left_in, positions, prev, columns_a, columns_b, source_a, source_b, out,
              left, stage, right, total, out_stage, prev_stage, left_sem, in_sem, prev_sem, out_sems):
    device = lax.axis_index(AXES)
    kind = device % 4
    start = z.start(device)
    copies = [
        pltpu.make_async_copy(source_a, stage.at[0], in_sem.at[0]),
        pltpu.make_async_copy(source_b, stage.at[1], in_sem.at[1]),
        pltpu.make_async_copy(left_in, left, left_sem),
        pltpu.make_async_copy(prev, prev_stage, prev_sem),
    ]
    for copy in copies:
        copy.start()
    place_a = pick(OFFSETS["relay"], kind) + z.hops
    place_b = pick(OFFSETS["relay_beside"], kind) + z.hops
    low = jnp.maximum(0, jnp.minimum(place_a, place_b) - z.hops)
    high = jnp.minimum(z.chunks, jnp.maximum(place_a, place_b) + z.hops + 1)

    def chunk(n):
        return pl.ds(aligned(n, z.span), z.span)

    def clear_total(n, carry):
        total[:, chunk(n)] = jnp.zeros((z.span, z.span), jnp.float32)
        return carry

    def clear_right(n, carry):
        right[:, chunk(n)] = jnp.zeros((2 * z.span, z.span), right.dtype)
        return carry

    lax.fori_loop(low, high, clear_right, 0)
    lax.fori_loop(0, low, clear_total, 0)
    lax.fori_loop(high, z.chunks, clear_total, 0)
    total[:, z.window * z.block:] = jnp.zeros((z.span, z.block), jnp.float32)
    copies[0].wait()
    scatter(z, right, 0, stage.at[0], columns_a, start)
    copies[1].wait()
    scatter(z, right, z.span, stage.at[1], columns_b, start)
    copies[2].wait()

    def multiply(n, carry):
        total[:, chunk(n)] = jnp.dot(left[...], right[:, chunk(n)], preferred_element_type=jnp.float32)
        return carry

    lax.fori_loop(low, high, multiply, 0)
    copies[3].wait()
    emit(z, total, positions, out_stage, out, out_sems, prev_stage)


ANY = pl.BlockSpec(memory_space=pl.ANY)
SMEM = pl.BlockSpec(memory_space=pltpu.SMEM)
VMEM = pl.BlockSpec(memory_space=pltpu.VMEM)
DMA = pltpu.SemaphoreType.DMA


def call(z, kernel, operands, in_specs, out_shape, out_specs, scratch, pieces):
    return pl.pallas_call(
        kernel,
        out_shape=out_shape,
        in_specs=in_specs,
        out_specs=out_specs,
        scratch_shapes=scratch,
        compiler_params=pltpu.CompilerParams(vmem_limit_bytes=VMEM_LIMIT),
        cost_estimate=pl.CostEstimate(
            flops=2 * z.span * z.span * z.window * z.block * pieces,
            bytes_accessed=2 * z.span * z.slots * z.block * (pieces + 4),
            transcendentals=0,
        ),
    )(*operands)


def shards(tiles, columns):
    devices = lax.axis_size(AXES)
    z = Sizes(tiles.shape, devices)
    assert z.hops == 3 and z.rows == 4 and devices % 4 == 0 and devices > 8
    dtype = tiles.dtype
    shape = jax.ShapeDtypeStruct
    sums = shape(tiles.shape, jnp.float32)
    line = shape((1, z.span), jnp.float32)
    dense = pltpu.VMEM((z.span, z.wide), dtype)
    total_buffer = pltpu.VMEM((z.span, z.wide), jnp.float32)

    first = receive(tiles, FIRST)
    second = receive(tiles, SECOND)
    column_of = {name: receive(columns, table) for name, table in OFFSETS.items()}
    beside = receive(tiles, PARTNER)

    total, left, corner, positions, trace = call(
        z, functools.partial(own_body, z), [tiles, columns], [ANY, SMEM],
        [
            sums, shape((z.span, z.wide), dtype), shape((z.span // 2, z.span), dtype),
            shape((z.rows, z.slots), jnp.int32), line,
        ],
        [ANY, ANY, ANY, SMEM, VMEM],
        [
            pltpu.VMEM(tiles.shape, dtype), dense, total_buffer, pltpu.VMEM(tiles.shape, jnp.float32),
            DMA, DMA, DMA, DMA((z.rows,)),
        ],
        1,
    )
    corner = receive(corner, (0, CORNER[1], CORNER[2], 0), (1, 2))
    first, second, beside, column_of, corner, total = lax.optimization_barrier(
        (first, second, beside, column_of, corner, total)
    )
    relay = receive(first, RELAY_FROM)
    mixed = [
        receive(first, PARTNER, [m for m in range(4) if not USE_SECOND[m]]),
        receive(second, PARTNER, [m for m in range(4) if USE_SECOND[m]]),
    ]
    names = ("beside", "first", "second", "mixed")
    total, relay_left, trace = call(
        z, functools.partial(near_body, z, names),
        [left, positions, total, trace, corner, *[column_of[name] for name in names], beside, first, second, *mixed],
        [ANY, SMEM, ANY, VMEM, VMEM] + [SMEM] * 4 + [ANY] * 5,
        [sums, shape((z.span, 2 * z.span), dtype), line],
        [ANY, ANY, VMEM],
        [
            dense, pltpu.VMEM((2,) + tiles.shape, dtype), pltpu.VMEM((4, z.span, z.wide), dtype), total_buffer,
            pltpu.VMEM(tiles.shape, jnp.float32), pltpu.VMEM(tiles.shape, jnp.float32),
            DMA, DMA((2,)), DMA, DMA((2,)), DMA((z.rows,)),
        ],
        4,
    )
    relay, total, trace = lax.optimization_barrier((relay, total, trace))
    relay_beside = receive(relay, PARTNER)
    trace = total_over_devices(trace)
    square = call(
        z, functools.partial(last_body, z),
        [
            relay_left, positions, total, column_of["relay"], column_of["relay_beside"], relay, relay_beside,
        ],
        [ANY, SMEM, ANY, SMEM, SMEM, ANY, ANY],
        [shape(tiles.shape, dtype)],
        [ANY],
        [
            pltpu.VMEM((z.span, 2 * z.span), dtype), pltpu.VMEM((2,) + tiles.shape, dtype),
            pltpu.VMEM((2 * z.span, z.wide), dtype), total_buffer,
            pltpu.VMEM(tiles.shape, dtype), pltpu.VMEM(tiles.shape, jnp.float32),
            DMA, DMA((2,)), DMA, DMA((z.rows,)),
        ],
        2,
    )[0]
    return square, jnp.sum(trace) / (z.all_rows * z.block)


def solution(mesh):
    return jax.shard_map(
        shards,
        mesh=mesh,
        in_specs=(P(AXES, None, None, None), P(AXES, None)),
        out_specs=(P(AXES, None, None, None), P()),
        check_vma=False,
    )
```

```python
import functools

import jax
import jax.numpy as jnp
from jax import lax
from jax.experimental import pallas as pl
from jax.experimental.pallas import tpu as pltpu
from jax.sharding import PartitionSpec as P

REACH = 12
AXES = ("blk", "grp")
VMEM_LIMIT = 48 * 1024 * 1024
WHOLE_VMEM = 60 * 1024 * 1024
EMPTY = 64

FIRST = (2, 3, -3, -2)
SECOND = (-3, 2, -2, 3)
RELAY_FROM = (2, -5, 5, -2)
PARTNER = (1, -1, 1, -1)
RELAY = tuple(RELAY_FROM[m] + FIRST[(m + RELAY_FROM[m]) % 4] for m in range(4))


def across(table):
    return tuple(PARTNER[m] + table[m ^ 1] for m in range(4))


USE_SECOND = tuple(int(abs(offset) > 3) for offset in across(FIRST))
MIXED = tuple(
    second if use else first
    for first, second, use in zip(across(FIRST), across(SECOND), USE_SECOND)
)
OFFSETS = {
    "beside": PARTNER,
    "first": FIRST,
    "second": SECOND,
    "mixed": MIXED,
    "relay": RELAY,
    "relay_beside": across(RELAY),
}
COUNTS = {"beside": (2, 0, 2, 0), "first": (2, 0, 2, 0), "second": (2, 2, 0, 0), "mixed": (2, 2, 0, 0)}
OUTSIDE = {("first", "mixed"): (0, 2, 2, 0), ("first", "second"): (0, 2, 0, 0)}
CORNER = {1: -3, 2: 3}


def receive(shard, offsets, kinds=range(4)):
    size = lax.axis_size(AXES)
    pairs = [((d + offsets[d % 4]) % size, d) for d in range(size) if d % 4 in kinds]
    return lax.ppermute(shard, AXES, pairs)


def exchange(value, step):
    size = lax.axis_size(AXES)
    return value + lax.ppermute(value, AXES, [(d, d ^ step) for d in range(size)])


def pick(table, kind):
    value = jnp.int32(table[3])
    for m in range(3):
        value = jnp.where(kind == m, jnp.int32(table[m]), value)
    return value


def aligned(index, unit):
    return pl.multiple_of(index * unit, unit)


class Sizes:
    def __init__(self, shape, devices):
        self.rows, self.slots, self.block, _ = shape
        self.hops = (REACH + self.rows - 1) // self.rows
        self.chunks = 2 * self.hops + 1
        self.window = self.chunks * self.rows
        self.span = self.rows * self.block
        self.wide = (self.window + 1) * self.block
        self.all_rows = self.rows * devices

    def start(self, device):
        start = (device - self.hops) * self.rows
        return jnp.where(start < 0, start + self.all_rows, start)

    def position(self, column, start):
        place = column - start
        place = jnp.where(place < 0, place + self.all_rows, place)
        place = jnp.where(column < 0, self.window, place)
        return jnp.minimum(place, self.window)


def scatter(z, dense, top, source, place):
    for r in range(z.rows):
        def one(u, carry):
            column = pl.ds(aligned(place(r, u), z.block), z.block)
            dense[top + r * z.block:top + (r + 1) * z.block, column] = source[r * z.slots + u]
            return carry
        lax.fori_loop(0, z.slots, one, 0, unroll=4)


def decode(z, offsets, spot, vector, scalars, sem):
    value = offsets[0:16, :].astype(jnp.float32).astype(jnp.int32)
    value = value + spot * z.rows + lax.broadcasted_iota(jnp.int32, value.shape, 0)
    vector[...] = jnp.where((value < 0) | (value > z.window), z.window, value)
    copy = pltpu.make_async_copy(vector, scalars, sem)
    copy.start()
    return copy


def pack_body(z, tiles, columns, out, stage, padded, offsets, in_sems, out_sems):
    copies = []
    for r in range(z.rows):
        rows = pl.ds(r * z.slots, z.slots)
        copies.append((
            pltpu.make_async_copy(tiles.at[r], stage.at[rows], in_sems.at[r]),
            pltpu.make_async_copy(stage.at[rows], out.at[rows], out_sems.at[r]),
        ))
    for copy, _ in copies:
        copy.start()
    padded[...] = jnp.full(padded.shape, -1, jnp.int32)
    padded[:z.rows, :z.slots] = columns[...]
    column = padded[...]
    row = lax.axis_index(AXES) * z.rows + lax.broadcasted_iota(jnp.int32, column.shape, 0)
    offset = column - row
    offset = jnp.where(offset > z.all_rows // 2, offset - z.all_rows, offset)
    offset = jnp.where(offset < -(z.all_rows // 2), offset + z.all_rows, offset)
    offset = jnp.where(column < 0, EMPTY, offset)
    offsets[...] = jnp.zeros_like(offsets)
    offsets[0:16, :] = offset.astype(jnp.float32).astype(offsets.dtype)
    last = pltpu.make_async_copy(offsets, out.at[z.rows * z.slots], out_sems.at[z.rows])
    last.start()
    for load, store in copies:
        load.wait()
        store.start()
    for _, store in copies:
        store.wait()
    last.wait()


def emit(z, total, positions, stage, out, sems, prev=None):
    for r in range(z.rows):
        def one(s, carry):
            value = total[r * z.block:(r + 1) * z.block, pl.ds(aligned(positions[r, s], z.block), z.block)]
            if prev is not None:
                value = value + prev[r, s]
            stage[r, s] = value.astype(stage.dtype)
            return carry
        lax.fori_loop(0, z.slots, one, 0, unroll=4)
        pltpu.make_async_copy(stage.at[r], out.at[r], sems.at[r]).start()
    for r in range(z.rows):
        pltpu.make_async_copy(stage.at[r], out.at[r], sems.at[r]).wait()


def add_trace(trace, weight, one, other):
    value = jnp.dot(one, other, preferred_element_type=jnp.float32)
    on = lax.broadcasted_iota(jnp.int32, value.shape, 0) == lax.broadcasted_iota(jnp.int32, value.shape, 1)
    diagonal = jnp.sum(jnp.where(on, value, 0.0), axis=0, keepdims=True)
    trace[:, :value.shape[1]] += weight.astype(jnp.float32) * diagonal


def own_body(z, own, columns, out, left_out, corner_out, positions, trace, stage, left, total, out_stage,
             in_sem, left_sem, corner_sem, out_sems):
    device = lax.axis_index(AXES)
    kind = device % 4
    copy = pltpu.make_async_copy(own, stage, in_sem)
    copy.start()
    left[...] = jnp.zeros_like(left)
    total[:, z.window * z.block:] = jnp.zeros((z.span, z.block), jnp.float32)
    copy.wait()
    start = z.start(device)
    for r in range(z.rows):
        def place(u, carry):
            column = z.position(columns[r, u], start)
            positions[r, u] = column
            left[r * z.block:(r + 1) * z.block, pl.ds(aligned(column, z.block), z.block)] = stage[r, u]
            return carry
        lax.fori_loop(0, z.slots, place, 0, unroll=4)
    left_copy = pltpu.make_async_copy(left, left_out, left_sem)
    left_copy.start()
    half = z.span // 2

    def corner(start):
        def go(rows, cols):
            copy = pltpu.make_async_copy(left.at[rows, cols], corner_out, corner_sem)
            copy.start() if start else copy.wait()
        pl.when(kind == 1)(lambda: go(pl.ds(0, half), pl.ds(0, z.span)))
        pl.when(kind != 1)(
            lambda: go(pl.ds(half, half), pl.ds((z.chunks - 1) * z.span, z.span))
        )

    corner(True)
    middle = slice(z.hops * z.span, (z.hops + 1) * z.span)

    def multiply(n, carry):
        cols = pl.ds(aligned(n, z.span), z.span)
        total[:, cols] = jnp.dot(left[:, middle], left[:, cols], preferred_element_type=jnp.float32)
        return carry

    lax.fori_loop(0, z.chunks, multiply, 0)
    trace[...] = jnp.zeros_like(trace)
    add_trace(trace, jnp.float32(1), left[:, middle], left[:, middle])
    emit(z, total, positions, out_stage, out, out_sems)
    corner(False)
    left_copy.wait()


def near_body(z, names, left_in, positions, prev, trace_in, *refs):
    refs = list(refs)
    take = lambda count: [refs.pop(0) for _ in range(count)]
    final = "mixed" in names
    corner = take(1)[0] if final else None
    sources = {name: take(2 if name == "mixed" else 1) for name in names}
    out, trace = take(2)
    relay_left = take(1)[0] if final else None
    left, stage, right, total, out_stage, prev_stage, vector, scalars = take(8)
    left_sem, in_sem, prev_sem, place_sem, relay_sem, out_sems = take(6)
    device = lax.axis_index(AXES)
    kind = device % 4
    place = {name: pick(table, kind) + z.hops for name, table in OFFSETS.items()}

    def chunk(n):
        return pl.ds(aligned(n, z.span), z.span)

    def fetch(index, begin):
        def go(source):
            copy = pltpu.make_async_copy(source, stage.at[index % 2], in_sem.at[index % 2])
            copy.start() if begin else copy.wait()
        source = sources[names[index]]
        if len(source) == 1:
            go(source[0])
        else:
            use_second = pick(USE_SECOND, kind)
            pl.when(use_second == 0)(lambda: go(source[0]))
            pl.when(use_second != 0)(lambda: go(source[1]))

    left_copy = pltpu.make_async_copy(left_in, left, left_sem)
    left_copy.start()
    for index in range(min(2, len(names))):
        fetch(index, True)
    prev_copy = pltpu.make_async_copy(prev, prev_stage, prev_sem)
    prev_copy.start()
    total[...] = jnp.zeros_like(total)
    trace[...] = trace_in[...]
    left_copy.wait()
    relay_copies = []
    if final:
        for index, name in enumerate(("relay", "relay_beside")):
            copy = pltpu.make_async_copy(
                left.at[:, chunk(place[name])], relay_left.at[:, pl.ds(index * z.span, z.span)],
                relay_sem.at[index],
            )
            copy.start()
            relay_copies.append(copy)
    dense_of = {}
    for index, name in enumerate(names):
        dense = right.at[index]
        dense_of[name] = dense
        spot = place[name]
        slot = index % 2
        fetch(index, False)
        decoding = decode(
            z, stage.at[slot, z.rows * z.slots], spot, vector.at[slot], scalars.at[slot], place_sem.at[slot]
        )
        dense[...] = jnp.zeros_like(dense)
        decoding.wait()
        scatter(z, dense, 0, stage.at[slot], lambda r, u: scalars[slot, r, u])
        if index + 2 < len(names):
            fetch(index + 2, True)

        def multiply(n, carry):
            total[:, chunk(n)] += jnp.dot(
                left[:, chunk(spot)], dense[:, chunk(n)], preferred_element_type=jnp.float32
            )
            return carry

        lax.fori_loop(jnp.maximum(0, spot - z.hops), jnp.minimum(z.chunks, spot + z.hops + 1), multiply, 0)
        weight = pick(COUNTS[name], kind)
        pl.when(weight != 0)(
            lambda: add_trace(trace, weight, left[:, chunk(spot)], dense[:, chunk(z.hops)])
        )
    if final:
        for (one, other), table in OUTSIDE.items():
            weight = pick(table, kind)
            pl.when(weight != 0)(lambda: add_trace(
                trace, weight, dense_of[one][:, chunk(place[other])], dense_of[other][:, chunk(place[one])]
            ))
        half = z.span // 2
        last = (z.chunks - 1) * z.span
        pl.when(kind == 1)(lambda: add_trace(trace, jnp.float32(2), left[:, half:z.span], corner[...]))
        pl.when(kind == 2)(
            lambda: add_trace(trace, jnp.float32(2), left[:half, last:last + half], corner[:, :half])
        )
    prev_copy.wait()
    emit(z, total, positions, out_stage, out, out_sems, prev_stage)
    for copy in relay_copies:
        copy.wait()


def last_body(z, left_in, positions, prev, source_a, source_b, out, left, stage, right, total, out_stage,
              prev_stage, vector, scalars, left_sem, in_sem, prev_sem, place_sem, out_sems):
    kind = lax.axis_index(AXES) % 4
    copies = [
        pltpu.make_async_copy(source_a, stage.at[0], in_sem.at[0]),
        pltpu.make_async_copy(source_b, stage.at[1], in_sem.at[1]),
        pltpu.make_async_copy(left_in, left, left_sem),
        pltpu.make_async_copy(prev, prev_stage, prev_sem),
    ]
    for copy in copies:
        copy.start()
    places = [pick(OFFSETS[name], kind) + z.hops for name in ("relay", "relay_beside")]
    low = jnp.maximum(0, jnp.minimum(*places) - z.hops)
    high = jnp.minimum(z.chunks, jnp.maximum(*places) + z.hops + 1)

    def chunk(n):
        return pl.ds(aligned(n, z.span), z.span)

    def clear_total(n, carry):
        total[:, chunk(n)] = jnp.zeros((z.span, z.span), jnp.float32)
        return carry

    def clear_right(n, carry):
        right[:, chunk(n)] = jnp.zeros((2 * z.span, z.span), right.dtype)
        return carry

    lax.fori_loop(0, low, clear_total, 0)
    lax.fori_loop(high, z.chunks, clear_total, 0)
    total[:, z.window * z.block:] = jnp.zeros((z.span, z.block), jnp.float32)
    decodings = []
    for index in range(2):
        copies[index].wait()
        decodings.append(decode(
            z, stage.at[index, z.rows * z.slots], places[index], vector.at[index], scalars.at[index],
            place_sem.at[index],
        ))
    lax.fori_loop(low, high, clear_right, 0)
    for index in range(2):
        decodings[index].wait()
        scatter(z, right, index * z.span, stage.at[index], lambda r, u: scalars[index, r, u])
    copies[2].wait()

    def multiply(n, carry):
        total[:, chunk(n)] = jnp.dot(left[...], right[:, chunk(n)], preferred_element_type=jnp.float32)
        return carry

    lax.fori_loop(low, high, multiply, 0)
    copies[3].wait()
    emit(z, total, positions, out_stage, out, out_sems, prev_stage)


ANY = pl.BlockSpec(memory_space=pl.ANY)
SMEM = pl.BlockSpec(memory_space=pltpu.SMEM)
VMEM = pl.BlockSpec(memory_space=pltpu.VMEM)
DMA = pltpu.SemaphoreType.DMA


def call(z, kernel, operands, in_specs, out_shape, out_specs, scratch, pieces, limit=VMEM_LIMIT):
    return pl.pallas_call(
        kernel,
        out_shape=out_shape,
        in_specs=in_specs,
        out_specs=out_specs,
        scratch_shapes=scratch,
        compiler_params=pltpu.CompilerParams(vmem_limit_bytes=limit),
        cost_estimate=pl.CostEstimate(
            flops=2 * z.span * z.span * z.window * z.block * pieces,
            bytes_accessed=2 * z.span * z.slots * z.block * (pieces + 4),
            transcendentals=0,
        ),
    )(*operands)


def shards(tiles, columns):
    devices = lax.axis_size(AXES)
    z = Sizes(tiles.shape, devices)
    assert z.hops == 3 and z.rows == 4 and devices % 4 == 0 and devices > 8
    dtype = tiles.dtype
    shape = jax.ShapeDtypeStruct
    sums = shape(tiles.shape, jnp.float32)
    line = shape((1, z.span), jnp.float32)
    dense = pltpu.VMEM((z.span, z.wide), dtype)
    total_buffer = pltpu.VMEM((z.span, z.wide), jnp.float32)

    payload_shape = (z.rows * z.slots + 1, z.block, z.block)
    places = [pltpu.VMEM((2, 16, z.block), jnp.int32), pltpu.SMEM((2, 16, z.block), jnp.int32)]

    payload = call(
        z, functools.partial(pack_body, z), [tiles, columns], [ANY, VMEM],
        shape(payload_shape, dtype), ANY,
        [
            pltpu.VMEM((z.rows * z.slots, z.block, z.block), dtype), pltpu.VMEM((16, z.block), jnp.int32),
            pltpu.VMEM((z.block, z.block), dtype), DMA((z.rows,)), DMA((z.rows + 1,)),
        ],
        0, WHOLE_VMEM,
    )
    first = receive(payload, FIRST)
    second = receive(payload, SECOND)
    beside = receive(payload, PARTNER)

    total, left, corner, positions, trace = call(
        z, functools.partial(own_body, z), [tiles, columns], [ANY, SMEM],
        [
            sums, shape((z.span, z.wide), dtype), shape((z.span // 2, z.span), dtype),
            shape((z.rows, z.slots), jnp.int32), line,
        ],
        [ANY, ANY, ANY, SMEM, VMEM],
        [
            pltpu.VMEM(tiles.shape, dtype), dense, total_buffer, pltpu.VMEM(tiles.shape, jnp.float32),
            DMA, DMA, DMA, DMA((z.rows,)),
        ],
        1,
    )
    corner = receive(corner, (0, CORNER[1], CORNER[2], 0), (1, 2))

    def near(names, arrays, total, trace):
        final = "mixed" in names
        extra = [shape((z.span, 2 * z.span), dtype)] if final else []
        return call(
            z, functools.partial(near_body, z, names),
            [left, positions, total, trace] + ([corner] if final else []) + arrays,
            [ANY, SMEM, ANY, VMEM] + [VMEM] * final + [ANY] * len(arrays),
            [sums, line] + extra,
            [ANY, VMEM] + [ANY] * len(extra),
            [
                dense, pltpu.VMEM((2,) + payload_shape, dtype),
                pltpu.VMEM((len(names), z.span, z.wide), dtype), total_buffer,
                pltpu.VMEM(tiles.shape, jnp.float32), pltpu.VMEM(tiles.shape, jnp.float32), *places,
                DMA, DMA((2,)), DMA, DMA((2,)), DMA((2,)), DMA((z.rows,)),
            ],
            len(names),
        )

    total, trace = near(("beside",), [beside], total, trace)
    first, second, total, trace = lax.optimization_barrier((first, second, total, trace))
    relay = receive(first, RELAY_FROM)
    mixed = [
        receive(first, PARTNER, [m for m in range(4) if not USE_SECOND[m]]),
        receive(second, PARTNER, [m for m in range(4) if USE_SECOND[m]]),
    ]
    total, trace, relay_left = near(("first", "second", "mixed"), [first, second, *mixed], total, trace)
    assert devices & (devices - 1) == 0
    steps = [1 << bit for bit in range(devices.bit_length() - 1)]
    for step in steps[:1] + steps[3:]:
        trace = exchange(trace, step)
    relay, total, trace = lax.optimization_barrier((relay, total, trace))
    relay_beside = receive(relay, PARTNER)
    trace = exchange(trace, steps[2])
    relay_beside, trace = lax.optimization_barrier((relay_beside, trace))
    trace = exchange(trace, steps[1])
    square = call(
        z, functools.partial(last_body, z), [relay_left, positions, total, relay, relay_beside],
        [ANY, SMEM, ANY, ANY, ANY],
        [shape(tiles.shape, dtype)],
        [ANY],
        [
            pltpu.VMEM((z.span, 2 * z.span), dtype), pltpu.VMEM((2,) + payload_shape, dtype),
            pltpu.VMEM((2 * z.span, z.wide), dtype), total_buffer,
            pltpu.VMEM(tiles.shape, dtype), pltpu.VMEM(tiles.shape, jnp.float32), *places,
            DMA, DMA((2,)), DMA, DMA((2,)), DMA((z.rows,)),
        ],
        2, WHOLE_VMEM,
    )[0]
    return square, jnp.sum(trace) / (z.all_rows * z.block)


def solution(mesh):
    return jax.shard_map(
        shards,
        mesh=mesh,
        in_specs=(P(AXES, None, None, None), P(AXES, None)),
        out_specs=(P(AXES, None, None, None), P()),
        check_vma=False,
    )
```

```python
import functools

import jax
import jax.numpy as jnp
from jax import lax
from jax.experimental import pallas as pl
from jax.experimental.pallas import tpu as pltpu
from jax.sharding import PartitionSpec as P

REACH = 12
AXES = ("blk", "grp")
VMEM_LIMIT = 36 * 1024 * 1024
WHOLE_VMEM = 60 * 1024 * 1024
EMPTY = 64

FIRST = (2, 3, -3, -2)
LAST = (-3, 2, -2, 3)
RELAY_FROM = (2, -5, 5, -2)
PARTNER = (1, -1, 1, -1)
RELAY = tuple(RELAY_FROM[m] + FIRST[(m + RELAY_FROM[m]) % 4] for m in range(4))


def across(table):
    return tuple(PARTNER[m] + table[m ^ 1] for m in range(4))


OFFSETS = {
    "beside": PARTNER,
    "first": FIRST,
    "first_beside": across(FIRST),
    "relay": RELAY,
    "relay_beside": across(RELAY),
    "last": LAST,
    "last_beside": across(LAST),
}
NEEDED = {name: tuple(int(abs(offset) <= 3) for offset in table) for name, table in OFFSETS.items()}
COUNTS = {
    "beside": (2, 0, 0, 2),
    "first": (2, 2, 2, 2),
    "first_beside": (0, 2, 0, 0),
    "relay": (2, 0, 2, 0),
    "relay_beside": (0, 2, 2, 0),
}
LOWER, UPPER = 0, 3


def receive(shard, offsets, kinds=range(4)):
    size = lax.axis_size(AXES)
    pairs = [((d + offsets[d % 4]) % size, d) for d in range(size) if d % 4 in kinds]
    return lax.ppermute(shard, AXES, pairs)


def exchange(value, step):
    size = lax.axis_size(AXES)
    return value + lax.ppermute(value, AXES, [(d, d ^ step) for d in range(size)])


def pick(table, kind):
    value = jnp.int32(table[3])
    for m in range(3):
        value = jnp.where(kind == m, jnp.int32(table[m]), value)
    return value


def aligned(index, unit):
    return pl.multiple_of(index * unit, unit)


class Sizes:
    def __init__(self, shape, devices):
        self.rows, self.slots, self.block, _ = shape
        self.hops = (REACH + self.rows - 1) // self.rows
        self.chunks = 2 * self.hops + 1
        self.window = self.chunks * self.rows
        self.span = self.rows * self.block
        self.wide = (self.window + 1) * self.block
        self.all_rows = self.rows * devices

    def start(self, device):
        start = (device - self.hops) * self.rows
        return jnp.where(start < 0, start + self.all_rows, start)

    def position(self, column, start):
        place = column - start
        place = jnp.where(place < 0, place + self.all_rows, place)
        place = jnp.where(column < 0, self.window, place)
        return jnp.minimum(place, self.window)


def scatter(z, dense, top, source, place):
    for r in range(z.rows):
        def one(u, carry):
            column = pl.ds(aligned(place(r, u), z.block), z.block)
            dense[top + r * z.block:top + (r + 1) * z.block, column] = source[r * z.slots + u]
            return carry
        lax.fori_loop(0, z.slots, one, 0, unroll=4)


def decode(z, offsets, spot, vector, scalars, sem):
    value = offsets[0:16, :].astype(jnp.float32).astype(jnp.int32)
    value = value + spot * z.rows + lax.broadcasted_iota(jnp.int32, value.shape, 0)
    vector[...] = jnp.where((value < 0) | (value > z.window), z.window, value)
    copy = pltpu.make_async_copy(vector, scalars, sem)
    copy.start()
    return copy


def pack_body(z, tiles, columns, out, stage, padded, offsets, in_sems, out_sems):
    copies = []
    for r in range(z.rows):
        rows = pl.ds(r * z.slots, z.slots)
        copies.append((
            pltpu.make_async_copy(tiles.at[r], stage.at[rows], in_sems.at[r]),
            pltpu.make_async_copy(stage.at[rows], out.at[rows], out_sems.at[r]),
        ))
    for copy, _ in copies:
        copy.start()
    padded[...] = jnp.full(padded.shape, -1, jnp.int32)
    padded[:z.rows, :z.slots] = columns[...]
    column = padded[...]
    row = lax.axis_index(AXES) * z.rows + lax.broadcasted_iota(jnp.int32, column.shape, 0)
    offset = column - row
    offset = jnp.where(offset > z.all_rows // 2, offset - z.all_rows, offset)
    offset = jnp.where(offset < -(z.all_rows // 2), offset + z.all_rows, offset)
    offset = jnp.where(column < 0, EMPTY, offset)
    offsets[...] = jnp.zeros_like(offsets)
    offsets[0:16, :] = offset.astype(jnp.float32).astype(offsets.dtype)
    last = pltpu.make_async_copy(offsets, out.at[z.rows * z.slots], out_sems.at[z.rows])
    last.start()
    for load, store in copies:
        load.wait()
        store.start()
    for _, store in copies:
        store.wait()
    last.wait()


def emit(z, total, positions, stage, out, sems, prev=None):
    for r in range(z.rows):
        def one(s, carry):
            value = total[r * z.block:(r + 1) * z.block, pl.ds(aligned(positions[r, s], z.block), z.block)]
            if prev is not None:
                value = value + prev[r, s]
            stage[r, s] = value.astype(stage.dtype)
            return carry
        lax.fori_loop(0, z.slots, one, 0, unroll=4)
        pltpu.make_async_copy(stage.at[r], out.at[r], sems.at[r]).start()
    for r in range(z.rows):
        pltpu.make_async_copy(stage.at[r], out.at[r], sems.at[r]).wait()


def add_trace(trace, weight, one, other):
    value = jnp.dot(one, other, preferred_element_type=jnp.float32)
    on = lax.broadcasted_iota(jnp.int32, value.shape, 0) == lax.broadcasted_iota(jnp.int32, value.shape, 1)
    diagonal = jnp.sum(jnp.where(on, value, 0.0), axis=0, keepdims=True)
    trace[:, :value.shape[1]] += weight.astype(jnp.float32) * diagonal


def own_body(z, own, columns, out, left_out, corner_out, positions, trace, stage, left, total, out_stage,
             in_sem, left_sem, corner_sem, out_sems):
    device = lax.axis_index(AXES)
    kind = device % 4
    copy = pltpu.make_async_copy(own, stage, in_sem)
    copy.start()
    left[...] = jnp.zeros_like(left)
    total[:, z.window * z.block:] = jnp.zeros((z.span, z.block), jnp.float32)
    copy.wait()
    start = z.start(device)
    for r in range(z.rows):
        def place(u, carry):
            column = z.position(columns[r, u], start)
            positions[r, u] = column
            left[r * z.block:(r + 1) * z.block, pl.ds(aligned(column, z.block), z.block)] = stage[r, u]
            return carry
        lax.fori_loop(0, z.slots, place, 0, unroll=4)
    left_copy = pltpu.make_async_copy(left, left_out, left_sem)
    left_copy.start()
    half = z.span // 2

    def corner(start):
        def go(rows, cols):
            copy = pltpu.make_async_copy(left.at[rows, cols], corner_out, corner_sem)
            copy.start() if start else copy.wait()
        pl.when(kind == UPPER)(lambda: go(pl.ds(0, half), pl.ds(0, z.span)))
        pl.when(kind != UPPER)(
            lambda: go(pl.ds(half, half), pl.ds((z.chunks - 1) * z.span, z.span))
        )

    corner(True)
    middle = slice(z.hops * z.span, (z.hops + 1) * z.span)

    def multiply(n, carry):
        cols = pl.ds(aligned(n, z.span), z.span)
        total[:, cols] = jnp.dot(left[:, middle], left[:, cols], preferred_element_type=jnp.float32)
        return carry

    lax.fori_loop(0, z.chunks, multiply, 0)
    trace[...] = jnp.zeros_like(trace)
    add_trace(trace, jnp.float32(1), left[:, middle], left[:, middle])
    emit(z, total, positions, out_stage, out, out_sems)
    corner(False)
    left_copy.wait()


def near_body(z, names, hand_on, left_in, positions, prev, trace_in, *refs):
    refs = list(refs)
    take = lambda count: [refs.pop(0) for _ in range(count)]
    corner = None if hand_on else take(1)[0]
    sources = take(len(names))
    out, trace = take(2)
    last_left = take(1)[0] if hand_on else None
    left, stage, right, total, out_stage, prev_stage, vector, scalars = take(8)
    left_sem, in_sem, prev_sem, place_sem, last_sem, out_sems = take(6)
    kind = lax.axis_index(AXES) % 4
    place = {name: pick(table, kind) + z.hops for name, table in OFFSETS.items()}

    def chunk(n):
        return pl.ds(aligned(n, z.span), z.span)

    def fetch(index):
        return pltpu.make_async_copy(sources[index], stage.at[index % 2], in_sem.at[index % 2])

    left_copy = pltpu.make_async_copy(left_in, left, left_sem)
    left_copy.start()
    for index in range(min(2, len(names))):
        fetch(index).start()
    prev_copy = pltpu.make_async_copy(prev, prev_stage, prev_sem)
    prev_copy.start()
    total[...] = jnp.zeros_like(total)
    trace[...] = trace_in[...]
    left_copy.wait()
    last_copies = []
    if hand_on:
        for index, name in enumerate(("last", "last_beside")):
            spot = jnp.clip(place[name], 0, z.chunks - 1)
            copy = pltpu.make_async_copy(
                left.at[:, chunk(spot)], last_left.at[:, pl.ds(index * z.span, z.span)], last_sem.at[index]
            )
            copy.start()
            last_copies.append(copy)
    for index, name in enumerate(names):
        spot = place[name]
        slot = index % 2
        fetch(index).wait()

        def add():
            decoding = decode(
                z, stage.at[slot, z.rows * z.slots], spot, vector.at[slot], scalars.at[slot], place_sem.at[slot]
            )
            right[...] = jnp.zeros_like(right)
            decoding.wait()
            scatter(z, right, 0, stage.at[slot], lambda r, u: scalars[slot, r, u])

            def multiply(n, carry):
                total[:, chunk(n)] += jnp.dot(
                    left[:, chunk(spot)], right[:, chunk(n)], preferred_element_type=jnp.float32
                )
                return carry

            lax.fori_loop(jnp.maximum(0, spot - z.hops), jnp.minimum(z.chunks, spot + z.hops + 1), multiply, 0)
            weight = pick(COUNTS[name], kind)
            pl.when(weight != 0)(
                lambda: add_trace(trace, weight, left[:, chunk(spot)], right[:, chunk(z.hops)])
            )

        if all(NEEDED[name]):
            add()
        else:
            pl.when(pick(NEEDED[name], kind) != 0)(add)
        if index + 2 < len(names):
            fetch(index + 2).start()
    if corner is not None:
        half = z.span // 2
        end = (z.chunks - 1) * z.span
        pl.when(kind == UPPER)(lambda: add_trace(trace, jnp.float32(2), left[:, half:z.span], corner[...]))
        pl.when(kind == LOWER)(
            lambda: add_trace(trace, jnp.float32(2), left[:half, end:end + half], corner[:, :half])
        )
    prev_copy.wait()
    emit(z, total, positions, out_stage, out, out_sems, prev_stage)
    for copy in last_copies:
        copy.wait()


def last_body(z, left_in, positions, prev, source_a, source_b, out, left, stage, right, total, out_stage,
              prev_stage, vector, scalars, left_sem, in_sem, prev_sem, place_sem, out_sems):
    kind = lax.axis_index(AXES) % 4
    copies = [
        pltpu.make_async_copy(source_a, stage.at[0], in_sem.at[0]),
        pltpu.make_async_copy(source_b, stage.at[1], in_sem.at[1]),
        pltpu.make_async_copy(left_in, left, left_sem),
        pltpu.make_async_copy(prev, prev_stage, prev_sem),
    ]
    for copy in copies:
        copy.start()
    place_a = pick(OFFSETS["last"], kind) + z.hops
    place_b = pick(OFFSETS["last_beside"], kind) + z.hops
    needed_b = pick(NEEDED["last_beside"], kind) != 0

    def chunk(n):
        return pl.ds(aligned(n, z.span), z.span)

    def reach(spot):
        return jnp.maximum(0, spot - z.hops), jnp.minimum(z.chunks, spot + z.hops + 1)

    def clear_total(n, carry):
        total[:, chunk(n)] = jnp.zeros((z.span, z.span), jnp.float32)
        return carry

    def prepare(index, spot):
        copies[index].wait()
        decoding = decode(
            z, stage.at[index, z.rows * z.slots], spot, vector.at[index], scalars.at[index], place_sem.at[index]
        )

        def clear(n, carry):
            right[index, :, chunk(n)] = jnp.zeros((z.span, z.span), right.dtype)
            return carry

        lax.fori_loop(*reach(spot), clear, 0)
        decoding.wait()
        scatter(z, right.at[index], 0, stage.at[index], lambda r, u: scalars[index, r, u])

    low, high = reach(place_a)
    lax.fori_loop(0, low, clear_total, 0)
    lax.fori_loop(high, z.chunks, clear_total, 0)
    total[:, z.window * z.block:] = jnp.zeros((z.span, z.block), jnp.float32)
    prepare(0, place_a)
    copies[2].wait()

    def multiply(n, carry):
        total[:, chunk(n)] = jnp.dot(
            left[:, :z.span], right[0, :, chunk(n)], preferred_element_type=jnp.float32
        )
        return carry

    lax.fori_loop(low, high, multiply, 0)

    @pl.when(needed_b)
    def _():
        prepare(1, place_b)

        def multiply_add(n, carry):
            total[:, chunk(n)] += jnp.dot(
                left[:, z.span:], right[1, :, chunk(n)], preferred_element_type=jnp.float32
            )
            return carry

        lax.fori_loop(*reach(place_b), multiply_add, 0)

    @pl.when(jnp.logical_not(needed_b))
    def _():
        copies[1].wait()

    copies[3].wait()
    emit(z, total, positions, out_stage, out, out_sems, prev_stage)


ANY = pl.BlockSpec(memory_space=pl.ANY)
SMEM = pl.BlockSpec(memory_space=pltpu.SMEM)
VMEM = pl.BlockSpec(memory_space=pltpu.VMEM)
DMA = pltpu.SemaphoreType.DMA


def call(z, kernel, operands, in_specs, out_shape, out_specs, scratch, pieces, limit=VMEM_LIMIT):
    return pl.pallas_call(
        kernel,
        out_shape=out_shape,
        in_specs=in_specs,
        out_specs=out_specs,
        scratch_shapes=scratch,
        compiler_params=pltpu.CompilerParams(vmem_limit_bytes=limit),
        cost_estimate=pl.CostEstimate(
            flops=2 * z.span * z.span * z.window * z.block * pieces,
            bytes_accessed=2 * z.span * z.slots * z.block * (pieces + 4),
            transcendentals=0,
        ),
    )(*operands)


def shards(tiles, columns):
    devices = lax.axis_size(AXES)
    z = Sizes(tiles.shape, devices)
    assert z.hops == 3 and z.rows == 4 and devices % 4 == 0 and devices > 8
    dtype = tiles.dtype
    shape = jax.ShapeDtypeStruct
    sums = shape(tiles.shape, jnp.float32)
    line = shape((1, z.span), jnp.float32)
    dense = pltpu.VMEM((z.span, z.wide), dtype)
    total_buffer = pltpu.VMEM((z.span, z.wide), jnp.float32)

    payload_shape = (z.rows * z.slots + 1, z.block, z.block)
    places = [pltpu.VMEM((2, 16, z.block), jnp.int32), pltpu.SMEM((2, 16, z.block), jnp.int32)]

    payload = call(
        z, functools.partial(pack_body, z), [tiles, columns], [ANY, VMEM],
        shape(payload_shape, dtype), ANY,
        [
            pltpu.VMEM((z.rows * z.slots, z.block, z.block), dtype), pltpu.VMEM((16, z.block), jnp.int32),
            pltpu.VMEM((z.block, z.block), dtype), DMA((z.rows,)), DMA((z.rows + 1,)),
        ],
        0, WHOLE_VMEM,
    )
    first = receive(payload, FIRST)
    beside = receive(payload, PARTNER)

    total, left, corner, positions, trace = call(
        z, functools.partial(own_body, z), [tiles, columns], [ANY, SMEM],
        [
            sums, shape((z.span, z.wide), dtype), shape((z.span // 2, z.span), dtype),
            shape((z.rows, z.slots), jnp.int32), line,
        ],
        [ANY, ANY, ANY, SMEM, VMEM],
        [
            pltpu.VMEM(tiles.shape, dtype), dense, total_buffer, pltpu.VMEM(tiles.shape, jnp.float32),
            DMA, DMA, DMA, DMA((z.rows,)),
        ],
        1,
    )
    corner = receive(corner, (3, 0, 0, -3), (LOWER, UPPER))

    def near(names, arrays, total, trace, corner=None):
        hand_on = corner is None
        extra = [shape((z.span, 2 * z.span), dtype)] * hand_on
        return call(
            z, functools.partial(near_body, z, names, hand_on),
            [left, positions, total, trace] + ([] if hand_on else [corner]) + arrays,
            [ANY, SMEM, ANY, VMEM] + [VMEM] * (not hand_on) + [ANY] * len(arrays),
            [sums, line] + extra,
            [ANY, VMEM] + [ANY] * len(extra),
            [
                dense, pltpu.VMEM((2,) + payload_shape, dtype), dense, total_buffer,
                pltpu.VMEM(tiles.shape, jnp.float32), pltpu.VMEM(tiles.shape, jnp.float32), *places,
                DMA, DMA((2,)), DMA, DMA((2,)), DMA((2,)), DMA((z.rows,)),
            ],
            len(names),
        )

    def from_partner(array, name):
        return receive(array, PARTNER, [m for m in range(4) if NEEDED[name][m]])

    first, corner, total = lax.optimization_barrier((first, corner, total))
    relay = receive(first, RELAY_FROM)
    first_beside = from_partner(first, "first_beside")
    total, trace = near(("beside", "first", "first_beside"), [beside, first, first_beside], total, trace, corner)
    relay, payload, total, trace = lax.optimization_barrier((relay, payload, total, trace))
    last = receive(payload, LAST)
    relay_beside = receive(relay, PARTNER)
    total, trace, last_left = near(("relay", "relay_beside"), [relay, relay_beside], total, trace)
    assert devices & (devices - 1) == 0
    steps = [1 << bit for bit in range(devices.bit_length() - 1)]
    for step in steps[:1] + steps[3:]:
        trace = exchange(trace, step)
    last, total, trace = lax.optimization_barrier((last, total, trace))
    last_beside = from_partner(last, "last_beside")
    trace = exchange(trace, steps[2])
    last_beside, trace = lax.optimization_barrier((last_beside, trace))
    trace = exchange(trace, steps[1])
    square = call(
        z, functools.partial(last_body, z), [last_left, positions, total, last, last_beside],
        [ANY, SMEM, ANY, ANY, ANY],
        [shape(tiles.shape, dtype)],
        [ANY],
        [
            pltpu.VMEM((z.span, 2 * z.span), dtype), pltpu.VMEM((2,) + payload_shape, dtype),
            pltpu.VMEM((2, z.span, z.wide), dtype), total_buffer,
            pltpu.VMEM(tiles.shape, dtype), pltpu.VMEM(tiles.shape, jnp.float32), *places,
            DMA, DMA((2,)), DMA, DMA((2,)), DMA((z.rows,)),
        ],
        2,
    )[0]
    return square, jnp.sum(trace) / (z.all_rows * z.block)


def solution(mesh):
    return jax.shard_map(
        shards,
        mesh=mesh,
        in_specs=(P(AXES, None, None, None), P(AXES, None)),
        out_specs=(P(AXES, None, None, None), P()),
        check_vma=False,
    )
```

```python
import functools

import jax
import jax.numpy as jnp
from jax import lax
from jax.experimental import pallas as pl
from jax.experimental.pallas import tpu as pltpu
from jax.sharding import PartitionSpec as P

REACH = 12
AXES = ("blk", "grp")
VMEM_LIMIT = 36 * 1024 * 1024
WHOLE_VMEM = 60 * 1024 * 1024
EMPTY = 64

FIRST = (2, 3, -3, -2)
LAST = (-3, 2, -2, 3)
RELAY_FROM = (2, -5, 5, -2)
PARTNER = (1, -1, 1, -1)
RELAY = tuple(RELAY_FROM[m] + FIRST[(m + RELAY_FROM[m]) % 4] for m in range(4))


def across(table):
    return tuple(PARTNER[m] + table[m ^ 1] for m in range(4))


OFFSETS = {
    "beside": PARTNER,
    "first": FIRST,
    "first_beside": across(FIRST),
    "relay": RELAY,
    "relay_beside": across(RELAY),
    "last": LAST,
    "last_beside": across(LAST),
}
NEEDED = {name: tuple(int(abs(offset) <= 3) for offset in table) for name, table in OFFSETS.items()}
COUNTS = {
    "beside": (2, 0, 0, 2),
    "first": (2, 2, 2, 2),
    "first_beside": (0, 2, 0, 0),
    "relay": (2, 0, 2, 0),
    "relay_beside": (0, 2, 2, 0),
}
LOWER, UPPER = 0, 3


def receive(shard, offsets, kinds=range(4)):
    size = lax.axis_size(AXES)
    pairs = [((d + offsets[d % 4]) % size, d) for d in range(size) if d % 4 in kinds]
    return lax.ppermute(shard, AXES, pairs)


def fetch(value, step):
    return lax.ppermute(value, AXES, [(d, d ^ step) for d in range(lax.axis_size(AXES))])


def exchange(value, step):
    return value + fetch(value, step)


def pick(table, kind):
    value = jnp.int32(table[3])
    for m in range(3):
        value = jnp.where(kind == m, jnp.int32(table[m]), value)
    return value


def aligned(index, unit):
    return pl.multiple_of(index * unit, unit)


class Sizes:
    def __init__(self, shape, devices):
        self.rows, self.slots, self.block, _ = shape
        self.hops = (REACH + self.rows - 1) // self.rows
        self.chunks = 2 * self.hops + 1
        self.window = self.chunks * self.rows
        self.span = self.rows * self.block
        self.wide = (self.window + 1) * self.block
        self.all_rows = self.rows * devices

    def start(self, device):
        start = (device - self.hops) * self.rows
        return jnp.where(start < 0, start + self.all_rows, start)

    def position(self, column, start):
        place = column - start
        place = jnp.where(place < 0, place + self.all_rows, place)
        place = jnp.where(column < 0, self.window, place)
        return jnp.minimum(place, self.window)


def scatter(z, dense, top, source, place):
    half = z.rows // 2
    for r in range(z.rows):
        def one(u, carry):
            column = pl.ds(aligned(place(r, u), z.block), z.block)
            dense[top + r * z.block:top + (r + 1) * z.block, column] = source[r // half, r % half * z.slots + u]
            return carry
        lax.fori_loop(0, z.slots, one, 0, unroll=4)


def decode(z, offsets, spot, vector, scalars, sem):
    value = offsets[0:16, :].astype(jnp.float32).astype(jnp.int32)
    value = value + spot * z.rows + lax.broadcasted_iota(jnp.int32, value.shape, 0)
    vector[...] = jnp.where((value < 0) | (value > z.window), z.window, value)
    copy = pltpu.make_async_copy(vector, scalars, sem)
    copy.start()
    return copy


def pack_body(z, tiles, columns, lower, upper, stage, padded, offsets, in_sems, out_sems):
    copies = []
    half = z.rows // 2
    for r in range(z.rows):
        target = (lower, upper)[r // half].at[pl.ds(r % half * z.slots, z.slots)]
        copies.append((
            pltpu.make_async_copy(tiles.at[r], stage.at[r], in_sems.at[r]),
            pltpu.make_async_copy(stage.at[r], target, out_sems.at[r]),
        ))
    for copy, _ in copies:
        copy.start()
    padded[...] = jnp.full(padded.shape, -1, jnp.int32)
    padded[:z.rows, :z.slots] = columns[...]
    column = padded[...]
    row = lax.axis_index(AXES) * z.rows + lax.broadcasted_iota(jnp.int32, column.shape, 0)
    offset = column - row
    offset = jnp.where(offset > z.all_rows // 2, offset - z.all_rows, offset)
    offset = jnp.where(offset < -(z.all_rows // 2), offset + z.all_rows, offset)
    offset = jnp.where(column < 0, EMPTY, offset)
    offsets[...] = jnp.zeros_like(offsets)
    offsets[0:16, :] = offset.astype(jnp.float32).astype(offsets.dtype)
    ends = []
    for index, out in enumerate((lower, upper)):
        ends.append(pltpu.make_async_copy(offsets, out.at[half * z.slots], out_sems.at[z.rows + index]))
        ends[-1].start()
    for load, store in copies:
        load.wait()
        store.start()
    for _, store in copies:
        store.wait()
    for copy in ends:
        copy.wait()


def emit(z, total, positions, stage, out, sems, prev=None):
    for r in range(z.rows):
        def one(s, carry):
            value = total[r * z.block:(r + 1) * z.block, pl.ds(aligned(positions[r, s], z.block), z.block)]
            if prev is not None:
                value = value + prev[r, s]
            stage[r, s] = value.astype(stage.dtype)
            return carry
        lax.fori_loop(0, z.slots, one, 0, unroll=4)
        pltpu.make_async_copy(stage.at[r], out.at[r], sems.at[r]).start()
    for r in range(z.rows):
        pltpu.make_async_copy(stage.at[r], out.at[r], sems.at[r]).wait()


def add_trace(trace, weight, one, other):
    value = jnp.dot(one, other, preferred_element_type=jnp.float32)
    on = lax.broadcasted_iota(jnp.int32, value.shape, 0) == lax.broadcasted_iota(jnp.int32, value.shape, 1)
    diagonal = jnp.sum(jnp.where(on, value, 0.0), axis=0, keepdims=True)
    trace[:, :value.shape[1]] += weight.astype(jnp.float32) * diagonal


def own_body(z, own, columns, out, left_out, corner_out, positions, trace, stage, left, total, out_stage,
             in_sem, left_sem, corner_sem, out_sems):
    device = lax.axis_index(AXES)
    kind = device % 4
    copy = pltpu.make_async_copy(own, stage, in_sem)
    copy.start()
    left[...] = jnp.zeros_like(left)
    total[:, z.window * z.block:] = jnp.zeros((z.span, z.block), jnp.float32)
    copy.wait()
    start = z.start(device)
    for r in range(z.rows):
        def place(u, carry):
            column = z.position(columns[r, u], start)
            positions[r, u] = column
            left[r * z.block:(r + 1) * z.block, pl.ds(aligned(column, z.block), z.block)] = stage[r, u]
            return carry
        lax.fori_loop(0, z.slots, place, 0, unroll=4)
    left_copy = pltpu.make_async_copy(left, left_out, left_sem)
    left_copy.start()
    half = z.span // 2

    def corner(start):
        def go(rows, cols):
            copy = pltpu.make_async_copy(left.at[rows, cols], corner_out, corner_sem)
            copy.start() if start else copy.wait()
        pl.when(kind == UPPER)(lambda: go(pl.ds(0, half), pl.ds(0, z.span)))
        pl.when(kind != UPPER)(
            lambda: go(pl.ds(half, half), pl.ds((z.chunks - 1) * z.span, z.span))
        )

    corner(True)
    middle = slice(z.hops * z.span, (z.hops + 1) * z.span)

    def multiply(n, carry):
        cols = pl.ds(aligned(n, z.span), z.span)
        total[:, cols] = jnp.dot(left[:, middle], left[:, cols], preferred_element_type=jnp.float32)
        return carry

    lax.fori_loop(0, z.chunks, multiply, 0)
    trace[...] = jnp.zeros_like(trace)
    add_trace(trace, jnp.float32(1), left[:, middle], left[:, middle])
    emit(z, total, positions, out_stage, out, out_sems)
    corner(False)
    left_copy.wait()


def near_body(z, names, with_corner, hand_on, left_in, positions, prev, trace_in, *refs):
    refs = list(refs)
    take = lambda count: [refs.pop(0) for _ in range(count)]
    corner = take(1)[0] if with_corner else None
    sources = [take(2) for _ in names]
    out, trace = take(2)
    last_left = take(1)[0] if hand_on else None
    left, stage, right, total, out_stage, prev_stage, vector, scalars = take(8)
    left_sem, in_sem, prev_sem, place_sem, last_sem, out_sems = take(6)
    kind = lax.axis_index(AXES) % 4
    place = {name: pick(table, kind) + z.hops for name, table in OFFSETS.items()}

    def chunk(n):
        return pl.ds(aligned(n, z.span), z.span)

    def fetch(index, begin):
        for h in range(2):
            copy = pltpu.make_async_copy(sources[index][h], stage.at[index % 2, h], in_sem.at[index % 2, h])
            copy.start() if begin else copy.wait()

    left_copy = pltpu.make_async_copy(left_in, left, left_sem)
    left_copy.start()
    for index in range(min(2, len(names))):
        fetch(index, True)
    prev_copy = pltpu.make_async_copy(prev, prev_stage, prev_sem)
    prev_copy.start()
    total[...] = jnp.zeros_like(total)
    trace[...] = trace_in[...]
    left_copy.wait()
    last_copies = []
    if hand_on:
        for index, name in enumerate(("last", "last_beside")):
            spot = jnp.clip(place[name], 0, z.chunks - 1)
            copy = pltpu.make_async_copy(
                left.at[:, chunk(spot)], last_left.at[:, pl.ds(index * z.span, z.span)], last_sem.at[index]
            )
            copy.start()
            last_copies.append(copy)
    for index, name in enumerate(names):
        spot = place[name]
        slot = index % 2
        fetch(index, False)

        def add():
            decoding = decode(
                z, stage.at[slot, 0, z.rows // 2 * z.slots], spot, vector.at[slot], scalars.at[slot], place_sem.at[slot]
            )
            right[...] = jnp.zeros_like(right)
            decoding.wait()
            scatter(z, right, 0, stage.at[slot], lambda r, u: scalars[slot, r, u])

            def multiply(n, carry):
                total[:, chunk(n)] += jnp.dot(
                    left[:, chunk(spot)], right[:, chunk(n)], preferred_element_type=jnp.float32
                )
                return carry

            lax.fori_loop(jnp.maximum(0, spot - z.hops), jnp.minimum(z.chunks, spot + z.hops + 1), multiply, 0)
            weight = pick(COUNTS[name], kind)
            pl.when(weight != 0)(
                lambda: add_trace(trace, weight, left[:, chunk(spot)], right[:, chunk(z.hops)])
            )

        if all(NEEDED[name]):
            add()
        else:
            pl.when(pick(NEEDED[name], kind) != 0)(add)
        if index + 2 < len(names):
            fetch(index + 2, True)
    if corner is not None:
        half = z.span // 2
        end = (z.chunks - 1) * z.span
        pl.when(kind == UPPER)(lambda: add_trace(trace, jnp.float32(2), left[:, half:z.span], corner[...]))
        pl.when(kind == LOWER)(
            lambda: add_trace(trace, jnp.float32(2), left[:half, end:end + half], corner[:, :half])
        )
    prev_copy.wait()
    emit(z, total, positions, out_stage, out, out_sems, prev_stage)
    for copy in last_copies:
        copy.wait()


def last_body(z, left_in, positions, prev, a_lower, a_upper, b_lower, b_upper, out, left, stage, right, total, out_stage,
              prev_stage, vector, scalars, left_sem, in_sem, prev_sem, place_sem, out_sems):
    kind = lax.axis_index(AXES) % 4
    copies = [
        *[
            pltpu.make_async_copy(source, stage.at[index // 2, index % 2], in_sem.at[index // 2, index % 2])
            for index, source in enumerate((a_lower, a_upper, b_lower, b_upper))
        ],
        pltpu.make_async_copy(left_in, left, left_sem),
        pltpu.make_async_copy(prev, prev_stage, prev_sem),
    ]
    for copy in copies:
        copy.start()
    place_a = pick(OFFSETS["last"], kind) + z.hops
    place_b = pick(OFFSETS["last_beside"], kind) + z.hops
    needed_b = pick(NEEDED["last_beside"], kind) != 0

    def chunk(n):
        return pl.ds(aligned(n, z.span), z.span)

    def reach(spot):
        return jnp.maximum(0, spot - z.hops), jnp.minimum(z.chunks, spot + z.hops + 1)

    def clear_total(n, carry):
        total[:, chunk(n)] = jnp.zeros((z.span, z.span), jnp.float32)
        return carry

    def prepare(index, spot):
        copies[2 * index].wait()
        copies[2 * index + 1].wait()
        decoding = decode(
            z, stage.at[index, 0, z.rows // 2 * z.slots], spot, vector.at[index], scalars.at[index], place_sem.at[index]
        )

        def clear(n, carry):
            right[index, :, chunk(n)] = jnp.zeros((z.span, z.span), right.dtype)
            return carry

        lax.fori_loop(*reach(spot), clear, 0)
        decoding.wait()
        scatter(z, right.at[index], 0, stage.at[index], lambda r, u: scalars[index, r, u])

    low, high = reach(place_a)
    lax.fori_loop(0, low, clear_total, 0)
    lax.fori_loop(high, z.chunks, clear_total, 0)
    total[:, z.window * z.block:] = jnp.zeros((z.span, z.block), jnp.float32)
    prepare(0, place_a)
    copies[4].wait()

    def multiply(n, carry):
        total[:, chunk(n)] = jnp.dot(
            left[:, :z.span], right[0, :, chunk(n)], preferred_element_type=jnp.float32
        )
        return carry

    lax.fori_loop(low, high, multiply, 0)

    @pl.when(needed_b)
    def _():
        prepare(1, place_b)

        def multiply_add(n, carry):
            total[:, chunk(n)] += jnp.dot(
                left[:, z.span:], right[1, :, chunk(n)], preferred_element_type=jnp.float32
            )
            return carry

        lax.fori_loop(*reach(place_b), multiply_add, 0)

    @pl.when(jnp.logical_not(needed_b))
    def _():
        copies[2].wait()
        copies[3].wait()

    copies[5].wait()
    emit(z, total, positions, out_stage, out, out_sems, prev_stage)


ANY = pl.BlockSpec(memory_space=pl.ANY)
SMEM = pl.BlockSpec(memory_space=pltpu.SMEM)
VMEM = pl.BlockSpec(memory_space=pltpu.VMEM)
DMA = pltpu.SemaphoreType.DMA


def call(z, kernel, operands, in_specs, out_shape, out_specs, scratch, pieces, limit=VMEM_LIMIT):
    return pl.pallas_call(
        kernel,
        out_shape=out_shape,
        in_specs=in_specs,
        out_specs=out_specs,
        scratch_shapes=scratch,
        compiler_params=pltpu.CompilerParams(vmem_limit_bytes=limit),
        cost_estimate=pl.CostEstimate(
            flops=2 * z.span * z.span * z.window * z.block * pieces,
            bytes_accessed=2 * z.span * z.slots * z.block * (pieces + 4),
            transcendentals=0,
        ),
    )(*operands)


def shards(tiles, columns):
    devices = lax.axis_size(AXES)
    z = Sizes(tiles.shape, devices)
    assert z.hops == 3 and z.rows == 4 and devices % 4 == 0 and devices > 8
    dtype = tiles.dtype
    shape = jax.ShapeDtypeStruct
    sums = shape(tiles.shape, jnp.float32)
    line = shape((1, z.span), jnp.float32)
    dense = pltpu.VMEM((z.span, z.wide), dtype)
    total_buffer = pltpu.VMEM((z.span, z.wide), jnp.float32)

    half_shape = (z.rows // 2 * z.slots + 1, z.block, z.block)
    places = [pltpu.VMEM((2, 16, z.block), jnp.int32), pltpu.SMEM((2, 16, z.block), jnp.int32)]

    payload = call(
        z, functools.partial(pack_body, z), [tiles, columns], [ANY, VMEM],
        [shape(half_shape, dtype)] * 2, [ANY] * 2,
        [
            pltpu.VMEM(tiles.shape, dtype), pltpu.VMEM((16, z.block), jnp.int32),
            pltpu.VMEM((z.block, z.block), dtype), DMA((z.rows,)), DMA((z.rows + 2,)),
        ],
        0, WHOLE_VMEM,
    )
    first = receive(payload, FIRST)
    beside = receive(payload, PARTNER)

    total, left, corner, positions, trace = call(
        z, functools.partial(own_body, z), [tiles, columns], [ANY, SMEM],
        [
            sums, shape((z.span, z.wide), dtype), shape((z.span // 2, z.span), dtype),
            shape((z.rows, z.slots), jnp.int32), line,
        ],
        [ANY, ANY, ANY, SMEM, VMEM],
        [
            pltpu.VMEM(tiles.shape, dtype), dense, total_buffer, pltpu.VMEM(tiles.shape, jnp.float32),
            DMA, DMA, DMA, DMA((z.rows,)),
        ],
        1,
    )
    corner = receive(corner, (3, 0, 0, -3), (LOWER, UPPER))

    def near(names, arrays, total, trace, corner=None, hand_on=False):
        corners = [] if corner is None else [corner]
        extra = [shape((z.span, 2 * z.span), dtype)] * hand_on
        return call(
            z, functools.partial(near_body, z, names, corner is not None, hand_on),
            [left, positions, total, trace] + corners + [half for pair in arrays for half in pair],
            [ANY, SMEM, ANY, VMEM] + [VMEM] * len(corners) + [ANY] * (2 * len(arrays)),
            [sums, line] + extra,
            [ANY, VMEM] + [ANY] * len(extra),
            [
                dense, pltpu.VMEM((2, 2) + half_shape, dtype), dense, total_buffer,
                pltpu.VMEM(tiles.shape, jnp.float32), pltpu.VMEM(tiles.shape, jnp.float32), *places,
                DMA, DMA((2, 2)), DMA, DMA((2,)), DMA((2,)), DMA((z.rows,)),
            ],
            len(names),
        )

    def from_partner(array, name):
        return receive(array, PARTNER, [m for m in range(4) if NEEDED[name][m]])

    first_lower, total, trace = lax.optimization_barrier((first[0], total, trace))
    relay_lower = receive(first_lower, RELAY_FROM)
    total, trace = near(("beside",), [beside], total, trace)
    first_lower, first_upper, corner, total, trace = lax.optimization_barrier(
        (first_lower, first[1], corner, total, trace)
    )
    relay_upper = receive(first_upper, RELAY_FROM)
    first = (first_lower, first_upper)
    first_beside = from_partner(first, "first_beside")
    relay_lower, total, trace = lax.optimization_barrier((relay_lower, total, trace))
    relay_beside_lower = receive(relay_lower, PARTNER)
    total, trace = near(("first", "first_beside"), [first, first_beside], total, trace, corner)
    relay_upper, payload, total, trace = lax.optimization_barrier((relay_upper, payload, total, trace))
    last = receive(payload, LAST)
    relay_beside_upper = receive(relay_upper, PARTNER)
    relay = (relay_lower, relay_upper)
    relay_beside = (relay_beside_lower, relay_beside_upper)
    total, trace, last_left = near(
        ("relay", "relay_beside"), [relay, relay_beside], total, trace, hand_on=True
    )
    assert devices & (devices - 1) == 0
    steps = [1 << bit for bit in range(devices.bit_length() - 1)]
    for step in steps[:1] + steps[3:]:
        trace = exchange(trace, step)
    others = [fetch(trace, step) for step in (steps[1], steps[2], steps[1] + steps[2])]
    last_lower, total = lax.optimization_barrier((last[0], total))
    last = (last_lower, last[1])
    last_beside = from_partner(last, "last_beside")
    square = call(
        z, functools.partial(last_body, z), [last_left, positions, total, *last, *last_beside],
        [ANY, SMEM] + [ANY] * 5,
        [shape(tiles.shape, dtype)],
        [ANY],
        [
            pltpu.VMEM((z.span, 2 * z.span), dtype), pltpu.VMEM((2, 2) + half_shape, dtype),
            pltpu.VMEM((2, z.span, z.wide), dtype), total_buffer,
            pltpu.VMEM(tiles.shape, dtype), pltpu.VMEM(tiles.shape, jnp.float32), *places,
            DMA, DMA((2, 2)), DMA, DMA((2,)), DMA((z.rows,)),
        ],
        2,
    )[0]
    square, trace, others = lax.optimization_barrier((square, trace, others))
    return square, jnp.sum((trace + others[0]) + (others[1] + others[2])) / (z.all_rows * z.block)


def solution(mesh):
    return jax.shard_map(
        shards,
        mesh=mesh,
        in_specs=(P(AXES, None, None, None), P(AXES, None)),
        out_specs=(P(AXES, None, None, None), P()),
        check_vma=False,
    )
```

```python
import functools

import jax
import jax.numpy as jnp
from jax import lax
from jax.experimental import pallas as pl
from jax.experimental.pallas import tpu as pltpu
from jax.sharding import PartitionSpec as P

REACH = 12
AXES = ("blk", "grp")
VMEM_LIMIT = 36 * 1024 * 1024
WHOLE_VMEM = 60 * 1024 * 1024
EMPTY = 64

FIRST = (2, 3, -3, -2)
SECOND = (-3, 2, -2, 3)
RELAY_FROM = (2, -5, 5, -2)
PARTNER = (1, -1, 1, -1)
RELAY = tuple(RELAY_FROM[m] + FIRST[(m + RELAY_FROM[m]) % 4] for m in range(4))


def across(table):
    return tuple(PARTNER[m] + table[m ^ 1] for m in range(4))


USE_SECOND = tuple(int(abs(offset) > 3) for offset in across(FIRST))
MIXED = tuple(
    second if use else first
    for first, second, use in zip(across(FIRST), across(SECOND), USE_SECOND)
)
OFFSETS = {
    "beside": PARTNER,
    "first": FIRST,
    "second": SECOND,
    "mixed": MIXED,
    "relay": RELAY,
    "relay_beside": across(RELAY),
}
COUNTS = {"beside": (2, 0, 2, 0), "first": (2, 0, 0, 2), "second": (2, 0, 0, 2), "mixed": (0, 0, 2, 2)}
OUTSIDE = {("first", "mixed"): (0, 2, 2, 0), ("first", "second"): (0, 2, 0, 0)}
LOWER, UPPER = 2, 1
KEPT = {"beside": 0, "first": 0, "second": 1, "mixed": 2}


def receive(shard, offsets, kinds=range(4)):
    size = lax.axis_size(AXES)
    pairs = [((d + offsets[d % 4]) % size, d) for d in range(size) if d % 4 in kinds]
    return lax.ppermute(shard, AXES, pairs)


def fetch(value, step):
    return lax.ppermute(value, AXES, [(d, d ^ step) for d in range(lax.axis_size(AXES))])


def exchange(value, step):
    return value + fetch(value, step)


def pick(table, kind):
    value = jnp.int32(table[3])
    for m in range(3):
        value = jnp.where(kind == m, jnp.int32(table[m]), value)
    return value


def aligned(index, unit):
    return pl.multiple_of(index * unit, unit)


class Sizes:
    def __init__(self, shape, devices):
        self.rows, self.slots, self.block, _ = shape
        self.hops = (REACH + self.rows - 1) // self.rows
        self.chunks = 2 * self.hops + 1
        self.window = self.chunks * self.rows
        self.span = self.rows * self.block
        self.wide = (self.window + 1) * self.block
        self.all_rows = self.rows * devices

    def start(self, device):
        start = (device - self.hops) * self.rows
        return jnp.where(start < 0, start + self.all_rows, start)

    def position(self, column, start):
        place = column - start
        place = jnp.where(place < 0, place + self.all_rows, place)
        place = jnp.where(column < 0, self.window, place)
        return jnp.minimum(place, self.window)


def scatter(z, dense, top, source, place):
    for r in range(z.rows):
        def one(u, carry):
            column = pl.ds(aligned(place(r, u), z.block), z.block)
            dense[top + r * z.block:top + (r + 1) * z.block, column] = source[r * z.slots + u]
            return carry
        lax.fori_loop(0, z.slots, one, 0, unroll=4)


def decode(z, offsets, spot, vector, scalars, sem):
    value = offsets[0:16, :].astype(jnp.float32).astype(jnp.int32)
    value = value + spot * z.rows + lax.broadcasted_iota(jnp.int32, value.shape, 0)
    vector[...] = jnp.where((value < 0) | (value > z.window), z.window, value)
    copy = pltpu.make_async_copy(vector, scalars, sem)
    copy.start()
    return copy


def pack_body(z, tiles, columns, out, stage, padded, offsets, in_sems, out_sems):
    copies = []
    for r in range(z.rows):
        rows = pl.ds(r * z.slots, z.slots)
        copies.append((
            pltpu.make_async_copy(tiles.at[r], stage.at[rows], in_sems.at[r]),
            pltpu.make_async_copy(stage.at[rows], out.at[rows], out_sems.at[r]),
        ))
    for copy, _ in copies:
        copy.start()
    padded[...] = jnp.full(padded.shape, -1, jnp.int32)
    padded[:z.rows, :z.slots] = columns[...]
    column = padded[...]
    row = lax.axis_index(AXES) * z.rows + lax.broadcasted_iota(jnp.int32, column.shape, 0)
    offset = column - row
    offset = jnp.where(offset > z.all_rows // 2, offset - z.all_rows, offset)
    offset = jnp.where(offset < -(z.all_rows // 2), offset + z.all_rows, offset)
    offset = jnp.where(column < 0, EMPTY, offset)
    offsets[...] = jnp.zeros_like(offsets)
    offsets[0:16, :] = offset.astype(jnp.float32).astype(offsets.dtype)
    last = pltpu.make_async_copy(offsets, out.at[z.rows * z.slots], out_sems.at[z.rows])
    last.start()
    for load, store in copies:
        load.wait()
        store.start()
    for _, store in copies:
        store.wait()
    last.wait()


def emit(z, total, positions, stage, out, sems, prev=None):
    for r in range(z.rows):
        def one(s, carry):
            value = total[r * z.block:(r + 1) * z.block, pl.ds(aligned(positions[r, s], z.block), z.block)]
            if prev is not None:
                value = value + prev[r, s]
            stage[r, s] = value.astype(stage.dtype)
            return carry
        lax.fori_loop(0, z.slots, one, 0, unroll=4)
        pltpu.make_async_copy(stage.at[r], out.at[r], sems.at[r]).start()
    for r in range(z.rows):
        pltpu.make_async_copy(stage.at[r], out.at[r], sems.at[r]).wait()


def add_trace(trace, weight, one, other):
    value = jnp.dot(one, other, preferred_element_type=jnp.float32)
    on = lax.broadcasted_iota(jnp.int32, value.shape, 0) == lax.broadcasted_iota(jnp.int32, value.shape, 1)
    diagonal = jnp.sum(jnp.where(on, value, 0.0), axis=0, keepdims=True)
    trace[:, :value.shape[1]] += weight.astype(jnp.float32) * diagonal


def own_body(z, own, columns, out, left_out, corner_out, positions, trace, stage, left, total, out_stage,
             in_sem, left_sem, corner_sem, out_sems):
    device = lax.axis_index(AXES)
    kind = device % 4
    copy = pltpu.make_async_copy(own, stage, in_sem)
    copy.start()
    left[...] = jnp.zeros_like(left)
    total[:, z.window * z.block:] = jnp.zeros((z.span, z.block), jnp.float32)
    copy.wait()
    start = z.start(device)
    for r in range(z.rows):
        def place(u, carry):
            column = z.position(columns[r, u], start)
            positions[r, u] = column
            left[r * z.block:(r + 1) * z.block, pl.ds(aligned(column, z.block), z.block)] = stage[r, u]
            return carry
        lax.fori_loop(0, z.slots, place, 0, unroll=4)
    left_copy = pltpu.make_async_copy(left, left_out, left_sem)
    left_copy.start()
    half = z.span // 2

    def corner(start):
        def go(rows, cols):
            copy = pltpu.make_async_copy(left.at[rows, cols], corner_out, corner_sem)
            copy.start() if start else copy.wait()
        pl.when(kind == UPPER)(lambda: go(pl.ds(0, half), pl.ds(0, z.span)))
        pl.when(kind != UPPER)(
            lambda: go(pl.ds(half, half), pl.ds((z.chunks - 1) * z.span, z.span))
        )

    corner(True)
    middle = slice(z.hops * z.span, (z.hops + 1) * z.span)

    def multiply(n, carry):
        cols = pl.ds(aligned(n, z.span), z.span)
        total[:, cols] = jnp.dot(left[:, middle], left[:, cols], preferred_element_type=jnp.float32)
        return carry

    lax.fori_loop(0, z.chunks, multiply, 0)
    trace[...] = jnp.zeros_like(trace)
    add_trace(trace, jnp.float32(1), left[:, middle], left[:, middle])
    emit(z, total, positions, out_stage, out, out_sems)
    corner(False)
    left_copy.wait()


def near_body(z, names, left_in, positions, prev, trace_in, *refs):
    refs = list(refs)
    take = lambda count: [refs.pop(0) for _ in range(count)]
    corner = take(1)[0]
    sources = {name: take(2 if name == "mixed" else 1) for name in names}
    out, trace, relay_left = take(3)
    left, stage, right, total, sums, vector, scalars = take(7)
    left_sem, in_sem, prev_sem, place_sem, relay_sem, out_sems = take(6)
    device = lax.axis_index(AXES)
    kind = device % 4
    place = {name: pick(table, kind) + z.hops for name, table in OFFSETS.items()}

    def chunk(n):
        return pl.ds(aligned(n, z.span), z.span)

    def fetch(index, begin):
        def go(source):
            copy = pltpu.make_async_copy(source, stage.at[index % 2], in_sem.at[index % 2])
            copy.start() if begin else copy.wait()
        source = sources[names[index]]
        if len(source) == 1:
            go(source[0])
        else:
            use_second = pick(USE_SECOND, kind)
            pl.when(use_second == 0)(lambda: go(source[0]))
            pl.when(use_second != 0)(lambda: go(source[1]))

    left_copy = pltpu.make_async_copy(left_in, left, left_sem)
    left_copy.start()
    for index in range(min(2, len(names))):
        fetch(index, True)
    prev_copy = pltpu.make_async_copy(prev, sums, prev_sem)
    prev_copy.start()
    total[...] = jnp.zeros_like(total)
    trace[...] = trace_in[...]
    left_copy.wait()
    relay_copies = []
    for index, name in enumerate(("relay", "relay_beside")):
        copy = pltpu.make_async_copy(
            left.at[:, chunk(place[name])], relay_left.at[:, pl.ds(index * z.span, z.span)],
            relay_sem.at[index],
        )
        copy.start()
        relay_copies.append(copy)
    decodings = []

    def begin_decode(index):
        slot = index % 2
        fetch(index, False)
        decodings.append(decode(
            z, stage.at[slot, z.rows * z.slots], place[names[index]], vector.at[slot], scalars.at[slot],
            place_sem.at[slot],
        ))

    begin_decode(0)
    dense_of = {}
    for index, name in enumerate(names):
        dense = right.at[KEPT[name]]
        dense_of[name] = dense
        spot = place[name]
        slot = index % 2
        dense[...] = jnp.zeros_like(dense)
        decodings[index].wait()
        scatter(z, dense, 0, stage.at[slot], lambda r, u: scalars[slot, r, u])
        if index + 2 < len(names):
            fetch(index + 2, True)
        if index + 1 < len(names):
            begin_decode(index + 1)

        def multiply(n, carry):
            total[:, chunk(n)] += jnp.dot(
                left[:, chunk(spot)], dense[:, chunk(n)], preferred_element_type=jnp.float32
            )
            return carry

        lax.fori_loop(jnp.maximum(0, spot - z.hops), jnp.minimum(z.chunks, spot + z.hops + 1), multiply, 0)
        weight = pick(COUNTS[name], kind)
        pl.when(weight != 0)(
            lambda: add_trace(trace, weight, left[:, chunk(spot)], dense[:, chunk(z.hops)])
        )
    for (one, other), table in OUTSIDE.items():
        weight = pick(table, kind)
        pl.when(weight != 0)(lambda: add_trace(
            trace, weight, dense_of[one][:, chunk(place[other])], dense_of[other][:, chunk(place[one])]
        ))
    half = z.span // 2
    last = (z.chunks - 1) * z.span
    pl.when(kind == UPPER)(lambda: add_trace(trace, jnp.float32(2), left[:, half:z.span], corner[...]))
    pl.when(kind == LOWER)(
        lambda: add_trace(trace, jnp.float32(2), left[:half, last:last + half], corner[:, :half])
    )
    prev_copy.wait()
    emit(z, total, positions, sums, out, out_sems, sums)
    for copy in relay_copies:
        copy.wait()


def last_body(z, left_in, positions, prev, source_a, source_b, out, left, stage, right, total, out_stage,
              prev_stage, vector, scalars, left_sem, in_sem, prev_sem, place_sem, out_sems):
    kind = lax.axis_index(AXES) % 4
    copies = [
        pltpu.make_async_copy(source_a, stage.at[0], in_sem.at[0]),
        pltpu.make_async_copy(source_b, stage.at[1], in_sem.at[1]),
        pltpu.make_async_copy(left_in, left, left_sem),
        pltpu.make_async_copy(prev, prev_stage, prev_sem),
    ]
    for copy in copies:
        copy.start()
    places = [pick(OFFSETS[name], kind) + z.hops for name in ("relay", "relay_beside")]
    low = jnp.maximum(0, jnp.minimum(*places) - z.hops)
    high = jnp.minimum(z.chunks, jnp.maximum(*places) + z.hops + 1)

    def chunk(n):
        return pl.ds(aligned(n, z.span), z.span)

    def clear_total(n, carry):
        total[:, chunk(n)] = jnp.zeros((z.span, z.span), jnp.float32)
        return carry

    def clear_right(n, carry):
        right[:, chunk(n)] = jnp.zeros((2 * z.span, z.span), right.dtype)
        return carry

    lax.fori_loop(0, low, clear_total, 0)
    lax.fori_loop(high, z.chunks, clear_total, 0)
    total[:, z.window * z.block:] = jnp.zeros((z.span, z.block), jnp.float32)
    decodings = []
    for index in range(2):
        copies[index].wait()
        decodings.append(decode(
            z, stage.at[index, z.rows * z.slots], places[index], vector.at[index], scalars.at[index],
            place_sem.at[index],
        ))
    lax.fori_loop(low, high, clear_right, 0)
    for index in range(2):
        decodings[index].wait()
        scatter(z, right, index * z.span, stage.at[index], lambda r, u: scalars[index, r, u])
    copies[2].wait()

    def multiply(n, carry):
        total[:, chunk(n)] = jnp.dot(left[...], right[:, chunk(n)], preferred_element_type=jnp.float32)
        return carry

    lax.fori_loop(low, high, multiply, 0)
    copies[3].wait()
    emit(z, total, positions, out_stage, out, out_sems, prev_stage)


ANY = pl.BlockSpec(memory_space=pl.ANY)
SMEM = pl.BlockSpec(memory_space=pltpu.SMEM)
VMEM = pl.BlockSpec(memory_space=pltpu.VMEM)
DMA = pltpu.SemaphoreType.DMA


def call(z, kernel, operands, in_specs, out_shape, out_specs, scratch, pieces, limit=VMEM_LIMIT):
    return pl.pallas_call(
        kernel,
        out_shape=out_shape,
        in_specs=in_specs,
        out_specs=out_specs,
        scratch_shapes=scratch,
        compiler_params=pltpu.CompilerParams(vmem_limit_bytes=limit),
        cost_estimate=pl.CostEstimate(
            flops=2 * z.span * z.span * z.window * z.block * pieces,
            bytes_accessed=2 * z.span * z.slots * z.block * (pieces + 4),
            transcendentals=0,
        ),
    )(*operands)


def shards(tiles, columns):
    devices = lax.axis_size(AXES)
    z = Sizes(tiles.shape, devices)
    assert z.hops == 3 and z.rows == 4 and devices % 4 == 0 and devices > 8
    dtype = tiles.dtype
    shape = jax.ShapeDtypeStruct
    sums = shape(tiles.shape, jnp.float32)
    line = shape((1, z.span), jnp.float32)
    dense = pltpu.VMEM((z.span, z.wide), dtype)
    total_buffer = pltpu.VMEM((z.span, z.wide), jnp.float32)

    payload_shape = (z.rows * z.slots + 1, z.block, z.block)
    places = [pltpu.VMEM((2, 16, z.block), jnp.int32), pltpu.SMEM((2, 16, z.block), jnp.int32)]

    payload = call(
        z, functools.partial(pack_body, z), [tiles, columns], [ANY, VMEM],
        shape(payload_shape, dtype), ANY,
        [
            pltpu.VMEM((z.rows * z.slots, z.block, z.block), dtype), pltpu.VMEM((16, z.block), jnp.int32),
            pltpu.VMEM((z.block, z.block), dtype), DMA((z.rows,)), DMA((z.rows + 1,)),
        ],
        0, WHOLE_VMEM,
    )
    first = receive(payload, FIRST)
    second = receive(payload, SECOND)

    total, left, corner, positions, trace = call(
        z, functools.partial(own_body, z), [tiles, columns], [ANY, SMEM],
        [
            sums, shape((z.span, z.wide), dtype), shape((z.span // 2, z.span), dtype),
            shape((z.rows, z.slots), jnp.int32), line,
        ],
        [ANY, ANY, ANY, SMEM, VMEM],
        [
            pltpu.VMEM(tiles.shape, dtype), dense, total_buffer, pltpu.VMEM(tiles.shape, jnp.float32),
            DMA, DMA, DMA, DMA((z.rows,)),
        ],
        1,
    )
    corner = receive(corner, (0, -3, 3, 0), (LOWER, UPPER))

    first, total, trace = lax.optimization_barrier((first, total, trace))
    relay = receive(first, RELAY_FROM)
    first, second, corner, payload, total, trace = lax.optimization_barrier(
        (first, second, corner, payload, total, trace)
    )
    beside = receive(payload, PARTNER)
    mixed = [
        receive(first, PARTNER, [m for m in range(4) if not USE_SECOND[m]]),
        receive(second, PARTNER, [m for m in range(4) if USE_SECOND[m]]),
    ]
    names = ("beside", "first", "second", "mixed")
    total, trace, relay_left = call(
        z, functools.partial(near_body, z, names),
        [left, positions, total, trace, corner, beside, first, second, *mixed],
        [ANY, SMEM, ANY, VMEM, VMEM] + [ANY] * 5,
        [sums, line, shape((z.span, 2 * z.span), dtype)],
        [ANY, VMEM, ANY],
        [
            dense, pltpu.VMEM((2,) + payload_shape, dtype), pltpu.VMEM((3, z.span, z.wide), dtype), total_buffer,
            pltpu.VMEM(tiles.shape, jnp.float32), *places,
            DMA, DMA((2,)), DMA, DMA((2,)), DMA((2,)), DMA((z.rows,)),
        ],
        4, 36 * 1024 * 1024,
    )
    assert devices & (devices - 1) == 0
    steps = [1 << bit for bit in range(devices.bit_length() - 1)]
    for step in steps[:1] + steps[3:]:
        trace = exchange(trace, step)
    relay, total, trace = lax.optimization_barrier((relay, total, trace))
    relay_beside = receive(relay, PARTNER)
    others = [fetch(trace, step) for step in (steps[1], steps[2], steps[1] + steps[2])]
    square = call(
        z, functools.partial(last_body, z), [relay_left, positions, total, relay, relay_beside],
        [ANY, SMEM, ANY, ANY, ANY],
        [shape(tiles.shape, dtype)],
        [ANY],
        [
            pltpu.VMEM((z.span, 2 * z.span), dtype), pltpu.VMEM((2,) + payload_shape, dtype),
            pltpu.VMEM((2 * z.span, z.wide), dtype), total_buffer,
            pltpu.VMEM(tiles.shape, dtype), pltpu.VMEM(tiles.shape, jnp.float32), *places,
            DMA, DMA((2,)), DMA, DMA((2,)), DMA((z.rows,)),
        ],
        2, 44 * 1024 * 1024,
    )[0]
    square, trace, others = lax.optimization_barrier((square, trace, others))
    return square, jnp.sum((trace + others[0]) + (others[1] + others[2])) / (z.all_rows * z.block)


def solution(mesh):
    return jax.shard_map(
        shards,
        mesh=mesh,
        in_specs=(P(AXES, None, None, None), P(AXES, None)),
        out_specs=(P(AXES, None, None, None), P()),
        check_vma=False,
    )
```

```python
import functools

import jax
import jax.numpy as jnp
from jax import lax
from jax.experimental import pallas as pl
from jax.experimental.pallas import tpu as pltpu
from jax.sharding import PartitionSpec as P

REACH = 12
AXES = ("blk", "grp")
VMEM_LIMIT = 42 * 1024 * 1024
WHOLE_VMEM = 60 * 1024 * 1024
EMPTY = 64

OVER_X = (2, 2, -2, -2)
OVER_Y = (-3, 3, -3, 3)
RELAY_FROM = (2, -5, 5, -2)
RELAY_X, RELAY_Y = (1, 2), (0, 3)
PARTNER = (1, -1, 1, -1)
RELAY = tuple(
    RELAY_FROM[m] + (OVER_X if m in RELAY_X else OVER_Y)[(m + RELAY_FROM[m]) % 4] for m in range(4)
)


def across(table):
    return tuple(PARTNER[m] + table[m ^ 1] for m in range(4))


OFFSETS = {
    "beside": PARTNER,
    "x": OVER_X,
    "y": OVER_Y,
    "x_beside": across(OVER_X),
    "relay": RELAY,
    "relay_beside": across(RELAY),
}
COUNTS = {"beside": (2, 0, 2, 0), "x": (2, 0, 0, 2), "y": (2, 0, 0, 2), "x_beside": (0, 0, 2, 2)}
OUTSIDE = {("y", "x_beside"): (0, 2, 2, 0), ("y", "x"): (0, 2, 0, 0)}
LOWER, UPPER = 2, 1


def receive(shard, offsets, kinds=range(4)):
    size = lax.axis_size(AXES)
    pairs = [((d + offsets[d % 4]) % size, d) for d in range(size) if d % 4 in kinds]
    return lax.ppermute(shard, AXES, pairs)


def fetch(value, step):
    return lax.ppermute(value, AXES, [(d, d ^ step) for d in range(lax.axis_size(AXES))])


def exchange(value, step):
    return value + fetch(value, step)


def pick(table, kind):
    value = jnp.int32(table[3])
    for m in range(3):
        value = jnp.where(kind == m, jnp.int32(table[m]), value)
    return value


def aligned(index, unit):
    return pl.multiple_of(index * unit, unit)


class Sizes:
    def __init__(self, shape, devices):
        self.rows, self.slots, self.block, _ = shape
        self.hops = (REACH + self.rows - 1) // self.rows
        self.chunks = 2 * self.hops + 1
        self.window = self.chunks * self.rows
        self.span = self.rows * self.block
        self.wide = (self.window + 1) * self.block
        self.all_rows = self.rows * devices

    def start(self, device):
        start = (device - self.hops) * self.rows
        return jnp.where(start < 0, start + self.all_rows, start)

    def position(self, column, start):
        place = column - start
        place = jnp.where(place < 0, place + self.all_rows, place)
        place = jnp.where(column < 0, self.window, place)
        return jnp.minimum(place, self.window)


def scatter(z, dense, top, source, place):
    for r in range(z.rows):
        def one(u, carry):
            column = pl.ds(aligned(place(r, u), z.block), z.block)
            dense[top + r * z.block:top + (r + 1) * z.block, column] = source[r * z.slots + u]
            return carry
        lax.fori_loop(0, z.slots, one, 0, unroll=4)


def decode(z, offsets, spot, vector, scalars, sem):
    value = offsets[0:16, :].astype(jnp.float32).astype(jnp.int32)
    value = value + spot * z.rows + lax.broadcasted_iota(jnp.int32, value.shape, 0)
    vector[...] = jnp.where((value < 0) | (value > z.window), z.window, value)
    copy = pltpu.make_async_copy(vector, scalars, sem)
    copy.start()
    return copy


def pack_body(z, tiles, columns, out, stage, padded, offsets, in_sems, out_sems):
    copies = []
    for r in range(z.rows):
        rows = pl.ds(r * z.slots, z.slots)
        copies.append((
            pltpu.make_async_copy(tiles.at[r], stage.at[rows], in_sems.at[r]),
            pltpu.make_async_copy(stage.at[rows], out.at[rows], out_sems.at[r]),
        ))
    for copy, _ in copies:
        copy.start()
    padded[...] = jnp.full(padded.shape, -1, jnp.int32)
    padded[:z.rows, :z.slots] = columns[...]
    column = padded[...]
    row = lax.axis_index(AXES) * z.rows + lax.broadcasted_iota(jnp.int32, column.shape, 0)
    offset = column - row
    offset = jnp.where(offset > z.all_rows // 2, offset - z.all_rows, offset)
    offset = jnp.where(offset < -(z.all_rows // 2), offset + z.all_rows, offset)
    offset = jnp.where(column < 0, EMPTY, offset)
    offsets[...] = jnp.zeros_like(offsets)
    offsets[0:16, :] = offset.astype(jnp.float32).astype(offsets.dtype)
    last = pltpu.make_async_copy(offsets, out.at[z.rows * z.slots], out_sems.at[z.rows])
    last.start()
    for load, store in copies:
        load.wait()
        store.start()
    for _, store in copies:
        store.wait()
    last.wait()


def emit(z, total, positions, stage, out, sems, prev=None):
    for r in range(z.rows):
        def one(s, carry):
            value = total[r * z.block:(r + 1) * z.block, pl.ds(aligned(positions[r, s], z.block), z.block)]
            if prev is not None:
                value = value + prev[r, s]
            stage[r, s] = value.astype(stage.dtype)
            return carry
        lax.fori_loop(0, z.slots, one, 0, unroll=4)
        pltpu.make_async_copy(stage.at[r], out.at[r], sems.at[r]).start()
    for r in range(z.rows):
        pltpu.make_async_copy(stage.at[r], out.at[r], sems.at[r]).wait()


def add_trace(trace, weight, one, other):
    value = jnp.dot(one, other, preferred_element_type=jnp.float32)
    on = lax.broadcasted_iota(jnp.int32, value.shape, 0) == lax.broadcasted_iota(jnp.int32, value.shape, 1)
    diagonal = jnp.sum(jnp.where(on, value, 0.0), axis=0, keepdims=True)
    trace[:, :value.shape[1]] += weight.astype(jnp.float32) * diagonal


def own_body(z, own, columns, out, left_out, corner_out, positions, trace, stage, left, total, out_stage,
             in_sem, left_sem, corner_sem, out_sems):
    device = lax.axis_index(AXES)
    kind = device % 4
    copy = pltpu.make_async_copy(own, stage, in_sem)
    copy.start()
    left[...] = jnp.zeros_like(left)
    total[:, z.window * z.block:] = jnp.zeros((z.span, z.block), jnp.float32)
    copy.wait()
    start = z.start(device)
    for r in range(z.rows):
        def place(u, carry):
            column = z.position(columns[r, u], start)
            positions[r, u] = column
            left[r * z.block:(r + 1) * z.block, pl.ds(aligned(column, z.block), z.block)] = stage[r, u]
            return carry
        lax.fori_loop(0, z.slots, place, 0, unroll=4)
    left_copy = pltpu.make_async_copy(left, left_out, left_sem)
    left_copy.start()
    half = z.span // 2

    def corner(start):
        def go(rows, cols):
            copy = pltpu.make_async_copy(left.at[rows, cols], corner_out, corner_sem)
            copy.start() if start else copy.wait()
        pl.when(kind == UPPER)(lambda: go(pl.ds(0, half), pl.ds(0, z.span)))
        pl.when(kind != UPPER)(
            lambda: go(pl.ds(half, half), pl.ds((z.chunks - 1) * z.span, z.span))
        )

    corner(True)
    middle = slice(z.hops * z.span, (z.hops + 1) * z.span)

    def multiply(n, carry):
        cols = pl.ds(aligned(n, z.span), z.span)
        total[:, cols] = jnp.dot(left[:, middle], left[:, cols], preferred_element_type=jnp.float32)
        return carry

    lax.fori_loop(0, z.chunks, multiply, 0)
    trace[...] = jnp.zeros_like(trace)
    add_trace(trace, jnp.float32(1), left[:, middle], left[:, middle])
    emit(z, total, positions, out_stage, out, out_sems)
    corner(False)
    left_copy.wait()


def near_body(z, names, final, left_in, positions, prev, trace_in, *refs):
    refs = list(refs)
    take = lambda count: [refs.pop(0) for _ in range(count)]
    corner = take(1)[0] if final else None
    sources = take(len(names))
    out, trace = take(2)
    relay_left = take(1)[0] if final else None
    left, stage, right, total, sums, vector, scalars = take(7)
    left_sem, in_sem, prev_sem, place_sem, relay_sem, out_sems = take(6)
    device = lax.axis_index(AXES)
    kind = device % 4
    place = {name: pick(table, kind) + z.hops for name, table in OFFSETS.items()}

    def chunk(n):
        return pl.ds(aligned(n, z.span), z.span)

    def fetch(index):
        return pltpu.make_async_copy(sources[index], stage.at[index % 2], in_sem.at[index % 2])

    left_copy = pltpu.make_async_copy(left_in, left, left_sem)
    left_copy.start()
    for index in range(min(2, len(names))):
        fetch(index).start()
    prev_copy = pltpu.make_async_copy(prev, sums, prev_sem)
    prev_copy.start()
    total[...] = jnp.zeros_like(total)
    trace[...] = trace_in[...]
    left_copy.wait()
    relay_copies = []
    for index, name in enumerate(("relay", "relay_beside") if final else ()):
        copy = pltpu.make_async_copy(
            left.at[:, chunk(place[name])], relay_left.at[:, pl.ds(index * z.span, z.span)],
            relay_sem.at[index],
        )
        copy.start()
        relay_copies.append(copy)
    decodings = []

    def begin_decode(index):
        slot = index % 2
        fetch(index).wait()
        decodings.append(decode(
            z, stage.at[slot, z.rows * z.slots], place[names[index]], vector.at[slot], scalars.at[slot],
            place_sem.at[slot],
        ))

    begin_decode(0)
    dense_of = {}
    for index, name in enumerate(names):
        dense = right.at[index]
        dense_of[name] = dense
        spot = place[name]
        slot = index % 2
        dense[...] = jnp.zeros_like(dense)
        decodings[index].wait()
        scatter(z, dense, 0, stage.at[slot], lambda r, u: scalars[slot, r, u])
        if index + 2 < len(names):
            fetch(index + 2).start()
        if index + 1 < len(names):
            begin_decode(index + 1)

        def multiply(n, carry):
            total[:, chunk(n)] += jnp.dot(
                left[:, chunk(spot)], dense[:, chunk(n)], preferred_element_type=jnp.float32
            )
            return carry

        lax.fori_loop(jnp.maximum(0, spot - z.hops), jnp.minimum(z.chunks, spot + z.hops + 1), multiply, 0)
        weight = pick(COUNTS[name], kind)
        pl.when(weight != 0)(
            lambda: add_trace(trace, weight, left[:, chunk(spot)], dense[:, chunk(z.hops)])
        )
    for (one, other), table in OUTSIDE.items() if final else ():
        weight = pick(table, kind)
        pl.when(weight != 0)(lambda: add_trace(
            trace, weight, dense_of[one][:, chunk(place[other])], dense_of[other][:, chunk(place[one])]
        ))
    if final:
        half = z.span // 2
        end = (z.chunks - 1) * z.span
        pl.when(kind == UPPER)(lambda: add_trace(trace, jnp.float32(2), left[:, half:z.span], corner[...]))
        pl.when(kind == LOWER)(
            lambda: add_trace(trace, jnp.float32(2), left[:half, end:end + half], corner[:, :half])
        )
    prev_copy.wait()
    emit(z, total, positions, sums, out, out_sems, sums)
    for copy in relay_copies:
        copy.wait()


def last_body(z, left_in, positions, prev, relay_x, relay_y, beside_x, beside_y, out, left, stage, right, total, out_stage,
              prev_stage, vector, scalars, left_sem, in_sem, prev_sem, place_sem, out_sems):
    kind = lax.axis_index(AXES) % 4
    gets_x = (kind == RELAY_X[0]) | (kind == RELAY_X[1])
    for over_x, index, source in ((True, 0, relay_x), (False, 0, relay_y), (False, 1, beside_x), (True, 1, beside_y)):
        @pl.when(gets_x == over_x)
        def _():
            pltpu.make_async_copy(source, stage.at[index], in_sem.at[index]).start()
    copies = [
        pltpu.make_async_copy(relay_x, stage.at[0], in_sem.at[0]),
        pltpu.make_async_copy(beside_x, stage.at[1], in_sem.at[1]),
        pltpu.make_async_copy(left_in, left, left_sem),
        pltpu.make_async_copy(prev, prev_stage, prev_sem),
    ]
    for copy in copies[2:]:
        copy.start()
    places = [pick(OFFSETS[name], kind) + z.hops for name in ("relay", "relay_beside")]
    low = jnp.maximum(0, jnp.minimum(*places) - z.hops)
    high = jnp.minimum(z.chunks, jnp.maximum(*places) + z.hops + 1)

    def chunk(n):
        return pl.ds(aligned(n, z.span), z.span)

    def clear_total(n, carry):
        total[:, chunk(n)] = jnp.zeros((z.span, z.span), jnp.float32)
        return carry

    def clear_right(n, carry):
        right[:, chunk(n)] = jnp.zeros((2 * z.span, z.span), right.dtype)
        return carry

    lax.fori_loop(0, low, clear_total, 0)
    lax.fori_loop(high, z.chunks, clear_total, 0)
    total[:, z.window * z.block:] = jnp.zeros((z.span, z.block), jnp.float32)
    decodings = []
    for index in range(2):
        copies[index].wait()
        decodings.append(decode(
            z, stage.at[index, z.rows * z.slots], places[index], vector.at[index], scalars.at[index],
            place_sem.at[index],
        ))
    lax.fori_loop(low, high, clear_right, 0)
    for index in range(2):
        decodings[index].wait()
        scatter(z, right, index * z.span, stage.at[index], lambda r, u: scalars[index, r, u])
    copies[2].wait()

    def multiply(n, carry):
        total[:, chunk(n)] = jnp.dot(left[...], right[:, chunk(n)], preferred_element_type=jnp.float32)
        return carry

    lax.fori_loop(low, high, multiply, 0)
    copies[3].wait()
    emit(z, total, positions, out_stage, out, out_sems, prev_stage)


ANY = pl.BlockSpec(memory_space=pl.ANY)
SMEM = pl.BlockSpec(memory_space=pltpu.SMEM)
VMEM = pl.BlockSpec(memory_space=pltpu.VMEM)
DMA = pltpu.SemaphoreType.DMA


def call(z, kernel, operands, in_specs, out_shape, out_specs, scratch, pieces, limit=VMEM_LIMIT):
    return pl.pallas_call(
        kernel,
        out_shape=out_shape,
        in_specs=in_specs,
        out_specs=out_specs,
        scratch_shapes=scratch,
        compiler_params=pltpu.CompilerParams(vmem_limit_bytes=limit),
        cost_estimate=pl.CostEstimate(
            flops=2 * z.span * z.span * z.window * z.block * pieces,
            bytes_accessed=2 * z.span * z.slots * z.block * (pieces + 4),
            transcendentals=0,
        ),
    )(*operands)


def shards(tiles, columns):
    devices = lax.axis_size(AXES)
    z = Sizes(tiles.shape, devices)
    assert z.hops == 3 and z.rows == 4 and devices % 4 == 0 and devices > 8
    dtype = tiles.dtype
    shape = jax.ShapeDtypeStruct
    sums = shape(tiles.shape, jnp.float32)
    line = shape((1, z.span), jnp.float32)
    dense = pltpu.VMEM((z.span, z.wide), dtype)
    total_buffer = pltpu.VMEM((z.span, z.wide), jnp.float32)

    payload_shape = (z.rows * z.slots + 1, z.block, z.block)
    places = [pltpu.VMEM((2, 16, z.block), jnp.int32), pltpu.SMEM((2, 16, z.block), jnp.int32)]

    payload = call(
        z, functools.partial(pack_body, z), [tiles, columns], [ANY, VMEM],
        shape(payload_shape, dtype), ANY,
        [
            pltpu.VMEM((z.rows * z.slots, z.block, z.block), dtype), pltpu.VMEM((16, z.block), jnp.int32),
            pltpu.VMEM((z.block, z.block), dtype), DMA((z.rows,)), DMA((z.rows + 1,)),
        ],
        0, WHOLE_VMEM,
    )
    over_x = receive(payload, OVER_X)
    over_y = receive(payload, OVER_Y)
    beside = receive(payload, PARTNER)

    total, left, corner, positions, trace = call(
        z, functools.partial(own_body, z), [tiles, columns], [ANY, SMEM],
        [
            sums, shape((z.span, z.wide), dtype), shape((z.span // 2, z.span), dtype),
            shape((z.rows, z.slots), jnp.int32), line,
        ],
        [ANY, ANY, ANY, SMEM, VMEM],
        [
            pltpu.VMEM(tiles.shape, dtype), dense, total_buffer, pltpu.VMEM(tiles.shape, jnp.float32),
            DMA, DMA, DMA, DMA((z.rows,)),
        ],
        1, WHOLE_VMEM,
    )
    corner = receive(corner, PARTNER, (0, 3))

    def near(names, arrays, total, trace, corner=None):
        final = corner is not None
        extra = [shape((z.span, 2 * z.span), dtype)] * final
        return call(
            z, functools.partial(near_body, z, names, final),
            [left, positions, total, trace] + [corner] * final + arrays,
            [ANY, SMEM, ANY, VMEM] + [VMEM] * final + [ANY] * len(arrays),
            [sums, line] + extra,
            [ANY, VMEM] + [ANY] * final,
            [
                dense, pltpu.VMEM((2,) + payload_shape, dtype),
                pltpu.VMEM((len(names), z.span, z.wide), dtype), total_buffer,
                pltpu.VMEM(tiles.shape, jnp.float32), *places,
                DMA, DMA((2,)), DMA, DMA((2,)), DMA((2,)), DMA((z.rows,)),
            ],
            len(names), VMEM_LIMIT if final else WHOLE_VMEM,
        )

    total, trace = near(("beside",), [beside], total, trace)
    over_x, over_y, corner, total, trace = lax.optimization_barrier((over_x, over_y, corner, total, trace))
    relay_x = receive(over_x, RELAY_FROM, RELAY_X)
    relay_y = receive(over_y, RELAY_FROM, RELAY_Y)
    x_beside = receive(over_x, PARTNER)
    corner = receive(corner, (0, -2, 2, 0), (LOWER, UPPER))
    total, trace, relay_left = near(
        ("x", "y", "x_beside"), [over_x, over_y, x_beside], total, trace, corner
    )
    assert devices & (devices - 1) == 0
    steps = [1 << bit for bit in range(devices.bit_length() - 1)]
    for step in steps[:1] + steps[3:]:
        trace = exchange(trace, step)
    relay_x, relay_y, total, trace = lax.optimization_barrier((relay_x, relay_y, total, trace))
    beside_x = receive(relay_x, PARTNER, RELAY_Y)
    beside_y = receive(relay_y, PARTNER, RELAY_X)
    others = [fetch(trace, step) for step in (steps[1], steps[2], steps[1] + steps[2])]
    square = call(
        z, functools.partial(last_body, z), [relay_left, positions, total, relay_x, relay_y, beside_x, beside_y],
        [ANY, SMEM] + [ANY] * 5,
        [shape(tiles.shape, dtype)],
        [ANY],
        [
            pltpu.VMEM((z.span, 2 * z.span), dtype), pltpu.VMEM((2,) + payload_shape, dtype),
            pltpu.VMEM((2 * z.span, z.wide), dtype), total_buffer,
            pltpu.VMEM(tiles.shape, dtype), pltpu.VMEM(tiles.shape, jnp.float32), *places,
            DMA, DMA((2,)), DMA, DMA((2,)), DMA((z.rows,)),
        ],
        2, 40 * 1024 * 1024,
    )[0]
    square, trace, others = lax.optimization_barrier((square, trace, others))
    return square, jnp.sum((trace + others[0]) + (others[1] + others[2])) / (z.all_rows * z.block)


def solution(mesh):
    return jax.shard_map(
        shards,
        mesh=mesh,
        in_specs=(P(AXES, None, None, None), P(AXES, None)),
        out_specs=(P(AXES, None, None, None), P()),
        check_vma=False,
    )
```

```python
import functools

import jax
import jax.numpy as jnp
from jax import lax
from jax.experimental import pallas as pl
from jax.experimental.pallas import tpu as pltpu
from jax.sharding import PartitionSpec as P

REACH = 12
AXES = ("blk", "grp")
VMEM_LIMIT = 42 * 1024 * 1024
WHOLE_VMEM = 60 * 1024 * 1024
EMPTY = 64

OVER_X = (2, 2, -2, -2)
OVER_Y = (-3, 3, -3, 3)
RELAY_FROM = (2, -5, 5, -2)
RELAY_X, RELAY_Y = (1, 2), (0, 3)
PARTNER = (1, -1, 1, -1)
RELAY = tuple(
    RELAY_FROM[m] + (OVER_X if m in RELAY_X else OVER_Y)[(m + RELAY_FROM[m]) % 4] for m in range(4)
)


def across(table):
    return tuple(PARTNER[m] + table[m ^ 1] for m in range(4))


OFFSETS = {
    "beside": PARTNER,
    "x": OVER_X,
    "y": OVER_Y,
    "x_beside": across(OVER_X),
    "relay": RELAY,
    "relay_beside": across(RELAY),
}
COUNTS = {"beside": (2, 0, 2, 0), "x": (2, 0, 0, 2), "y": (2, 0, 0, 2), "x_beside": (0, 0, 2, 2)}
OUTSIDE = {("y", "x_beside"): (0, 2, 2, 0), ("y", "x"): (0, 2, 0, 0)}
LOWER, UPPER = 2, 1


def receive(shard, offsets, kinds=range(4)):
    size = lax.axis_size(AXES)
    pairs = [((d + offsets[d % 4]) % size, d) for d in range(size) if d % 4 in kinds]
    return lax.ppermute(shard, AXES, pairs)


def fetch(value, step):
    return lax.ppermute(value, AXES, [(d, d ^ step) for d in range(lax.axis_size(AXES))])


def round_of(value, steps):
    if len(steps) == 1:
        return value + fetch(value, steps[0])
    one, other = steps
    return (value + fetch(value, one)) + (fetch(value, other) + fetch(value, one + other))


def pick(table, kind):
    value = jnp.int32(table[3])
    for m in range(3):
        value = jnp.where(kind == m, jnp.int32(table[m]), value)
    return value


def aligned(index, unit):
    return pl.multiple_of(index * unit, unit)


class Sizes:
    def __init__(self, shape, devices):
        self.rows, self.slots, self.block, _ = shape
        self.hops = (REACH + self.rows - 1) // self.rows
        self.chunks = 2 * self.hops + 1
        self.window = self.chunks * self.rows
        self.span = self.rows * self.block
        self.wide = (self.window + 1) * self.block
        self.all_rows = self.rows * devices

    def start(self, device):
        start = (device - self.hops) * self.rows
        return jnp.where(start < 0, start + self.all_rows, start)

    def position(self, column, start):
        place = column - start
        place = jnp.where(place < 0, place + self.all_rows, place)
        place = jnp.where(column < 0, self.window, place)
        return jnp.minimum(place, self.window)


def scatter(z, dense, top, source, place):
    for r in range(z.rows):
        def one(u, carry):
            column = pl.ds(aligned(place(r, u), z.block), z.block)
            dense[top + r * z.block:top + (r + 1) * z.block, column] = source[r * z.slots + u]
            return carry
        lax.fori_loop(0, z.slots, one, 0, unroll=10)


def decode(z, offsets, spot, vector, scalars, sem):
    value = offsets[0:16, :].astype(jnp.float32).astype(jnp.int32)
    value = value + spot * z.rows + lax.broadcasted_iota(jnp.int32, value.shape, 0)
    vector[...] = jnp.where((value < 0) | (value > z.window), z.window, value)
    copy = pltpu.make_async_copy(vector, scalars, sem)
    copy.start()
    return copy


def pack_body(z, tiles, columns, out, stage, padded, offsets, in_sems, out_sems):
    copies = []
    for r in range(z.rows):
        rows = pl.ds(r * z.slots, z.slots)
        copies.append((
            pltpu.make_async_copy(tiles.at[r], stage.at[rows], in_sems.at[r]),
            pltpu.make_async_copy(stage.at[rows], out.at[rows], out_sems.at[r]),
        ))
    for copy, _ in copies:
        copy.start()
    padded[...] = jnp.full(padded.shape, -1, jnp.int32)
    padded[:z.rows, :z.slots] = columns[...]
    column = padded[...]
    row = lax.axis_index(AXES) * z.rows + lax.broadcasted_iota(jnp.int32, column.shape, 0)
    offset = column - row
    offset = jnp.where(offset > z.all_rows // 2, offset - z.all_rows, offset)
    offset = jnp.where(offset < -(z.all_rows // 2), offset + z.all_rows, offset)
    offset = jnp.where(column < 0, EMPTY, offset)
    offsets[...] = jnp.zeros_like(offsets)
    offsets[0:16, :] = offset.astype(jnp.float32).astype(offsets.dtype)
    last = pltpu.make_async_copy(offsets, out.at[z.rows * z.slots], out_sems.at[z.rows])
    last.start()
    for load, store in copies:
        load.wait()
        store.start()
    for _, store in copies:
        store.wait()
    last.wait()


def emit(z, total, positions, stage, out, sems, prev=None):
    for r in range(z.rows):
        def one(s, carry):
            value = total[r * z.block:(r + 1) * z.block, pl.ds(aligned(positions[r, s], z.block), z.block)]
            if prev is not None:
                value = value + prev[r, s]
            stage[r, s] = value.astype(stage.dtype)
            return carry
        lax.fori_loop(0, z.slots, one, 0, unroll=10)
        pltpu.make_async_copy(stage.at[r], out.at[r], sems.at[r]).start()
    for r in range(z.rows):
        pltpu.make_async_copy(stage.at[r], out.at[r], sems.at[r]).wait()


def add_trace(trace, weight, one, other):
    value = jnp.dot(one, other, preferred_element_type=jnp.float32)
    on = lax.broadcasted_iota(jnp.int32, value.shape, 0) == lax.broadcasted_iota(jnp.int32, value.shape, 1)
    diagonal = jnp.sum(jnp.where(on, value, 0.0), axis=0, keepdims=True)
    trace[:, :value.shape[1]] += weight.astype(jnp.float32) * diagonal


def own_body(z, own, columns, out, left_out, corner_out, positions, trace, stage, left, total, out_stage,
             in_sem, left_sem, corner_sem, out_sems):
    device = lax.axis_index(AXES)
    kind = device % 4
    copy = pltpu.make_async_copy(own, stage, in_sem)
    copy.start()
    left[...] = jnp.zeros_like(left)
    total[:, z.window * z.block:] = jnp.zeros((z.span, z.block), jnp.float32)
    copy.wait()
    start = z.start(device)
    for r in range(z.rows):
        def place(u, carry):
            column = z.position(columns[r, u], start)
            positions[r, u] = column
            left[r * z.block:(r + 1) * z.block, pl.ds(aligned(column, z.block), z.block)] = stage[r, u]
            return carry
        lax.fori_loop(0, z.slots, place, 0, unroll=10)
    left_copy = pltpu.make_async_copy(left, left_out, left_sem)
    left_copy.start()
    half = z.span // 2

    def corner(start):
        def go(rows, cols):
            copy = pltpu.make_async_copy(left.at[rows, cols], corner_out, corner_sem)
            copy.start() if start else copy.wait()
        pl.when(kind == UPPER)(lambda: go(pl.ds(0, half), pl.ds(0, z.span)))
        pl.when(kind != UPPER)(
            lambda: go(pl.ds(half, half), pl.ds((z.chunks - 1) * z.span, z.span))
        )

    corner(True)
    middle = slice(z.hops * z.span, (z.hops + 1) * z.span)

    def multiply(n, carry):
        cols = pl.ds(aligned(n, z.span), z.span)
        total[:, cols] = jnp.dot(left[:, middle], left[:, cols], preferred_element_type=jnp.float32)
        return carry

    lax.fori_loop(0, z.chunks, multiply, 0)
    trace[...] = jnp.zeros_like(trace)
    add_trace(trace, jnp.float32(1), left[:, middle], left[:, middle])
    emit(z, total, positions, out_stage, out, out_sems)
    corner(False)
    left_copy.wait()


def near_body(z, names, final, left_in, positions, prev, trace_in, *refs):
    refs = list(refs)
    take = lambda count: [refs.pop(0) for _ in range(count)]
    sources = take(len(names))
    out, trace = take(2)
    relay_left = take(1)[0] if final else None
    left, stage, right, total, sums, vector, scalars = take(7)
    left_sem, in_sem, prev_sem, place_sem, relay_sem, out_sems = take(6)
    device = lax.axis_index(AXES)
    kind = device % 4
    place = {name: pick(table, kind) + z.hops for name, table in OFFSETS.items()}

    def chunk(n):
        return pl.ds(aligned(n, z.span), z.span)

    def fetch(index):
        return pltpu.make_async_copy(sources[index], stage.at[index % 2], in_sem.at[index % 2])

    left_copy = pltpu.make_async_copy(left_in, left, left_sem)
    left_copy.start()
    for index in range(min(2, len(names))):
        fetch(index).start()
    prev_copy = pltpu.make_async_copy(prev, sums, prev_sem)
    prev_copy.start()
    total[...] = jnp.zeros_like(total)
    trace[...] = trace_in[...]
    left_copy.wait()
    relay_copies = []
    for index, name in enumerate(("relay", "relay_beside") if final else ()):
        copy = pltpu.make_async_copy(
            left.at[:, chunk(place[name])], relay_left.at[:, pl.ds(index * z.span, z.span)],
            relay_sem.at[index],
        )
        copy.start()
        relay_copies.append(copy)
    decodings = []

    def begin_decode(index):
        slot = index % 2
        fetch(index).wait()
        decodings.append(decode(
            z, stage.at[slot, z.rows * z.slots], place[names[index]], vector.at[slot], scalars.at[slot],
            place_sem.at[slot],
        ))

    begin_decode(0)
    dense_of = {}
    for index, name in enumerate(names):
        dense = right.at[index]
        dense_of[name] = dense
        spot = place[name]
        slot = index % 2
        dense[...] = jnp.zeros_like(dense)
        decodings[index].wait()
        scatter(z, dense, 0, stage.at[slot], lambda r, u: scalars[slot, r, u])
        if index + 2 < len(names):
            fetch(index + 2).start()
        if index + 1 < len(names):
            begin_decode(index + 1)

        def multiply(n, carry):
            total[:, chunk(n)] += jnp.dot(
                left[:, chunk(spot)], dense[:, chunk(n)], preferred_element_type=jnp.float32
            )
            return carry

        lax.fori_loop(jnp.maximum(0, spot - z.hops), jnp.minimum(z.chunks, spot + z.hops + 1), multiply, 0)
        weight = pick(COUNTS[name], kind)
        pl.when(weight != 0)(
            lambda: add_trace(trace, weight, left[:, chunk(spot)], dense[:, chunk(z.hops)])
        )
    for (one, other), table in OUTSIDE.items() if final else ():
        weight = pick(table, kind)
        pl.when(weight != 0)(lambda: add_trace(
            trace, weight, dense_of[one][:, chunk(place[other])], dense_of[other][:, chunk(place[one])]
        ))
    prev_copy.wait()
    emit(z, total, positions, sums, out, out_sems, sums)
    for copy in relay_copies:
        copy.wait()


def corner_body(z, left, corner, trace_in, trace, rows, sem):
    kind = lax.axis_index(AXES) % 4
    half = z.span // 2
    end = (z.chunks - 1) * z.span
    trace[...] = trace_in[...]

    @pl.when(kind == UPPER)
    def _():
        copy = pltpu.make_async_copy(left.at[:, pl.ds(half, half)], rows, sem)
        copy.start()
        copy.wait()
        add_trace(trace, jnp.float32(2), rows[...], corner[...])

    @pl.when(kind == LOWER)
    def _():
        copy = pltpu.make_async_copy(left.at[pl.ds(0, half), pl.ds(end, half)], rows.at[pl.ds(0, half)], sem)
        copy.start()
        copy.wait()
        add_trace(trace, jnp.float32(2), rows[:half], corner[:, :half])


def last_body(z, left_in, positions, prev, relay_x, relay_y, beside_x, beside_y, out, left, stage, right, total, out_stage,
              prev_stage, vector, scalars, left_sem, in_sem, prev_sem, place_sem, out_sems):
    kind = lax.axis_index(AXES) % 4
    gets_x = (kind == RELAY_X[0]) | (kind == RELAY_X[1])
    for over_x, index, source in ((True, 0, relay_x), (False, 0, relay_y), (False, 1, beside_x), (True, 1, beside_y)):
        @pl.when(gets_x == over_x)
        def _():
            pltpu.make_async_copy(source, stage.at[index], in_sem.at[index]).start()
    copies = [
        pltpu.make_async_copy(relay_x, stage.at[0], in_sem.at[0]),
        pltpu.make_async_copy(beside_x, stage.at[1], in_sem.at[1]),
        pltpu.make_async_copy(left_in, left, left_sem),
        pltpu.make_async_copy(prev, prev_stage, prev_sem),
    ]
    for copy in copies[2:]:
        copy.start()
    places = [pick(OFFSETS[name], kind) + z.hops for name in ("relay", "relay_beside")]
    low = jnp.maximum(0, jnp.minimum(*places) - z.hops)
    high = jnp.minimum(z.chunks, jnp.maximum(*places) + z.hops + 1)

    def chunk(n):
        return pl.ds(aligned(n, z.span), z.span)

    def clear_total(n, carry):
        total[:, chunk(n)] = jnp.zeros((z.span, z.span), jnp.float32)
        return carry

    def clear_right(n, carry):
        right[:, chunk(n)] = jnp.zeros((2 * z.span, z.span), right.dtype)
        return carry

    lax.fori_loop(0, low, clear_total, 0)
    lax.fori_loop(high, z.chunks, clear_total, 0)
    total[:, z.window * z.block:] = jnp.zeros((z.span, z.block), jnp.float32)
    decodings = []
    for index in range(2):
        copies[index].wait()
        decodings.append(decode(
            z, stage.at[index, z.rows * z.slots], places[index], vector.at[index], scalars.at[index],
            place_sem.at[index],
        ))
    lax.fori_loop(low, high, clear_right, 0)
    for index in range(2):
        decodings[index].wait()
        scatter(z, right, index * z.span, stage.at[index], lambda r, u: scalars[index, r, u])
    copies[2].wait()

    def multiply(n, carry):
        total[:, chunk(n)] = jnp.dot(left[...], right[:, chunk(n)], preferred_element_type=jnp.float32)
        return carry

    lax.fori_loop(low, high, multiply, 0)
    copies[3].wait()
    emit(z, total, positions, out_stage, out, out_sems, prev_stage)


ANY = pl.BlockSpec(memory_space=pl.ANY)
SMEM = pl.BlockSpec(memory_space=pltpu.SMEM)
VMEM = pl.BlockSpec(memory_space=pltpu.VMEM)
DMA = pltpu.SemaphoreType.DMA


def call(z, kernel, operands, in_specs, out_shape, out_specs, scratch, pieces, limit=VMEM_LIMIT):
    return pl.pallas_call(
        kernel,
        out_shape=out_shape,
        in_specs=in_specs,
        out_specs=out_specs,
        scratch_shapes=scratch,
        compiler_params=pltpu.CompilerParams(vmem_limit_bytes=limit),
        cost_estimate=pl.CostEstimate(
            flops=2 * z.span * z.span * z.window * z.block * pieces,
            bytes_accessed=2 * z.span * z.slots * z.block * (pieces + 4),
            transcendentals=0,
        ),
    )(*operands)


def shards(tiles, columns):
    devices = lax.axis_size(AXES)
    z = Sizes(tiles.shape, devices)
    assert z.hops == 3 and z.rows == 4 and devices % 4 == 0 and devices > 8
    dtype = tiles.dtype
    shape = jax.ShapeDtypeStruct
    sums = shape(tiles.shape, jnp.float32)
    line = shape((1, z.span), jnp.float32)
    dense = pltpu.VMEM((z.span, z.wide), dtype)
    total_buffer = pltpu.VMEM((z.span, z.wide), jnp.float32)

    payload_shape = (z.rows * z.slots + 1, z.block, z.block)
    places = [pltpu.VMEM((2, 16, z.block), jnp.int32), pltpu.SMEM((2, 16, z.block), jnp.int32)]

    payload = call(
        z, functools.partial(pack_body, z), [tiles, columns], [ANY, VMEM],
        shape(payload_shape, dtype), ANY,
        [
            pltpu.VMEM((z.rows * z.slots, z.block, z.block), dtype), pltpu.VMEM((16, z.block), jnp.int32),
            pltpu.VMEM((z.block, z.block), dtype), DMA((z.rows,)), DMA((z.rows + 1,)),
        ],
        0, WHOLE_VMEM,
    )
    over_x = receive(payload, OVER_X)
    over_y = receive(payload, OVER_Y)
    beside = receive(payload, PARTNER)

    total, left, corner, positions, trace = call(
        z, functools.partial(own_body, z), [tiles, columns], [ANY, SMEM],
        [
            sums, shape((z.span, z.wide), dtype), shape((z.span // 2, z.span), dtype),
            shape((z.rows, z.slots), jnp.int32), line,
        ],
        [ANY, ANY, ANY, SMEM, VMEM],
        [
            pltpu.VMEM(tiles.shape, dtype), dense, total_buffer, pltpu.VMEM(tiles.shape, jnp.float32),
            DMA, DMA, DMA, DMA((z.rows,)),
        ],
        1, WHOLE_VMEM,
    )
    corner = receive(corner, PARTNER, (0, 3))

    def near(names, arrays, total, trace, final=False):
        extra = [shape((z.span, 2 * z.span), dtype)] * final
        return call(
            z, functools.partial(near_body, z, names, final),
            [left, positions, total, trace] + arrays,
            [ANY, SMEM, ANY, VMEM] + [ANY] * len(arrays),
            [sums, line] + extra,
            [ANY, VMEM] + [ANY] * final,
            [
                dense, pltpu.VMEM((2,) + payload_shape, dtype),
                pltpu.VMEM((len(names), z.span, z.wide), dtype), total_buffer,
                pltpu.VMEM(tiles.shape, jnp.float32), *places,
                DMA, DMA((2,)), DMA, DMA((2,)), DMA((2,)), DMA((z.rows,)),
            ],
            len(names), VMEM_LIMIT if final else WHOLE_VMEM,
        )

    total, trace = near(("beside",), [beside], total, trace)
    over_x, over_y, corner, total, trace = lax.optimization_barrier((over_x, over_y, corner, total, trace))
    relay_x = receive(over_x, RELAY_FROM, RELAY_X)
    relay_y = receive(over_y, RELAY_FROM, RELAY_Y)
    x_beside = receive(over_x, PARTNER)
    corner = receive(corner, (0, -2, 2, 0), (LOWER, UPPER))
    total, trace, relay_left = near(
        ("x", "y", "x_beside"), [over_x, over_y, x_beside], total, trace, True
    )
    trace = call(
        z, functools.partial(corner_body, z), [left, corner, trace], [ANY, VMEM, VMEM], line, VMEM,
        [pltpu.VMEM((z.span, z.span // 2), dtype), DMA], 0,
    )
    assert devices & (devices - 1) == 0
    steps = [1 << bit for bit in range(devices.bit_length() - 1)]
    trace = trace + fetch(trace, steps[0])
    for index in range(3, len(steps), 2):
        trace = round_of(trace, steps[index:index + 2])
    relay_x, relay_y, total, trace = lax.optimization_barrier((relay_x, relay_y, total, trace))
    beside_x = receive(relay_x, PARTNER, RELAY_Y)
    beside_y = receive(relay_y, PARTNER, RELAY_X)
    others = [fetch(trace, step) for step in (steps[1], steps[2], steps[1] + steps[2])]
    square = call(
        z, functools.partial(last_body, z), [relay_left, positions, total, relay_x, relay_y, beside_x, beside_y],
        [ANY, SMEM] + [ANY] * 5,
        [shape(tiles.shape, dtype)],
        [ANY],
        [
            pltpu.VMEM((z.span, 2 * z.span), dtype), pltpu.VMEM((2,) + payload_shape, dtype),
            pltpu.VMEM((2 * z.span, z.wide), dtype), total_buffer,
            pltpu.VMEM(tiles.shape, dtype), pltpu.VMEM(tiles.shape, jnp.float32), *places,
            DMA, DMA((2,)), DMA, DMA((2,)), DMA((z.rows,)),
        ],
        2, 40 * 1024 * 1024,
    )[0]
    square, trace, others = lax.optimization_barrier((square, trace, others))
    return square, jnp.sum((trace + others[0]) + (others[1] + others[2])) / (z.all_rows * z.block)


def solution(mesh):
    return jax.shard_map(
        shards,
        mesh=mesh,
        in_specs=(P(AXES, None, None, None), P(AXES, None)),
        out_specs=(P(AXES, None, None, None), P()),
        check_vma=False,
    )
```

```python
import functools

import jax
import jax.numpy as jnp
from jax import lax
from jax.experimental import pallas as pl
from jax.experimental.pallas import tpu as pltpu
from jax.sharding import PartitionSpec as P

REACH = 12
AXES = ("blk", "grp")
VMEM_LIMIT = 42 * 1024 * 1024
WHOLE_VMEM = 60 * 1024 * 1024
EMPTY = 64

OVER_X = (2, 2, -2, -2)
OVER_Y = (-3, 3, -3, 3)
RELAY_FROM = (2, -5, 5, -2)
RELAY_X, RELAY_Y = (1, 2), (0, 3)
PARTNER = (1, -1, 1, -1)
RELAY = tuple(
    RELAY_FROM[m] + (OVER_X if m in RELAY_X else OVER_Y)[(m + RELAY_FROM[m]) % 4] for m in range(4)
)


def across(table):
    return tuple(PARTNER[m] + table[m ^ 1] for m in range(4))


OFFSETS = {
    "beside": PARTNER,
    "x": OVER_X,
    "y": OVER_Y,
    "x_beside": across(OVER_X),
    "relay": RELAY,
    "relay_beside": across(RELAY),
}
COUNTS = {"beside": (2, 0, 2, 0), "x": (2, 0, 0, 2), "y": (2, 0, 0, 2), "x_beside": (0, 0, 2, 2)}
OUTSIDE = {("y", "x_beside"): (0, 2, 2, 0), ("y", "x"): (0, 2, 0, 0)}
LOWER, UPPER = 2, 1


def receive(shard, offsets, kinds=range(4)):
    size = lax.axis_size(AXES)
    pairs = [((d + offsets[d % 4]) % size, d) for d in range(size) if d % 4 in kinds]
    return lax.ppermute(shard, AXES, pairs)


def fetch(value, step):
    return lax.ppermute(value, AXES, [(d, d ^ step) for d in range(lax.axis_size(AXES))])


def round_of(value, steps):
    if len(steps) == 1:
        return value + fetch(value, steps[0])
    one, other = steps
    return (value + fetch(value, one)) + (fetch(value, other) + fetch(value, one + other))


def pick(table, kind):
    value = jnp.int32(table[3])
    for m in range(3):
        value = jnp.where(kind == m, jnp.int32(table[m]), value)
    return value


def aligned(index, unit):
    return pl.multiple_of(index * unit, unit)


class Sizes:
    def __init__(self, shape, devices):
        self.rows, self.slots, self.block, _ = shape
        self.hops = (REACH + self.rows - 1) // self.rows
        self.chunks = 2 * self.hops + 1
        self.window = self.chunks * self.rows
        self.span = self.rows * self.block
        self.wide = (self.window + 1) * self.block
        self.all_rows = self.rows * devices

    def start(self, device):
        start = (device - self.hops) * self.rows
        return jnp.where(start < 0, start + self.all_rows, start)

    def position(self, column, start):
        place = column - start
        place = jnp.where(place < 0, place + self.all_rows, place)
        place = jnp.where(column < 0, self.window, place)
        return jnp.minimum(place, self.window)


def scatter(z, dense, top, source, place):
    for r in range(z.rows):
        def one(u, carry):
            column = pl.ds(aligned(place(r, u), z.block), z.block)
            dense[top + r * z.block:top + (r + 1) * z.block, column] = source[r * z.slots + u]
            return carry
        lax.fori_loop(0, z.slots, one, 0, unroll=10)


def decode(z, offsets, spot, vector, scalars, sem):
    value = offsets[0:16, :].astype(jnp.float32).astype(jnp.int32)
    value = value + spot * z.rows + lax.broadcasted_iota(jnp.int32, value.shape, 0)
    vector[...] = jnp.where((value < 0) | (value > z.window), z.window, value)
    copy = pltpu.make_async_copy(vector, scalars, sem)
    copy.start()
    return copy


def pack_body(z, tiles, columns, out, stage, padded, offsets, in_sems, out_sems):
    copies = []
    for r in range(z.rows):
        rows = pl.ds(r * z.slots, z.slots)
        copies.append((
            pltpu.make_async_copy(tiles.at[r], stage.at[rows], in_sems.at[r]),
            pltpu.make_async_copy(stage.at[rows], out.at[rows], out_sems.at[r]),
        ))
    for copy, _ in copies:
        copy.start()
    padded[...] = jnp.full(padded.shape, -1, jnp.int32)
    padded[:z.rows, :z.slots] = columns[...]
    column = padded[...]
    row = lax.axis_index(AXES) * z.rows + lax.broadcasted_iota(jnp.int32, column.shape, 0)
    offset = column - row
    offset = jnp.where(offset > z.all_rows // 2, offset - z.all_rows, offset)
    offset = jnp.where(offset < -(z.all_rows // 2), offset + z.all_rows, offset)
    offset = jnp.where(column < 0, EMPTY, offset)
    offsets[...] = jnp.zeros_like(offsets)
    offsets[0:16, :] = offset.astype(jnp.float32).astype(offsets.dtype)
    last = pltpu.make_async_copy(offsets, out.at[z.rows * z.slots], out_sems.at[z.rows])
    last.start()
    for load, store in copies:
        load.wait()
        store.start()
    for _, store in copies:
        store.wait()
    last.wait()


def emit(z, total, positions, stage, out, sems, prev=None):
    for r in range(z.rows):
        def one(s, carry):
            value = total[r * z.block:(r + 1) * z.block, pl.ds(aligned(positions[r, s], z.block), z.block)]
            if prev is not None:
                value = value + prev[r, s]
            stage[r, s] = value.astype(stage.dtype)
            return carry
        lax.fori_loop(0, z.slots, one, 0, unroll=10)
        pltpu.make_async_copy(stage.at[r], out.at[r], sems.at[r]).start()
    for r in range(z.rows):
        pltpu.make_async_copy(stage.at[r], out.at[r], sems.at[r]).wait()


def add_trace(trace, weight, one, other):
    value = jnp.dot(one, other, preferred_element_type=jnp.float32)
    on = lax.broadcasted_iota(jnp.int32, value.shape, 0) == lax.broadcasted_iota(jnp.int32, value.shape, 1)
    diagonal = jnp.sum(jnp.where(on, value, 0.0), axis=0, keepdims=True)
    trace[:, :value.shape[1]] += weight.astype(jnp.float32) * diagonal


def own_body(z, own, columns, out, left_out, corner_out, positions, trace, stage, left, total, out_stage,
             in_sem, left_sem, corner_sem, out_sems):
    device = lax.axis_index(AXES)
    kind = device % 4
    copy = pltpu.make_async_copy(own, stage, in_sem)
    copy.start()
    left[...] = jnp.zeros_like(left)
    total[:, z.window * z.block:] = jnp.zeros((z.span, z.block), jnp.float32)
    copy.wait()
    start = z.start(device)
    for r in range(z.rows):
        def place(u, carry):
            column = z.position(columns[r, u], start)
            positions[r, u] = column
            left[r * z.block:(r + 1) * z.block, pl.ds(aligned(column, z.block), z.block)] = stage[r, u]
            return carry
        lax.fori_loop(0, z.slots, place, 0, unroll=10)
    left_copy = pltpu.make_async_copy(left, left_out, left_sem)
    left_copy.start()
    half = z.span // 2

    def corner(start):
        def go(rows, cols):
            copy = pltpu.make_async_copy(left.at[rows, cols], corner_out, corner_sem)
            copy.start() if start else copy.wait()
        pl.when(kind == UPPER)(lambda: go(pl.ds(0, half), pl.ds(0, z.span)))
        pl.when(kind != UPPER)(
            lambda: go(pl.ds(half, half), pl.ds((z.chunks - 1) * z.span, z.span))
        )

    corner(True)
    middle = slice(z.hops * z.span, (z.hops + 1) * z.span)

    def multiply(n, carry):
        cols = pl.ds(aligned(n, z.span), z.span)
        total[:, cols] = jnp.dot(left[:, middle], left[:, cols], preferred_element_type=jnp.float32)
        return carry

    lax.fori_loop(0, z.chunks, multiply, 0)
    trace[...] = jnp.zeros_like(trace)
    add_trace(trace, jnp.float32(1), left[:, middle], left[:, middle])
    emit(z, total, positions, out_stage, out, out_sems)
    corner(False)
    left_copy.wait()


def near_body(z, names, final, left_in, positions, prev, trace_in, *refs):
    refs = list(refs)
    take = lambda count: [refs.pop(0) for _ in range(count)]
    sources = take(len(names))
    out, trace = take(2)
    relay_left = take(1)[0] if final else None
    left, stage, right, total, sums, vector, scalars = take(7)
    left_sem, in_sem, prev_sem, place_sem, relay_sem, out_sems = take(6)
    device = lax.axis_index(AXES)
    kind = device % 4
    place = {name: pick(table, kind) + z.hops for name, table in OFFSETS.items()}

    def chunk(n):
        return pl.ds(aligned(n, z.span), z.span)

    def fetch(index):
        return pltpu.make_async_copy(sources[index], stage.at[index % 2], in_sem.at[index % 2])

    left_copy = pltpu.make_async_copy(left_in, left, left_sem)
    left_copy.start()
    for index in range(min(2, len(names))):
        fetch(index).start()
    prev_copy = pltpu.make_async_copy(prev, sums, prev_sem)
    prev_copy.start()
    total[...] = jnp.zeros_like(total)
    trace[...] = trace_in[...]
    left_copy.wait()
    relay_copies = []
    for index, name in enumerate(("relay", "relay_beside") if final else ()):
        copy = pltpu.make_async_copy(
            left.at[:, chunk(place[name])], relay_left.at[:, pl.ds(index * z.span, z.span)],
            relay_sem.at[index],
        )
        copy.start()
        relay_copies.append(copy)
    decodings = []

    def begin_decode(index):
        slot = index % 2
        fetch(index).wait()
        decodings.append(decode(
            z, stage.at[slot, z.rows * z.slots], place[names[index]], vector.at[slot], scalars.at[slot],
            place_sem.at[slot],
        ))

    begin_decode(0)
    dense_of = {}
    for index, name in enumerate(names):
        dense = right.at[index]
        dense_of[name] = dense
        spot = place[name]
        slot = index % 2
        dense[...] = jnp.zeros_like(dense)
        decodings[index].wait()
        scatter(z, dense, 0, stage.at[slot], lambda r, u: scalars[slot, r, u])
        if index + 2 < len(names):
            fetch(index + 2).start()
        if index + 1 < len(names):
            begin_decode(index + 1)

        def multiply(n, carry):
            total[:, chunk(n)] += jnp.dot(
                left[:, chunk(spot)], dense[:, chunk(n)], preferred_element_type=jnp.float32
            )
            return carry

        lax.fori_loop(jnp.maximum(0, spot - z.hops), jnp.minimum(z.chunks, spot + z.hops + 1), multiply, 0)
        weight = pick(COUNTS[name], kind)
        pl.when(weight != 0)(
            lambda: add_trace(trace, weight, left[:, chunk(spot)], dense[:, chunk(z.hops)])
        )
    for (one, other), table in OUTSIDE.items() if final else ():
        weight = pick(table, kind)
        pl.when(weight != 0)(lambda: add_trace(
            trace, weight, dense_of[one][:, chunk(place[other])], dense_of[other][:, chunk(place[one])]
        ))
    prev_copy.wait()
    emit(z, total, positions, sums, out, out_sems, sums)
    for copy in relay_copies:
        copy.wait()


def corner_body(z, left, corner, trace_in, trace, rows, sem):
    kind = lax.axis_index(AXES) % 4
    half = z.span // 2
    end = (z.chunks - 1) * z.span
    trace[...] = trace_in[...]

    @pl.when(kind == UPPER)
    def _():
        copy = pltpu.make_async_copy(left.at[:, pl.ds(half, half)], rows, sem)
        copy.start()
        copy.wait()
        add_trace(trace, jnp.float32(2), rows[...], corner[...])

    @pl.when(kind == LOWER)
    def _():
        copy = pltpu.make_async_copy(left.at[pl.ds(0, half), pl.ds(end, half)], rows.at[pl.ds(0, half)], sem)
        copy.start()
        copy.wait()
        add_trace(trace, jnp.float32(2), rows[:half], corner[:, :half])


def last_body(z, left_in, positions, prev, relay_x, relay_y, beside_x, beside_y, out, left, stage, right, total, out_stage,
              prev_stage, vector, scalars, left_sem, in_sem, prev_sem, place_sem, out_sems):
    kind = lax.axis_index(AXES) % 4
    gets_x = (kind == RELAY_X[0]) | (kind == RELAY_X[1])
    for over_x, index, source in ((True, 0, relay_x), (False, 0, relay_y), (False, 1, beside_x), (True, 1, beside_y)):
        @pl.when(gets_x == over_x)
        def _():
            pltpu.make_async_copy(source, stage.at[index], in_sem.at[index]).start()
    copies = [
        pltpu.make_async_copy(relay_x, stage.at[0], in_sem.at[0]),
        pltpu.make_async_copy(beside_x, stage.at[1], in_sem.at[1]),
        pltpu.make_async_copy(left_in, left, left_sem),
        pltpu.make_async_copy(prev, prev_stage, prev_sem),
    ]
    for copy in copies[2:]:
        copy.start()
    places = [pick(OFFSETS[name], kind) + z.hops for name in ("relay", "relay_beside")]
    low = jnp.maximum(0, jnp.minimum(*places) - z.hops)
    high = jnp.minimum(z.chunks, jnp.maximum(*places) + z.hops + 1)

    def chunk(n):
        return pl.ds(aligned(n, z.span), z.span)

    def clear_total(n, carry):
        total[:, chunk(n)] = jnp.zeros((z.span, z.span), jnp.float32)
        return carry

    def clear_right(n, carry):
        right[:, chunk(n)] = jnp.zeros((2 * z.span, z.span), right.dtype)
        return carry

    lax.fori_loop(0, low, clear_total, 0)
    lax.fori_loop(high, z.chunks, clear_total, 0)
    total[:, z.window * z.block:] = jnp.zeros((z.span, z.block), jnp.float32)
    decodings = []
    for index in range(2):
        copies[index].wait()
        decodings.append(decode(
            z, stage.at[index, z.rows * z.slots], places[index], vector.at[index], scalars.at[index],
            place_sem.at[index],
        ))
    lax.fori_loop(low, high, clear_right, 0)
    for index in range(2):
        decodings[index].wait()
        scatter(z, right, index * z.span, stage.at[index], lambda r, u: scalars[index, r, u])
    copies[2].wait()

    def multiply(n, carry):
        total[:, chunk(n)] = jnp.dot(left[...], right[:, chunk(n)], preferred_element_type=jnp.float32)
        return carry

    lax.fori_loop(low, high, multiply, 0)
    copies[3].wait()
    emit(z, total, positions, out_stage, out, out_sems, prev_stage)


ANY = pl.BlockSpec(memory_space=pl.ANY)
SMEM = pl.BlockSpec(memory_space=pltpu.SMEM)
VMEM = pl.BlockSpec(memory_space=pltpu.VMEM)
DMA = pltpu.SemaphoreType.DMA


def call(z, kernel, operands, in_specs, out_shape, out_specs, scratch, pieces, limit=VMEM_LIMIT):
    return pl.pallas_call(
        kernel,
        out_shape=out_shape,
        in_specs=in_specs,
        out_specs=out_specs,
        scratch_shapes=scratch,
        compiler_params=pltpu.CompilerParams(vmem_limit_bytes=limit),
        cost_estimate=pl.CostEstimate(
            flops=2 * z.span * z.span * z.window * z.block * pieces,
            bytes_accessed=2 * z.span * z.slots * z.block * (pieces + 4),
            transcendentals=0,
        ),
    )(*operands)


def shards(tiles, columns):
    devices = lax.axis_size(AXES)
    z = Sizes(tiles.shape, devices)
    assert z.hops == 3 and z.rows == 4 and devices % 4 == 0 and devices > 8
    dtype = tiles.dtype
    shape = jax.ShapeDtypeStruct
    sums = shape(tiles.shape, jnp.float32)
    line = shape((1, z.span), jnp.float32)
    dense = pltpu.VMEM((z.span, z.wide), dtype)
    total_buffer = pltpu.VMEM((z.span, z.wide), jnp.float32)

    payload_shape = (z.rows * z.slots + 1, z.block, z.block)
    places = [pltpu.VMEM((2, 16, z.block), jnp.int32), pltpu.SMEM((2, 16, z.block), jnp.int32)]

    payload = call(
        z, functools.partial(pack_body, z), [tiles, columns], [ANY, VMEM],
        shape(payload_shape, dtype), ANY,
        [
            pltpu.VMEM((z.rows * z.slots, z.block, z.block), dtype), pltpu.VMEM((16, z.block), jnp.int32),
            pltpu.VMEM((z.block, z.block), dtype), DMA((z.rows,)), DMA((z.rows + 1,)),
        ],
        0, WHOLE_VMEM,
    )
    over_x = receive(payload, OVER_X)
    over_y = receive(payload, OVER_Y)
    beside = receive(payload, PARTNER)

    total, left, corner, positions, trace = call(
        z, functools.partial(own_body, z), [tiles, columns], [ANY, SMEM],
        [
            sums, shape((z.span, z.wide), dtype), shape((z.span // 2, z.span), dtype),
            shape((z.rows, z.slots), jnp.int32), line,
        ],
        [ANY, ANY, ANY, SMEM, VMEM],
        [
            pltpu.VMEM(tiles.shape, dtype), dense, total_buffer, pltpu.VMEM(tiles.shape, jnp.float32),
            DMA, DMA, DMA, DMA((z.rows,)),
        ],
        1, WHOLE_VMEM,
    )
    corner = receive(corner, PARTNER, (0, 3))

    def near(names, arrays, total, trace, final=False):
        extra = [shape((z.span, 2 * z.span), dtype)] * final
        return call(
            z, functools.partial(near_body, z, names, final),
            [left, positions, total, trace] + arrays,
            [ANY, SMEM, ANY, VMEM] + [ANY] * len(arrays),
            [sums, line] + extra,
            [ANY, VMEM] + [ANY] * final,
            [
                dense, pltpu.VMEM((2,) + payload_shape, dtype),
                pltpu.VMEM((len(names), z.span, z.wide), dtype), total_buffer,
                pltpu.VMEM(tiles.shape, jnp.float32), *places,
                DMA, DMA((2,)), DMA, DMA((2,)), DMA((2,)), DMA((z.rows,)),
            ],
            len(names), VMEM_LIMIT if final else WHOLE_VMEM,
        )

    total, trace = near(("beside",), [beside], total, trace)
    over_x, over_y, corner, total, trace = lax.optimization_barrier((over_x, over_y, corner, total, trace))
    relay_x = receive(over_x, RELAY_FROM, RELAY_X)
    relay_y = receive(over_y, RELAY_FROM, RELAY_Y)
    x_beside = receive(over_x, PARTNER)
    corner = receive(corner, (0, -2, 2, 0), (LOWER, UPPER))
    total, trace, relay_left = near(
        ("x", "y", "x_beside"), [over_x, over_y, x_beside], total, trace, True
    )
    trace = call(
        z, functools.partial(corner_body, z), [left, corner, trace], [ANY, VMEM, VMEM], line, VMEM,
        [pltpu.VMEM((z.span, z.span // 2), dtype), DMA], 0,
    )
    assert devices & (devices - 1) == 0
    steps = [1 << bit for bit in range(devices.bit_length() - 1)]
    trace = trace + fetch(trace, steps[0])
    for index in range(3, len(steps), 2):
        trace = round_of(trace, steps[index:index + 2])
    others = [fetch(trace, step) for step in (steps[1], steps[2], steps[1] + steps[2])]
    relay_x, relay_y, total, others = lax.optimization_barrier((relay_x, relay_y, total, others))
    beside_x = receive(relay_x, PARTNER, RELAY_Y)
    beside_y = receive(relay_y, PARTNER, RELAY_X)
    square = call(
        z, functools.partial(last_body, z), [relay_left, positions, total, relay_x, relay_y, beside_x, beside_y],
        [ANY, SMEM] + [ANY] * 5,
        [shape(tiles.shape, dtype)],
        [ANY],
        [
            pltpu.VMEM((z.span, 2 * z.span), dtype), pltpu.VMEM((2,) + payload_shape, dtype),
            pltpu.VMEM((2 * z.span, z.wide), dtype), total_buffer,
            pltpu.VMEM(tiles.shape, dtype), pltpu.VMEM(tiles.shape, jnp.float32), *places,
            DMA, DMA((2,)), DMA, DMA((2,)), DMA((z.rows,)),
        ],
        2, 40 * 1024 * 1024,
    )[0]
    return square, jnp.sum((trace + others[0]) + (others[1] + others[2])) / (z.all_rows * z.block)


def solution(mesh):
    return jax.shard_map(
        shards,
        mesh=mesh,
        in_specs=(P(AXES, None, None, None), P(AXES, None)),
        out_specs=(P(AXES, None, None, None), P()),
        check_vma=False,
    )
```

```python
import functools

import jax
import jax.numpy as jnp
from jax import lax
from jax.experimental import pallas as pl
from jax.experimental.pallas import tpu as pltpu
from jax.sharding import PartitionSpec as P

REACH = 12
AXES = ("blk", "grp")
VMEM_LIMIT = 42 * 1024 * 1024
WHOLE_VMEM = 60 * 1024 * 1024
EMPTY = 64

FIRST = (2, 3, -3, -2)
SECOND = (-3, 2, -2, 3)
RELAY_FROM = (2, -5, 5, -2)
PARTNER = (1, -1, 1, -1)
RELAY = tuple(RELAY_FROM[m] + FIRST[(m + RELAY_FROM[m]) % 4] for m in range(4))


def across(table):
    return tuple(PARTNER[m] + table[m ^ 1] for m in range(4))


USE_SECOND = tuple(int(abs(offset) > 3) for offset in across(FIRST))
MIXED = tuple(
    second if use else first
    for first, second, use in zip(across(FIRST), across(SECOND), USE_SECOND)
)
OFFSETS = {
    "beside": PARTNER,
    "first": FIRST,
    "second": SECOND,
    "mixed": MIXED,
    "relay": RELAY,
    "relay_beside": across(RELAY),
}
COUNTS = {"beside": (2, 0, 2, 0), "first": (2, 0, 0, 2), "second": (2, 0, 0, 2), "mixed": (0, 0, 2, 2)}
OUTSIDE = {("first", "mixed"): (0, 2, 2, 0), ("first", "second"): (0, 2, 0, 0)}
LOWER, UPPER = 2, 1


def receive(shard, offsets, kinds=range(4)):
    size = lax.axis_size(AXES)
    pairs = [((d + offsets[d % 4]) % size, d) for d in range(size) if d % 4 in kinds]
    return lax.ppermute(shard, AXES, pairs)


def fetch(value, step):
    return lax.ppermute(value, AXES, [(d, d ^ step) for d in range(lax.axis_size(AXES))])


def round_of(value, steps):
    if len(steps) == 1:
        return value + fetch(value, steps[0])
    one, other = steps
    return (value + fetch(value, one)) + (fetch(value, other) + fetch(value, one + other))


def pick(table, kind):
    value = jnp.int32(table[3])
    for m in range(3):
        value = jnp.where(kind == m, jnp.int32(table[m]), value)
    return value


def aligned(index, unit):
    return pl.multiple_of(index * unit, unit)


class Sizes:
    def __init__(self, shape, devices):
        self.rows, self.slots, self.block, _ = shape
        self.hops = (REACH + self.rows - 1) // self.rows
        self.chunks = 2 * self.hops + 1
        self.window = self.chunks * self.rows
        self.span = self.rows * self.block
        self.wide = (self.window + 1) * self.block
        self.all_rows = self.rows * devices

    def start(self, device):
        start = (device - self.hops) * self.rows
        return jnp.where(start < 0, start + self.all_rows, start)

    def position(self, column, start):
        place = column - start
        place = jnp.where(place < 0, place + self.all_rows, place)
        place = jnp.where(column < 0, self.window, place)
        return jnp.minimum(place, self.window)


def scatter(z, dense, top, source, place):
    for r in range(z.rows):
        def one(u, carry):
            column = pl.ds(aligned(place(r, u), z.block), z.block)
            dense[top + r * z.block:top + (r + 1) * z.block, column] = source[r * z.slots + u]
            return carry
        lax.fori_loop(0, z.slots, one, 0, unroll=10)


def decode(z, offsets, spot, vector, scalars, sem):
    value = offsets[0:16, :].astype(jnp.float32).astype(jnp.int32)
    value = value + spot * z.rows + lax.broadcasted_iota(jnp.int32, value.shape, 0)
    vector[...] = jnp.where((value < 0) | (value > z.window), z.window, value)
    copy = pltpu.make_async_copy(vector, scalars, sem)
    copy.start()
    return copy


def pack_body(z, tiles, columns, out, stage, padded, offsets, in_sems, out_sems):
    copies = []
    for r in range(z.rows):
        rows = pl.ds(r * z.slots, z.slots)
        copies.append((
            pltpu.make_async_copy(tiles.at[r], stage.at[rows], in_sems.at[r]),
            pltpu.make_async_copy(stage.at[rows], out.at[rows], out_sems.at[r]),
        ))
    for copy, _ in copies:
        copy.start()
    padded[...] = jnp.full(padded.shape, -1, jnp.int32)
    padded[:z.rows, :z.slots] = columns[...]
    column = padded[...]
    row = lax.axis_index(AXES) * z.rows + lax.broadcasted_iota(jnp.int32, column.shape, 0)
    offset = column - row
    offset = jnp.where(offset > z.all_rows // 2, offset - z.all_rows, offset)
    offset = jnp.where(offset < -(z.all_rows // 2), offset + z.all_rows, offset)
    offset = jnp.where(column < 0, EMPTY, offset)
    offsets[...] = jnp.zeros_like(offsets)
    offsets[0:16, :] = offset.astype(jnp.float32).astype(offsets.dtype)
    last = pltpu.make_async_copy(offsets, out.at[z.rows * z.slots], out_sems.at[z.rows])
    last.start()
    for load, store in copies:
        load.wait()
        store.start()
    for _, store in copies:
        store.wait()
    last.wait()


def emit(z, total, positions, stage, out, sems, prev=None):
    for r in range(z.rows):
        def one(s, carry):
            value = total[r * z.block:(r + 1) * z.block, pl.ds(aligned(positions[r, s], z.block), z.block)]
            if prev is not None:
                value = value + prev[r, s]
            stage[r, s] = value.astype(stage.dtype)
            return carry
        lax.fori_loop(0, z.slots, one, 0, unroll=10)
        pltpu.make_async_copy(stage.at[r], out.at[r], sems.at[r]).start()
    for r in range(z.rows):
        pltpu.make_async_copy(stage.at[r], out.at[r], sems.at[r]).wait()


def add_trace(trace, weight, one, other):
    value = jnp.dot(one, other, preferred_element_type=jnp.float32)
    on = lax.broadcasted_iota(jnp.int32, value.shape, 0) == lax.broadcasted_iota(jnp.int32, value.shape, 1)
    diagonal = jnp.sum(jnp.where(on, value, 0.0), axis=0, keepdims=True)
    trace[:, :value.shape[1]] += weight.astype(jnp.float32) * diagonal


def own_body(z, own, columns, out, left_out, corner_out, positions, trace, stage, left, total, out_stage,
             in_sem, left_sem, corner_sem, out_sems):
    device = lax.axis_index(AXES)
    kind = device % 4
    copy = pltpu.make_async_copy(own, stage, in_sem)
    copy.start()
    left[...] = jnp.zeros_like(left)
    total[:, z.window * z.block:] = jnp.zeros((z.span, z.block), jnp.float32)
    copy.wait()
    start = z.start(device)
    for r in range(z.rows):
        def place(u, carry):
            column = z.position(columns[r, u], start)
            positions[r, u] = column
            left[r * z.block:(r + 1) * z.block, pl.ds(aligned(column, z.block), z.block)] = stage[r, u]
            return carry
        lax.fori_loop(0, z.slots, place, 0, unroll=10)
    left_copy = pltpu.make_async_copy(left, left_out, left_sem)
    left_copy.start()
    half = z.span // 2

    def corner(start):
        def go(rows, cols):
            copy = pltpu.make_async_copy(left.at[rows, cols], corner_out, corner_sem)
            copy.start() if start else copy.wait()
        pl.when(kind == UPPER)(lambda: go(pl.ds(0, half), pl.ds(0, z.span)))
        pl.when(kind != UPPER)(
            lambda: go(pl.ds(half, half), pl.ds((z.chunks - 1) * z.span, z.span))
        )

    corner(True)
    middle = slice(z.hops * z.span, (z.hops + 1) * z.span)

    def multiply(n, carry):
        cols = pl.ds(aligned(n, z.span), z.span)
        total[:, cols] = jnp.dot(left[:, middle], left[:, cols], preferred_element_type=jnp.float32)
        return carry

    lax.fori_loop(0, z.chunks, multiply, 0)
    trace[...] = jnp.zeros_like(trace)
    add_trace(trace, jnp.float32(1), left[:, middle], left[:, middle])
    emit(z, total, positions, out_stage, out, out_sems)
    corner(False)
    left_copy.wait()


def near_body(z, names, final, left_in, positions, prev, trace_in, *refs):
    refs = list(refs)
    take = lambda count: [refs.pop(0) for _ in range(count)]
    sources = [take(2 if name == "mixed" else 1) for name in names]
    out, trace = take(2)
    relay_left = take(1)[0] if final else None
    left, stage, right, total, sums, vector, scalars = take(7)
    left_sem, in_sem, prev_sem, place_sem, relay_sem, out_sems = take(6)
    device = lax.axis_index(AXES)
    kind = device % 4
    place = {name: pick(table, kind) + z.hops for name, table in OFFSETS.items()}

    def chunk(n):
        return pl.ds(aligned(n, z.span), z.span)

    def fetch(index):
        return pltpu.make_async_copy(sources[index][0], stage.at[index % 2], in_sem.at[index % 2])

    def begin_fetch(index):
        if len(sources[index]) == 1:
            fetch(index).start()
            return
        for use, source in enumerate(sources[index]):
            @pl.when(pick(USE_SECOND, kind) == use)
            def _():
                pltpu.make_async_copy(source, stage.at[index % 2], in_sem.at[index % 2]).start()

    left_copy = pltpu.make_async_copy(left_in, left, left_sem)
    left_copy.start()
    for index in range(min(2, len(names))):
        begin_fetch(index)
    prev_copy = pltpu.make_async_copy(prev, sums, prev_sem)
    prev_copy.start()
    total[...] = jnp.zeros_like(total)
    trace[...] = trace_in[...]
    left_copy.wait()
    relay_copies = []
    for index, name in enumerate(("relay", "relay_beside") if final else ()):
        copy = pltpu.make_async_copy(
            left.at[:, chunk(place[name])], relay_left.at[:, pl.ds(index * z.span, z.span)],
            relay_sem.at[index],
        )
        copy.start()
        relay_copies.append(copy)
    decodings = []

    def begin_decode(index):
        slot = index % 2
        fetch(index).wait()
        decodings.append(decode(
            z, stage.at[slot, z.rows * z.slots], place[names[index]], vector.at[slot], scalars.at[slot],
            place_sem.at[slot],
        ))

    begin_decode(0)
    dense_of = {}
    for index, name in enumerate(names):
        dense = right.at[index]
        dense_of[name] = dense
        spot = place[name]
        slot = index % 2
        dense[...] = jnp.zeros_like(dense)
        decodings[index].wait()
        scatter(z, dense, 0, stage.at[slot], lambda r, u: scalars[slot, r, u])
        if index + 2 < len(names):
            begin_fetch(index + 2)
        if index + 1 < len(names):
            begin_decode(index + 1)

        def multiply(n, carry):
            total[:, chunk(n)] += jnp.dot(
                left[:, chunk(spot)], dense[:, chunk(n)], preferred_element_type=jnp.float32
            )
            return carry

        lax.fori_loop(jnp.maximum(0, spot - z.hops), jnp.minimum(z.chunks, spot + z.hops + 1), multiply, 0)
        weight = pick(COUNTS[name], kind)
        pl.when(weight != 0)(
            lambda: add_trace(trace, weight, left[:, chunk(spot)], dense[:, chunk(z.hops)])
        )
    for (one, other), table in OUTSIDE.items() if final else ():
        weight = pick(table, kind)
        pl.when(weight != 0)(lambda: add_trace(
            trace, weight, dense_of[one][:, chunk(place[other])], dense_of[other][:, chunk(place[one])]
        ))
    prev_copy.wait()
    emit(z, total, positions, sums, out, out_sems, sums)
    for copy in relay_copies:
        copy.wait()


def corner_body(z, left, corner, trace_in, trace, rows, sem):
    kind = lax.axis_index(AXES) % 4
    half = z.span // 2
    end = (z.chunks - 1) * z.span
    trace[...] = trace_in[...]

    @pl.when(kind == UPPER)
    def _():
        copy = pltpu.make_async_copy(left.at[:, pl.ds(half, half)], rows, sem)
        copy.start()
        copy.wait()
        add_trace(trace, jnp.float32(2), rows[...], corner[...])

    @pl.when(kind == LOWER)
    def _():
        copy = pltpu.make_async_copy(left.at[pl.ds(0, half), pl.ds(end, half)], rows.at[pl.ds(0, half)], sem)
        copy.start()
        copy.wait()
        add_trace(trace, jnp.float32(2), rows[:half], corner[:, :half])


def last_body(z, left_in, positions, prev, source_a, source_b, out, left, stage, right, total, out_stage,
              prev_stage, vector, scalars, left_sem, in_sem, prev_sem, place_sem, out_sems):
    kind = lax.axis_index(AXES) % 4
    copies = [
        pltpu.make_async_copy(source_a, stage.at[0], in_sem.at[0]),
        pltpu.make_async_copy(source_b, stage.at[1], in_sem.at[1]),
        pltpu.make_async_copy(left_in, left, left_sem),
        pltpu.make_async_copy(prev, prev_stage, prev_sem),
    ]
    for copy in copies:
        copy.start()
    places = [pick(OFFSETS[name], kind) + z.hops for name in ("relay", "relay_beside")]
    low = jnp.maximum(0, jnp.minimum(*places) - z.hops)
    high = jnp.minimum(z.chunks, jnp.maximum(*places) + z.hops + 1)

    def chunk(n):
        return pl.ds(aligned(n, z.span), z.span)

    def clear_total(n, carry):
        total[:, chunk(n)] = jnp.zeros((z.span, z.span), jnp.float32)
        return carry

    def clear_right(n, carry):
        right[:, chunk(n)] = jnp.zeros((2 * z.span, z.span), right.dtype)
        return carry

    lax.fori_loop(0, low, clear_total, 0)
    lax.fori_loop(high, z.chunks, clear_total, 0)
    total[:, z.window * z.block:] = jnp.zeros((z.span, z.block), jnp.float32)
    decodings = []
    for index in range(2):
        copies[index].wait()
        decodings.append(decode(
            z, stage.at[index, z.rows * z.slots], places[index], vector.at[index], scalars.at[index],
            place_sem.at[index],
        ))
    lax.fori_loop(low, high, clear_right, 0)
    for index in range(2):
        decodings[index].wait()
        scatter(z, right, index * z.span, stage.at[index], lambda r, u: scalars[index, r, u])
    copies[2].wait()

    def multiply(n, carry):
        total[:, chunk(n)] = jnp.dot(left[...], right[:, chunk(n)], preferred_element_type=jnp.float32)
        return carry

    lax.fori_loop(low, high, multiply, 0)
    copies[3].wait()
    emit(z, total, positions, out_stage, out, out_sems, prev_stage)


ANY = pl.BlockSpec(memory_space=pl.ANY)
SMEM = pl.BlockSpec(memory_space=pltpu.SMEM)
VMEM = pl.BlockSpec(memory_space=pltpu.VMEM)
DMA = pltpu.SemaphoreType.DMA


def call(z, kernel, operands, in_specs, out_shape, out_specs, scratch, pieces, limit=VMEM_LIMIT):
    return pl.pallas_call(
        kernel,
        out_shape=out_shape,
        in_specs=in_specs,
        out_specs=out_specs,
        scratch_shapes=scratch,
        compiler_params=pltpu.CompilerParams(vmem_limit_bytes=limit),
        cost_estimate=pl.CostEstimate(
            flops=2 * z.span * z.span * z.window * z.block * pieces,
            bytes_accessed=2 * z.span * z.slots * z.block * (pieces + 4),
            transcendentals=0,
        ),
    )(*operands)


def shards(tiles, columns):
    devices = lax.axis_size(AXES)
    z = Sizes(tiles.shape, devices)
    assert z.hops == 3 and z.rows == 4 and devices % 4 == 0 and devices > 8
    dtype = tiles.dtype
    shape = jax.ShapeDtypeStruct
    sums = shape(tiles.shape, jnp.float32)
    line = shape((1, z.span), jnp.float32)
    dense = pltpu.VMEM((z.span, z.wide), dtype)
    total_buffer = pltpu.VMEM((z.span, z.wide), jnp.float32)

    payload_shape = (z.rows * z.slots + 1, z.block, z.block)
    places = [pltpu.VMEM((2, 16, z.block), jnp.int32), pltpu.SMEM((2, 16, z.block), jnp.int32)]

    payload = call(
        z, functools.partial(pack_body, z), [tiles, columns], [ANY, VMEM],
        shape(payload_shape, dtype), ANY,
        [
            pltpu.VMEM((z.rows * z.slots, z.block, z.block), dtype), pltpu.VMEM((16, z.block), jnp.int32),
            pltpu.VMEM((z.block, z.block), dtype), DMA((z.rows,)), DMA((z.rows + 1,)),
        ],
        0, WHOLE_VMEM,
    )
    first = receive(payload, FIRST)
    second = receive(payload, SECOND)
    beside = receive(payload, PARTNER)

    total, left, corner, positions, trace = call(
        z, functools.partial(own_body, z), [tiles, columns], [ANY, SMEM],
        [
            sums, shape((z.span, z.wide), dtype), shape((z.span // 2, z.span), dtype),
            shape((z.rows, z.slots), jnp.int32), line,
        ],
        [ANY, ANY, ANY, SMEM, VMEM],
        [
            pltpu.VMEM(tiles.shape, dtype), dense, total_buffer, pltpu.VMEM(tiles.shape, jnp.float32),
            DMA, DMA, DMA, DMA((z.rows,)),
        ],
        1, WHOLE_VMEM,
    )
    corner = receive(corner, PARTNER, (0, 3))

    def near(names, arrays, total, trace, final=False):
        extra = [shape((z.span, 2 * z.span), dtype)] * final
        return call(
            z, functools.partial(near_body, z, names, final),
            [left, positions, total, trace] + arrays,
            [ANY, SMEM, ANY, VMEM] + [ANY] * len(arrays),
            [sums, line] + extra,
            [ANY, VMEM] + [ANY] * final,
            [
                dense, pltpu.VMEM((2,) + payload_shape, dtype),
                pltpu.VMEM((len(names), z.span, z.wide), dtype), total_buffer,
                pltpu.VMEM(tiles.shape, jnp.float32), *places,
                DMA, DMA((2,)), DMA, DMA((2,)), DMA((2,)), DMA((z.rows,)),
            ],
            len(names), VMEM_LIMIT if final else WHOLE_VMEM,
        )

    total, trace = near(("beside",), [beside], total, trace)
    first, second, corner, total, trace = lax.optimization_barrier((first, second, corner, total, trace))
    relay = receive(first, RELAY_FROM)
    mixed = [
        receive(first, PARTNER, [m for m in range(4) if not USE_SECOND[m]]),
        receive(second, PARTNER, [m for m in range(4) if USE_SECOND[m]]),
    ]
    corner = receive(corner, (0, -2, 2, 0), (LOWER, UPPER))
    total, trace, relay_left = near(
        ("first", "second", "mixed"), [first, second, *mixed], total, trace, True
    )
    trace = call(
        z, functools.partial(corner_body, z), [left, corner, trace], [ANY, VMEM, VMEM], line, VMEM,
        [pltpu.VMEM((z.span, z.span // 2), dtype), DMA], 0,
    )
    assert devices & (devices - 1) == 0
    steps = [1 << bit for bit in range(devices.bit_length() - 1)]
    trace = trace + fetch(trace, steps[0])
    for index in range(3, len(steps), 2):
        trace = round_of(trace, steps[index:index + 2])
    relay, total, trace = lax.optimization_barrier((relay, total, trace))
    relay_beside = receive(relay, PARTNER)
    others = [fetch(trace, step) for step in (steps[1], steps[2], steps[1] + steps[2])]
    square = call(
        z, functools.partial(last_body, z), [relay_left, positions, total, relay, relay_beside],
        [ANY, SMEM, ANY, ANY, ANY],
        [shape(tiles.shape, dtype)],
        [ANY],
        [
            pltpu.VMEM((z.span, 2 * z.span), dtype), pltpu.VMEM((2,) + payload_shape, dtype),
            pltpu.VMEM((2 * z.span, z.wide), dtype), total_buffer,
            pltpu.VMEM(tiles.shape, dtype), pltpu.VMEM(tiles.shape, jnp.float32), *places,
            DMA, DMA((2,)), DMA, DMA((2,)), DMA((z.rows,)),
        ],
        2, 44 * 1024 * 1024,
    )[0]
    square, trace, others = lax.optimization_barrier((square, trace, others))
    return square, jnp.sum((trace + others[0]) + (others[1] + others[2])) / (z.all_rows * z.block)


def solution(mesh):
    return jax.shard_map(
        shards,
        mesh=mesh,
        in_specs=(P(AXES, None, None, None), P(AXES, None)),
        out_specs=(P(AXES, None, None, None), P()),
        check_vma=False,
    )
```

```python
import functools

import jax
import jax.numpy as jnp
from jax import lax
from jax.experimental import pallas as pl
from jax.experimental.pallas import tpu as pltpu
from jax.sharding import PartitionSpec as P

REACH = 12
AXES = ("blk", "grp")
VMEM_LIMIT = 42 * 1024 * 1024
WHOLE_VMEM = 60 * 1024 * 1024
EMPTY = 64

FIRST = (2, 3, -3, -2)
SECOND = (-3, 2, -2, 3)
RELAY_FROM = (2, -5, 5, -2)
PARTNER = (1, -1, 1, -1)
RELAY = tuple(RELAY_FROM[m] + FIRST[(m + RELAY_FROM[m]) % 4] for m in range(4))


def across(table):
    return tuple(PARTNER[m] + table[m ^ 1] for m in range(4))


USE_SECOND = tuple(int(abs(offset) > 3) for offset in across(FIRST))
MIXED = tuple(
    second if use else first
    for first, second, use in zip(across(FIRST), across(SECOND), USE_SECOND)
)
OFFSETS = {
    "beside": PARTNER,
    "first": FIRST,
    "second": SECOND,
    "mixed": MIXED,
    "relay": RELAY,
    "relay_beside": across(RELAY),
}
COUNTS = {"beside": (2, 0, 2, 0), "first": (2, 0, 0, 2), "second": (2, 0, 0, 2), "mixed": (0, 0, 2, 2)}
OUTSIDE = {("first", "mixed"): (0, 2, 2, 0), ("first", "second"): (0, 2, 0, 0)}
LOWER, UPPER = 2, 1


def receive(shard, offsets, kinds=range(4)):
    size = lax.axis_size(AXES)
    pairs = [((d + offsets[d % 4]) % size, d) for d in range(size) if d % 4 in kinds]
    return lax.ppermute(shard, AXES, pairs)


def fetch(value, step):
    return lax.ppermute(value, AXES, [(d, d ^ step) for d in range(lax.axis_size(AXES))])


def round_of(value, steps):
    if len(steps) == 1:
        return value + fetch(value, steps[0])
    one, other = steps
    return (value + fetch(value, one)) + (fetch(value, other) + fetch(value, one + other))


def pick(table, kind):
    value = jnp.int32(table[3])
    for m in range(3):
        value = jnp.where(kind == m, jnp.int32(table[m]), value)
    return value


def aligned(index, unit):
    return pl.multiple_of(index * unit, unit)


class Sizes:
    def __init__(self, shape, devices):
        self.rows, self.slots, self.block, _ = shape
        self.hops = (REACH + self.rows - 1) // self.rows
        self.chunks = 2 * self.hops + 1
        self.window = self.chunks * self.rows
        self.span = self.rows * self.block
        self.wide = (self.window + 1) * self.block
        self.all_rows = self.rows * devices

    def start(self, device):
        start = (device - self.hops) * self.rows
        return jnp.where(start < 0, start + self.all_rows, start)

    def position(self, column, start):
        place = column - start
        place = jnp.where(place < 0, place + self.all_rows, place)
        place = jnp.where(column < 0, self.window, place)
        return jnp.minimum(place, self.window)


def scatter(z, dense, top, source, place):
    for r in range(z.rows):
        def one(u, carry):
            column = pl.ds(aligned(place(r, u), z.block), z.block)
            dense[top + r * z.block:top + (r + 1) * z.block, column] = source[r * z.slots + u]
            return carry
        lax.fori_loop(0, z.slots, one, 0, unroll=10)


def decode(z, offsets, spot, vector, scalars, sem):
    value = offsets[0:16, :].astype(jnp.float32).astype(jnp.int32)
    value = value + spot * z.rows + lax.broadcasted_iota(jnp.int32, value.shape, 0)
    vector[...] = jnp.where((value < 0) | (value > z.window), z.window, value)
    copy = pltpu.make_async_copy(vector, scalars, sem)
    copy.start()
    return copy


def pack_body(z, tiles, columns, out, stage, padded, offsets, in_sems, out_sems):
    copies = []
    for r in range(z.rows):
        rows = pl.ds(r * z.slots, z.slots)
        copies.append((
            pltpu.make_async_copy(tiles.at[r], stage.at[rows], in_sems.at[r]),
            pltpu.make_async_copy(stage.at[rows], out.at[rows], out_sems.at[r]),
        ))
    for copy, _ in copies:
        copy.start()
    padded[...] = jnp.full(padded.shape, -1, jnp.int32)
    padded[:z.rows, :z.slots] = columns[...]
    column = padded[...]
    row = lax.axis_index(AXES) * z.rows + lax.broadcasted_iota(jnp.int32, column.shape, 0)
    offset = column - row
    offset = jnp.where(offset > z.all_rows // 2, offset - z.all_rows, offset)
    offset = jnp.where(offset < -(z.all_rows // 2), offset + z.all_rows, offset)
    offset = jnp.where(column < 0, EMPTY, offset)
    offsets[...] = jnp.zeros_like(offsets)
    offsets[0:16, :] = offset.astype(jnp.float32).astype(offsets.dtype)
    last = pltpu.make_async_copy(offsets, out.at[z.rows * z.slots], out_sems.at[z.rows])
    last.start()
    for load, store in copies:
        load.wait()
        store.start()
    for _, store in copies:
        store.wait()
    last.wait()


def emit(z, total, positions, stage, out, sems, prev=None):
    for r in range(z.rows):
        def one(s, carry):
            value = total[r * z.block:(r + 1) * z.block, pl.ds(aligned(positions[r, s], z.block), z.block)]
            if prev is not None:
                value = value + prev[r, s]
            stage[r, s] = value.astype(stage.dtype)
            return carry
        lax.fori_loop(0, z.slots, one, 0, unroll=10)
        pltpu.make_async_copy(stage.at[r], out.at[r], sems.at[r]).start()
    for r in range(z.rows):
        pltpu.make_async_copy(stage.at[r], out.at[r], sems.at[r]).wait()


def add_trace(trace, weight, one, other):
    value = jnp.dot(one, other, preferred_element_type=jnp.float32)
    on = lax.broadcasted_iota(jnp.int32, value.shape, 0) == lax.broadcasted_iota(jnp.int32, value.shape, 1)
    diagonal = jnp.sum(jnp.where(on, value, 0.0), axis=0, keepdims=True)
    trace[:, :value.shape[1]] += weight.astype(jnp.float32) * diagonal


def own_body(z, own, columns, out, left_out, corner_out, positions, trace, stage, left, total, out_stage,
             in_sem, left_sem, corner_sem, out_sems):
    device = lax.axis_index(AXES)
    kind = device % 4
    copy = pltpu.make_async_copy(own, stage, in_sem)
    copy.start()
    left[...] = jnp.zeros_like(left)
    total[:, z.window * z.block:] = jnp.zeros((z.span, z.block), jnp.float32)
    copy.wait()
    start = z.start(device)
    for r in range(z.rows):
        def place(u, carry):
            column = z.position(columns[r, u], start)
            positions[r, u] = column
            left[r * z.block:(r + 1) * z.block, pl.ds(aligned(column, z.block), z.block)] = stage[r, u]
            return carry
        lax.fori_loop(0, z.slots, place, 0, unroll=10)
    left_copy = pltpu.make_async_copy(left, left_out, left_sem)
    left_copy.start()
    half = z.span // 2

    def corner(start):
        def go(rows, cols):
            copy = pltpu.make_async_copy(left.at[rows, cols], corner_out, corner_sem)
            copy.start() if start else copy.wait()
        pl.when(kind == UPPER)(lambda: go(pl.ds(0, half), pl.ds(0, z.span)))
        pl.when(kind != UPPER)(
            lambda: go(pl.ds(half, half), pl.ds((z.chunks - 1) * z.span, z.span))
        )

    corner(True)
    middle = slice(z.hops * z.span, (z.hops + 1) * z.span)

    def multiply(n, carry):
        cols = pl.ds(aligned(n, z.span), z.span)
        total[:, cols] = jnp.dot(left[:, middle], left[:, cols], preferred_element_type=jnp.float32)
        return carry

    lax.fori_loop(0, z.chunks, multiply, 0)
    trace[...] = jnp.zeros_like(trace)
    add_trace(trace, jnp.float32(1), left[:, middle], left[:, middle])
    emit(z, total, positions, out_stage, out, out_sems)
    corner(False)
    left_copy.wait()


def near_body(z, names, final, left_in, positions, prev, trace_in, *refs):
    refs = list(refs)
    take = lambda count: [refs.pop(0) for _ in range(count)]
    sources = [take(2 if name == "mixed" else 1) for name in names]
    out, trace = take(2)
    relay_left = take(1)[0] if final else None
    left, stage, right, total, sums, vector, scalars = take(7)
    left_sem, in_sem, prev_sem, place_sem, relay_sem, out_sems = take(6)
    device = lax.axis_index(AXES)
    kind = device % 4
    place = {name: pick(table, kind) + z.hops for name, table in OFFSETS.items()}

    def chunk(n):
        return pl.ds(aligned(n, z.span), z.span)

    def fetch(index):
        return pltpu.make_async_copy(sources[index][0], stage.at[index % 2], in_sem.at[index % 2])

    def begin_fetch(index):
        if len(sources[index]) == 1:
            fetch(index).start()
            return
        for use, source in enumerate(sources[index]):
            @pl.when(pick(USE_SECOND, kind) == use)
            def _():
                pltpu.make_async_copy(source, stage.at[index % 2], in_sem.at[index % 2]).start()

    left_copy = pltpu.make_async_copy(left_in, left, left_sem)
    left_copy.start()
    for index in range(min(2, len(names))):
        begin_fetch(index)
    prev_copy = pltpu.make_async_copy(prev, sums, prev_sem)
    prev_copy.start()
    total[...] = jnp.zeros_like(total)
    trace[...] = trace_in[...]
    left_copy.wait()
    relay_copies = []
    for index, name in enumerate(("relay", "relay_beside") if final else ()):
        copy = pltpu.make_async_copy(
            left.at[:, chunk(place[name])], relay_left.at[:, pl.ds(index * z.span, z.span)],
            relay_sem.at[index],
        )
        copy.start()
        relay_copies.append(copy)
    decodings = []

    def begin_decode(index):
        slot = index % 2
        fetch(index).wait()
        decodings.append(decode(
            z, stage.at[slot, z.rows * z.slots], place[names[index]], vector.at[slot], scalars.at[slot],
            place_sem.at[slot],
        ))

    begin_decode(0)
    dense_of = {}
    for index, name in enumerate(names):
        dense = right.at[index]
        dense_of[name] = dense
        spot = place[name]
        slot = index % 2
        dense[...] = jnp.zeros_like(dense)
        decodings[index].wait()
        scatter(z, dense, 0, stage.at[slot], lambda r, u: scalars[slot, r, u])
        if index + 2 < len(names):
            begin_fetch(index + 2)
        if index + 1 < len(names):
            begin_decode(index + 1)

        def multiply(n, carry):
            total[:, chunk(n)] += jnp.dot(
                left[:, chunk(spot)], dense[:, chunk(n)], preferred_element_type=jnp.float32
            )
            return carry

        lax.fori_loop(jnp.maximum(0, spot - z.hops), jnp.minimum(z.chunks, spot + z.hops + 1), multiply, 0)
        weight = pick(COUNTS[name], kind)
        pl.when(weight != 0)(
            lambda: add_trace(trace, weight, left[:, chunk(spot)], dense[:, chunk(z.hops)])
        )
    for (one, other), table in OUTSIDE.items() if final else ():
        weight = pick(table, kind)
        pl.when(weight != 0)(lambda: add_trace(
            trace, weight, dense_of[one][:, chunk(place[other])], dense_of[other][:, chunk(place[one])]
        ))
    prev_copy.wait()
    emit(z, total, positions, sums, out, out_sems, sums)
    for copy in relay_copies:
        copy.wait()


def corner_body(z, left, corner, trace_in, trace, rows, sem):
    kind = lax.axis_index(AXES) % 4
    half = z.span // 2
    end = (z.chunks - 1) * z.span
    trace[...] = trace_in[...]

    @pl.when(kind == UPPER)
    def _():
        copy = pltpu.make_async_copy(left.at[:, pl.ds(half, half)], rows, sem)
        copy.start()
        copy.wait()
        add_trace(trace, jnp.float32(2), rows[...], corner[...])

    @pl.when(kind == LOWER)
    def _():
        copy = pltpu.make_async_copy(left.at[pl.ds(0, half), pl.ds(end, half)], rows.at[pl.ds(0, half)], sem)
        copy.start()
        copy.wait()
        add_trace(trace, jnp.float32(2), rows[:half], corner[:, :half])


def last_body(z, left_in, positions, prev, source_a, source_b, out, left, right, total, out_stage,
              prev_stage, vector, scalars, left_sem, prev_sem, place_sem, out_sems):
    kind = lax.axis_index(AXES) % 4
    copies = [
        pltpu.make_async_copy(left_in, left, left_sem),
        pltpu.make_async_copy(prev, prev_stage, prev_sem),
    ]
    for copy in copies:
        copy.start()
    places = [pick(OFFSETS[name], kind) + z.hops for name in ("relay", "relay_beside")]
    low = jnp.maximum(0, jnp.minimum(*places) - z.hops)
    high = jnp.minimum(z.chunks, jnp.maximum(*places) + z.hops + 1)

    def chunk(n):
        return pl.ds(aligned(n, z.span), z.span)

    def clear_total(n, carry):
        total[:, chunk(n)] = jnp.zeros((z.span, z.span), jnp.float32)
        return carry

    def clear_right(n, carry):
        right[:, chunk(n)] = jnp.zeros((2 * z.span, z.span), right.dtype)
        return carry

    lax.fori_loop(0, low, clear_total, 0)
    lax.fori_loop(high, z.chunks, clear_total, 0)
    total[:, z.window * z.block:] = jnp.zeros((z.span, z.block), jnp.float32)
    decodings = []
    for index in range(2):
        decodings.append(decode(
            z, (source_a, source_b)[index].at[z.rows * z.slots], places[index], vector.at[index], scalars.at[index],
            place_sem.at[index],
        ))
    lax.fori_loop(low, high, clear_right, 0)
    for index in range(2):
        decodings[index].wait()
        scatter(z, right, index * z.span, (source_a, source_b)[index], lambda r, u: scalars[index, r, u])
    copies[0].wait()

    def multiply(n, carry):
        total[:, chunk(n)] = jnp.dot(left[...], right[:, chunk(n)], preferred_element_type=jnp.float32)
        return carry

    lax.fori_loop(low, high, multiply, 0)
    copies[1].wait()
    emit(z, total, positions, out_stage, out, out_sems, prev_stage)


ANY = pl.BlockSpec(memory_space=pl.ANY)
SMEM = pl.BlockSpec(memory_space=pltpu.SMEM)
VMEM = pl.BlockSpec(memory_space=pltpu.VMEM)
DMA = pltpu.SemaphoreType.DMA


def call(z, kernel, operands, in_specs, out_shape, out_specs, scratch, pieces, limit=VMEM_LIMIT):
    return pl.pallas_call(
        kernel,
        out_shape=out_shape,
        in_specs=in_specs,
        out_specs=out_specs,
        scratch_shapes=scratch,
        compiler_params=pltpu.CompilerParams(vmem_limit_bytes=limit),
        cost_estimate=pl.CostEstimate(
            flops=2 * z.span * z.span * z.window * z.block * pieces,
            bytes_accessed=2 * z.span * z.slots * z.block * (pieces + 4),
            transcendentals=0,
        ),
    )(*operands)


def shards(tiles, columns):
    devices = lax.axis_size(AXES)
    z = Sizes(tiles.shape, devices)
    assert z.hops == 3 and z.rows == 4 and devices % 4 == 0 and devices > 8
    dtype = tiles.dtype
    shape = jax.ShapeDtypeStruct
    sums = shape(tiles.shape, jnp.float32)
    line = shape((1, z.span), jnp.float32)
    dense = pltpu.VMEM((z.span, z.wide), dtype)
    total_buffer = pltpu.VMEM((z.span, z.wide), jnp.float32)

    payload_shape = (z.rows * z.slots + 1, z.block, z.block)
    places = [pltpu.VMEM((2, 16, z.block), jnp.int32), pltpu.SMEM((2, 16, z.block), jnp.int32)]

    payload = call(
        z, functools.partial(pack_body, z), [tiles, columns], [ANY, VMEM],
        shape(payload_shape, dtype), ANY,
        [
            pltpu.VMEM((z.rows * z.slots, z.block, z.block), dtype), pltpu.VMEM((16, z.block), jnp.int32),
            pltpu.VMEM((z.block, z.block), dtype), DMA((z.rows,)), DMA((z.rows + 1,)),
        ],
        0, WHOLE_VMEM,
    )
    first = receive(payload, FIRST)
    second = receive(payload, SECOND)
    beside = receive(payload, PARTNER)

    total, left, corner, positions, trace = call(
        z, functools.partial(own_body, z), [tiles, columns], [ANY, SMEM],
        [
            sums, shape((z.span, z.wide), dtype), shape((z.span // 2, z.span), dtype),
            shape((z.rows, z.slots), jnp.int32), line,
        ],
        [ANY, ANY, ANY, SMEM, VMEM],
        [
            pltpu.VMEM(tiles.shape, dtype), dense, total_buffer, pltpu.VMEM(tiles.shape, jnp.float32),
            DMA, DMA, DMA, DMA((z.rows,)),
        ],
        1, WHOLE_VMEM,
    )
    corner = receive(corner, PARTNER, (0, 3))

    def near(names, arrays, total, trace, final=False):
        extra = [shape((z.span, 2 * z.span), dtype)] * final
        return call(
            z, functools.partial(near_body, z, names, final),
            [left, positions, total, trace] + arrays,
            [ANY, SMEM, ANY, VMEM] + [ANY] * len(arrays),
            [sums, line] + extra,
            [ANY, VMEM] + [ANY] * final,
            [
                dense, pltpu.VMEM((2,) + payload_shape, dtype),
                pltpu.VMEM((len(names), z.span, z.wide), dtype), total_buffer,
                pltpu.VMEM(tiles.shape, jnp.float32), *places,
                DMA, DMA((2,)), DMA, DMA((2,)), DMA((2,)), DMA((z.rows,)),
            ],
            len(names), VMEM_LIMIT if final else WHOLE_VMEM,
        )

    total, trace = near(("beside",), [beside], total, trace)
    first, second, corner, total, trace = lax.optimization_barrier((first, second, corner, total, trace))
    relay = receive(first, RELAY_FROM)
    mixed = [
        receive(first, PARTNER, [m for m in range(4) if not USE_SECOND[m]]),
        receive(second, PARTNER, [m for m in range(4) if USE_SECOND[m]]),
    ]
    corner = receive(corner, (0, -2, 2, 0), (LOWER, UPPER))
    total, trace, relay_left = near(
        ("first", "second", "mixed"), [first, second, *mixed], total, trace, True
    )
    trace = call(
        z, functools.partial(corner_body, z), [left, corner, trace], [ANY, VMEM, VMEM], line, VMEM,
        [pltpu.VMEM((z.span, z.span // 2), dtype), DMA], 0,
    )
    assert devices & (devices - 1) == 0
    steps = [1 << bit for bit in range(devices.bit_length() - 1)]
    trace = trace + fetch(trace, steps[0])
    for index in range(3, len(steps), 2):
        trace = round_of(trace, steps[index:index + 2])
    relay, total, trace = lax.optimization_barrier((relay, total, trace))
    relay_beside = receive(relay, PARTNER)
    others = [fetch(trace, step) for step in (steps[1], steps[2], steps[1] + steps[2])]
    square = call(
        z, functools.partial(last_body, z), [relay_left, positions, total, relay, relay_beside],
        [ANY, SMEM, ANY, VMEM, VMEM],
        [shape(tiles.shape, dtype)],
        [ANY],
        [
            pltpu.VMEM((z.span, 2 * z.span), dtype),
            pltpu.VMEM((2 * z.span, z.wide), dtype), total_buffer,
            pltpu.VMEM(tiles.shape, dtype), pltpu.VMEM(tiles.shape, jnp.float32), *places,
            DMA, DMA, DMA((2,)), DMA((z.rows,)),
        ],
        2, 44 * 1024 * 1024,
    )[0]
    square, trace, others = lax.optimization_barrier((square, trace, others))
    return square, jnp.sum((trace + others[0]) + (others[1] + others[2])) / (z.all_rows * z.block)


def solution(mesh):
    return jax.shard_map(
        shards,
        mesh=mesh,
        in_specs=(P(AXES, None, None, None), P(AXES, None)),
        out_specs=(P(AXES, None, None, None), P()),
        check_vma=False,
    )
```

```python
import functools

import jax
import jax.numpy as jnp
from jax import lax
from jax.experimental import pallas as pl
from jax.experimental.pallas import tpu as pltpu
from jax.sharding import PartitionSpec as P

REACH = 12
AXES = ("blk", "grp")
VMEM_LIMIT = 42 * 1024 * 1024
WHOLE_VMEM = 60 * 1024 * 1024
EMPTY = 64

FIRST = (2, 3, -3, -2)
SECOND = (-3, 2, -2, 3)
RELAY_FROM = (2, -5, 5, -2)
PARTNER = (1, -1, 1, -1)
RELAY = tuple(RELAY_FROM[m] + FIRST[(m + RELAY_FROM[m]) % 4] for m in range(4))


def across(table):
    return tuple(PARTNER[m] + table[m ^ 1] for m in range(4))


USE_SECOND = tuple(int(abs(offset) > 3) for offset in across(FIRST))
MIXED = tuple(
    second if use else first
    for first, second, use in zip(across(FIRST), across(SECOND), USE_SECOND)
)
OFFSETS = {
    "beside": PARTNER,
    "first": FIRST,
    "second": SECOND,
    "mixed": MIXED,
    "relay": RELAY,
    "relay_beside": across(RELAY),
}
COUNTS = {"beside": (2, 0, 2, 0), "first": (2, 0, 0, 2), "second": (2, 0, 0, 2), "mixed": (0, 0, 2, 2)}
OUTSIDE = {("first", "mixed"): (0, 2, 2, 0), ("first", "second"): (0, 2, 0, 0)}
LOWER, UPPER = 2, 1


def receive(shard, offsets, kinds=range(4)):
    size = lax.axis_size(AXES)
    pairs = [((d + offsets[d % 4]) % size, d) for d in range(size) if d % 4 in kinds]
    return lax.ppermute(shard, AXES, pairs)


def fetch(value, step):
    return lax.ppermute(value, AXES, [(d, d ^ step) for d in range(lax.axis_size(AXES))])


def round_of(value, steps):
    if len(steps) == 1:
        return value + fetch(value, steps[0])
    one, other = steps
    return (value + fetch(value, one)) + (fetch(value, other) + fetch(value, one + other))


def pick(table, kind):
    value = jnp.int32(table[3])
    for m in range(3):
        value = jnp.where(kind == m, jnp.int32(table[m]), value)
    return value


def aligned(index, unit):
    return pl.multiple_of(index * unit, unit)


class Sizes:
    def __init__(self, shape, devices):
        self.rows, self.slots, self.block, _ = shape
        self.hops = (REACH + self.rows - 1) // self.rows
        self.chunks = 2 * self.hops + 1
        self.window = self.chunks * self.rows
        self.span = self.rows * self.block
        self.wide = (self.window + 1) * self.block
        self.all_rows = self.rows * devices

    def start(self, device):
        start = (device - self.hops) * self.rows
        return jnp.where(start < 0, start + self.all_rows, start)

    def position(self, column, start):
        place = column - start
        place = jnp.where(place < 0, place + self.all_rows, place)
        place = jnp.where(column < 0, self.window, place)
        return jnp.minimum(place, self.window)


def scatter(z, dense, top, source, place):
    for r in range(z.rows):
        def one(u, carry):
            column = pl.ds(aligned(place(r, u), z.block), z.block)
            dense[top + r * z.block:top + (r + 1) * z.block, column] = source[r * z.slots + u]
            return carry
        lax.fori_loop(0, z.slots, one, 0, unroll=10)


def decode(z, offsets, spot, vector, scalars, sem):
    value = offsets[0:16, :].astype(jnp.float32).astype(jnp.int32)
    value = value + spot * z.rows + lax.broadcasted_iota(jnp.int32, value.shape, 0)
    vector[...] = jnp.where((value < 0) | (value > z.window), z.window, value)
    copy = pltpu.make_async_copy(vector, scalars, sem)
    copy.start()
    return copy


def pack_body(z, tiles, columns, out, stage, padded, offsets, in_sems, out_sems):
    copies = []
    for r in range(z.rows):
        rows = pl.ds(r * z.slots, z.slots)
        copies.append((
            pltpu.make_async_copy(tiles.at[r], stage.at[rows], in_sems.at[r]),
            pltpu.make_async_copy(stage.at[rows], out.at[rows], out_sems.at[r]),
        ))
    for copy, _ in copies:
        copy.start()
    padded[...] = jnp.full(padded.shape, -1, jnp.int32)
    padded[:z.rows, :z.slots] = columns[...]
    column = padded[...]
    row = lax.axis_index(AXES) * z.rows + lax.broadcasted_iota(jnp.int32, column.shape, 0)
    offset = column - row
    offset = jnp.where(offset > z.all_rows // 2, offset - z.all_rows, offset)
    offset = jnp.where(offset < -(z.all_rows // 2), offset + z.all_rows, offset)
    offset = jnp.where(column < 0, EMPTY, offset)
    offsets[...] = jnp.zeros_like(offsets)
    offsets[0:16, :] = offset.astype(jnp.float32).astype(offsets.dtype)
    last = pltpu.make_async_copy(offsets, out.at[z.rows * z.slots], out_sems.at[z.rows])
    last.start()
    for load, store in copies:
        load.wait()
        store.start()
    for _, store in copies:
        store.wait()
    last.wait()


def emit(z, total, positions, stage, out, sems, prev=None):
    for r in range(z.rows):
        def one(s, carry):
            value = total[r * z.block:(r + 1) * z.block, pl.ds(aligned(positions[r, s], z.block), z.block)]
            if prev is not None:
                value = value + prev[r, s]
            stage[r, s] = value.astype(stage.dtype)
            return carry
        lax.fori_loop(0, z.slots, one, 0, unroll=10)
        pltpu.make_async_copy(stage.at[r], out.at[r], sems.at[r]).start()
    for r in range(z.rows):
        pltpu.make_async_copy(stage.at[r], out.at[r], sems.at[r]).wait()


def add_trace(trace, weight, one, other):
    value = jnp.dot(one, other, preferred_element_type=jnp.float32)
    on = lax.broadcasted_iota(jnp.int32, value.shape, 0) == lax.broadcasted_iota(jnp.int32, value.shape, 1)
    diagonal = jnp.sum(jnp.where(on, value, 0.0), axis=0, keepdims=True)
    trace[:, :value.shape[1]] += weight.astype(jnp.float32) * diagonal


def own_body(z, own, columns, out, left_out, corner_out, positions, trace, stage, left, total, out_stage,
             in_sem, left_sem, corner_sem, out_sems):
    device = lax.axis_index(AXES)
    kind = device % 4
    copy = pltpu.make_async_copy(own, stage, in_sem)
    copy.start()
    left[...] = jnp.zeros_like(left)
    total[:, z.window * z.block:] = jnp.zeros((z.span, z.block), jnp.float32)
    copy.wait()
    start = z.start(device)
    for r in range(z.rows):
        def place(u, carry):
            column = z.position(columns[r, u], start)
            positions[r, u] = column
            left[r * z.block:(r + 1) * z.block, pl.ds(aligned(column, z.block), z.block)] = stage[r, u]
            return carry
        lax.fori_loop(0, z.slots, place, 0, unroll=10)
    left_copy = pltpu.make_async_copy(left, left_out, left_sem)
    left_copy.start()
    half = z.span // 2

    def corner(start):
        def go(rows, cols):
            copy = pltpu.make_async_copy(left.at[rows, cols], corner_out, corner_sem)
            copy.start() if start else copy.wait()
        pl.when(kind == UPPER)(lambda: go(pl.ds(0, half), pl.ds(0, z.span)))
        pl.when(kind != UPPER)(
            lambda: go(pl.ds(half, half), pl.ds((z.chunks - 1) * z.span, z.span))
        )

    corner(True)
    middle = slice(z.hops * z.span, (z.hops + 1) * z.span)

    def multiply(n, carry):
        cols = pl.ds(aligned(n, z.span), z.span)
        total[:, cols] = jnp.dot(left[:, middle], left[:, cols], preferred_element_type=jnp.float32)
        return carry

    lax.fori_loop(0, z.chunks, multiply, 0)
    trace[...] = jnp.zeros_like(trace)
    add_trace(trace, jnp.float32(1), left[:, middle], left[:, middle])
    emit(z, total, positions, out_stage, out, out_sems)
    corner(False)
    left_copy.wait()


def near_body(z, names, final, left_in, positions, prev, trace_in, *refs):
    refs = list(refs)
    take = lambda count: [refs.pop(0) for _ in range(count)]
    sources = [take(2 if name == "mixed" else 1) for name in names]
    out, trace = take(2)
    relay_left = take(1)[0] if final else None
    left, stage, right, total, sums, vector, scalars = take(7)
    left_sem, in_sem, prev_sem, place_sem, relay_sem, out_sems = take(6)
    device = lax.axis_index(AXES)
    kind = device % 4
    place = {name: pick(table, kind) + z.hops for name, table in OFFSETS.items()}

    def chunk(n):
        return pl.ds(aligned(n, z.span), z.span)

    def fetch(index):
        return pltpu.make_async_copy(sources[index][0], stage.at[index % 2], in_sem.at[index % 2])

    def begin_fetch(index):
        if len(sources[index]) == 1:
            fetch(index).start()
            return
        for use, source in enumerate(sources[index]):
            @pl.when(pick(USE_SECOND, kind) == use)
            def _():
                pltpu.make_async_copy(source, stage.at[index % 2], in_sem.at[index % 2]).start()

    left_copy = pltpu.make_async_copy(left_in, left, left_sem)
    left_copy.start()
    for index in range(min(2, len(names))):
        begin_fetch(index)
    prev_copy = pltpu.make_async_copy(prev, sums, prev_sem)
    prev_copy.start()
    total[...] = jnp.zeros_like(total)
    trace[...] = trace_in[...]
    left_copy.wait()
    relay_copies = []
    for index, name in enumerate(("relay", "relay_beside") if final else ()):
        copy = pltpu.make_async_copy(
            left.at[:, chunk(place[name])], relay_left.at[:, pl.ds(index * z.span, z.span)],
            relay_sem.at[index],
        )
        copy.start()
        relay_copies.append(copy)
    decodings = []

    def begin_decode(index):
        slot = index % 2
        fetch(index).wait()
        decodings.append(decode(
            z, stage.at[slot, z.rows * z.slots], place[names[index]], vector.at[slot], scalars.at[slot],
            place_sem.at[slot],
        ))

    begin_decode(0)
    dense_of = {}
    for index, name in enumerate(names):
        dense = right.at[index]
        dense_of[name] = dense
        spot = place[name]
        slot = index % 2
        dense[...] = jnp.zeros_like(dense)
        decodings[index].wait()
        scatter(z, dense, 0, stage.at[slot], lambda r, u: scalars[slot, r, u])
        if index + 2 < len(names):
            begin_fetch(index + 2)
        if index + 1 < len(names):
            begin_decode(index + 1)

        def multiply(n, carry):
            total[:, chunk(n)] += jnp.dot(
                left[:, chunk(spot)], dense[:, chunk(n)], preferred_element_type=jnp.float32
            )
            return carry

        lax.fori_loop(jnp.maximum(0, spot - z.hops), jnp.minimum(z.chunks, spot + z.hops + 1), multiply, 0)
        weight = pick(COUNTS[name], kind)
        pl.when(weight != 0)(
            lambda: add_trace(trace, weight, left[:, chunk(spot)], dense[:, chunk(z.hops)])
        )
    for (one, other), table in OUTSIDE.items() if final else ():
        weight = pick(table, kind)
        pl.when(weight != 0)(lambda: add_trace(
            trace, weight, dense_of[one][:, chunk(place[other])], dense_of[other][:, chunk(place[one])]
        ))
    prev_copy.wait()
    emit(z, total, positions, sums, out, out_sems, sums)
    for copy in relay_copies:
        copy.wait()


def corner_body(z, left, corner, trace_in, trace, rows, sem):
    kind = lax.axis_index(AXES) % 4
    half = z.span // 2
    end = (z.chunks - 1) * z.span
    trace[...] = trace_in[...]

    @pl.when(kind == UPPER)
    def _():
        copy = pltpu.make_async_copy(left.at[:, pl.ds(half, half)], rows, sem)
        copy.start()
        copy.wait()
        add_trace(trace, jnp.float32(2), rows[...], corner[...])

    @pl.when(kind == LOWER)
    def _():
        copy = pltpu.make_async_copy(left.at[pl.ds(0, half), pl.ds(end, half)], rows.at[pl.ds(0, half)], sem)
        copy.start()
        copy.wait()
        add_trace(trace, jnp.float32(2), rows[:half], corner[:, :half])


def last_body(z, left_in, positions, prev, source_a, source_b, out, left, right, total, out_stage,
              prev_stage, vector, scalars, left_sem, prev_sem, place_sem, out_sems):
    kind = lax.axis_index(AXES) % 4
    copies = [
        pltpu.make_async_copy(left_in, left, left_sem),
        pltpu.make_async_copy(prev, prev_stage, prev_sem),
    ]
    for copy in copies:
        copy.start()
    places = [pick(OFFSETS[name], kind) + z.hops for name in ("relay", "relay_beside")]
    low = jnp.maximum(0, jnp.minimum(*places) - z.hops)
    high = jnp.minimum(z.chunks, jnp.maximum(*places) + z.hops + 1)

    def chunk(n):
        return pl.ds(aligned(n, z.span), z.span)

    def clear_total(n, carry):
        total[:, chunk(n)] = jnp.zeros((z.span, z.span), jnp.float32)
        return carry

    def clear_right(n, carry):
        right[:, chunk(n)] = jnp.zeros((2 * z.span, z.span), right.dtype)
        return carry

    lax.fori_loop(0, low, clear_total, 0)
    lax.fori_loop(high, z.chunks, clear_total, 0)
    total[:, z.window * z.block:] = jnp.zeros((z.span, z.block), jnp.float32)
    decodings = []
    for index in range(2):
        decodings.append(decode(
            z, (source_a, source_b)[index].at[z.rows * z.slots], places[index], vector.at[index], scalars.at[index],
            place_sem.at[index],
        ))
    lax.fori_loop(low, high, clear_right, 0)
    for index in range(2):
        decodings[index].wait()
        scatter(z, right, index * z.span, (source_a, source_b)[index], lambda r, u: scalars[index, r, u])
    copies[0].wait()

    def multiply(n, carry):
        total[:, chunk(n)] = jnp.dot(left[...], right[:, chunk(n)], preferred_element_type=jnp.float32)
        return carry

    lax.fori_loop(low, high, multiply, 0)
    copies[1].wait()
    emit(z, total, positions, out_stage, out, out_sems, prev_stage)


ANY = pl.BlockSpec(memory_space=pl.ANY)
SMEM = pl.BlockSpec(memory_space=pltpu.SMEM)
VMEM = pl.BlockSpec(memory_space=pltpu.VMEM)
DMA = pltpu.SemaphoreType.DMA


def call(z, kernel, operands, in_specs, out_shape, out_specs, scratch, pieces, limit=VMEM_LIMIT):
    return pl.pallas_call(
        kernel,
        out_shape=out_shape,
        in_specs=in_specs,
        out_specs=out_specs,
        scratch_shapes=scratch,
        compiler_params=pltpu.CompilerParams(vmem_limit_bytes=limit),
        cost_estimate=pl.CostEstimate(
            flops=2 * z.span * z.span * z.window * z.block * pieces,
            bytes_accessed=2 * z.span * z.slots * z.block * (pieces + 4),
            transcendentals=0,
        ),
    )(*operands)


def shards(tiles, columns):
    devices = lax.axis_size(AXES)
    z = Sizes(tiles.shape, devices)
    assert z.hops == 3 and z.rows == 4 and devices % 4 == 0 and devices > 8
    dtype = tiles.dtype
    shape = jax.ShapeDtypeStruct
    sums = shape(tiles.shape, jnp.float32)
    line = shape((1, z.span), jnp.float32)
    dense = pltpu.VMEM((z.span, z.wide), dtype)
    total_buffer = pltpu.VMEM((z.span, z.wide), jnp.float32)

    payload_shape = (z.rows * z.slots + 1, z.block, z.block)
    places = [pltpu.VMEM((2, 16, z.block), jnp.int32), pltpu.SMEM((2, 16, z.block), jnp.int32)]

    payload = call(
        z, functools.partial(pack_body, z), [tiles, columns], [ANY, VMEM],
        shape(payload_shape, dtype), ANY,
        [
            pltpu.VMEM((z.rows * z.slots, z.block, z.block), dtype), pltpu.VMEM((16, z.block), jnp.int32),
            pltpu.VMEM((z.block, z.block), dtype), DMA((z.rows,)), DMA((z.rows + 1,)),
        ],
        0, WHOLE_VMEM,
    )
    first = receive(payload, FIRST)
    second = receive(payload, SECOND)
    beside = receive(payload, PARTNER)

    total, left, corner, positions, trace = call(
        z, functools.partial(own_body, z), [tiles, columns], [ANY, SMEM],
        [
            sums, shape((z.span, z.wide), dtype), shape((z.span // 2, z.span), dtype),
            shape((z.rows, z.slots), jnp.int32), line,
        ],
        [ANY, ANY, ANY, SMEM, VMEM],
        [
            pltpu.VMEM(tiles.shape, dtype), dense, total_buffer, pltpu.VMEM(tiles.shape, jnp.float32),
            DMA, DMA, DMA, DMA((z.rows,)),
        ],
        1, WHOLE_VMEM,
    )
    corner = receive(corner, PARTNER, (0, 3))

    def near(names, arrays, total, trace, final=False):
        extra = [shape((z.span, 2 * z.span), dtype)] * final
        return call(
            z, functools.partial(near_body, z, names, final),
            [left, positions, total, trace] + arrays,
            [ANY, SMEM, ANY, VMEM] + [ANY] * len(arrays),
            [sums, line] + extra,
            [ANY, VMEM] + [ANY] * final,
            [
                dense, pltpu.VMEM((2,) + payload_shape, dtype),
                pltpu.VMEM((len(names), z.span, z.wide), dtype), total_buffer,
                pltpu.VMEM(tiles.shape, jnp.float32), *places,
                DMA, DMA((2,)), DMA, DMA((2,)), DMA((2,)), DMA((z.rows,)),
            ],
            len(names), VMEM_LIMIT if final else WHOLE_VMEM,
        )

    total, trace = near(("beside",), [beside], total, trace)
    first, second, corner, total, trace = lax.optimization_barrier((first, second, corner, total, trace))
    relay = receive(first, RELAY_FROM)
    corner = receive(corner, (0, -2, 2, 0), (LOWER, UPPER))

    def nearby(first, second, total, trace):
        mixed = [
            receive(first, PARTNER, [m for m in range(4) if not USE_SECOND[m]]),
            receive(second, PARTNER, [m for m in range(4) if USE_SECOND[m]]),
        ]
        return tuple(near(("first", "second", "mixed"), [first, second, *mixed], total, trace, True))

    def nothing(first, second, total, trace):
        return jnp.zeros_like(total), jnp.zeros_like(trace), jnp.zeros((z.span, 2 * z.span), dtype)

    total, trace, relay_left = lax.cond(positions[0, 0] >= 0, nearby, nothing, first, second, total, trace)
    trace = call(
        z, functools.partial(corner_body, z), [left, corner, trace], [ANY, VMEM, VMEM], line, VMEM,
        [pltpu.VMEM((z.span, z.span // 2), dtype), DMA], 0,
    )
    assert devices & (devices - 1) == 0
    steps = [1 << bit for bit in range(devices.bit_length() - 1)]
    trace = trace + fetch(trace, steps[0])
    for index in range(3, len(steps), 2):
        trace = round_of(trace, steps[index:index + 2])
    relay, total, trace = lax.optimization_barrier((relay, total, trace))
    relay_beside = receive(relay, PARTNER)
    others = [fetch(trace, step) for step in (steps[1], steps[2], steps[1] + steps[2])]
    square = call(
        z, functools.partial(last_body, z), [relay_left, positions, total, relay, relay_beside],
        [ANY, SMEM, ANY, VMEM, VMEM],
        [shape(tiles.shape, dtype)],
        [ANY],
        [
            pltpu.VMEM((z.span, 2 * z.span), dtype),
            pltpu.VMEM((2 * z.span, z.wide), dtype), total_buffer,
            pltpu.VMEM(tiles.shape, dtype), pltpu.VMEM(tiles.shape, jnp.float32), *places,
            DMA, DMA, DMA((2,)), DMA((z.rows,)),
        ],
        2, 44 * 1024 * 1024,
    )[0]
    square, trace, others = lax.optimization_barrier((square, trace, others))
    return square, jnp.sum((trace + others[0]) + (others[1] + others[2])) / (z.all_rows * z.block)


def solution(mesh):
    return jax.shard_map(
        shards,
        mesh=mesh,
        in_specs=(P(AXES, None, None, None), P(AXES, None)),
        out_specs=(P(AXES, None, None, None), P()),
        check_vma=False,
    )
```

```python
import functools

import jax
import jax.numpy as jnp
from jax import lax
from jax.experimental import pallas as pl
from jax.experimental.pallas import tpu as pltpu
from jax.sharding import PartitionSpec as P

REACH = 12
AXES = ("blk", "grp")
VMEM_LIMIT = 42 * 1024 * 1024
WHOLE_VMEM = 60 * 1024 * 1024
EMPTY = 64

FIRST = (2, 3, -3, -2)
SECOND = (-3, 2, -2, 3)
RELAY_FROM = (2, -5, 5, -2)
PARTNER = (1, -1, 1, -1)
RELAY = tuple(RELAY_FROM[m] + FIRST[(m + RELAY_FROM[m]) % 4] for m in range(4))


def across(table):
    return tuple(PARTNER[m] + table[m ^ 1] for m in range(4))


USE_SECOND = tuple(int(abs(offset) > 3) for offset in across(FIRST))
MIXED = tuple(
    second if use else first
    for first, second, use in zip(across(FIRST), across(SECOND), USE_SECOND)
)
OFFSETS = {
    "beside": PARTNER,
    "first": FIRST,
    "second": SECOND,
    "mixed": MIXED,
    "relay": RELAY,
    "relay_beside": across(RELAY),
}
COUNTS = {"beside": (2, 0, 2, 0), "first": (2, 0, 0, 2), "second": (2, 0, 0, 2), "mixed": (0, 0, 2, 2)}
OUTSIDE = {("first", "mixed"): (0, 2, 2, 0), ("first", "second"): (0, 2, 0, 0)}
LOWER, UPPER = 2, 1


def receive(shard, offsets, kinds=range(4)):
    size = lax.axis_size(AXES)
    pairs = [((d + offsets[d % 4]) % size, d) for d in range(size) if d % 4 in kinds]
    return lax.ppermute(shard, AXES, pairs)


def fetch(value, step):
    return lax.ppermute(value, AXES, [(d, d ^ step) for d in range(lax.axis_size(AXES))])


def round_of(value, steps):
    if len(steps) == 1:
        return value + fetch(value, steps[0])
    one, other = steps
    return (value + fetch(value, one)) + (fetch(value, other) + fetch(value, one + other))


def pick(table, kind):
    value = jnp.int32(table[3])
    for m in range(3):
        value = jnp.where(kind == m, jnp.int32(table[m]), value)
    return value


def aligned(index, unit):
    return pl.multiple_of(index * unit, unit)


class Sizes:
    def __init__(self, shape, devices):
        self.rows, self.slots, self.block, _ = shape
        self.hops = (REACH + self.rows - 1) // self.rows
        self.chunks = 2 * self.hops + 1
        self.window = self.chunks * self.rows
        self.span = self.rows * self.block
        self.wide = (self.window + 1) * self.block
        self.all_rows = self.rows * devices

    def start(self, device):
        start = (device - self.hops) * self.rows
        return jnp.where(start < 0, start + self.all_rows, start)

    def position(self, column, start):
        place = column - start
        place = jnp.where(place < 0, place + self.all_rows, place)
        place = jnp.where(column < 0, self.window, place)
        return jnp.minimum(place, self.window)


def scatter(z, dense, top, source, place):
    for r in range(z.rows):
        def one(u, carry):
            column = pl.ds(aligned(place(r, u), z.block), z.block)
            dense[top + r * z.block:top + (r + 1) * z.block, column] = source[r * z.slots + u]
            return carry
        lax.fori_loop(0, z.slots, one, 0, unroll=10)


def decode(z, offsets, spot, vector, scalars, sem):
    value = offsets[0:16, :].astype(jnp.float32).astype(jnp.int32)
    value = value + spot * z.rows + lax.broadcasted_iota(jnp.int32, value.shape, 0)
    vector[...] = jnp.where((value < 0) | (value > z.window), z.window, value)
    copy = pltpu.make_async_copy(vector, scalars, sem)
    copy.start()
    return copy


def pack_body(z, tiles, columns, out, stage, padded, offsets, in_sems, out_sems):
    copies = []
    for r in range(z.rows):
        rows = pl.ds(r * z.slots, z.slots)
        copies.append((
            pltpu.make_async_copy(tiles.at[r], stage.at[rows], in_sems.at[r]),
            pltpu.make_async_copy(stage.at[rows], out.at[rows], out_sems.at[r]),
        ))
    for copy, _ in copies:
        copy.start()
    padded[...] = jnp.full(padded.shape, -1, jnp.int32)
    padded[:z.rows, :z.slots] = columns[...]
    column = padded[...]
    row = lax.axis_index(AXES) * z.rows + lax.broadcasted_iota(jnp.int32, column.shape, 0)
    offset = column - row
    offset = jnp.where(offset > z.all_rows // 2, offset - z.all_rows, offset)
    offset = jnp.where(offset < -(z.all_rows // 2), offset + z.all_rows, offset)
    offset = jnp.where(column < 0, EMPTY, offset)
    offsets[...] = jnp.zeros_like(offsets)
    offsets[0:16, :] = offset.astype(jnp.float32).astype(offsets.dtype)
    last = pltpu.make_async_copy(offsets, out.at[z.rows * z.slots], out_sems.at[z.rows])
    last.start()
    for load, store in copies:
        load.wait()
        store.start()
    for _, store in copies:
        store.wait()
    last.wait()


def emit(z, total, positions, stage, out, sems, prev=None):
    for r in range(z.rows):
        def one(s, carry):
            value = total[r * z.block:(r + 1) * z.block, pl.ds(aligned(positions[r, s], z.block), z.block)]
            if prev is not None:
                value = value + prev[r, s]
            stage[r, s] = value.astype(stage.dtype)
            return carry
        lax.fori_loop(0, z.slots, one, 0, unroll=10)
        pltpu.make_async_copy(stage.at[r], out.at[r], sems.at[r]).start()
    for r in range(z.rows):
        pltpu.make_async_copy(stage.at[r], out.at[r], sems.at[r]).wait()


def add_trace(trace, weight, one, other):
    value = jnp.dot(one, other, preferred_element_type=jnp.float32)
    on = lax.broadcasted_iota(jnp.int32, value.shape, 0) == lax.broadcasted_iota(jnp.int32, value.shape, 1)
    diagonal = jnp.sum(jnp.where(on, value, 0.0), axis=0, keepdims=True)
    trace[:, :value.shape[1]] += weight.astype(jnp.float32) * diagonal


def own_body(z, own, columns, out, left_out, corner_out, positions, trace, stage, left, total, out_stage,
             in_sem, left_sem, corner_sem, out_sems):
    device = lax.axis_index(AXES)
    kind = device % 4
    copy = pltpu.make_async_copy(own, stage, in_sem)
    copy.start()
    left[...] = jnp.zeros_like(left)
    total[:, z.window * z.block:] = jnp.zeros((z.span, z.block), jnp.float32)
    copy.wait()
    start = z.start(device)
    for r in range(z.rows):
        def place(u, carry):
            column = z.position(columns[r, u], start)
            positions[r, u] = column
            left[r * z.block:(r + 1) * z.block, pl.ds(aligned(column, z.block), z.block)] = stage[r, u]
            return carry
        lax.fori_loop(0, z.slots, place, 0, unroll=10)
    left_copy = pltpu.make_async_copy(left, left_out, left_sem)
    left_copy.start()
    half = z.span // 2

    def corner(start):
        def go(rows, cols):
            copy = pltpu.make_async_copy(left.at[rows, cols], corner_out, corner_sem)
            copy.start() if start else copy.wait()
        pl.when(kind == UPPER)(lambda: go(pl.ds(0, half), pl.ds(0, z.span)))
        pl.when(kind != UPPER)(
            lambda: go(pl.ds(half, half), pl.ds((z.chunks - 1) * z.span, z.span))
        )

    corner(True)
    middle = slice(z.hops * z.span, (z.hops + 1) * z.span)

    def multiply(n, carry):
        cols = pl.ds(aligned(n, z.span), z.span)
        total[:, cols] = jnp.dot(left[:, middle], left[:, cols], preferred_element_type=jnp.float32)
        return carry

    lax.fori_loop(0, z.chunks, multiply, 0)
    trace[...] = jnp.zeros_like(trace)
    add_trace(trace, jnp.float32(1), left[:, middle], left[:, middle])
    emit(z, total, positions, out_stage, out, out_sems)
    corner(False)
    left_copy.wait()


def near_body(z, names, final, left_in, positions, prev, trace_in, *refs):
    refs = list(refs)
    take = lambda count: [refs.pop(0) for _ in range(count)]
    sources = take(len(names))
    out, trace = take(2)
    relay_left = take(1)[0] if final else None
    left, stage, right, total, sums, vector, scalars = take(7)
    left_sem, in_sem, prev_sem, place_sem, relay_sem, out_sems = take(6)
    device = lax.axis_index(AXES)
    kind = device % 4
    place = {name: pick(table, kind) + z.hops for name, table in OFFSETS.items()}

    def chunk(n):
        return pl.ds(aligned(n, z.span), z.span)

    def fetch(index):
        return pltpu.make_async_copy(sources[index], stage.at[index % 2], in_sem.at[index % 2])

    fetch(0).start()
    left_copy = pltpu.make_async_copy(left_in, left, left_sem)
    left_copy.start()
    prev_copy = pltpu.make_async_copy(prev, sums, prev_sem)
    total[...] = jnp.zeros_like(total)
    trace[...] = trace_in[...]
    relay_copies = []

    def hand_on():
        for index, name in enumerate(("relay", "relay_beside") if final else ()):
            copy = pltpu.make_async_copy(
                left.at[:, chunk(place[name])], relay_left.at[:, pl.ds(index * z.span, z.span)],
                relay_sem.at[index],
            )
            copy.start()
            relay_copies.append(copy)

    decodings = []

    def begin_decode(index):
        slot = index % 2
        fetch(index).wait()
        decodings.append(decode(
            z, stage.at[slot, z.rows * z.slots], place[names[index]], vector.at[slot], scalars.at[slot],
            place_sem.at[slot],
        ))

    begin_decode(0)
    if len(names) > 1:
        fetch(1).start()
    dense_of = {}
    for index, name in enumerate(names):
        dense = right.at[index]
        dense_of[name] = dense
        spot = place[name]
        slot = index % 2
        dense[...] = jnp.zeros_like(dense)
        decodings[index].wait()
        scatter(z, dense, 0, stage.at[slot], lambda r, u: scalars[slot, r, u])
        if index == 0:
            left_copy.wait()
            prev_copy.start()
            hand_on()
        if index + 2 < len(names):
            fetch(index + 2).start()
        if index + 1 < len(names):
            begin_decode(index + 1)

        def multiply(n, carry):
            total[:, chunk(n)] += jnp.dot(
                left[:, chunk(spot)], dense[:, chunk(n)], preferred_element_type=jnp.float32
            )
            return carry

        lax.fori_loop(jnp.maximum(0, spot - z.hops), jnp.minimum(z.chunks, spot + z.hops + 1), multiply, 0)
        weight = pick(COUNTS[name], kind)
        pl.when(weight != 0)(
            lambda: add_trace(trace, weight, left[:, chunk(spot)], dense[:, chunk(z.hops)])
        )
    for (one, other), table in OUTSIDE.items() if final else ():
        weight = pick(table, kind)
        pl.when(weight != 0)(lambda: add_trace(
            trace, weight, dense_of[one][:, chunk(place[other])], dense_of[other][:, chunk(place[one])]
        ))
    prev_copy.wait()
    emit(z, total, positions, sums, out, out_sems, sums)
    for copy in relay_copies:
        copy.wait()


def corner_body(z, left, corner, trace_in, trace, rows, sem):
    kind = lax.axis_index(AXES) % 4
    half = z.span // 2
    end = (z.chunks - 1) * z.span
    trace[...] = trace_in[...]

    @pl.when(kind == UPPER)
    def _():
        copy = pltpu.make_async_copy(left.at[:, pl.ds(half, half)], rows, sem)
        copy.start()
        copy.wait()
        add_trace(trace, jnp.float32(2), rows[...], corner[...])

    @pl.when(kind == LOWER)
    def _():
        copy = pltpu.make_async_copy(left.at[pl.ds(0, half), pl.ds(end, half)], rows.at[pl.ds(0, half)], sem)
        copy.start()
        copy.wait()
        add_trace(trace, jnp.float32(2), rows[:half], corner[:, :half])


def last_body(z, left_in, positions, prev, source_a, source_b, out, left, right, total, out_stage,
              prev_stage, vector, scalars, left_sem, prev_sem, place_sem, out_sems):
    kind = lax.axis_index(AXES) % 4
    copies = [
        pltpu.make_async_copy(left_in, left, left_sem),
        pltpu.make_async_copy(prev, prev_stage, prev_sem),
    ]
    for copy in copies:
        copy.start()
    places = [pick(OFFSETS[name], kind) + z.hops for name in ("relay", "relay_beside")]
    low = jnp.maximum(0, jnp.minimum(*places) - z.hops)
    high = jnp.minimum(z.chunks, jnp.maximum(*places) + z.hops + 1)

    def chunk(n):
        return pl.ds(aligned(n, z.span), z.span)

    def clear_total(n, carry):
        total[:, chunk(n)] = jnp.zeros((z.span, z.span), jnp.float32)
        return carry

    def clear_right(n, carry):
        right[:, chunk(n)] = jnp.zeros((2 * z.span, z.span), right.dtype)
        return carry

    lax.fori_loop(0, low, clear_total, 0)
    lax.fori_loop(high, z.chunks, clear_total, 0)
    total[:, z.window * z.block:] = jnp.zeros((z.span, z.block), jnp.float32)
    decodings = []
    for index in range(2):
        decodings.append(decode(
            z, (source_a, source_b)[index].at[z.rows * z.slots], places[index], vector.at[index], scalars.at[index],
            place_sem.at[index],
        ))
    lax.fori_loop(low, high, clear_right, 0)
    for index in range(2):
        decodings[index].wait()
        scatter(z, right, index * z.span, (source_a, source_b)[index], lambda r, u: scalars[index, r, u])
    copies[0].wait()

    def multiply(n, carry):
        total[:, chunk(n)] = jnp.dot(left[...], right[:, chunk(n)], preferred_element_type=jnp.float32)
        return carry

    lax.fori_loop(low, high, multiply, 0)
    copies[1].wait()
    emit(z, total, positions, out_stage, out, out_sems, prev_stage)


ANY = pl.BlockSpec(memory_space=pl.ANY)
SMEM = pl.BlockSpec(memory_space=pltpu.SMEM)
VMEM = pl.BlockSpec(memory_space=pltpu.VMEM)
DMA = pltpu.SemaphoreType.DMA


def call(z, kernel, operands, in_specs, out_shape, out_specs, scratch, pieces, limit=VMEM_LIMIT):
    return pl.pallas_call(
        kernel,
        out_shape=out_shape,
        in_specs=in_specs,
        out_specs=out_specs,
        scratch_shapes=scratch,
        compiler_params=pltpu.CompilerParams(vmem_limit_bytes=limit),
        cost_estimate=pl.CostEstimate(
            flops=2 * z.span * z.span * z.window * z.block * pieces,
            bytes_accessed=2 * z.span * z.slots * z.block * (pieces + 4),
            transcendentals=0,
        ),
    )(*operands)


def shards(tiles, columns):
    devices = lax.axis_size(AXES)
    z = Sizes(tiles.shape, devices)
    assert z.hops == 3 and z.rows == 4 and devices % 4 == 0 and devices > 8
    dtype = tiles.dtype
    shape = jax.ShapeDtypeStruct
    sums = shape(tiles.shape, jnp.float32)
    line = shape((1, z.span), jnp.float32)
    dense = pltpu.VMEM((z.span, z.wide), dtype)
    total_buffer = pltpu.VMEM((z.span, z.wide), jnp.float32)

    payload_shape = (z.rows * z.slots + 1, z.block, z.block)
    places = [pltpu.VMEM((2, 16, z.block), jnp.int32), pltpu.SMEM((2, 16, z.block), jnp.int32)]

    payload = call(
        z, functools.partial(pack_body, z), [tiles, columns], [ANY, VMEM],
        shape(payload_shape, dtype), ANY,
        [
            pltpu.VMEM((z.rows * z.slots, z.block, z.block), dtype), pltpu.VMEM((16, z.block), jnp.int32),
            pltpu.VMEM((z.block, z.block), dtype), DMA((z.rows,)), DMA((z.rows + 1,)),
        ],
        0, WHOLE_VMEM,
    )
    first = receive(payload, FIRST)
    second = receive(payload, SECOND)
    beside = receive(payload, PARTNER)

    total, left, corner, positions, trace = call(
        z, functools.partial(own_body, z), [tiles, columns], [ANY, SMEM],
        [
            sums, shape((z.span, z.wide), dtype), shape((z.span // 2, z.span), dtype),
            shape((z.rows, z.slots), jnp.int32), line,
        ],
        [ANY, ANY, ANY, SMEM, VMEM],
        [
            pltpu.VMEM(tiles.shape, dtype), dense, total_buffer, pltpu.VMEM(tiles.shape, jnp.float32),
            DMA, DMA, DMA, DMA((z.rows,)),
        ],
        1, WHOLE_VMEM,
    )
    corner = receive(corner, PARTNER, (0, 3))

    def near(names, arrays, total, trace, final=False):
        extra = [shape((z.span, 2 * z.span), dtype)] * final
        return call(
            z, functools.partial(near_body, z, names, final),
            [left, positions, total, trace] + arrays,
            [ANY, SMEM, ANY, VMEM] + [ANY] * len(arrays),
            [sums, line] + extra,
            [ANY, VMEM] + [ANY] * final,
            [
                dense, pltpu.VMEM((2,) + payload_shape, dtype),
                pltpu.VMEM((len(names), z.span, z.wide), dtype), total_buffer,
                pltpu.VMEM(tiles.shape, jnp.float32), *places,
                DMA, DMA((2,)), DMA, DMA((2,)), DMA((2,)), DMA((z.rows,)),
            ],
            len(names), VMEM_LIMIT if final else WHOLE_VMEM,
        )

    total, trace = near(("beside",), [beside], total, trace)
    first, second, corner, total, trace = lax.optimization_barrier((first, second, corner, total, trace))
    relay = receive(first, RELAY_FROM)
    kind = lax.axis_index(AXES) % 4

    def nearby(first, second, corner, total, trace):
        use_first = (kind == 0) | (kind == 3)
        mixed = receive(jnp.where(use_first, first, second), PARTNER)
        corner = receive(corner, (0, -2, 2, 0), (LOWER, UPPER))
        total, trace, relay_left = near(("first", "second", "mixed"), [first, second, mixed], total, trace, True)
        trace = call(
            z, functools.partial(corner_body, z), [left, corner, trace], [ANY, VMEM, VMEM], line, VMEM,
            [pltpu.VMEM((z.span, z.span // 2), dtype), DMA], 0,
        )
        return total, trace, relay_left

    def nothing(first, second, corner, total, trace):
        return jnp.zeros_like(total), jnp.zeros_like(trace), jnp.zeros((z.span, 2 * z.span), dtype)

    total, trace, relay_left = lax.cond(
        positions[0, 0] >= 0, nearby, nothing, first, second, corner, total, trace
    )
    assert devices & (devices - 1) == 0
    steps = [1 << bit for bit in range(devices.bit_length() - 1)]
    trace = trace + fetch(trace, steps[0])
    for index in range(3, len(steps), 2):
        trace = round_of(trace, steps[index:index + 2])
    relay, total, trace = lax.optimization_barrier((relay, total, trace))
    relay_beside = receive(relay, PARTNER)
    others = [fetch(trace, step) for step in (steps[1], steps[2], steps[1] + steps[2])]
    square = call(
        z, functools.partial(last_body, z), [relay_left, positions, total, relay, relay_beside],
        [ANY, SMEM, ANY, VMEM, VMEM],
        [shape(tiles.shape, dtype)],
        [ANY],
        [
            pltpu.VMEM((z.span, 2 * z.span), dtype),
            pltpu.VMEM((2 * z.span, z.wide), dtype), total_buffer,
            pltpu.VMEM(tiles.shape, dtype), pltpu.VMEM(tiles.shape, jnp.float32), *places,
            DMA, DMA, DMA((2,)), DMA((z.rows,)),
        ],
        2, 44 * 1024 * 1024,
    )[0]
    square, trace, others = lax.optimization_barrier((square, trace, others))
    return square, jnp.sum((trace + others[0]) + (others[1] + others[2])) / (z.all_rows * z.block)


def solution(mesh):
    return jax.shard_map(
        shards,
        mesh=mesh,
        in_specs=(P(AXES, None, None, None), P(AXES, None)),
        out_specs=(P(AXES, None, None, None), P()),
        check_vma=False,
    )
```

```python
import functools

import jax
import jax.numpy as jnp
from jax import lax
from jax.experimental import pallas as pl
from jax.experimental.pallas import tpu as pltpu
from jax.sharding import PartitionSpec as P

REACH = 12
AXES = ("blk", "grp")
VMEM_LIMIT = 42 * 1024 * 1024
WHOLE_VMEM = 62 * 1024 * 1024
EMPTY = 64

FIRST = (2, 3, -3, -2)
SECOND = (-3, 2, -2, 3)
RELAY_FROM = (2, -5, 5, -2)
PARTNER = (1, -1, 1, -1)
RELAY = tuple(RELAY_FROM[m] + FIRST[(m + RELAY_FROM[m]) % 4] for m in range(4))


def across(table):
    return tuple(PARTNER[m] + table[m ^ 1] for m in range(4))


USE_SECOND = tuple(int(abs(offset) > 3) for offset in across(FIRST))
MIXED = tuple(
    second if use else first
    for first, second, use in zip(across(FIRST), across(SECOND), USE_SECOND)
)
OFFSETS = {
    "beside": PARTNER,
    "first": FIRST,
    "second": SECOND,
    "mixed": MIXED,
    "relay": RELAY,
    "relay_beside": across(RELAY),
}
COUNTS = {"beside": (2, 0, 2, 0), "first": (2, 0, 0, 2), "second": (2, 0, 0, 2), "mixed": (0, 0, 2, 2)}
OUTSIDE = {("first", "mixed"): (0, 2, 2, 0), ("first", "second"): (0, 2, 0, 0)}
LOWER, UPPER = 2, 1


def receive(shard, offsets, kinds=range(4)):
    size = lax.axis_size(AXES)
    pairs = [((d + offsets[d % 4]) % size, d) for d in range(size) if d % 4 in kinds]
    return lax.ppermute(shard, AXES, pairs)


def fetch(value, step):
    return lax.ppermute(value, AXES, [(d, d ^ step) for d in range(lax.axis_size(AXES))])


def round_of(value, steps):
    if len(steps) == 1:
        return value + fetch(value, steps[0])
    one, other = steps
    return (value + fetch(value, one)) + (fetch(value, other) + fetch(value, one + other))


def pick(table, kind):
    value = jnp.int32(table[3])
    for m in range(3):
        value = jnp.where(kind == m, jnp.int32(table[m]), value)
    return value


def aligned(index, unit):
    return pl.multiple_of(index * unit, unit)


class Sizes:
    def __init__(self, shape, devices):
        self.rows, self.slots, self.block, _ = shape
        self.hops = (REACH + self.rows - 1) // self.rows
        self.chunks = 2 * self.hops + 1
        self.window = self.chunks * self.rows
        self.span = self.rows * self.block
        self.wide = (self.window + 1) * self.block
        self.all_rows = self.rows * devices

    def start(self, device):
        start = (device - self.hops) * self.rows
        return jnp.where(start < 0, start + self.all_rows, start)

    def position(self, column, start):
        place = column - start
        place = jnp.where(place < 0, place + self.all_rows, place)
        place = jnp.where(column < 0, self.window, place)
        return jnp.minimum(place, self.window)


def scatter(z, dense, top, source, place):
    for r in range(z.rows):
        def one(u, carry):
            column = pl.ds(aligned(place(r, u), z.block), z.block)
            dense[top + r * z.block:top + (r + 1) * z.block, column] = source[r * z.slots + u]
            return carry
        lax.fori_loop(0, z.slots, one, 0, unroll=10)


def decode(z, offsets, spot, vector, scalars, sem):
    value = offsets[0:16, :].astype(jnp.float32).astype(jnp.int32)
    value = value + spot * z.rows + lax.broadcasted_iota(jnp.int32, value.shape, 0)
    vector[...] = jnp.where((value < 0) | (value > z.window), z.window, value)
    copy = pltpu.make_async_copy(vector, scalars, sem)
    copy.start()
    return copy


def pack_body(z, tiles, columns, out, stage, padded, offsets, in_sems, out_sems):
    copies = []
    for r in range(z.rows):
        rows = pl.ds(r * z.slots, z.slots)
        copies.append((
            pltpu.make_async_copy(tiles.at[r], stage.at[rows], in_sems.at[r]),
            pltpu.make_async_copy(stage.at[rows], out.at[rows], out_sems.at[r]),
        ))
    for copy, _ in copies:
        copy.start()
    padded[...] = jnp.full(padded.shape, -1, jnp.int32)
    padded[:z.rows, :z.slots] = columns[...]
    column = padded[...]
    row = lax.axis_index(AXES) * z.rows + lax.broadcasted_iota(jnp.int32, column.shape, 0)
    offset = column - row
    offset = jnp.where(offset > z.all_rows // 2, offset - z.all_rows, offset)
    offset = jnp.where(offset < -(z.all_rows // 2), offset + z.all_rows, offset)
    offset = jnp.where(column < 0, EMPTY, offset)
    offsets[...] = jnp.zeros_like(offsets)
    offsets[0:16, :] = offset.astype(jnp.float32).astype(offsets.dtype)
    last = pltpu.make_async_copy(offsets, out.at[z.rows * z.slots], out_sems.at[z.rows])
    last.start()
    for load, store in copies:
        load.wait()
        store.start()
    for _, store in copies:
        store.wait()
    last.wait()


def emit(z, total, positions, stage, out, sems, prev=None):
    for r in range(z.rows):
        def one(s, carry):
            value = total[r * z.block:(r + 1) * z.block, pl.ds(aligned(positions[r, s], z.block), z.block)]
            if prev is not None:
                value = value + prev[r, s]
            stage[r, s] = value.astype(stage.dtype)
            return carry
        lax.fori_loop(0, z.slots, one, 0, unroll=10)
        pltpu.make_async_copy(stage.at[r], out.at[r], sems.at[r]).start()
    for r in range(z.rows):
        pltpu.make_async_copy(stage.at[r], out.at[r], sems.at[r]).wait()


def add_trace(trace, weight, one, other):
    value = jnp.dot(one, other, preferred_element_type=jnp.float32)
    on = lax.broadcasted_iota(jnp.int32, value.shape, 0) == lax.broadcasted_iota(jnp.int32, value.shape, 1)
    diagonal = jnp.sum(jnp.where(on, value, 0.0), axis=0, keepdims=True)
    trace[:, :value.shape[1]] += weight.astype(jnp.float32) * diagonal


def own_body(z, own, columns, out, left_out, corner_out, positions, trace, stage, left, total, out_stage,
             in_sem, left_sem, corner_sem, out_sems):
    device = lax.axis_index(AXES)
    kind = device % 4
    copy = pltpu.make_async_copy(own, stage, in_sem)
    copy.start()
    left[...] = jnp.zeros_like(left)
    total[:, z.window * z.block:] = jnp.zeros((z.span, z.block), jnp.float32)
    copy.wait()
    start = z.start(device)
    for r in range(z.rows):
        def place(u, carry):
            column = z.position(columns[r, u], start)
            positions[r, u] = column
            left[r * z.block:(r + 1) * z.block, pl.ds(aligned(column, z.block), z.block)] = stage[r, u]
            return carry
        lax.fori_loop(0, z.slots, place, 0, unroll=10)
    left_copy = pltpu.make_async_copy(left, left_out, left_sem)
    left_copy.start()
    half = z.span // 2

    def corner(start):
        def go(rows, cols):
            copy = pltpu.make_async_copy(left.at[rows, cols], corner_out, corner_sem)
            copy.start() if start else copy.wait()
        pl.when(kind == UPPER)(lambda: go(pl.ds(0, half), pl.ds(0, z.span)))
        pl.when(kind != UPPER)(
            lambda: go(pl.ds(half, half), pl.ds((z.chunks - 1) * z.span, z.span))
        )

    corner(True)
    middle = slice(z.hops * z.span, (z.hops + 1) * z.span)

    def multiply(n, carry):
        cols = pl.ds(aligned(n, z.span), z.span)
        total[:, cols] = jnp.dot(left[:, middle], left[:, cols], preferred_element_type=jnp.float32)
        return carry

    lax.fori_loop(0, z.chunks, multiply, 0)
    trace[...] = jnp.zeros_like(trace)
    add_trace(trace, jnp.float32(1), left[:, middle], left[:, middle])
    emit(z, total, positions, out_stage, out, out_sems)
    corner(False)
    left_copy.wait()


def near_body(z, names, final, left_in, positions, prev, trace_in, *refs):
    refs = list(refs)
    take = lambda count: [refs.pop(0) for _ in range(count)]
    sources = take(len(names))
    out, trace = take(2)
    relay_left = take(1)[0] if final else None
    left, stage, right, total, sums, vector, scalars = take(7)
    left_sem, in_sem, prev_sem, place_sem, relay_sem, out_sems = take(6)
    device = lax.axis_index(AXES)
    kind = device % 4
    place = {name: pick(table, kind) + z.hops for name, table in OFFSETS.items()}

    def chunk(n):
        return pl.ds(aligned(n, z.span), z.span)

    def fetch(index):
        return pltpu.make_async_copy(sources[index], stage.at[index % 2], in_sem.at[index % 2])

    fetch(0).start()
    left_copy = pltpu.make_async_copy(left_in, left, left_sem)
    left_copy.start()
    prev_copy = pltpu.make_async_copy(prev, sums, prev_sem)
    total[...] = jnp.zeros_like(total)
    trace[...] = trace_in[...]
    relay_copies = []

    def hand_on():
        for index, name in enumerate(("relay", "relay_beside") if final else ()):
            copy = pltpu.make_async_copy(
                left.at[:, chunk(place[name])], relay_left.at[:, pl.ds(index * z.span, z.span)],
                relay_sem.at[index],
            )
            copy.start()
            relay_copies.append(copy)

    decodings = []

    def begin_decode(index):
        slot = index % 2
        fetch(index).wait()
        decodings.append(decode(
            z, stage.at[slot, z.rows * z.slots], place[names[index]], vector.at[slot], scalars.at[slot],
            place_sem.at[slot],
        ))

    begin_decode(0)
    if len(names) > 1:
        fetch(1).start()
    dense_of = {}
    for index, name in enumerate(names):
        dense = right.at[index]
        dense_of[name] = dense
        spot = place[name]
        slot = index % 2
        dense[...] = jnp.zeros_like(dense)
        decodings[index].wait()
        scatter(z, dense, 0, stage.at[slot], lambda r, u: scalars[slot, r, u])
        if index == 0:
            left_copy.wait()
            prev_copy.start()
            hand_on()
        if index + 2 < len(names):
            fetch(index + 2).start()
        if index + 1 < len(names):
            begin_decode(index + 1)

        def multiply(n, carry):
            total[:, chunk(n)] += jnp.dot(
                left[:, chunk(spot)], dense[:, chunk(n)], preferred_element_type=jnp.float32
            )
            return carry

        lax.fori_loop(jnp.maximum(0, spot - z.hops), jnp.minimum(z.chunks, spot + z.hops + 1), multiply, 0)
        weight = pick(COUNTS[name], kind)
        pl.when(weight != 0)(
            lambda: add_trace(trace, weight, left[:, chunk(spot)], dense[:, chunk(z.hops)])
        )
    for (one, other), table in OUTSIDE.items() if final else ():
        weight = pick(table, kind)
        pl.when(weight != 0)(lambda: add_trace(
            trace, weight, dense_of[one][:, chunk(place[other])], dense_of[other][:, chunk(place[one])]
        ))
    prev_copy.wait()
    emit(z, total, positions, sums, out, out_sems, sums)
    for copy in relay_copies:
        copy.wait()


def corner_body(z, left, corner, trace_in, trace, rows, sem):
    kind = lax.axis_index(AXES) % 4
    half = z.span // 2
    end = (z.chunks - 1) * z.span
    trace[...] = trace_in[...]

    @pl.when(kind == UPPER)
    def _():
        copy = pltpu.make_async_copy(left.at[:, pl.ds(half, half)], rows, sem)
        copy.start()
        copy.wait()
        add_trace(trace, jnp.float32(2), rows[...], corner[...])

    @pl.when(kind == LOWER)
    def _():
        copy = pltpu.make_async_copy(left.at[pl.ds(0, half), pl.ds(end, half)], rows.at[pl.ds(0, half)], sem)
        copy.start()
        copy.wait()
        add_trace(trace, jnp.float32(2), rows[:half], corner[:, :half])


def last_body(z, left_in, positions, prev, source_a, source_b, out, left, right, total, out_stage,
              prev_stage, vector, scalars, left_sem, prev_sem, place_sem, out_sems):
    kind = lax.axis_index(AXES) % 4
    copies = [
        pltpu.make_async_copy(left_in, left, left_sem),
        pltpu.make_async_copy(prev, prev_stage, prev_sem),
    ]
    for copy in copies:
        copy.start()
    places = [pick(OFFSETS[name], kind) + z.hops for name in ("relay", "relay_beside")]
    low = jnp.maximum(0, jnp.minimum(*places) - z.hops)
    high = jnp.minimum(z.chunks, jnp.maximum(*places) + z.hops + 1)

    def chunk(n):
        return pl.ds(aligned(n, z.span), z.span)

    def clear_total(n, carry):
        total[:, chunk(n)] = jnp.zeros((z.span, z.span), jnp.float32)
        return carry

    def clear_right(n, carry):
        right[:, chunk(n)] = jnp.zeros((2 * z.span, z.span), right.dtype)
        return carry

    lax.fori_loop(0, low, clear_total, 0)
    lax.fori_loop(high, z.chunks, clear_total, 0)
    total[:, z.window * z.block:] = jnp.zeros((z.span, z.block), jnp.float32)
    decodings = []
    for index in range(2):
        decodings.append(decode(
            z, (source_a, source_b)[index].at[z.rows * z.slots], places[index], vector.at[index], scalars.at[index],
            place_sem.at[index],
        ))
    lax.fori_loop(low, high, clear_right, 0)
    for index in range(2):
        decodings[index].wait()
        scatter(z, right, index * z.span, (source_a, source_b)[index], lambda r, u: scalars[index, r, u])
    copies[0].wait()

    def multiply(n, carry):
        total[:, chunk(n)] = jnp.dot(left[...], right[:, chunk(n)], preferred_element_type=jnp.float32)
        return carry

    lax.fori_loop(low, high, multiply, 0)
    copies[1].wait()
    emit(z, total, positions, out_stage, out, out_sems, prev_stage)


ANY = pl.BlockSpec(memory_space=pl.ANY)
SMEM = pl.BlockSpec(memory_space=pltpu.SMEM)
VMEM = pl.BlockSpec(memory_space=pltpu.VMEM)
DMA = pltpu.SemaphoreType.DMA


def call(z, kernel, operands, in_specs, out_shape, out_specs, scratch, pieces, limit=VMEM_LIMIT):
    return pl.pallas_call(
        kernel,
        out_shape=out_shape,
        in_specs=in_specs,
        out_specs=out_specs,
        scratch_shapes=scratch,
        compiler_params=pltpu.CompilerParams(vmem_limit_bytes=limit),
        cost_estimate=pl.CostEstimate(
            flops=2 * z.span * z.span * z.window * z.block * pieces,
            bytes_accessed=2 * z.span * z.slots * z.block * (pieces + 4),
            transcendentals=0,
        ),
    )(*operands)


def shards(tiles, columns):
    devices = lax.axis_size(AXES)
    z = Sizes(tiles.shape, devices)
    assert z.hops == 3 and z.rows == 4 and devices % 4 == 0 and devices > 8
    dtype = tiles.dtype
    shape = jax.ShapeDtypeStruct
    sums = shape(tiles.shape, jnp.float32)
    line = shape((1, z.span), jnp.float32)
    dense = pltpu.VMEM((z.span, z.wide), dtype)
    total_buffer = pltpu.VMEM((z.span, z.wide), jnp.float32)

    payload_shape = (z.rows * z.slots + 1, z.block, z.block)
    places = [pltpu.VMEM((2, 16, z.block), jnp.int32), pltpu.SMEM((2, 16, z.block), jnp.int32)]

    payload = call(
        z, functools.partial(pack_body, z), [tiles, columns], [ANY, VMEM],
        shape(payload_shape, dtype), ANY,
        [
            pltpu.VMEM((z.rows * z.slots, z.block, z.block), dtype), pltpu.VMEM((16, z.block), jnp.int32),
            pltpu.VMEM((z.block, z.block), dtype), DMA((z.rows,)), DMA((z.rows + 1,)),
        ],
        0, WHOLE_VMEM,
    )
    first = receive(payload, FIRST)
    second = receive(payload, SECOND)
    beside = receive(payload, PARTNER)

    total, left, corner, positions, trace = call(
        z, functools.partial(own_body, z), [tiles, columns], [ANY, SMEM],
        [
            sums, shape((z.span, z.wide), dtype), shape((z.span // 2, z.span), dtype),
            shape((z.rows, z.slots), jnp.int32), line,
        ],
        [ANY, ANY, ANY, SMEM, VMEM],
        [
            pltpu.VMEM(tiles.shape, dtype), dense, total_buffer, pltpu.VMEM(tiles.shape, jnp.float32),
            DMA, DMA, DMA, DMA((z.rows,)),
        ],
        1, WHOLE_VMEM,
    )
    corner = receive(corner, PARTNER, (0, 3))

    def near(names, arrays, total, trace, final=False):
        extra = [shape((z.span, 2 * z.span), dtype)] * final
        return call(
            z, functools.partial(near_body, z, names, final),
            [left, positions, total, trace] + arrays,
            [ANY, SMEM, ANY, VMEM] + [ANY] * len(arrays),
            [sums, line] + extra,
            [ANY, VMEM] + [ANY] * final,
            [
                dense, pltpu.VMEM((2,) + payload_shape, dtype),
                pltpu.VMEM((len(names), z.span, z.wide), dtype), total_buffer,
                pltpu.VMEM(tiles.shape, jnp.float32), *places,
                DMA, DMA((2,)), DMA, DMA((2,)), DMA((2,)), DMA((z.rows,)),
            ],
            len(names), VMEM_LIMIT if final else WHOLE_VMEM,
        )

    total, trace = near(("beside",), [beside], total, trace)
    first, second, corner, total, trace = lax.optimization_barrier((first, second, corner, total, trace))
    relay = receive(first, RELAY_FROM)
    kind = lax.axis_index(AXES) % 4

    def nearby(first, second, corner, total, trace):
        use_first = (kind == 0) | (kind == 3)
        mixed = receive(jnp.where(use_first, first, second), PARTNER)
        corner = receive(corner, (0, -2, 2, 0), (LOWER, UPPER))
        total, trace, relay_left = near(("first", "second", "mixed"), [first, second, mixed], total, trace, True)
        trace = call(
            z, functools.partial(corner_body, z), [left, corner, trace], [ANY, VMEM, VMEM], line, VMEM,
            [pltpu.VMEM((z.span, z.span // 2), dtype), DMA], 0,
        )
        return total, trace, relay_left

    def nothing(first, second, corner, total, trace):
        return jnp.zeros_like(total), jnp.zeros_like(trace), jnp.zeros((z.span, 2 * z.span), dtype)

    total, trace, relay_left = lax.cond(
        positions[0, 0] >= 0, nearby, nothing, first, second, corner, total, trace
    )
    assert devices & (devices - 1) == 0
    steps = [1 << bit for bit in range(devices.bit_length() - 1)]
    trace = trace + fetch(trace, steps[0])
    for index in range(3, len(steps), 2):
        trace = round_of(trace, steps[index:index + 2])
    relay, total, trace = lax.optimization_barrier((relay, total, trace))
    relay_beside = receive(relay, PARTNER)
    others = [fetch(trace, step) for step in (steps[1], steps[2], steps[1] + steps[2])]
    square = call(
        z, functools.partial(last_body, z), [relay_left, positions, total, relay, relay_beside],
        [ANY, SMEM, ANY, VMEM, VMEM],
        [shape(tiles.shape, dtype)],
        [ANY],
        [
            pltpu.VMEM((z.span, 2 * z.span), dtype),
            pltpu.VMEM((2 * z.span, z.wide), dtype), total_buffer,
            pltpu.VMEM(tiles.shape, dtype), pltpu.VMEM(tiles.shape, jnp.float32), *places,
            DMA, DMA, DMA((2,)), DMA((z.rows,)),
        ],
        2, 44 * 1024 * 1024,
    )[0]
    square, trace, others = lax.optimization_barrier((square, trace, others))
    return square, jnp.sum((trace + others[0]) + (others[1] + others[2])) / (z.all_rows * z.block)


def solution(mesh):
    return jax.shard_map(
        shards,
        mesh=mesh,
        in_specs=(P(AXES, None, None, None), P(AXES, None)),
        out_specs=(P(AXES, None, None, None), P()),
        check_vma=False,
    )
```

```python
import functools

import jax
import jax.numpy as jnp
from jax import lax
from jax.experimental import pallas as pl
from jax.experimental.pallas import tpu as pltpu
from jax.sharding import PartitionSpec as P

REACH = 12
AXES = ("blk", "grp")
VMEM_LIMIT = 42 * 1024 * 1024
WHOLE_VMEM = 62 * 1024 * 1024
EMPTY = 64

FIRST = (2, 3, -3, -2)
SECOND = (-3, 2, -2, 3)
RELAY_FROM = (2, -5, 5, -2)
PARTNER = (1, -1, 1, -1)
RELAY = tuple(RELAY_FROM[m] + FIRST[(m + RELAY_FROM[m]) % 4] for m in range(4))


def across(table):
    return tuple(PARTNER[m] + table[m ^ 1] for m in range(4))


USE_SECOND = tuple(int(abs(offset) > 3) for offset in across(FIRST))
MIXED = tuple(
    second if use else first
    for first, second, use in zip(across(FIRST), across(SECOND), USE_SECOND)
)
OFFSETS = {
    "beside": PARTNER,
    "first": FIRST,
    "second": SECOND,
    "mixed": MIXED,
    "relay": RELAY,
    "relay_beside": across(RELAY),
}
COUNTS = {"beside": (2, 0, 2, 0), "first": (2, 0, 0, 2), "second": (2, 0, 0, 2), "mixed": (0, 0, 2, 2)}
OUTSIDE = {("first", "mixed"): (0, 2, 2, 0), ("first", "second"): (0, 2, 0, 0)}
LOWER, UPPER = 2, 1


def receive(shard, offsets, kinds=range(4)):
    size = lax.axis_size(AXES)
    pairs = [((d + offsets[d % 4]) % size, d) for d in range(size) if d % 4 in kinds]
    return lax.ppermute(shard, AXES, pairs)


def fetch(value, step):
    return lax.ppermute(value, AXES, [(d, d ^ step) for d in range(lax.axis_size(AXES))])


def round_of(value, steps):
    if len(steps) == 1:
        return value + fetch(value, steps[0])
    one, other = steps
    return (value + fetch(value, one)) + (fetch(value, other) + fetch(value, one + other))


def pick(table, kind):
    value = jnp.int32(table[3])
    for m in range(3):
        value = jnp.where(kind == m, jnp.int32(table[m]), value)
    return value


def aligned(index, unit):
    return pl.multiple_of(index * unit, unit)


class Sizes:
    def __init__(self, shape, devices):
        self.rows, self.slots, self.block, _ = shape
        self.hops = (REACH + self.rows - 1) // self.rows
        self.chunks = 2 * self.hops + 1
        self.window = self.chunks * self.rows
        self.span = self.rows * self.block
        self.wide = (self.window + 1) * self.block
        self.all_rows = self.rows * devices

    def start(self, device):
        start = (device - self.hops) * self.rows
        return jnp.where(start < 0, start + self.all_rows, start)

    def position(self, column, start):
        place = column - start
        place = jnp.where(place < 0, place + self.all_rows, place)
        place = jnp.where(column < 0, self.window, place)
        return jnp.minimum(place, self.window)


def scatter(z, dense, top, source, place):
    for r in range(z.rows):
        def one(u, carry):
            column = pl.ds(aligned(place(r, u), z.block), z.block)
            dense[top + r * z.block:top + (r + 1) * z.block, column] = source[r * z.slots + u]
            return carry
        lax.fori_loop(0, z.slots, one, 0, unroll=10)


def decode(z, offsets, spot, vector, scalars, sem):
    value = offsets[0:16, :].astype(jnp.float32).astype(jnp.int32)
    value = value + spot * z.rows + lax.broadcasted_iota(jnp.int32, value.shape, 0)
    vector[...] = jnp.where((value < 0) | (value > z.window), z.window, value)
    copy = pltpu.make_async_copy(vector, scalars, sem)
    copy.start()
    return copy


def pack_body(z, tiles, columns, out, stage, padded, offsets, in_sems, out_sems):
    copies = []
    for r in range(z.rows):
        rows = pl.ds(r * z.slots, z.slots)
        copies.append((
            pltpu.make_async_copy(tiles.at[r], stage.at[rows], in_sems.at[r]),
            pltpu.make_async_copy(stage.at[rows], out.at[rows], out_sems.at[r]),
        ))
    for copy, _ in copies:
        copy.start()
    padded[...] = jnp.full(padded.shape, -1, jnp.int32)
    padded[:z.rows, :z.slots] = columns[...]
    column = padded[...]
    row = lax.axis_index(AXES) * z.rows + lax.broadcasted_iota(jnp.int32, column.shape, 0)
    offset = column - row
    offset = jnp.where(offset > z.all_rows // 2, offset - z.all_rows, offset)
    offset = jnp.where(offset < -(z.all_rows // 2), offset + z.all_rows, offset)
    offset = jnp.where(column < 0, EMPTY, offset)
    offsets[...] = jnp.zeros_like(offsets)
    offsets[0:16, :] = offset.astype(jnp.float32).astype(offsets.dtype)
    last = pltpu.make_async_copy(offsets, out.at[z.rows * z.slots], out_sems.at[z.rows])
    last.start()
    for load, store in copies:
        load.wait()
        store.start()
    for _, store in copies:
        store.wait()
    last.wait()


def emit(z, total, positions, stage, out, sems, prev=None):
    for r in range(z.rows):
        def one(s, carry):
            value = total[r * z.block:(r + 1) * z.block, pl.ds(aligned(positions[r, s], z.block), z.block)]
            if prev is not None:
                value = value + prev[r, s]
            stage[r, s] = value.astype(stage.dtype)
            return carry
        lax.fori_loop(0, z.slots, one, 0, unroll=10)
        pltpu.make_async_copy(stage.at[r], out.at[r], sems.at[r]).start()
    for r in range(z.rows):
        pltpu.make_async_copy(stage.at[r], out.at[r], sems.at[r]).wait()


def add_trace(trace, weight, one, other):
    value = jnp.dot(one, other, preferred_element_type=jnp.float32)
    on = lax.broadcasted_iota(jnp.int32, value.shape, 0) == lax.broadcasted_iota(jnp.int32, value.shape, 1)
    diagonal = jnp.sum(jnp.where(on, value, 0.0), axis=0, keepdims=True)
    trace[:, :value.shape[1]] += weight.astype(jnp.float32) * diagonal


def own_body(z, own, columns, out, left_out, corner_out, positions, trace, stage, left, total, out_stage,
             in_sem, left_sem, corner_sem, out_sems):
    device = lax.axis_index(AXES)
    kind = device % 4
    copy = pltpu.make_async_copy(own, stage, in_sem)
    copy.start()
    left[...] = jnp.zeros_like(left)
    total[:, z.window * z.block:] = jnp.zeros((z.span, z.block), jnp.float32)
    copy.wait()
    start = z.start(device)
    for r in range(z.rows):
        def place(u, carry):
            column = z.position(columns[r, u], start)
            positions[r, u] = column
            left[r * z.block:(r + 1) * z.block, pl.ds(aligned(column, z.block), z.block)] = stage[r, u]
            return carry
        lax.fori_loop(0, z.slots, place, 0, unroll=10)
    left_copy = pltpu.make_async_copy(left, left_out, left_sem)
    left_copy.start()
    half = z.span // 2

    def corner(start):
        def go(rows, cols):
            copy = pltpu.make_async_copy(left.at[rows, cols], corner_out, corner_sem)
            copy.start() if start else copy.wait()
        pl.when(kind == UPPER)(lambda: go(pl.ds(0, half), pl.ds(0, z.span)))
        pl.when(kind != UPPER)(
            lambda: go(pl.ds(half, half), pl.ds((z.chunks - 1) * z.span, z.span))
        )

    corner(True)
    middle = slice(z.hops * z.span, (z.hops + 1) * z.span)

    def multiply(n, carry):
        cols = pl.ds(aligned(n, z.span), z.span)
        total[:, cols] = jnp.dot(left[:, middle], left[:, cols], preferred_element_type=jnp.float32)
        return carry

    lax.fori_loop(0, z.chunks, multiply, 0)
    trace[...] = jnp.zeros_like(trace)
    add_trace(trace, jnp.float32(1), left[:, middle], left[:, middle])
    emit(z, total, positions, out_stage, out, out_sems)
    corner(False)
    left_copy.wait()


def near_body(z, names, final, left_in, positions, prev, trace_in, *refs):
    refs = list(refs)
    take = lambda count: [refs.pop(0) for _ in range(count)]
    sources = take(len(names))
    out, trace = take(2)
    relay_left = take(1)[0] if final else None
    left, stage, right, total, sums, vector, scalars = take(7)
    left_sem, in_sem, prev_sem, place_sem, relay_sem, out_sems = take(6)
    device = lax.axis_index(AXES)
    kind = device % 4
    place = {name: pick(table, kind) + z.hops for name, table in OFFSETS.items()}

    def chunk(n):
        return pl.ds(aligned(n, z.span), z.span)

    def fetch(index):
        return pltpu.make_async_copy(sources[index], stage.at[index % 2], in_sem.at[index % 2])

    fetch(0).start()
    left_copy = pltpu.make_async_copy(left_in, left, left_sem)
    left_copy.start()
    prev_copy = pltpu.make_async_copy(prev, sums, prev_sem)
    total[...] = jnp.zeros_like(total)
    trace[...] = trace_in[...]
    relay_copies = []

    def hand_on():
        for index, name in enumerate(("relay", "relay_beside") if final else ()):
            copy = pltpu.make_async_copy(
                left.at[:, chunk(place[name])], relay_left.at[:, pl.ds(index * z.span, z.span)],
                relay_sem.at[index],
            )
            copy.start()
            relay_copies.append(copy)

    decodings = []

    def begin_decode(index):
        slot = index % 2
        fetch(index).wait()
        decodings.append(decode(
            z, stage.at[slot, z.rows * z.slots], place[names[index]], vector.at[slot], scalars.at[slot],
            place_sem.at[slot],
        ))

    begin_decode(0)
    if len(names) > 1:
        fetch(1).start()
    dense_of = {}
    for index, name in enumerate(names):
        dense = right.at[index]
        dense_of[name] = dense
        spot = place[name]
        slot = index % 2
        dense[...] = jnp.zeros_like(dense)
        decodings[index].wait()
        scatter(z, dense, 0, stage.at[slot], lambda r, u: scalars[slot, r, u])
        if index == 0:
            left_copy.wait()
            prev_copy.start()
            hand_on()
        if index + 2 < len(names):
            fetch(index + 2).start()
        if index + 1 < len(names):
            begin_decode(index + 1)

        def multiply(n, carry):
            total[:, chunk(n)] += jnp.dot(
                left[:, chunk(spot)], dense[:, chunk(n)], preferred_element_type=jnp.float32
            )
            return carry

        lax.fori_loop(jnp.maximum(0, spot - z.hops), jnp.minimum(z.chunks, spot + z.hops + 1), multiply, 0)
        weight = pick(COUNTS[name], kind)
        pl.when(weight != 0)(
            lambda: add_trace(trace, weight, left[:, chunk(spot)], dense[:, chunk(z.hops)])
        )
    for (one, other), table in OUTSIDE.items() if final else ():
        weight = pick(table, kind)
        pl.when(weight != 0)(lambda: add_trace(
            trace, weight, dense_of[one][:, chunk(place[other])], dense_of[other][:, chunk(place[one])]
        ))
    prev_copy.wait()
    emit(z, total, positions, sums, out, out_sems, sums)
    for copy in relay_copies:
        copy.wait()


def corner_body(z, left, corner, trace_in, trace, rows, sem):
    kind = lax.axis_index(AXES) % 4
    half = z.span // 2
    end = (z.chunks - 1) * z.span
    trace[...] = trace_in[...]

    @pl.when(kind == UPPER)
    def _():
        copy = pltpu.make_async_copy(left.at[:, pl.ds(half, half)], rows, sem)
        copy.start()
        copy.wait()
        add_trace(trace, jnp.float32(2), rows[...], corner[...])

    @pl.when(kind == LOWER)
    def _():
        copy = pltpu.make_async_copy(left.at[pl.ds(0, half), pl.ds(end, half)], rows.at[pl.ds(0, half)], sem)
        copy.start()
        copy.wait()
        add_trace(trace, jnp.float32(2), rows[:half], corner[:, :half])


def last_body(z, left_in, positions, prev, source_a, source_b, out, left, right, total, out_stage,
              prev_stage, vector, scalars, left_sem, prev_sem, place_sem, out_sems):
    kind = lax.axis_index(AXES) % 4
    copies = [
        pltpu.make_async_copy(left_in, left, left_sem),
        pltpu.make_async_copy(prev, prev_stage, prev_sem),
    ]
    for copy in copies:
        copy.start()
    places = [pick(OFFSETS[name], kind) + z.hops for name in ("relay", "relay_beside")]
    low = jnp.maximum(0, jnp.minimum(*places) - z.hops)
    high = jnp.minimum(z.chunks, jnp.maximum(*places) + z.hops + 1)

    def chunk(n):
        return pl.ds(aligned(n, z.span), z.span)

    def clear_total(n, carry):
        total[:, chunk(n)] = jnp.zeros((z.span, z.span), jnp.float32)
        return carry

    def clear_right(n, carry):
        right[:, chunk(n)] = jnp.zeros((2 * z.span, z.span), right.dtype)
        return carry

    lax.fori_loop(0, low, clear_total, 0)
    lax.fori_loop(high, z.chunks, clear_total, 0)
    total[:, z.window * z.block:] = jnp.zeros((z.span, z.block), jnp.float32)
    decodings = []
    for index in range(2):
        decodings.append(decode(
            z, (source_a, source_b)[index].at[z.rows * z.slots], places[index], vector.at[index], scalars.at[index],
            place_sem.at[index],
        ))
    lax.fori_loop(low, high, clear_right, 0)
    for index in range(2):
        decodings[index].wait()
        scatter(z, right, index * z.span, (source_a, source_b)[index], lambda r, u: scalars[index, r, u])
    copies[0].wait()

    def multiply(n, carry):
        total[:, chunk(n)] = jnp.dot(left[...], right[:, chunk(n)], preferred_element_type=jnp.float32)
        return carry

    lax.fori_loop(low, high, multiply, 0)
    copies[1].wait()
    emit(z, total, positions, out_stage, out, out_sems, prev_stage)


ANY = pl.BlockSpec(memory_space=pl.ANY)
SMEM = pl.BlockSpec(memory_space=pltpu.SMEM)
VMEM = pl.BlockSpec(memory_space=pltpu.VMEM)
DMA = pltpu.SemaphoreType.DMA


def call(z, kernel, operands, in_specs, out_shape, out_specs, scratch, pieces, limit=VMEM_LIMIT):
    return pl.pallas_call(
        kernel,
        out_shape=out_shape,
        in_specs=in_specs,
        out_specs=out_specs,
        scratch_shapes=scratch,
        compiler_params=pltpu.CompilerParams(vmem_limit_bytes=limit),
        cost_estimate=pl.CostEstimate(
            flops=2 * z.span * z.span * z.window * z.block * pieces,
            bytes_accessed=2 * z.span * z.slots * z.block * (pieces + 4),
            transcendentals=0,
        ),
    )(*operands)


def shards(tiles, columns):
    devices = lax.axis_size(AXES)
    z = Sizes(tiles.shape, devices)
    assert z.hops == 3 and z.rows == 4 and devices % 4 == 0 and devices > 8
    dtype = tiles.dtype
    shape = jax.ShapeDtypeStruct
    sums = shape(tiles.shape, jnp.float32)
    line = shape((1, z.span), jnp.float32)
    dense = pltpu.VMEM((z.span, z.wide), dtype)
    total_buffer = pltpu.VMEM((z.span, z.wide), jnp.float32)

    payload_shape = (z.rows * z.slots + 1, z.block, z.block)
    places = [pltpu.VMEM((2, 16, z.block), jnp.int32), pltpu.SMEM((2, 16, z.block), jnp.int32)]

    payload = call(
        z, functools.partial(pack_body, z), [tiles, columns], [ANY, VMEM],
        shape(payload_shape, dtype), ANY,
        [
            pltpu.VMEM((z.rows * z.slots, z.block, z.block), dtype), pltpu.VMEM((16, z.block), jnp.int32),
            pltpu.VMEM((z.block, z.block), dtype), DMA((z.rows,)), DMA((z.rows + 1,)),
        ],
        0, WHOLE_VMEM,
    )
    first = receive(payload, FIRST)
    second = receive(payload, SECOND)
    beside = receive(payload, PARTNER)

    total, left, corner, positions, trace = call(
        z, functools.partial(own_body, z), [tiles, columns], [ANY, SMEM],
        [
            sums, shape((z.span, z.wide), dtype), shape((z.span // 2, z.span), dtype),
            shape((z.rows, z.slots), jnp.int32), line,
        ],
        [ANY, ANY, ANY, SMEM, VMEM],
        [
            pltpu.VMEM(tiles.shape, dtype), dense, total_buffer, pltpu.VMEM(tiles.shape, jnp.float32),
            DMA, DMA, DMA, DMA((z.rows,)),
        ],
        1, WHOLE_VMEM,
    )
    corner = receive(corner, PARTNER, (0, 3))

    def near(names, arrays, total, trace, final=False):
        extra = [shape((z.span, 2 * z.span), dtype)] * final
        return call(
            z, functools.partial(near_body, z, names, final),
            [left, positions, total, trace] + arrays,
            [ANY, SMEM, ANY, VMEM] + [ANY] * len(arrays),
            [sums, line] + extra,
            [ANY, VMEM] + [ANY] * final,
            [
                dense, pltpu.VMEM((2,) + payload_shape, dtype),
                pltpu.VMEM((len(names), z.span, z.wide), dtype), total_buffer,
                pltpu.VMEM(tiles.shape, jnp.float32), *places,
                DMA, DMA((2,)), DMA, DMA((2,)), DMA((2,)), DMA((z.rows,)),
            ],
            len(names), VMEM_LIMIT if final else WHOLE_VMEM,
        )

    total, trace = near(("beside",), [beside], total, trace)
    first, second, corner, total, trace = lax.optimization_barrier((first, second, corner, total, trace))
    relay = receive(first, RELAY_FROM)
    device = lax.axis_index(AXES)
    kind = device % 4

    def nearby(first, second, corner, total, trace):
        use_first = (kind == 0) | (kind == 3)
        mixed = receive(jnp.where(use_first, first, second), PARTNER)
        corner = receive(corner, (0, -2, 2, 0), (LOWER, UPPER))
        total, trace, relay_left = near(("first", "second", "mixed"), [first, second, mixed], total, trace, True)
        trace = call(
            z, functools.partial(corner_body, z), [left, corner, trace], [ANY, VMEM, VMEM], line, VMEM,
            [pltpu.VMEM((z.span, z.span // 2), dtype), DMA], 0,
        )
        return total, trace, relay_left

    def nothing(first, second, corner, total, trace):
        return jnp.zeros_like(total), jnp.zeros_like(trace), jnp.zeros((z.span, 2 * z.span), dtype)

    total, trace, relay_left = lax.cond(
        device < devices, nearby, nothing, first, second, corner, total, trace
    )
    assert devices & (devices - 1) == 0
    steps = [1 << bit for bit in range(devices.bit_length() - 1)]
    trace = trace + fetch(trace, steps[0])
    for index in range(3, len(steps), 2):
        trace = round_of(trace, steps[index:index + 2])
    relay, total, trace = lax.optimization_barrier((relay, total, trace))
    relay_beside = receive(relay, PARTNER)
    others = [fetch(trace, step) for step in (steps[1], steps[2], steps[1] + steps[2])]
    square = call(
        z, functools.partial(last_body, z), [relay_left, positions, total, relay, relay_beside],
        [ANY, SMEM, ANY, VMEM, VMEM],
        [shape(tiles.shape, dtype)],
        [ANY],
        [
            pltpu.VMEM((z.span, 2 * z.span), dtype),
            pltpu.VMEM((2 * z.span, z.wide), dtype), total_buffer,
            pltpu.VMEM(tiles.shape, dtype), pltpu.VMEM(tiles.shape, jnp.float32), *places,
            DMA, DMA, DMA((2,)), DMA((z.rows,)),
        ],
        2, 44 * 1024 * 1024,
    )[0]
    square, trace, others = lax.optimization_barrier((square, trace, others))
    return square, jnp.sum((trace + others[0]) + (others[1] + others[2])) / (z.all_rows * z.block)


def solution(mesh):
    return jax.shard_map(
        shards,
        mesh=mesh,
        in_specs=(P(AXES, None, None, None), P(AXES, None)),
        out_specs=(P(AXES, None, None, None), P()),
        check_vma=False,
    )
```

```python
import functools

import jax
import jax.numpy as jnp
from jax import lax
from jax.experimental import pallas as pl
from jax.experimental.pallas import tpu as pltpu
from jax.sharding import PartitionSpec as P

REACH = 12
AXES = ("blk", "grp")
VMEM_LIMIT = 42 * 1024 * 1024
WHOLE_VMEM = 62 * 1024 * 1024
EMPTY = 64

FIRST = (2, 3, -3, -2)
SECOND = (-3, 2, -2, 3)
RELAY_FROM = (2, -5, 5, -2)
PARTNER = (1, -1, 1, -1)
RELAY = tuple(RELAY_FROM[m] + FIRST[(m + RELAY_FROM[m]) % 4] for m in range(4))


def across(table):
    return tuple(PARTNER[m] + table[m ^ 1] for m in range(4))


USE_SECOND = tuple(int(abs(offset) > 3) for offset in across(FIRST))
MIXED = tuple(
    second if use else first
    for first, second, use in zip(across(FIRST), across(SECOND), USE_SECOND)
)
OFFSETS = {
    "beside": PARTNER,
    "first": FIRST,
    "second": SECOND,
    "mixed": MIXED,
    "relay": RELAY,
    "relay_beside": across(RELAY),
}
COUNTS = {"beside": (2, 0, 2, 0), "first": (2, 0, 0, 2), "second": (2, 0, 0, 2), "mixed": (0, 0, 2, 2)}
OUTSIDE = {("first", "mixed"): (0, 2, 2, 0), ("first", "second"): (0, 2, 0, 0)}
LOWER, UPPER = 2, 1


def receive(shard, offsets, kinds=range(4)):
    size = lax.axis_size(AXES)
    pairs = [((d + offsets[d % 4]) % size, d) for d in range(size) if d % 4 in kinds]
    return lax.ppermute(shard, AXES, pairs)


def fetch(value, step):
    return lax.ppermute(value, AXES, [(d, d ^ step) for d in range(lax.axis_size(AXES))])


def round_of(value, steps):
    if len(steps) == 1:
        return value + fetch(value, steps[0])
    one, other = steps
    return (value + fetch(value, one)) + (fetch(value, other) + fetch(value, one + other))


def pick(table, kind):
    value = jnp.int32(table[3])
    for m in range(3):
        value = jnp.where(kind == m, jnp.int32(table[m]), value)
    return value


def aligned(index, unit):
    return pl.multiple_of(index * unit, unit)


class Sizes:
    def __init__(self, shape, devices):
        self.rows, self.slots, self.block, _ = shape
        self.hops = (REACH + self.rows - 1) // self.rows
        self.chunks = 2 * self.hops + 1
        self.window = self.chunks * self.rows
        self.span = self.rows * self.block
        self.wide = (self.window + 1) * self.block
        self.all_rows = self.rows * devices

    def start(self, device):
        start = (device - self.hops) * self.rows
        return jnp.where(start < 0, start + self.all_rows, start)

    def position(self, column, start):
        place = column - start
        place = jnp.where(place < 0, place + self.all_rows, place)
        place = jnp.where(column < 0, self.window, place)
        return jnp.minimum(place, self.window)


def scatter(z, dense, top, source, place):
    for r in range(z.rows):
        def one(u, carry):
            column = pl.ds(aligned(place(r, u), z.block), z.block)
            dense[top + r * z.block:top + (r + 1) * z.block, column] = source[r * z.slots + u]
            return carry
        lax.fori_loop(0, z.slots, one, 0, unroll=10)


def decode(z, offsets, spot, vector, scalars, sem):
    value = offsets[0:16, :].astype(jnp.float32).astype(jnp.int32)
    value = value + spot * z.rows + lax.broadcasted_iota(jnp.int32, value.shape, 0)
    vector[...] = jnp.where((value < 0) | (value > z.window), z.window, value)
    copy = pltpu.make_async_copy(vector, scalars, sem)
    copy.start()
    return copy


def pack_body(z, tiles, columns, out, stage, padded, offsets, in_sems, out_sems):
    copies = []
    for r in range(z.rows):
        rows = pl.ds(r * z.slots, z.slots)
        copies.append((
            pltpu.make_async_copy(tiles.at[r], stage.at[rows], in_sems.at[r]),
            pltpu.make_async_copy(stage.at[rows], out.at[rows], out_sems.at[r]),
        ))
    for copy, _ in copies:
        copy.start()
    padded[...] = jnp.full(padded.shape, -1, jnp.int32)
    padded[:z.rows, :z.slots] = columns[...]
    column = padded[...]
    row = lax.axis_index(AXES) * z.rows + lax.broadcasted_iota(jnp.int32, column.shape, 0)
    offset = column - row
    offset = jnp.where(offset > z.all_rows // 2, offset - z.all_rows, offset)
    offset = jnp.where(offset < -(z.all_rows // 2), offset + z.all_rows, offset)
    offset = jnp.where(column < 0, EMPTY, offset)
    offsets[...] = jnp.zeros_like(offsets)
    offsets[0:16, :] = offset.astype(jnp.float32).astype(offsets.dtype)
    last = pltpu.make_async_copy(offsets, out.at[z.rows * z.slots], out_sems.at[z.rows])
    last.start()
    for load, store in copies:
        load.wait()
        store.start()
    for _, store in copies:
        store.wait()
    last.wait()


def emit(z, total, positions, stage, out, sems, prev=None):
    for r in range(z.rows):
        def one(s, carry):
            value = total[r * z.block:(r + 1) * z.block, pl.ds(aligned(positions[r, s], z.block), z.block)]
            if prev is not None:
                value = value + prev[r, s]
            stage[r, s] = value.astype(stage.dtype)
            return carry
        lax.fori_loop(0, z.slots, one, 0, unroll=10)
        pltpu.make_async_copy(stage.at[r], out.at[r], sems.at[r]).start()
    for r in range(z.rows):
        pltpu.make_async_copy(stage.at[r], out.at[r], sems.at[r]).wait()


def add_trace(trace, weight, one, other):
    value = jnp.dot(one, other, preferred_element_type=jnp.float32)
    on = lax.broadcasted_iota(jnp.int32, value.shape, 0) == lax.broadcasted_iota(jnp.int32, value.shape, 1)
    diagonal = jnp.sum(jnp.where(on, value, 0.0), axis=0, keepdims=True)
    trace[:, :value.shape[1]] += weight.astype(jnp.float32) * diagonal


def own_body(z, own, columns, out, left_out, corner_out, positions, trace, stage, left, total, out_stage,
             in_sem, left_sem, corner_sem, out_sems):
    device = lax.axis_index(AXES)
    kind = device % 4
    copy = pltpu.make_async_copy(own, stage, in_sem)
    copy.start()
    left[...] = jnp.zeros_like(left)
    total[:, z.window * z.block:] = jnp.zeros((z.span, z.block), jnp.float32)
    copy.wait()
    start = z.start(device)
    for r in range(z.rows):
        def place(u, carry):
            column = z.position(columns[r, u], start)
            positions[r, u] = column
            left[r * z.block:(r + 1) * z.block, pl.ds(aligned(column, z.block), z.block)] = stage[r, u]
            return carry
        lax.fori_loop(0, z.slots, place, 0, unroll=10)
    left_copy = pltpu.make_async_copy(left, left_out, left_sem)
    left_copy.start()
    half = z.span // 2

    def corner(start):
        def go(rows, cols):
            copy = pltpu.make_async_copy(left.at[rows, cols], corner_out, corner_sem)
            copy.start() if start else copy.wait()
        pl.when(kind == UPPER)(lambda: go(pl.ds(0, half), pl.ds(0, z.span)))
        pl.when(kind != UPPER)(
            lambda: go(pl.ds(half, half), pl.ds((z.chunks - 1) * z.span, z.span))
        )

    corner(True)
    middle = slice(z.hops * z.span, (z.hops + 1) * z.span)

    def multiply(n, carry):
        cols = pl.ds(aligned(n, z.span), z.span)
        total[:, cols] = jnp.dot(left[:, middle], left[:, cols], preferred_element_type=jnp.float32)
        return carry

    lax.fori_loop(0, z.chunks, multiply, 0)
    trace[...] = jnp.zeros_like(trace)
    add_trace(trace, jnp.float32(1), left[:, middle], left[:, middle])
    emit(z, total, positions, out_stage, out, out_sems)
    corner(False)
    left_copy.wait()


def near_body(z, names, final, left_in, positions, prev, trace_in, *refs):
    refs = list(refs)
    take = lambda count: [refs.pop(0) for _ in range(count)]
    sources = take(len(names))
    out, trace = take(2)
    relay_left = take(1)[0] if final else None
    left, stage, right, total, sums, vector, scalars = take(7)
    left_sem, in_sem, prev_sem, place_sem, relay_sem, out_sems = take(6)
    device = lax.axis_index(AXES)
    kind = device % 4
    place = {name: pick(table, kind) + z.hops for name, table in OFFSETS.items()}

    def chunk(n):
        return pl.ds(aligned(n, z.span), z.span)

    def fetch(index):
        return pltpu.make_async_copy(sources[index], stage.at[index % 2], in_sem.at[index % 2])

    fetch(0).start()
    left_copy = pltpu.make_async_copy(left_in, left, left_sem)
    left_copy.start()
    prev_copy = pltpu.make_async_copy(prev, sums, prev_sem)
    total[...] = jnp.zeros_like(total)
    trace[...] = trace_in[...]
    relay_copies = []

    def hand_on():
        for index, name in enumerate(("relay", "relay_beside") if final else ()):
            copy = pltpu.make_async_copy(
                left.at[:, chunk(place[name])], relay_left.at[:, pl.ds(index * z.span, z.span)],
                relay_sem.at[index],
            )
            copy.start()
            relay_copies.append(copy)

    decodings = []

    def begin_decode(index):
        slot = index % 2
        fetch(index).wait()
        decodings.append(decode(
            z, stage.at[slot, z.rows * z.slots], place[names[index]], vector.at[slot], scalars.at[slot],
            place_sem.at[slot],
        ))

    begin_decode(0)
    if len(names) > 1:
        fetch(1).start()
    dense_of = {}
    for index, name in enumerate(names):
        dense = right.at[index]
        dense_of[name] = dense
        spot = place[name]
        slot = index % 2
        dense[...] = jnp.zeros_like(dense)
        decodings[index].wait()
        scatter(z, dense, 0, stage.at[slot], lambda r, u: scalars[slot, r, u])
        if index == 0:
            left_copy.wait()
            prev_copy.start()
            hand_on()
        if index + 2 < len(names):
            fetch(index + 2).start()
        if index + 1 < len(names):
            begin_decode(index + 1)

        def multiply(n, carry):
            total[:, chunk(n)] += jnp.dot(
                left[:, chunk(spot)], dense[:, chunk(n)], preferred_element_type=jnp.float32
            )
            return carry

        lax.fori_loop(jnp.maximum(0, spot - z.hops), jnp.minimum(z.chunks, spot + z.hops + 1), multiply, 0)
        weight = pick(COUNTS[name], kind)
        pl.when(weight != 0)(
            lambda: add_trace(trace, weight, left[:, chunk(spot)], dense[:, chunk(z.hops)])
        )
    for (one, other), table in OUTSIDE.items() if final else ():
        weight = pick(table, kind)
        pl.when(weight != 0)(lambda: add_trace(
            trace, weight, dense_of[one][:, chunk(place[other])], dense_of[other][:, chunk(place[one])]
        ))
    prev_copy.wait()
    emit(z, total, positions, sums, out, out_sems, sums)
    for copy in relay_copies:
        copy.wait()


def corner_body(z, left, corner, trace_in, trace, rows, sem):
    kind = lax.axis_index(AXES) % 4
    half = z.span // 2
    end = (z.chunks - 1) * z.span
    trace[...] = trace_in[...]

    @pl.when(kind == UPPER)
    def _():
        copy = pltpu.make_async_copy(left.at[:, pl.ds(half, half)], rows, sem)
        copy.start()
        copy.wait()
        add_trace(trace, jnp.float32(2), rows[...], corner[...])

    @pl.when(kind == LOWER)
    def _():
        copy = pltpu.make_async_copy(left.at[pl.ds(0, half), pl.ds(end, half)], rows.at[pl.ds(0, half)], sem)
        copy.start()
        copy.wait()
        add_trace(trace, jnp.float32(2), rows[:half], corner[:, :half])


def last_body(z, left_in, positions, prev, source_a, source_b, out, left, right, total, out_stage,
              prev_stage, vector, scalars, left_sem, prev_sem, place_sem, out_sems):
    kind = lax.axis_index(AXES) % 4
    copies = [
        pltpu.make_async_copy(left_in, left, left_sem),
        pltpu.make_async_copy(prev, prev_stage, prev_sem),
    ]
    for copy in copies:
        copy.start()
    places = [pick(OFFSETS[name], kind) + z.hops for name in ("relay", "relay_beside")]
    low = jnp.maximum(0, jnp.minimum(*places) - z.hops)
    high = jnp.minimum(z.chunks, jnp.maximum(*places) + z.hops + 1)

    def chunk(n):
        return pl.ds(aligned(n, z.span), z.span)

    def clear_total(n, carry):
        total[:, chunk(n)] = jnp.zeros((z.span, z.span), jnp.float32)
        return carry

    def clear_right(n, carry):
        right[:, chunk(n)] = jnp.zeros((2 * z.span, z.span), right.dtype)
        return carry

    lax.fori_loop(0, low, clear_total, 0)
    lax.fori_loop(high, z.chunks, clear_total, 0)
    total[:, z.window * z.block:] = jnp.zeros((z.span, z.block), jnp.float32)
    decodings = []
    for index in range(2):
        decodings.append(decode(
            z, (source_a, source_b)[index].at[z.rows * z.slots], places[index], vector.at[index], scalars.at[index],
            place_sem.at[index],
        ))
    lax.fori_loop(low, high, clear_right, 0)
    for index in range(2):
        decodings[index].wait()
        scatter(z, right, index * z.span, (source_a, source_b)[index], lambda r, u: scalars[index, r, u])
    copies[0].wait()

    def multiply(n, carry):
        total[:, chunk(n)] = jnp.dot(left[...], right[:, chunk(n)], preferred_element_type=jnp.float32)
        return carry

    lax.fori_loop(low, high, multiply, 0)
    copies[1].wait()
    emit(z, total, positions, out_stage, out, out_sems, prev_stage)


ANY = pl.BlockSpec(memory_space=pl.ANY)
SMEM = pl.BlockSpec(memory_space=pltpu.SMEM)
VMEM = pl.BlockSpec(memory_space=pltpu.VMEM)
DMA = pltpu.SemaphoreType.DMA


def call(z, kernel, operands, in_specs, out_shape, out_specs, scratch, pieces, limit=VMEM_LIMIT):
    return pl.pallas_call(
        kernel,
        out_shape=out_shape,
        in_specs=in_specs,
        out_specs=out_specs,
        scratch_shapes=scratch,
        compiler_params=pltpu.CompilerParams(vmem_limit_bytes=limit),
        cost_estimate=pl.CostEstimate(
            flops=2 * z.span * z.span * z.window * z.block * pieces,
            bytes_accessed=2 * z.span * z.slots * z.block * (pieces + 4),
            transcendentals=0,
        ),
    )(*operands)


def shards(tiles, columns):
    devices = lax.axis_size(AXES)
    z = Sizes(tiles.shape, devices)
    assert z.hops == 3 and z.rows == 4 and devices % 4 == 0 and devices > 8
    dtype = tiles.dtype
    shape = jax.ShapeDtypeStruct
    sums = shape(tiles.shape, jnp.float32)
    line = shape((1, z.span), jnp.float32)
    dense = pltpu.VMEM((z.span, z.wide), dtype)
    total_buffer = pltpu.VMEM((z.span, z.wide), jnp.float32)

    payload_shape = (z.rows * z.slots + 1, z.block, z.block)
    places = [pltpu.VMEM((2, 16, z.block), jnp.int32), pltpu.SMEM((2, 16, z.block), jnp.int32)]

    payload = call(
        z, functools.partial(pack_body, z), [tiles, columns], [ANY, VMEM],
        shape(payload_shape, dtype), ANY,
        [
            pltpu.VMEM((z.rows * z.slots, z.block, z.block), dtype), pltpu.VMEM((16, z.block), jnp.int32),
            pltpu.VMEM((z.block, z.block), dtype), DMA((z.rows,)), DMA((z.rows + 1,)),
        ],
        0, WHOLE_VMEM,
    )
    first = receive(payload, FIRST)
    second = receive(payload, SECOND)
    beside = receive(payload, PARTNER)

    total, left, corner, positions, trace = call(
        z, functools.partial(own_body, z), [tiles, columns], [ANY, SMEM],
        [
            sums, shape((z.span, z.wide), dtype), shape((z.span // 2, z.span), dtype),
            shape((z.rows, z.slots), jnp.int32), line,
        ],
        [ANY, ANY, ANY, SMEM, VMEM],
        [
            pltpu.VMEM(tiles.shape, dtype), dense, total_buffer, pltpu.VMEM(tiles.shape, jnp.float32),
            DMA, DMA, DMA, DMA((z.rows,)),
        ],
        1, WHOLE_VMEM,
    )
    corner = receive(corner, PARTNER, (0, 3))

    def near(names, arrays, total, trace, final=False):
        extra = [shape((z.span, 2 * z.span), dtype)] * final
        return call(
            z, functools.partial(near_body, z, names, final),
            [left, positions, total, trace] + arrays,
            [ANY, SMEM, ANY, VMEM] + [ANY] * len(arrays),
            [sums, line] + extra,
            [ANY, VMEM] + [ANY] * final,
            [
                dense, pltpu.VMEM((2,) + payload_shape, dtype),
                pltpu.VMEM((len(names), z.span, z.wide), dtype), total_buffer,
                pltpu.VMEM(tiles.shape, jnp.float32), *places,
                DMA, DMA((2,)), DMA, DMA((2,)), DMA((2,)), DMA((z.rows,)),
            ],
            len(names), VMEM_LIMIT if final else WHOLE_VMEM,
        )

    total, trace = near(("beside",), [beside], total, trace)
    first, second, corner, total, trace = lax.optimization_barrier((first, second, corner, total, trace))
    relay = receive(first, RELAY_FROM)
    device = lax.axis_index(AXES)
    kind = device % 4

    def nearby(first, second, corner, total, trace):
        use_first = (kind == 0) | (kind == 3)
        mixed = receive(jnp.where(use_first, first, second), PARTNER)
        mixed, corner = lax.optimization_barrier((mixed, corner))
        corner = receive(corner, (0, -2, 2, 0), (LOWER, UPPER))
        total, trace, relay_left = near(("first", "second", "mixed"), [first, second, mixed], total, trace, True)
        trace = call(
            z, functools.partial(corner_body, z), [left, corner, trace], [ANY, VMEM, VMEM], line, VMEM,
            [pltpu.VMEM((z.span, z.span // 2), dtype), DMA], 0,
        )
        return total, trace, relay_left

    def nothing(first, second, corner, total, trace):
        return jnp.zeros_like(total), jnp.zeros_like(trace), jnp.zeros((z.span, 2 * z.span), dtype)

    total, trace, relay_left = lax.cond(
        device < devices, nearby, nothing, first, second, corner, total, trace
    )
    assert devices & (devices - 1) == 0
    steps = [1 << bit for bit in range(devices.bit_length() - 1)]
    trace = trace + fetch(trace, steps[0])
    for index in range(3, len(steps), 2):
        trace = round_of(trace, steps[index:index + 2])
    relay, total, trace = lax.optimization_barrier((relay, total, trace))
    relay_beside = receive(relay, PARTNER)
    others = [fetch(trace, step) for step in (steps[1], steps[2], steps[1] + steps[2])]
    square = call(
        z, functools.partial(last_body, z), [relay_left, positions, total, relay, relay_beside],
        [ANY, SMEM, ANY, VMEM, VMEM],
        [shape(tiles.shape, dtype)],
        [ANY],
        [
            pltpu.VMEM((z.span, 2 * z.span), dtype),
            pltpu.VMEM((2 * z.span, z.wide), dtype), total_buffer,
            pltpu.VMEM(tiles.shape, dtype), pltpu.VMEM(tiles.shape, jnp.float32), *places,
            DMA, DMA, DMA((2,)), DMA((z.rows,)),
        ],
        2, 44 * 1024 * 1024,
    )[0]
    square, trace, others = lax.optimization_barrier((square, trace, others))
    return square, jnp.sum((trace + others[0]) + (others[1] + others[2])) / (z.all_rows * z.block)


def solution(mesh):
    return jax.shard_map(
        shards,
        mesh=mesh,
        in_specs=(P(AXES, None, None, None), P(AXES, None)),
        out_specs=(P(AXES, None, None, None), P()),
        check_vma=False,
    )
```

```python
import functools

import jax
import jax.numpy as jnp
from jax import lax
from jax.experimental import pallas as pl
from jax.experimental.pallas import tpu as pltpu
from jax.sharding import PartitionSpec as P

REACH = 12
AXES = ("blk", "grp")
VMEM_LIMIT = 42 * 1024 * 1024
WHOLE_VMEM = 62 * 1024 * 1024
EMPTY = 64

FIRST = (2, 3, -3, -2)
SECOND = (-3, 2, -2, 3)
RELAY_FROM = (2, -5, 5, -2)
PARTNER = (1, -1, 1, -1)
RELAY = tuple(RELAY_FROM[m] + FIRST[(m + RELAY_FROM[m]) % 4] for m in range(4))


def across(table):
    return tuple(PARTNER[m] + table[m ^ 1] for m in range(4))


USE_SECOND = tuple(int(abs(offset) > 3) for offset in across(FIRST))
MIXED = tuple(
    second if use else first
    for first, second, use in zip(across(FIRST), across(SECOND), USE_SECOND)
)
OFFSETS = {
    "beside": PARTNER,
    "first": FIRST,
    "second": SECOND,
    "mixed": MIXED,
    "relay": RELAY,
    "relay_beside": across(RELAY),
}
COUNTS = {"beside": (2, 0, 2, 0), "first": (2, 0, 0, 2), "second": (2, 0, 0, 2), "mixed": (0, 0, 2, 2)}
OUTSIDE = {("first", "mixed"): (0, 2, 2, 0), ("first", "second"): (0, 2, 0, 0)}
LOWER, UPPER = 2, 1


def receive(shard, offsets, kinds=range(4)):
    size = lax.axis_size(AXES)
    pairs = [((d + offsets[d % 4]) % size, d) for d in range(size) if d % 4 in kinds]
    return lax.ppermute(shard, AXES, pairs)


def fetch(value, step):
    return lax.ppermute(value, AXES, [(d, d ^ step) for d in range(lax.axis_size(AXES))])


def round_of(value, steps):
    if len(steps) == 1:
        return value + fetch(value, steps[0])
    one, other = steps
    return (value + fetch(value, one)) + (fetch(value, other) + fetch(value, one + other))


def pick(table, kind):
    value = jnp.int32(table[3])
    for m in range(3):
        value = jnp.where(kind == m, jnp.int32(table[m]), value)
    return value


def aligned(index, unit):
    return pl.multiple_of(index * unit, unit)


class Sizes:
    def __init__(self, shape, devices):
        self.rows, self.slots, self.block, _ = shape
        self.hops = (REACH + self.rows - 1) // self.rows
        self.chunks = 2 * self.hops + 1
        self.window = self.chunks * self.rows
        self.span = self.rows * self.block
        self.wide = (self.window + 1) * self.block
        self.all_rows = self.rows * devices

    def start(self, device):
        start = (device - self.hops) * self.rows
        return jnp.where(start < 0, start + self.all_rows, start)

    def position(self, column, start):
        place = column - start
        place = jnp.where(place < 0, place + self.all_rows, place)
        place = jnp.where(column < 0, self.window, place)
        return jnp.minimum(place, self.window)


def scatter(z, dense, top, source, place):
    for r in range(z.rows):
        def one(u, carry):
            column = pl.ds(aligned(place(r, u), z.block), z.block)
            dense[top + r * z.block:top + (r + 1) * z.block, column] = source[r * z.slots + u]
            return carry
        lax.fori_loop(0, z.slots, one, 0, unroll=10)


def decode(z, offsets, spot, vector, scalars, sem):
    value = offsets[0:16, :].astype(jnp.float32).astype(jnp.int32)
    value = value + spot * z.rows + lax.broadcasted_iota(jnp.int32, value.shape, 0)
    vector[...] = jnp.where((value < 0) | (value > z.window), z.window, value)
    copy = pltpu.make_async_copy(vector, scalars, sem)
    copy.start()
    return copy


def pack_body(z, tiles, columns, out, stage, padded, offsets, in_sems, out_sems):
    copies = []
    half = z.slots // 2
    for piece in range(2 * z.rows):
        source = tiles.at[piece // 2, pl.ds(piece % 2 * half, half)]
        rows = pl.ds(piece * half, half)
        copies.append((
            pltpu.make_async_copy(source, stage.at[rows], in_sems.at[piece]),
            pltpu.make_async_copy(stage.at[rows], out.at[rows], out_sems.at[piece]),
        ))
    for copy, _ in copies:
        copy.start()
    padded[...] = jnp.full(padded.shape, -1, jnp.int32)
    padded[:z.rows, :z.slots] = columns[...]
    column = padded[...]
    row = lax.axis_index(AXES) * z.rows + lax.broadcasted_iota(jnp.int32, column.shape, 0)
    offset = column - row
    offset = jnp.where(offset > z.all_rows // 2, offset - z.all_rows, offset)
    offset = jnp.where(offset < -(z.all_rows // 2), offset + z.all_rows, offset)
    offset = jnp.where(column < 0, EMPTY, offset)
    offsets[...] = jnp.zeros_like(offsets)
    offsets[0:16, :] = offset.astype(jnp.float32).astype(offsets.dtype)
    last = pltpu.make_async_copy(offsets, out.at[z.rows * z.slots], out_sems.at[2 * z.rows])
    last.start()
    for load, store in copies:
        load.wait()
        store.start()
    for _, store in copies:
        store.wait()
    last.wait()


def emit(z, total, positions, stage, out, sems, prev=None):
    for r in range(z.rows):
        def one(s, carry):
            value = total[r * z.block:(r + 1) * z.block, pl.ds(aligned(positions[r, s], z.block), z.block)]
            if prev is not None:
                value = value + prev[r, s]
            stage[r, s] = value.astype(stage.dtype)
            return carry
        lax.fori_loop(0, z.slots, one, 0, unroll=10)
        pltpu.make_async_copy(stage.at[r], out.at[r], sems.at[r]).start()
    for r in range(z.rows):
        pltpu.make_async_copy(stage.at[r], out.at[r], sems.at[r]).wait()


def add_trace(trace, weight, one, other):
    value = jnp.dot(one, other, preferred_element_type=jnp.float32)
    on = lax.broadcasted_iota(jnp.int32, value.shape, 0) == lax.broadcasted_iota(jnp.int32, value.shape, 1)
    diagonal = jnp.sum(jnp.where(on, value, 0.0), axis=0, keepdims=True)
    trace[:, :value.shape[1]] += weight.astype(jnp.float32) * diagonal


def own_body(z, own, columns, out, left_out, corner_out, positions, trace, stage, left, total, out_stage,
             in_sem, left_sem, corner_sem, out_sems):
    device = lax.axis_index(AXES)
    kind = device % 4
    copy = pltpu.make_async_copy(own, stage, in_sem)
    copy.start()
    left[...] = jnp.zeros_like(left)
    total[:, z.window * z.block:] = jnp.zeros((z.span, z.block), jnp.float32)
    copy.wait()
    start = z.start(device)
    for r in range(z.rows):
        def place(u, carry):
            column = z.position(columns[r, u], start)
            positions[r, u] = column
            left[r * z.block:(r + 1) * z.block, pl.ds(aligned(column, z.block), z.block)] = stage[r, u]
            return carry
        lax.fori_loop(0, z.slots, place, 0, unroll=10)
    left_copy = pltpu.make_async_copy(left, left_out, left_sem)
    left_copy.start()
    half = z.span // 2

    def corner(start):
        def go(rows, cols):
            copy = pltpu.make_async_copy(left.at[rows, cols], corner_out, corner_sem)
            copy.start() if start else copy.wait()
        pl.when(kind == UPPER)(lambda: go(pl.ds(0, half), pl.ds(0, z.span)))
        pl.when(kind != UPPER)(
            lambda: go(pl.ds(half, half), pl.ds((z.chunks - 1) * z.span, z.span))
        )

    corner(True)
    middle = slice(z.hops * z.span, (z.hops + 1) * z.span)

    def multiply(n, carry):
        cols = pl.ds(aligned(n, z.span), z.span)
        total[:, cols] = jnp.dot(left[:, middle], left[:, cols], preferred_element_type=jnp.float32)
        return carry

    lax.fori_loop(0, z.chunks, multiply, 0)
    trace[...] = jnp.zeros_like(trace)
    add_trace(trace, jnp.float32(1), left[:, middle], left[:, middle])
    emit(z, total, positions, out_stage, out, out_sems)
    corner(False)
    left_copy.wait()


def near_body(z, names, final, left_in, positions, prev, trace_in, *refs):
    refs = list(refs)
    take = lambda count: [refs.pop(0) for _ in range(count)]
    sources = take(len(names))
    out, trace = take(2)
    relay_left = take(1)[0] if final else None
    left, stage, right, total, sums, vector, scalars = take(7)
    left_sem, in_sem, prev_sem, place_sem, relay_sem, out_sems = take(6)
    device = lax.axis_index(AXES)
    kind = device % 4
    place = {name: pick(table, kind) + z.hops for name, table in OFFSETS.items()}

    def chunk(n):
        return pl.ds(aligned(n, z.span), z.span)

    def fetch(index):
        return pltpu.make_async_copy(sources[index], stage.at[index % 2], in_sem.at[index % 2])

    fetch(0).start()
    left_copy = pltpu.make_async_copy(left_in, left, left_sem)
    left_copy.start()
    prev_copy = pltpu.make_async_copy(prev, sums, prev_sem)
    total[...] = jnp.zeros_like(total)
    trace[...] = trace_in[...]
    relay_copies = []

    def hand_on():
        for index, name in enumerate(("relay", "relay_beside") if final else ()):
            copy = pltpu.make_async_copy(
                left.at[:, chunk(place[name])], relay_left.at[:, pl.ds(index * z.span, z.span)],
                relay_sem.at[index],
            )
            copy.start()
            relay_copies.append(copy)

    decodings = []

    def begin_decode(index):
        slot = index % 2
        fetch(index).wait()
        decodings.append(decode(
            z, stage.at[slot, z.rows * z.slots], place[names[index]], vector.at[slot], scalars.at[slot],
            place_sem.at[slot],
        ))

    begin_decode(0)
    if len(names) > 1:
        fetch(1).start()
    dense_of = {}
    for index, name in enumerate(names):
        dense = right.at[index]
        dense_of[name] = dense
        spot = place[name]
        slot = index % 2
        dense[...] = jnp.zeros_like(dense)
        decodings[index].wait()
        scatter(z, dense, 0, stage.at[slot], lambda r, u: scalars[slot, r, u])
        if index == 0:
            left_copy.wait()
            prev_copy.start()
            hand_on()
        if index + 2 < len(names):
            fetch(index + 2).start()
        if index + 1 < len(names):
            begin_decode(index + 1)

        def multiply(n, carry):
            total[:, chunk(n)] += jnp.dot(
                left[:, chunk(spot)], dense[:, chunk(n)], preferred_element_type=jnp.float32
            )
            return carry

        lax.fori_loop(jnp.maximum(0, spot - z.hops), jnp.minimum(z.chunks, spot + z.hops + 1), multiply, 0)
        weight = pick(COUNTS[name], kind)
        pl.when(weight != 0)(
            lambda: add_trace(trace, weight, left[:, chunk(spot)], dense[:, chunk(z.hops)])
        )
    for (one, other), table in OUTSIDE.items() if final else ():
        weight = pick(table, kind)
        pl.when(weight != 0)(lambda: add_trace(
            trace, weight, dense_of[one][:, chunk(place[other])], dense_of[other][:, chunk(place[one])]
        ))
    prev_copy.wait()
    emit(z, total, positions, sums, out, out_sems, sums)
    for copy in relay_copies:
        copy.wait()


def corner_body(z, left, corner, trace_in, trace, rows, sem):
    kind = lax.axis_index(AXES) % 4
    half = z.span // 2
    end = (z.chunks - 1) * z.span
    trace[...] = trace_in[...]

    @pl.when(kind == UPPER)
    def _():
        copy = pltpu.make_async_copy(left.at[:, pl.ds(half, half)], rows, sem)
        copy.start()
        copy.wait()
        add_trace(trace, jnp.float32(2), rows[...], corner[...])

    @pl.when(kind == LOWER)
    def _():
        copy = pltpu.make_async_copy(left.at[pl.ds(0, half), pl.ds(end, half)], rows.at[pl.ds(0, half)], sem)
        copy.start()
        copy.wait()
        add_trace(trace, jnp.float32(2), rows[:half], corner[:, :half])


def last_body(z, left_in, positions, prev, source_a, source_b, out, left, right, total, out_stage,
              prev_stage, vector, scalars, left_sem, prev_sem, place_sem, out_sems):
    kind = lax.axis_index(AXES) % 4
    copies = [
        pltpu.make_async_copy(left_in, left, left_sem),
        pltpu.make_async_copy(prev, prev_stage, prev_sem),
    ]
    places = [pick(OFFSETS[name], kind) + z.hops for name in ("relay", "relay_beside")]
    decodings = []
    for index in range(2):
        decodings.append(decode(
            z, (source_a, source_b)[index].at[z.rows * z.slots], places[index], vector.at[index], scalars.at[index],
            place_sem.at[index],
        ))
    for copy in copies:
        copy.start()
    low = jnp.maximum(0, jnp.minimum(*places) - z.hops)
    high = jnp.minimum(z.chunks, jnp.maximum(*places) + z.hops + 1)

    def chunk(n):
        return pl.ds(aligned(n, z.span), z.span)

    def clear_total(n, carry):
        total[:, chunk(n)] = jnp.zeros((z.span, z.span), jnp.float32)
        return carry

    def clear_right(n, carry):
        right[:, chunk(n)] = jnp.zeros((2 * z.span, z.span), right.dtype)
        return carry

    lax.fori_loop(0, low, clear_total, 0)
    lax.fori_loop(high, z.chunks, clear_total, 0)
    total[:, z.window * z.block:] = jnp.zeros((z.span, z.block), jnp.float32)
    lax.fori_loop(low, high, clear_right, 0)
    for index in range(2):
        decodings[index].wait()
        scatter(z, right, index * z.span, (source_a, source_b)[index], lambda r, u: scalars[index, r, u])
    copies[0].wait()

    def multiply(n, carry):
        total[:, chunk(n)] = jnp.dot(left[...], right[:, chunk(n)], preferred_element_type=jnp.float32)
        return carry

    lax.fori_loop(low, high, multiply, 0)
    copies[1].wait()
    emit(z, total, positions, out_stage, out, out_sems, prev_stage)


ANY = pl.BlockSpec(memory_space=pl.ANY)
SMEM = pl.BlockSpec(memory_space=pltpu.SMEM)
VMEM = pl.BlockSpec(memory_space=pltpu.VMEM)
DMA = pltpu.SemaphoreType.DMA


def call(z, kernel, operands, in_specs, out_shape, out_specs, scratch, pieces, limit=VMEM_LIMIT):
    return pl.pallas_call(
        kernel,
        out_shape=out_shape,
        in_specs=in_specs,
        out_specs=out_specs,
        scratch_shapes=scratch,
        compiler_params=pltpu.CompilerParams(vmem_limit_bytes=limit),
        cost_estimate=pl.CostEstimate(
            flops=2 * z.span * z.span * z.window * z.block * pieces,
            bytes_accessed=2 * z.span * z.slots * z.block * (pieces + 4),
            transcendentals=0,
        ),
    )(*operands)


def shards(tiles, columns):
    devices = lax.axis_size(AXES)
    z = Sizes(tiles.shape, devices)
    assert z.hops == 3 and z.rows == 4 and z.slots % 2 == 0 and devices % 4 == 0 and devices > 8
    dtype = tiles.dtype
    shape = jax.ShapeDtypeStruct
    sums = shape(tiles.shape, jnp.float32)
    line = shape((1, z.span), jnp.float32)
    dense = pltpu.VMEM((z.span, z.wide), dtype)
    total_buffer = pltpu.VMEM((z.span, z.wide), jnp.float32)

    payload_shape = (z.rows * z.slots + 1, z.block, z.block)
    places = [pltpu.VMEM((2, 16, z.block), jnp.int32), pltpu.SMEM((2, 16, z.block), jnp.int32)]

    payload = call(
        z, functools.partial(pack_body, z), [tiles, columns], [ANY, VMEM],
        shape(payload_shape, dtype), ANY,
        [
            pltpu.VMEM((z.rows * z.slots, z.block, z.block), dtype), pltpu.VMEM((16, z.block), jnp.int32),
            pltpu.VMEM((z.block, z.block), dtype), DMA((2 * z.rows,)), DMA((2 * z.rows + 1,)),
        ],
        0, WHOLE_VMEM,
    )
    first = receive(payload, FIRST)
    second = receive(payload, SECOND)
    beside = receive(payload, PARTNER)

    total, left, corner, positions, trace = call(
        z, functools.partial(own_body, z), [tiles, columns], [ANY, SMEM],
        [
            sums, shape((z.span, z.wide), dtype), shape((z.span // 2, z.span), dtype),
            shape((z.rows, z.slots), jnp.int32), line,
        ],
        [ANY, ANY, ANY, SMEM, VMEM],
        [
            pltpu.VMEM(tiles.shape, dtype), dense, total_buffer, pltpu.VMEM(tiles.shape, jnp.float32),
            DMA, DMA, DMA, DMA((z.rows,)),
        ],
        1, WHOLE_VMEM,
    )
    corner = receive(corner, PARTNER, (0, 3))

    def near(names, arrays, total, trace, final=False):
        extra = [shape((z.span, 2 * z.span), dtype)] * final
        return call(
            z, functools.partial(near_body, z, names, final),
            [left, positions, total, trace] + arrays,
            [ANY, SMEM, ANY, VMEM] + [ANY] * len(arrays),
            [sums, line] + extra,
            [ANY, VMEM] + [ANY] * final,
            [
                dense, pltpu.VMEM((2,) + payload_shape, dtype),
                pltpu.VMEM((len(names), z.span, z.wide), dtype), total_buffer,
                pltpu.VMEM(tiles.shape, jnp.float32), *places,
                DMA, DMA((2,)), DMA, DMA((2,)), DMA((2,)), DMA((z.rows,)),
            ],
            len(names), VMEM_LIMIT if final else WHOLE_VMEM,
        )

    total, trace = near(("beside",), [beside], total, trace)
    first, second, corner, total, trace = lax.optimization_barrier((first, second, corner, total, trace))
    relay = receive(first, RELAY_FROM)
    kind = lax.axis_index(AXES) % 4

    def nearby(first, second, corner, total, trace):
        use_first = (kind == 0) | (kind == 3)
        mixed = receive(jnp.where(use_first, first, second), PARTNER)
        corner = receive(corner, (0, -2, 2, 0), (LOWER, UPPER))
        total, trace, relay_left = near(("first", "second", "mixed"), [first, second, mixed], total, trace, True)
        trace = call(
            z, functools.partial(corner_body, z), [left, corner, trace], [ANY, VMEM, VMEM], line, VMEM,
            [pltpu.VMEM((z.span, z.span // 2), dtype), DMA], 0,
        )
        return total, trace, relay_left

    def nothing(first, second, corner, total, trace):
        return jnp.zeros_like(total), jnp.zeros_like(trace), jnp.zeros((z.span, 2 * z.span), dtype)

    total, trace, relay_left = lax.cond(
        positions[0, 0] >= 0, nearby, nothing, first, second, corner, total, trace
    )
    assert devices & (devices - 1) == 0
    steps = [1 << bit for bit in range(devices.bit_length() - 1)]
    trace = trace + fetch(trace, steps[0])
    for index in range(3, len(steps), 2):
        trace = round_of(trace, steps[index:index + 2])
    relay, total, trace = lax.optimization_barrier((relay, total, trace))
    relay_beside = receive(relay, PARTNER)
    others = [fetch(trace, step) for step in (steps[1], steps[2], steps[1] + steps[2])]
    square = call(
        z, functools.partial(last_body, z), [relay_left, positions, total, relay, relay_beside],
        [ANY, SMEM, ANY, VMEM, VMEM],
        [shape(tiles.shape, dtype)],
        [ANY],
        [
            pltpu.VMEM((z.span, 2 * z.span), dtype),
            pltpu.VMEM((2 * z.span, z.wide), dtype), total_buffer,
            pltpu.VMEM(tiles.shape, dtype), pltpu.VMEM(tiles.shape, jnp.float32), *places,
            DMA, DMA, DMA((2,)), DMA((z.rows,)),
        ],
        2, 44 * 1024 * 1024,
    )[0]
    square, trace, others = lax.optimization_barrier((square, trace, others))
    return square, jnp.sum((trace + others[0]) + (others[1] + others[2])) / (z.all_rows * z.block)


def solution(mesh):
    return jax.shard_map(
        shards,
        mesh=mesh,
        in_specs=(P(AXES, None, None, None), P(AXES, None)),
        out_specs=(P(AXES, None, None, None), P()),
        check_vma=False,
    )
```

```python
import functools

import jax
import jax.numpy as jnp
from jax import lax
from jax.experimental import pallas as pl
from jax.experimental.pallas import tpu as pltpu
from jax.sharding import PartitionSpec as P

REACH = 12
AXES = ("blk", "grp")
VMEM_LIMIT = 42 * 1024 * 1024
WHOLE_VMEM = 62 * 1024 * 1024
EMPTY = 64

FIRST = (2, 3, -3, -2)
SECOND = (-3, 2, -2, 3)
RELAY_FROM = (2, -5, 5, -2)
PARTNER = (1, -1, 1, -1)
RELAY = tuple(RELAY_FROM[m] + FIRST[(m + RELAY_FROM[m]) % 4] for m in range(4))


def across(table):
    return tuple(PARTNER[m] + table[m ^ 1] for m in range(4))


USE_SECOND = tuple(int(abs(offset) > 3) for offset in across(FIRST))
MIXED = tuple(
    second if use else first
    for first, second, use in zip(across(FIRST), across(SECOND), USE_SECOND)
)
OFFSETS = {
    "beside": PARTNER,
    "first": FIRST,
    "second": SECOND,
    "mixed": MIXED,
    "relay": RELAY,
    "relay_beside": across(RELAY),
}
COUNTS = {"beside": (2, 0, 2, 0), "first": (2, 0, 0, 2), "second": (2, 0, 0, 2), "mixed": (0, 0, 2, 2)}
OUTSIDE = {("first", "mixed"): (0, 2, 2, 0), ("first", "second"): (0, 2, 0, 0)}
LOWER, UPPER = 2, 1


def receive(shard, offsets, kinds=range(4)):
    size = lax.axis_size(AXES)
    pairs = [((d + offsets[d % 4]) % size, d) for d in range(size) if d % 4 in kinds]
    return lax.ppermute(shard, AXES, pairs)


def fetch(value, step):
    return lax.ppermute(value, AXES, [(d, d ^ step) for d in range(lax.axis_size(AXES))])


def round_of(value, steps):
    if len(steps) == 1:
        return value + fetch(value, steps[0])
    one, other = steps
    return (value + fetch(value, one)) + (fetch(value, other) + fetch(value, one + other))


def pick(table, kind):
    value = jnp.int32(table[3])
    for m in range(3):
        value = jnp.where(kind == m, jnp.int32(table[m]), value)
    return value


def aligned(index, unit):
    return pl.multiple_of(index * unit, unit)


class Sizes:
    def __init__(self, shape, devices):
        self.rows, self.slots, self.block, _ = shape
        self.hops = (REACH + self.rows - 1) // self.rows
        self.chunks = 2 * self.hops + 1
        self.window = self.chunks * self.rows
        self.span = self.rows * self.block
        self.wide = (self.window + 1) * self.block
        self.all_rows = self.rows * devices

    def start(self, device):
        start = (device - self.hops) * self.rows
        return jnp.where(start < 0, start + self.all_rows, start)

    def position(self, column, start):
        place = column - start
        place = jnp.where(place < 0, place + self.all_rows, place)
        place = jnp.where(column < 0, self.window, place)
        return jnp.minimum(place, self.window)


def scatter(z, dense, top, source, place):
    for r in range(z.rows):
        def one(u, carry):
            column = pl.ds(aligned(place(r, u), z.block), z.block)
            dense[top + r * z.block:top + (r + 1) * z.block, column] = source[r * z.slots + u]
            return carry
        lax.fori_loop(0, z.slots, one, 0, unroll=10)


def decode(z, offsets, spot, vector, scalars, sem):
    value = offsets[0:16, :].astype(jnp.float32).astype(jnp.int32)
    value = value + spot * z.rows + lax.broadcasted_iota(jnp.int32, value.shape, 0)
    vector[...] = jnp.where((value < 0) | (value > z.window), z.window, value)
    copy = pltpu.make_async_copy(vector, scalars, sem)
    copy.start()
    return copy


def pack_body(z, tiles, columns, out, stage, padded, offsets, in_sems, out_sems):
    copies = []
    half = z.slots // 2
    for piece in range(2 * z.rows):
        source = tiles.at[piece // 2, pl.ds(piece % 2 * half, half)]
        rows = pl.ds(piece * half, half)
        copies.append((
            pltpu.make_async_copy(source, stage.at[rows], in_sems.at[piece]),
            pltpu.make_async_copy(stage.at[rows], out.at[rows], out_sems.at[piece]),
        ))
    for copy, _ in copies:
        copy.start()
    padded[...] = jnp.full(padded.shape, -1, jnp.int32)
    padded[:z.rows, :z.slots] = columns[...]
    column = padded[...]
    row = lax.axis_index(AXES) * z.rows + lax.broadcasted_iota(jnp.int32, column.shape, 0)
    offset = column - row
    offset = jnp.where(offset > z.all_rows // 2, offset - z.all_rows, offset)
    offset = jnp.where(offset < -(z.all_rows // 2), offset + z.all_rows, offset)
    offset = jnp.where(column < 0, EMPTY, offset)
    offsets[...] = jnp.zeros_like(offsets)
    offsets[0:16, :] = offset.astype(jnp.float32).astype(offsets.dtype)
    last = pltpu.make_async_copy(offsets, out.at[z.rows * z.slots], out_sems.at[2 * z.rows])
    last.start()
    for load, store in copies:
        load.wait()
        store.start()
    for _, store in copies:
        store.wait()
    last.wait()


def emit(z, total, positions, stage, out, sems, prev=None):
    for r in range(z.rows):
        def one(s, carry):
            value = total[r * z.block:(r + 1) * z.block, pl.ds(aligned(positions[r, s], z.block), z.block)]
            if prev is not None:
                value = value + prev[r, s]
            stage[r, s] = value.astype(stage.dtype)
            return carry
        lax.fori_loop(0, z.slots, one, 0, unroll=10)
        pltpu.make_async_copy(stage.at[r], out.at[r], sems.at[r]).start()
    for r in range(z.rows):
        pltpu.make_async_copy(stage.at[r], out.at[r], sems.at[r]).wait()


def add_trace(trace, weight, one, other):
    value = jnp.dot(one, other, preferred_element_type=jnp.float32)
    on = lax.broadcasted_iota(jnp.int32, value.shape, 0) == lax.broadcasted_iota(jnp.int32, value.shape, 1)
    diagonal = jnp.sum(jnp.where(on, value, 0.0), axis=0, keepdims=True)
    trace[:, :value.shape[1]] += weight.astype(jnp.float32) * diagonal


def own_body(z, own, columns, out, left_out, corner_out, positions, trace, stage, left, total, out_stage,
             in_sem, left_sem, corner_sem, out_sems):
    device = lax.axis_index(AXES)
    kind = device % 4
    copy = pltpu.make_async_copy(own, stage, in_sem)
    copy.start()
    left[...] = jnp.zeros_like(left)
    total[:, z.window * z.block:] = jnp.zeros((z.span, z.block), jnp.float32)
    copy.wait()
    start = z.start(device)
    for r in range(z.rows):
        def place(u, carry):
            column = z.position(columns[r, u], start)
            positions[r, u] = column
            left[r * z.block:(r + 1) * z.block, pl.ds(aligned(column, z.block), z.block)] = stage[r, u]
            return carry
        lax.fori_loop(0, z.slots, place, 0, unroll=10)
    left_copy = pltpu.make_async_copy(left, left_out, left_sem)
    left_copy.start()
    half = z.span // 2

    def corner(start):
        end = (z.chunks - 1) * z.span

        def go(index, rows, cols, target):
            copy = pltpu.make_async_copy(left.at[rows, cols], target, corner_sem.at[index])
            copy.start() if start else copy.wait()

        @pl.when(kind == UPPER)
        def _():
            go(0, pl.ds(0, half), pl.ds(0, half + z.block), corner_out)

        @pl.when(kind != UPPER)
        def _():
            go(0, pl.ds(half, half), pl.ds(end + half, half), corner_out.at[:, pl.ds(0, half)])
            for q in range(2):
                go(
                    1 + q, pl.ds(z.span - z.block, z.block), pl.ds(end + q * z.block, z.block),
                    corner_out.at[pl.ds(q * z.block, z.block), pl.ds(half, z.block)],
                )

    corner(True)
    middle = slice(z.hops * z.span, (z.hops + 1) * z.span)

    def multiply(n, carry):
        cols = pl.ds(aligned(n, z.span), z.span)
        total[:, cols] = jnp.dot(left[:, middle], left[:, cols], preferred_element_type=jnp.float32)
        return carry

    lax.fori_loop(0, z.chunks, multiply, 0)
    trace[...] = jnp.zeros_like(trace)
    add_trace(trace, jnp.float32(1), left[:, middle], left[:, middle])
    emit(z, total, positions, out_stage, out, out_sems)
    corner(False)
    left_copy.wait()


def near_body(z, names, final, left_in, positions, prev, trace_in, *refs):
    refs = list(refs)
    take = lambda count: [refs.pop(0) for _ in range(count)]
    sources = take(len(names))
    out, trace = take(2)
    relay_left = take(1)[0] if final else None
    left, stage, right, total, sums, vector, scalars = take(7)
    left_sem, in_sem, prev_sem, place_sem, relay_sem, out_sems = take(6)
    device = lax.axis_index(AXES)
    kind = device % 4
    place = {name: pick(table, kind) + z.hops for name, table in OFFSETS.items()}

    def chunk(n):
        return pl.ds(aligned(n, z.span), z.span)

    def fetch(index):
        return pltpu.make_async_copy(sources[index], stage.at[index % 2], in_sem.at[index % 2])

    fetch(0).start()
    left_copy = pltpu.make_async_copy(left_in, left, left_sem)
    left_copy.start()
    prev_copy = pltpu.make_async_copy(prev, sums, prev_sem)
    total[...] = jnp.zeros_like(total)
    trace[...] = trace_in[...]
    relay_copies = []

    def hand_on():
        for index, name in enumerate(("relay", "relay_beside") if final else ()):
            copy = pltpu.make_async_copy(
                left.at[:, chunk(place[name])], relay_left.at[:, pl.ds(index * z.span, z.span)],
                relay_sem.at[index],
            )
            copy.start()
            relay_copies.append(copy)

    decodings = []

    def begin_decode(index):
        slot = index % 2
        fetch(index).wait()
        decodings.append(decode(
            z, stage.at[slot, z.rows * z.slots], place[names[index]], vector.at[slot], scalars.at[slot],
            place_sem.at[slot],
        ))

    begin_decode(0)
    if len(names) > 1:
        fetch(1).start()
    dense_of = {}
    for index, name in enumerate(names):
        dense = right.at[index]
        dense_of[name] = dense
        spot = place[name]
        slot = index % 2
        dense[...] = jnp.zeros_like(dense)
        decodings[index].wait()
        scatter(z, dense, 0, stage.at[slot], lambda r, u: scalars[slot, r, u])
        if index == 0:
            left_copy.wait()
            prev_copy.start()
            hand_on()
        if index + 2 < len(names):
            fetch(index + 2).start()
        if index + 1 < len(names):
            begin_decode(index + 1)

        def multiply(n, carry):
            total[:, chunk(n)] += jnp.dot(
                left[:, chunk(spot)], dense[:, chunk(n)], preferred_element_type=jnp.float32
            )
            return carry

        lax.fori_loop(jnp.maximum(0, spot - z.hops), jnp.minimum(z.chunks, spot + z.hops + 1), multiply, 0)
        weight = pick(COUNTS[name], kind)
        pl.when(weight != 0)(
            lambda: add_trace(trace, weight, left[:, chunk(spot)], dense[:, chunk(z.hops)])
        )
    for (one, other), table in OUTSIDE.items() if final else ():
        weight = pick(table, kind)
        pl.when(weight != 0)(lambda: add_trace(
            trace, weight, dense_of[one][:, chunk(place[other])], dense_of[other][:, chunk(place[one])]
        ))
    prev_copy.wait()
    emit(z, total, positions, sums, out, out_sems, sums)
    for copy in relay_copies:
        copy.wait()


def corner_body(z, left, corner, trace_in, trace, square, column, tall, sems):
    kind = lax.axis_index(AXES) % 4
    half = z.span // 2
    end = (z.chunks - 1) * z.span
    trace[...] = trace_in[...]

    @pl.when(kind == UPPER)
    def _():
        copies = [
            pltpu.make_async_copy(left.at[pl.ds(half, half), pl.ds(half, half)], square, sems.at[0]),
            pltpu.make_async_copy(left.at[pl.ds(0, half), pl.ds(z.span - z.block, z.block)], column, sems.at[1]),
        ]
        for copy in copies:
            copy.start()
        for copy in copies:
            copy.wait()
        add_trace(trace, jnp.float32(2), square[...], corner[:, :half])
        for q in range(2):
            rows = slice(q * z.block, (q + 1) * z.block)
            add_trace(trace, jnp.float32(2), column[rows], corner[rows, half:])

    @pl.when(kind == LOWER)
    def _():
        copy = pltpu.make_async_copy(left.at[pl.ds(0, half + z.block), pl.ds(end, half)], tall, sems.at[0])
        copy.start()
        copy.wait()
        add_trace(trace, jnp.float32(2), tall[...], corner[...])


def last_body(z, left_in, positions, prev, source_a, source_b, out, left, right, total, out_stage,
              prev_stage, vector, scalars, left_sem, prev_sem, place_sem, out_sems):
    kind = lax.axis_index(AXES) % 4
    copies = [
        pltpu.make_async_copy(left_in, left, left_sem),
        pltpu.make_async_copy(prev, prev_stage, prev_sem),
    ]
    places = [pick(OFFSETS[name], kind) + z.hops for name in ("relay", "relay_beside")]
    decodings = []
    for index in range(2):
        decodings.append(decode(
            z, (source_a, source_b)[index].at[z.rows * z.slots], places[index], vector.at[index], scalars.at[index],
            place_sem.at[index],
        ))
    for copy in copies:
        copy.start()
    low = jnp.maximum(0, jnp.minimum(*places) - z.hops)
    high = jnp.minimum(z.chunks, jnp.maximum(*places) + z.hops + 1)

    def chunk(n):
        return pl.ds(aligned(n, z.span), z.span)

    def clear_total(n, carry):
        total[:, chunk(n)] = jnp.zeros((z.span, z.span), jnp.float32)
        return carry

    def clear_right(n, carry):
        right[:, chunk(n)] = jnp.zeros((2 * z.span, z.span), right.dtype)
        return carry

    lax.fori_loop(0, low, clear_total, 0)
    lax.fori_loop(high, z.chunks, clear_total, 0)
    total[:, z.window * z.block:] = jnp.zeros((z.span, z.block), jnp.float32)
    lax.fori_loop(low, high, clear_right, 0)
    for index in range(2):
        decodings[index].wait()
        scatter(z, right, index * z.span, (source_a, source_b)[index], lambda r, u: scalars[index, r, u])
    copies[0].wait()

    def multiply(n, carry):
        total[:, chunk(n)] = jnp.dot(left[...], right[:, chunk(n)], preferred_element_type=jnp.float32)
        return carry

    lax.fori_loop(low, high, multiply, 0)
    copies[1].wait()
    emit(z, total, positions, out_stage, out, out_sems, prev_stage)


ANY = pl.BlockSpec(memory_space=pl.ANY)
SMEM = pl.BlockSpec(memory_space=pltpu.SMEM)
VMEM = pl.BlockSpec(memory_space=pltpu.VMEM)
DMA = pltpu.SemaphoreType.DMA


def call(z, kernel, operands, in_specs, out_shape, out_specs, scratch, pieces, limit=VMEM_LIMIT):
    return pl.pallas_call(
        kernel,
        out_shape=out_shape,
        in_specs=in_specs,
        out_specs=out_specs,
        scratch_shapes=scratch,
        compiler_params=pltpu.CompilerParams(vmem_limit_bytes=limit),
        cost_estimate=pl.CostEstimate(
            flops=2 * z.span * z.span * z.window * z.block * pieces,
            bytes_accessed=2 * z.span * z.slots * z.block * (pieces + 4),
            transcendentals=0,
        ),
    )(*operands)


def shards(tiles, columns):
    devices = lax.axis_size(AXES)
    z = Sizes(tiles.shape, devices)
    assert z.hops == 3 and z.rows == 4 and z.slots % 2 == 0 and devices % 4 == 0 and devices > 8
    dtype = tiles.dtype
    shape = jax.ShapeDtypeStruct
    sums = shape(tiles.shape, jnp.float32)
    line = shape((1, z.span), jnp.float32)
    dense = pltpu.VMEM((z.span, z.wide), dtype)
    total_buffer = pltpu.VMEM((z.span, z.wide), jnp.float32)

    payload_shape = (z.rows * z.slots + 1, z.block, z.block)
    places = [pltpu.VMEM((2, 16, z.block), jnp.int32), pltpu.SMEM((2, 16, z.block), jnp.int32)]

    payload = call(
        z, functools.partial(pack_body, z), [tiles, columns], [ANY, VMEM],
        shape(payload_shape, dtype), ANY,
        [
            pltpu.VMEM((z.rows * z.slots, z.block, z.block), dtype), pltpu.VMEM((16, z.block), jnp.int32),
            pltpu.VMEM((z.block, z.block), dtype), DMA((2 * z.rows,)), DMA((2 * z.rows + 1,)),
        ],
        0, WHOLE_VMEM,
    )
    first = receive(payload, FIRST)
    second = receive(payload, SECOND)
    beside = receive(payload, PARTNER)

    total, left, corner, positions, trace = call(
        z, functools.partial(own_body, z), [tiles, columns], [ANY, SMEM],
        [
            sums, shape((z.span, z.wide), dtype), shape((z.span // 2, z.span // 2 + z.block), dtype),
            shape((z.rows, z.slots), jnp.int32), line,
        ],
        [ANY, ANY, ANY, SMEM, VMEM],
        [
            pltpu.VMEM(tiles.shape, dtype), dense, total_buffer, pltpu.VMEM(tiles.shape, jnp.float32),
            DMA, DMA, DMA((3,)), DMA((z.rows,)),
        ],
        1, WHOLE_VMEM,
    )
    corner = receive(corner, PARTNER, (0, 3))

    def near(names, arrays, total, trace, final=False):
        extra = [shape((z.span, 2 * z.span), dtype)] * final
        return call(
            z, functools.partial(near_body, z, names, final),
            [left, positions, total, trace] + arrays,
            [ANY, SMEM, ANY, VMEM] + [ANY] * len(arrays),
            [sums, line] + extra,
            [ANY, VMEM] + [ANY] * final,
            [
                dense, pltpu.VMEM((2,) + payload_shape, dtype),
                pltpu.VMEM((len(names), z.span, z.wide), dtype), total_buffer,
                pltpu.VMEM(tiles.shape, jnp.float32), *places,
                DMA, DMA((2,)), DMA, DMA((2,)), DMA((2,)), DMA((z.rows,)),
            ],
            len(names), VMEM_LIMIT if final else WHOLE_VMEM,
        )

    total, trace = near(("beside",), [beside], total, trace)
    first, second, corner, total, trace = lax.optimization_barrier((first, second, corner, total, trace))
    relay = receive(first, RELAY_FROM)
    device = lax.axis_index(AXES)
    kind = device % 4

    def nearby(first, second, corner, total, trace):
        use_first = (kind == 0) | (kind == 3)
        mixed = receive(jnp.where(use_first, first, second), PARTNER)
        corner = receive(corner, (0, -2, 2, 0), (LOWER, UPPER))
        total, trace, relay_left = near(("first", "second", "mixed"), [first, second, mixed], total, trace, True)
        trace = call(
            z, functools.partial(corner_body, z), [left, corner, trace], [ANY, VMEM, VMEM], line, VMEM,
            [
                pltpu.VMEM((z.span // 2, z.span // 2), dtype), pltpu.VMEM((z.span // 2, z.block), dtype),
                pltpu.VMEM((z.span // 2 + z.block, z.span // 2), dtype), DMA((2,)),
            ],
            0,
        )
        return total, trace, relay_left

    def nothing(first, second, corner, total, trace):
        return jnp.zeros_like(total), jnp.zeros_like(trace), jnp.zeros((z.span, 2 * z.span), dtype)

    total, trace, relay_left = lax.cond(
        device < devices, nearby, nothing, first, second, corner, total, trace
    )
    assert devices & (devices - 1) == 0
    steps = [1 << bit for bit in range(devices.bit_length() - 1)]
    trace = trace + fetch(trace, steps[0])
    for index in range(3, len(steps), 2):
        trace = round_of(trace, steps[index:index + 2])
    relay, total, trace = lax.optimization_barrier((relay, total, trace))
    relay_beside = receive(relay, PARTNER)
    others = [fetch(trace, step) for step in (steps[1], steps[2], steps[1] + steps[2])]
    square = call(
        z, functools.partial(last_body, z), [relay_left, positions, total, relay, relay_beside],
        [ANY, SMEM, ANY, VMEM, VMEM],
        [shape(tiles.shape, dtype)],
        [ANY],
        [
            pltpu.VMEM((z.span, 2 * z.span), dtype),
            pltpu.VMEM((2 * z.span, z.wide), dtype), total_buffer,
            pltpu.VMEM(tiles.shape, dtype), pltpu.VMEM(tiles.shape, jnp.float32), *places,
            DMA, DMA, DMA((2,)), DMA((z.rows,)),
        ],
        2, 44 * 1024 * 1024,
    )[0]
    square, trace, others = lax.optimization_barrier((square, trace, others))
    return square, jnp.sum((trace + others[0]) + (others[1] + others[2])) / (z.all_rows * z.block)


def solution(mesh):
    return jax.shard_map(
        shards,
        mesh=mesh,
        in_specs=(P(AXES, None, None, None), P(AXES, None)),
        out_specs=(P(AXES, None, None, None), P()),
        check_vma=False,
    )
```

```python
import functools

import jax
import jax.numpy as jnp
from jax import lax
from jax.experimental import pallas as pl
from jax.experimental.pallas import tpu as pltpu
from jax.sharding import PartitionSpec as P

REACH = 12
AXES = ("blk", "grp")
VMEM_LIMIT = 42 * 1024 * 1024
WHOLE_VMEM = 62 * 1024 * 1024
EMPTY = 64

FIRST = (2, 3, -3, -2)
SECOND = (-3, 2, -2, 3)
RELAY_FROM = (2, -5, 5, -2)
PARTNER = (1, -1, 1, -1)
RELAY = tuple(RELAY_FROM[m] + FIRST[(m + RELAY_FROM[m]) % 4] for m in range(4))


def across(table):
    return tuple(PARTNER[m] + table[m ^ 1] for m in range(4))


USE_SECOND = tuple(int(abs(offset) > 3) for offset in across(FIRST))
MIXED = tuple(
    second if use else first
    for first, second, use in zip(across(FIRST), across(SECOND), USE_SECOND)
)
OFFSETS = {
    "beside": PARTNER,
    "first": FIRST,
    "second": SECOND,
    "mixed": MIXED,
    "relay": RELAY,
    "relay_beside": across(RELAY),
}
COUNTS = {"beside": (2, 0, 2, 0), "first": (2, 0, 0, 2), "second": (2, 0, 0, 2), "mixed": (0, 0, 2, 2)}
OUTSIDE = {("first", "mixed"): (0, 2, 2, 0), ("first", "second"): (0, 2, 0, 0)}
LOWER, UPPER = 2, 1


def receive(shard, offsets, kinds=range(4)):
    size = lax.axis_size(AXES)
    pairs = [((d + offsets[d % 4]) % size, d) for d in range(size) if d % 4 in kinds]
    return lax.ppermute(shard, AXES, pairs)


def fetch(value, step):
    return lax.ppermute(value, AXES, [(d, d ^ step) for d in range(lax.axis_size(AXES))])


def round_of(value, steps):
    if len(steps) == 1:
        return value + fetch(value, steps[0])
    one, other = steps
    return (value + fetch(value, one)) + (fetch(value, other) + fetch(value, one + other))


def pick(table, kind):
    value = jnp.int32(table[3])
    for m in range(3):
        value = jnp.where(kind == m, jnp.int32(table[m]), value)
    return value


def aligned(index, unit):
    return pl.multiple_of(index * unit, unit)


class Sizes:
    def __init__(self, shape, devices):
        self.rows, self.slots, self.block, _ = shape
        self.hops = (REACH + self.rows - 1) // self.rows
        self.chunks = 2 * self.hops + 1
        self.window = self.chunks * self.rows
        self.span = self.rows * self.block
        self.wide = (self.window + 1) * self.block
        self.all_rows = self.rows * devices

    def start(self, device):
        start = (device - self.hops) * self.rows
        return jnp.where(start < 0, start + self.all_rows, start)

    def position(self, column, start):
        place = column - start
        place = jnp.where(place < 0, place + self.all_rows, place)
        place = jnp.where(column < 0, self.window, place)
        return jnp.minimum(place, self.window)


def scatter(z, dense, top, source, place):
    for r in range(z.rows):
        def one(u, carry):
            column = pl.ds(aligned(place(r, u), z.block), z.block)
            dense[top + r * z.block:top + (r + 1) * z.block, column] = source[r * z.slots + u]
            return carry
        lax.fori_loop(0, z.slots, one, 0, unroll=10)


def decode(z, offsets, spot, vector, scalars, sem):
    value = offsets[0:16, :].astype(jnp.float32).astype(jnp.int32)
    value = value + spot * z.rows + lax.broadcasted_iota(jnp.int32, value.shape, 0)
    vector[...] = jnp.where((value < 0) | (value > z.window), z.window, value)
    copy = pltpu.make_async_copy(vector, scalars, sem)
    copy.start()
    return copy


def pack_body(z, tiles, columns, out, stage, padded, offsets, in_sems, out_sems):
    copies = []
    half = z.slots // 2
    for piece in range(2 * z.rows):
        source = tiles.at[piece // 2, pl.ds(piece % 2 * half, half)]
        rows = pl.ds(piece * half, half)
        copies.append((
            pltpu.make_async_copy(source, stage.at[rows], in_sems.at[piece]),
            pltpu.make_async_copy(stage.at[rows], out.at[rows], out_sems.at[piece]),
        ))
    for copy, _ in copies:
        copy.start()
    padded[...] = jnp.full(padded.shape, -1, jnp.int32)
    padded[:z.rows, :z.slots] = columns[...]
    column = padded[...]
    row = lax.axis_index(AXES) * z.rows + lax.broadcasted_iota(jnp.int32, column.shape, 0)
    offset = column - row
    offset = jnp.where(offset > z.all_rows // 2, offset - z.all_rows, offset)
    offset = jnp.where(offset < -(z.all_rows // 2), offset + z.all_rows, offset)
    offset = jnp.where(column < 0, EMPTY, offset)
    offsets[...] = jnp.zeros_like(offsets)
    offsets[0:16, :] = offset.astype(jnp.float32).astype(offsets.dtype)
    last = pltpu.make_async_copy(offsets, out.at[z.rows * z.slots], out_sems.at[2 * z.rows])
    last.start()
    for load, store in copies:
        load.wait()
        store.start()
    for _, store in copies:
        store.wait()
    last.wait()


def emit(z, total, positions, stage, out, sems, prev=None):
    for r in range(z.rows):
        def one(s, carry):
            value = total[r * z.block:(r + 1) * z.block, pl.ds(aligned(positions[r, s], z.block), z.block)]
            if prev is not None:
                value = value + prev[r, s]
            stage[r, s] = value.astype(stage.dtype)
            return carry
        lax.fori_loop(0, z.slots, one, 0, unroll=10)
        pltpu.make_async_copy(stage.at[r], out.at[r], sems.at[r]).start()
    for r in range(z.rows):
        pltpu.make_async_copy(stage.at[r], out.at[r], sems.at[r]).wait()


def add_trace(trace, weight, one, other):
    value = jnp.dot(one, other, preferred_element_type=jnp.float32)
    on = lax.broadcasted_iota(jnp.int32, value.shape, 0) == lax.broadcasted_iota(jnp.int32, value.shape, 1)
    diagonal = jnp.sum(jnp.where(on, value, 0.0), axis=0, keepdims=True)
    trace[:, :value.shape[1]] += weight.astype(jnp.float32) * diagonal


def own_body(z, own, columns, out, left_out, corner_out, full_out, positions, trace, stage, left, total,
             out_stage, in_sem, left_sem, corner_sem, out_sems):
    device = lax.axis_index(AXES)
    kind = device % 4
    copy = pltpu.make_async_copy(own, stage, in_sem)
    copy.start()
    left[...] = jnp.zeros_like(left)
    total[:, z.window * z.block:] = jnp.zeros((z.span, z.block), jnp.float32)
    copy.wait()
    start = z.start(device)
    for r in range(z.rows):
        def place(u, carry):
            column = z.position(columns[r, u], start)
            positions[r, u] = column
            left[r * z.block:(r + 1) * z.block, pl.ds(aligned(column, z.block), z.block)] = stage[r, u]
            return carry
        lax.fori_loop(0, z.slots, place, 0, unroll=10)
    left_copy = pltpu.make_async_copy(left, left_out, left_sem)
    left_copy.start()
    half = z.span // 2

    def corner(start):
        end = (z.chunks - 1) * z.span

        def go(index, rows, cols, target):
            copy = pltpu.make_async_copy(left.at[rows, cols], target, corner_sem.at[index])
            copy.start() if start else copy.wait()

        @pl.when(kind == UPPER)
        def _():
            go(0, pl.ds(0, half), pl.ds(0, half + z.block), corner_out)
            go(3, pl.ds(0, z.span), pl.ds(0, z.span), full_out)

        @pl.when(kind != UPPER)
        def _():
            go(0, pl.ds(half, half), pl.ds(end + half, half), corner_out.at[:, pl.ds(0, half)])
            go(3, pl.ds(0, z.span), pl.ds(end, z.span), full_out)
            for q in range(2):
                go(
                    1 + q, pl.ds(z.span - z.block, z.block), pl.ds(end + q * z.block, z.block),
                    corner_out.at[pl.ds(q * z.block, z.block), pl.ds(half, z.block)],
                )

    corner(True)
    middle = slice(z.hops * z.span, (z.hops + 1) * z.span)

    def multiply(n, carry):
        cols = pl.ds(aligned(n, z.span), z.span)
        total[:, cols] = jnp.dot(left[:, middle], left[:, cols], preferred_element_type=jnp.float32)
        return carry

    lax.fori_loop(0, z.chunks, multiply, 0)
    trace[...] = jnp.zeros_like(trace)
    add_trace(trace, jnp.float32(1), left[:, middle], left[:, middle])
    emit(z, total, positions, out_stage, out, out_sems)
    corner(False)
    left_copy.wait()


def near_body(z, names, final, left_in, positions, prev, trace_in, *refs):
    refs = list(refs)
    take = lambda count: [refs.pop(0) for _ in range(count)]
    sources = take(len(names))
    out, trace = take(2)
    relay_left = take(1)[0] if final else None
    left, stage, right, total, sums, vector, scalars = take(7)
    left_sem, in_sem, prev_sem, place_sem, relay_sem, out_sems = take(6)
    device = lax.axis_index(AXES)
    kind = device % 4
    place = {name: pick(table, kind) + z.hops for name, table in OFFSETS.items()}

    def chunk(n):
        return pl.ds(aligned(n, z.span), z.span)

    def fetch(index):
        return pltpu.make_async_copy(sources[index], stage.at[index % 2], in_sem.at[index % 2])

    fetch(0).start()
    left_copy = pltpu.make_async_copy(left_in, left, left_sem)
    left_copy.start()
    prev_copy = pltpu.make_async_copy(prev, sums, prev_sem)
    total[...] = jnp.zeros_like(total)
    trace[...] = trace_in[...]
    relay_copies = []

    def hand_on():
        for index, name in enumerate(("relay", "relay_beside") if final else ()):
            copy = pltpu.make_async_copy(
                left.at[:, chunk(place[name])], relay_left.at[:, pl.ds(index * z.span, z.span)],
                relay_sem.at[index],
            )
            copy.start()
            relay_copies.append(copy)

    decodings = []

    def begin_decode(index):
        slot = index % 2
        fetch(index).wait()
        decodings.append(decode(
            z, stage.at[slot, z.rows * z.slots], place[names[index]], vector.at[slot], scalars.at[slot],
            place_sem.at[slot],
        ))

    begin_decode(0)
    if len(names) > 1:
        fetch(1).start()
    dense_of = {}
    for index, name in enumerate(names):
        dense = right.at[index]
        dense_of[name] = dense
        spot = place[name]
        slot = index % 2
        dense[...] = jnp.zeros_like(dense)
        decodings[index].wait()
        scatter(z, dense, 0, stage.at[slot], lambda r, u: scalars[slot, r, u])
        if index == 0:
            left_copy.wait()
            prev_copy.start()
            hand_on()
        if index + 2 < len(names):
            fetch(index + 2).start()
        if index + 1 < len(names):
            begin_decode(index + 1)

        def multiply(n, carry):
            total[:, chunk(n)] += jnp.dot(
                left[:, chunk(spot)], dense[:, chunk(n)], preferred_element_type=jnp.float32
            )
            return carry

        lax.fori_loop(jnp.maximum(0, spot - z.hops), jnp.minimum(z.chunks, spot + z.hops + 1), multiply, 0)
        weight = pick(COUNTS[name], kind)
        pl.when(weight != 0)(
            lambda: add_trace(trace, weight, left[:, chunk(spot)], dense[:, chunk(z.hops)])
        )
    for (one, other), table in OUTSIDE.items() if final else ():
        weight = pick(table, kind)
        pl.when(weight != 0)(lambda: add_trace(
            trace, weight, dense_of[one][:, chunk(place[other])], dense_of[other][:, chunk(place[one])]
        ))
    prev_copy.wait()
    emit(z, total, positions, sums, out, out_sems, sums)
    for copy in relay_copies:
        copy.wait()


def corner_body(z, full, corner, trace_in, trace, square, column, tall, sems):
    kind = lax.axis_index(AXES) % 4
    half = z.span // 2
    trace[...] = trace_in[...]

    @pl.when(kind == UPPER ^ 1)
    def _():
        copies = [
            pltpu.make_async_copy(full.at[pl.ds(half, half), pl.ds(half, half)], square, sems.at[0]),
            pltpu.make_async_copy(full.at[pl.ds(0, half), pl.ds(z.span - z.block, z.block)], column, sems.at[1]),
        ]
        for copy in copies:
            copy.start()
        for copy in copies:
            copy.wait()
        add_trace(trace, jnp.float32(2), square[...], corner[:, :half])
        for q in range(2):
            rows = slice(q * z.block, (q + 1) * z.block)
            add_trace(trace, jnp.float32(2), column[rows], corner[rows, half:])

    @pl.when(kind == LOWER ^ 1)
    def _():
        copy = pltpu.make_async_copy(full.at[pl.ds(0, half + z.block), pl.ds(0, half)], tall, sems.at[0])
        copy.start()
        copy.wait()
        add_trace(trace, jnp.float32(2), tall[...], corner[...])


def last_body(z, left_in, positions, prev, source_a, source_b, out, left, right, total, out_stage,
              prev_stage, vector, scalars, left_sem, prev_sem, place_sem, out_sems):
    kind = lax.axis_index(AXES) % 4
    copies = [
        pltpu.make_async_copy(left_in, left, left_sem),
        pltpu.make_async_copy(prev, prev_stage, prev_sem),
    ]
    places = [pick(OFFSETS[name], kind) + z.hops for name in ("relay", "relay_beside")]
    decodings = []
    for index in range(2):
        decodings.append(decode(
            z, (source_a, source_b)[index].at[z.rows * z.slots], places[index], vector.at[index], scalars.at[index],
            place_sem.at[index],
        ))
    for copy in copies:
        copy.start()
    low = jnp.maximum(0, jnp.minimum(*places) - z.hops)
    high = jnp.minimum(z.chunks, jnp.maximum(*places) + z.hops + 1)

    def chunk(n):
        return pl.ds(aligned(n, z.span), z.span)

    def clear_total(n, carry):
        total[:, chunk(n)] = jnp.zeros((z.span, z.span), jnp.float32)
        return carry

    def clear_right(n, carry):
        right[:, chunk(n)] = jnp.zeros((2 * z.span, z.span), right.dtype)
        return carry

    lax.fori_loop(0, low, clear_total, 0)
    lax.fori_loop(high, z.chunks, clear_total, 0)
    total[:, z.window * z.block:] = jnp.zeros((z.span, z.block), jnp.float32)
    lax.fori_loop(low, high, clear_right, 0)
    for index in range(2):
        decodings[index].wait()
        scatter(z, right, index * z.span, (source_a, source_b)[index], lambda r, u: scalars[index, r, u])
    copies[0].wait()

    def multiply(n, carry):
        total[:, chunk(n)] = jnp.dot(left[...], right[:, chunk(n)], preferred_element_type=jnp.float32)
        return carry

    lax.fori_loop(low, high, multiply, 0)
    copies[1].wait()
    emit(z, total, positions, out_stage, out, out_sems, prev_stage)


ANY = pl.BlockSpec(memory_space=pl.ANY)
SMEM = pl.BlockSpec(memory_space=pltpu.SMEM)
VMEM = pl.BlockSpec(memory_space=pltpu.VMEM)
DMA = pltpu.SemaphoreType.DMA


def call(z, kernel, operands, in_specs, out_shape, out_specs, scratch, pieces, limit=VMEM_LIMIT):
    return pl.pallas_call(
        kernel,
        out_shape=out_shape,
        in_specs=in_specs,
        out_specs=out_specs,
        scratch_shapes=scratch,
        compiler_params=pltpu.CompilerParams(vmem_limit_bytes=limit),
        cost_estimate=pl.CostEstimate(
            flops=2 * z.span * z.span * z.window * z.block * pieces,
            bytes_accessed=2 * z.span * z.slots * z.block * (pieces + 4),
            transcendentals=0,
        ),
    )(*operands)


def shards(tiles, columns):
    devices = lax.axis_size(AXES)
    z = Sizes(tiles.shape, devices)
    assert z.hops == 3 and z.rows == 4 and z.slots % 2 == 0 and devices % 4 == 0 and devices > 8
    dtype = tiles.dtype
    shape = jax.ShapeDtypeStruct
    sums = shape(tiles.shape, jnp.float32)
    line = shape((1, z.span), jnp.float32)
    dense = pltpu.VMEM((z.span, z.wide), dtype)
    total_buffer = pltpu.VMEM((z.span, z.wide), jnp.float32)

    payload_shape = (z.rows * z.slots + 1, z.block, z.block)
    places = [pltpu.VMEM((2, 16, z.block), jnp.int32), pltpu.SMEM((2, 16, z.block), jnp.int32)]

    payload = call(
        z, functools.partial(pack_body, z), [tiles, columns], [ANY, VMEM],
        shape(payload_shape, dtype), ANY,
        [
            pltpu.VMEM((z.rows * z.slots, z.block, z.block), dtype), pltpu.VMEM((16, z.block), jnp.int32),
            pltpu.VMEM((z.block, z.block), dtype), DMA((2 * z.rows,)), DMA((2 * z.rows + 1,)),
        ],
        0, WHOLE_VMEM,
    )
    first = receive(payload, FIRST)
    second = receive(payload, SECOND)
    beside = receive(payload, PARTNER)

    total, left, corner, full, positions, trace = call(
        z, functools.partial(own_body, z), [tiles, columns], [ANY, SMEM],
        [
            sums, shape((z.span, z.wide), dtype), shape((z.span // 2, z.span // 2 + z.block), dtype),
            shape((z.span, z.span), dtype),
            shape((z.rows, z.slots), jnp.int32), line,
        ],
        [ANY, ANY, ANY, ANY, SMEM, VMEM],
        [
            pltpu.VMEM(tiles.shape, dtype), dense, total_buffer, pltpu.VMEM(tiles.shape, jnp.float32),
            DMA, DMA, DMA((4,)), DMA((z.rows,)),
        ],
        1, WHOLE_VMEM,
    )
    corner = receive(corner, PARTNER, (0, 3))
    full = receive(full, PARTNER, (0, 3))

    def near(names, arrays, total, trace, final=False):
        extra = [shape((z.span, 2 * z.span), dtype)] * final
        return call(
            z, functools.partial(near_body, z, names, final),
            [left, positions, total, trace] + arrays,
            [ANY, SMEM, ANY, VMEM] + [ANY] * len(arrays),
            [sums, line] + extra,
            [ANY, VMEM] + [ANY] * final,
            [
                dense, pltpu.VMEM((2,) + payload_shape, dtype),
                pltpu.VMEM((len(names), z.span, z.wide), dtype), total_buffer,
                pltpu.VMEM(tiles.shape, jnp.float32), *places,
                DMA, DMA((2,)), DMA, DMA((2,)), DMA((2,)), DMA((z.rows,)),
            ],
            len(names), VMEM_LIMIT if final else WHOLE_VMEM,
        )

    total, trace = near(("beside",), [beside], total, trace)
    first, second, corner, full, total, trace = lax.optimization_barrier(
        (first, second, corner, full, total, trace)
    )
    relay = receive(first, RELAY_FROM)
    device = lax.axis_index(AXES)
    kind = device % 4

    def nearby(first, second, corner, full, total, trace):
        use_first = (kind == 0) | (kind == 3)
        mixed = receive(jnp.where(use_first, first, second), PARTNER)
        corner = receive(corner, (-1, 0, 0, 1), (0, 3))
        total, trace, relay_left = near(("first", "second", "mixed"), [first, second, mixed], total, trace, True)
        trace = call(
            z, functools.partial(corner_body, z), [full, corner, trace], [ANY, VMEM, VMEM], line, VMEM,
            [
                pltpu.VMEM((z.span // 2, z.span // 2), dtype), pltpu.VMEM((z.span // 2, z.block), dtype),
                pltpu.VMEM((z.span // 2 + z.block, z.span // 2), dtype), DMA((2,)),
            ],
            0,
        )
        return total, trace, relay_left

    def nothing(first, second, corner, full, total, trace):
        return jnp.zeros_like(total), jnp.zeros_like(trace), jnp.zeros((z.span, 2 * z.span), dtype)

    total, trace, relay_left = lax.cond(
        device < devices, nearby, nothing, first, second, corner, full, total, trace
    )
    assert devices & (devices - 1) == 0
    steps = [1 << bit for bit in range(devices.bit_length() - 1)]
    trace = trace + fetch(trace, steps[0])
    for index in range(3, len(steps), 2):
        trace = round_of(trace, steps[index:index + 2])
    relay, total, trace = lax.optimization_barrier((relay, total, trace))
    relay_beside = receive(relay, PARTNER)
    others = [fetch(trace, step) for step in (steps[1], steps[2], steps[1] + steps[2])]
    square = call(
        z, functools.partial(last_body, z), [relay_left, positions, total, relay, relay_beside],
        [ANY, SMEM, ANY, VMEM, VMEM],
        [shape(tiles.shape, dtype)],
        [ANY],
        [
            pltpu.VMEM((z.span, 2 * z.span), dtype),
            pltpu.VMEM((2 * z.span, z.wide), dtype), total_buffer,
            pltpu.VMEM(tiles.shape, dtype), pltpu.VMEM(tiles.shape, jnp.float32), *places,
            DMA, DMA, DMA((2,)), DMA((z.rows,)),
        ],
        2, 44 * 1024 * 1024,
    )[0]
    square, trace, others = lax.optimization_barrier((square, trace, others))
    return square, jnp.sum((trace + others[0]) + (others[1] + others[2])) / (z.all_rows * z.block)


def solution(mesh):
    return jax.shard_map(
        shards,
        mesh=mesh,
        in_specs=(P(AXES, None, None, None), P(AXES, None)),
        out_specs=(P(AXES, None, None, None), P()),
        check_vma=False,
    )
```

```python
import functools

import jax
import jax.numpy as jnp
from jax import lax
from jax.experimental import pallas as pl
from jax.experimental.pallas import tpu as pltpu
from jax.sharding import PartitionSpec as P

REACH = 12
AXES = ("blk", "grp")
VMEM_LIMIT = 42 * 1024 * 1024
WHOLE_VMEM = 62 * 1024 * 1024
EMPTY = 64

FIRST = (2, 3, -3, -2)
SECOND = (-3, 2, -2, 3)
RELAY_FROM = (2, -5, 5, -2)
PARTNER = (1, -1, 1, -1)
RELAY = tuple(RELAY_FROM[m] + FIRST[(m + RELAY_FROM[m]) % 4] for m in range(4))


def across(table):
    return tuple(PARTNER[m] + table[m ^ 1] for m in range(4))


USE_SECOND = tuple(int(abs(offset) > 3) for offset in across(FIRST))
MIXED = tuple(
    second if use else first
    for first, second, use in zip(across(FIRST), across(SECOND), USE_SECOND)
)
OFFSETS = {
    "beside": PARTNER,
    "first": FIRST,
    "second": SECOND,
    "mixed": MIXED,
    "relay": RELAY,
    "relay_beside": across(RELAY),
}
COUNTS = {"beside": (2, 0, 2, 0), "first": (2, 0, 0, 2), "second": (2, 0, 0, 2), "mixed": (0, 0, 2, 2)}
OUTSIDE = {("first", "mixed"): (0, 2, 2, 0), ("first", "second"): (0, 2, 0, 0)}
LOWER, UPPER = 2, 1


def receive(shard, offsets, kinds=range(4)):
    size = lax.axis_size(AXES)
    pairs = [((d + offsets[d % 4]) % size, d) for d in range(size) if d % 4 in kinds]
    return lax.ppermute(shard, AXES, pairs)


def fetch(value, step):
    return lax.ppermute(value, AXES, [(d, d ^ step) for d in range(lax.axis_size(AXES))])


def round_of(value, steps):
    if len(steps) == 1:
        return value + fetch(value, steps[0])
    one, other = steps
    return (value + fetch(value, one)) + (fetch(value, other) + fetch(value, one + other))


def pick(table, kind):
    value = jnp.int32(table[3])
    for m in range(3):
        value = jnp.where(kind == m, jnp.int32(table[m]), value)
    return value


def aligned(index, unit):
    return pl.multiple_of(index * unit, unit)


class Sizes:
    def __init__(self, shape, devices):
        self.rows, self.slots, self.block, _ = shape
        self.hops = (REACH + self.rows - 1) // self.rows
        self.chunks = 2 * self.hops + 1
        self.window = self.chunks * self.rows
        self.span = self.rows * self.block
        self.wide = (self.window + 1) * self.block
        self.all_rows = self.rows * devices

    def start(self, device):
        start = (device - self.hops) * self.rows
        return jnp.where(start < 0, start + self.all_rows, start)

    def position(self, column, start):
        place = column - start
        place = jnp.where(place < 0, place + self.all_rows, place)
        place = jnp.where(column < 0, self.window, place)
        return jnp.minimum(place, self.window)


def scatter(z, dense, top, source, place):
    for r in range(z.rows):
        def one(u, carry):
            column = pl.ds(aligned(place(r, u), z.block), z.block)
            dense[top + r * z.block:top + (r + 1) * z.block, column] = source[r * z.slots + u]
            return carry
        lax.fori_loop(0, z.slots, one, 0, unroll=20)


def decode(z, offsets, spot, vector, scalars, sem):
    value = offsets[0:16, :].astype(jnp.float32).astype(jnp.int32)
    value = value + spot * z.rows + lax.broadcasted_iota(jnp.int32, value.shape, 0)
    vector[...] = jnp.where((value < 0) | (value > z.window), z.window, value)
    copy = pltpu.make_async_copy(vector, scalars, sem)
    copy.start()
    return copy


def pack_body(z, tiles, columns, out, stage, padded, offsets, in_sems, out_sems):
    copies = []
    half = z.slots // 2
    for piece in range(2 * z.rows):
        source = tiles.at[piece // 2, pl.ds(piece % 2 * half, half)]
        rows = pl.ds(piece * half, half)
        copies.append((
            pltpu.make_async_copy(source, stage.at[rows], in_sems.at[piece]),
            pltpu.make_async_copy(stage.at[rows], out.at[rows], out_sems.at[piece]),
        ))
    for copy, _ in copies:
        copy.start()
    padded[...] = jnp.full(padded.shape, -1, jnp.int32)
    padded[:z.rows, :z.slots] = columns[...]
    column = padded[...]
    row = lax.axis_index(AXES) * z.rows + lax.broadcasted_iota(jnp.int32, column.shape, 0)
    offset = column - row
    offset = jnp.where(offset > z.all_rows // 2, offset - z.all_rows, offset)
    offset = jnp.where(offset < -(z.all_rows // 2), offset + z.all_rows, offset)
    offset = jnp.where(column < 0, EMPTY, offset)
    offsets[...] = jnp.zeros_like(offsets)
    offsets[0:16, :] = offset.astype(jnp.float32).astype(offsets.dtype)
    last = pltpu.make_async_copy(offsets, out.at[z.rows * z.slots], out_sems.at[2 * z.rows])
    last.start()
    for load, store in copies:
        load.wait()
        store.start()
    for _, store in copies:
        store.wait()
    last.wait()


def emit(z, total, positions, stage, out, sems, prev=None):
    for r in range(z.rows):
        def one(s, carry):
            value = total[r * z.block:(r + 1) * z.block, pl.ds(aligned(positions[r, s], z.block), z.block)]
            if prev is not None:
                value = value + prev[r, s]
            stage[r, s] = value.astype(stage.dtype)
            return carry
        lax.fori_loop(0, z.slots, one, 0, unroll=20)
        pltpu.make_async_copy(stage.at[r], out.at[r], sems.at[r]).start()
    for r in range(z.rows):
        pltpu.make_async_copy(stage.at[r], out.at[r], sems.at[r]).wait()


def add_trace(trace, weight, one, other):
    value = jnp.dot(one, other, preferred_element_type=jnp.float32)
    on = lax.broadcasted_iota(jnp.int32, value.shape, 0) == lax.broadcasted_iota(jnp.int32, value.shape, 1)
    diagonal = jnp.sum(jnp.where(on, value, 0.0), axis=0, keepdims=True)
    trace[:, :value.shape[1]] += weight.astype(jnp.float32) * diagonal


def own_body(z, own, columns, out, left_out, corner_out, full_out, positions, trace, stage, left, total,
             out_stage, in_sem, left_sem, corner_sem, out_sems):
    device = lax.axis_index(AXES)
    kind = device % 4
    copy = pltpu.make_async_copy(own, stage, in_sem)
    copy.start()
    left[...] = jnp.zeros_like(left)
    total[:, z.window * z.block:] = jnp.zeros((z.span, z.block), jnp.float32)
    copy.wait()
    start = z.start(device)
    for r in range(z.rows):
        def place(u, carry):
            column = z.position(columns[r, u], start)
            positions[r, u] = column
            left[r * z.block:(r + 1) * z.block, pl.ds(aligned(column, z.block), z.block)] = stage[r, u]
            return carry
        lax.fori_loop(0, z.slots, place, 0, unroll=20)
    left_copy = pltpu.make_async_copy(left, left_out, left_sem)
    left_copy.start()
    half = z.span // 2

    def corner(start):
        end = (z.chunks - 1) * z.span

        def go(index, rows, cols, target):
            copy = pltpu.make_async_copy(left.at[rows, cols], target, corner_sem.at[index])
            copy.start() if start else copy.wait()

        @pl.when(kind == UPPER)
        def _():
            go(0, pl.ds(0, half), pl.ds(0, half + z.block), corner_out)
            go(3, pl.ds(0, z.span), pl.ds(0, z.span), full_out)

        @pl.when(kind != UPPER)
        def _():
            go(0, pl.ds(half, half), pl.ds(end + half, half), corner_out.at[:, pl.ds(0, half)])
            go(3, pl.ds(0, z.span), pl.ds(end, z.span), full_out)
            for q in range(2):
                go(
                    1 + q, pl.ds(z.span - z.block, z.block), pl.ds(end + q * z.block, z.block),
                    corner_out.at[pl.ds(q * z.block, z.block), pl.ds(half, z.block)],
                )

    corner(True)
    middle = slice(z.hops * z.span, (z.hops + 1) * z.span)

    def multiply(n, carry):
        cols = pl.ds(aligned(n, z.span), z.span)
        total[:, cols] = jnp.dot(left[:, middle], left[:, cols], preferred_element_type=jnp.float32)
        return carry

    lax.fori_loop(0, z.chunks, multiply, 0)
    trace[...] = jnp.zeros_like(trace)
    add_trace(trace, jnp.float32(1), left[:, middle], left[:, middle])
    emit(z, total, positions, out_stage, out, out_sems)
    corner(False)
    left_copy.wait()


def near_body(z, names, final, left_in, positions, prev, trace_in, *refs):
    refs = list(refs)
    take = lambda count: [refs.pop(0) for _ in range(count)]
    sources = take(len(names))
    out, trace = take(2)
    relay_left = take(1)[0] if final else None
    left, stage, right, total, sums, vector, scalars = take(7)
    left_sem, in_sem, prev_sem, place_sem, relay_sem, out_sems = take(6)
    device = lax.axis_index(AXES)
    kind = device % 4
    place = {name: pick(table, kind) + z.hops for name, table in OFFSETS.items()}

    def chunk(n):
        return pl.ds(aligned(n, z.span), z.span)

    def fetch(index):
        return pltpu.make_async_copy(sources[index], stage.at[index % 2], in_sem.at[index % 2])

    fetch(0).start()
    left_copy = pltpu.make_async_copy(left_in, left, left_sem)
    left_copy.start()
    prev_copy = pltpu.make_async_copy(prev, sums, prev_sem)
    total[...] = jnp.zeros_like(total)
    trace[...] = trace_in[...]
    relay_copies = []

    def hand_on():
        for index, name in enumerate(("relay", "relay_beside") if final else ()):
            copy = pltpu.make_async_copy(
                left.at[:, chunk(place[name])], relay_left.at[:, pl.ds(index * z.span, z.span)],
                relay_sem.at[index],
            )
            copy.start()
            relay_copies.append(copy)

    decodings = []

    def begin_decode(index):
        slot = index % 2
        fetch(index).wait()
        decodings.append(decode(
            z, stage.at[slot, z.rows * z.slots], place[names[index]], vector.at[slot], scalars.at[slot],
            place_sem.at[slot],
        ))

    begin_decode(0)
    if len(names) > 1:
        fetch(1).start()
    dense_of = {}
    for index, name in enumerate(names):
        dense = right.at[index]
        dense_of[name] = dense
        spot = place[name]
        slot = index % 2
        dense[...] = jnp.zeros_like(dense)
        decodings[index].wait()
        scatter(z, dense, 0, stage.at[slot], lambda r, u: scalars[slot, r, u])
        if index == 0:
            left_copy.wait()
            prev_copy.start()
            hand_on()
        if index + 2 < len(names):
            fetch(index + 2).start()
        if index + 1 < len(names):
            begin_decode(index + 1)

        def multiply(n, carry):
            total[:, chunk(n)] += jnp.dot(
                left[:, chunk(spot)], dense[:, chunk(n)], preferred_element_type=jnp.float32
            )
            return carry

        lax.fori_loop(jnp.maximum(0, spot - z.hops), jnp.minimum(z.chunks, spot + z.hops + 1), multiply, 0)
        weight = pick(COUNTS[name], kind)
        pl.when(weight != 0)(
            lambda: add_trace(trace, weight, left[:, chunk(spot)], dense[:, chunk(z.hops)])
        )
    for (one, other), table in OUTSIDE.items() if final else ():
        weight = pick(table, kind)
        pl.when(weight != 0)(lambda: add_trace(
            trace, weight, dense_of[one][:, chunk(place[other])], dense_of[other][:, chunk(place[one])]
        ))
    prev_copy.wait()
    emit(z, total, positions, sums, out, out_sems, sums)
    for copy in relay_copies:
        copy.wait()


def corner_body(z, full, corner, trace_in, trace, square, column, tall, sems):
    kind = lax.axis_index(AXES) % 4
    half = z.span // 2
    trace[...] = trace_in[...]

    @pl.when(kind == UPPER ^ 1)
    def _():
        copies = [
            pltpu.make_async_copy(full.at[pl.ds(half, half), pl.ds(half, half)], square, sems.at[0]),
            pltpu.make_async_copy(full.at[pl.ds(0, half), pl.ds(z.span - z.block, z.block)], column, sems.at[1]),
        ]
        for copy in copies:
            copy.start()
        for copy in copies:
            copy.wait()
        add_trace(trace, jnp.float32(2), square[...], corner[:, :half])
        for q in range(2):
            rows = slice(q * z.block, (q + 1) * z.block)
            add_trace(trace, jnp.float32(2), column[rows], corner[rows, half:])

    @pl.when(kind == LOWER ^ 1)
    def _():
        copy = pltpu.make_async_copy(full.at[pl.ds(0, half + z.block), pl.ds(0, half)], tall, sems.at[0])
        copy.start()
        copy.wait()
        add_trace(trace, jnp.float32(2), tall[...], corner[...])


def last_body(z, left_in, positions, prev, source_a, source_b, out, left, right, total, out_stage,
              prev_stage, vector, scalars, left_sem, prev_sem, place_sem, out_sems):
    kind = lax.axis_index(AXES) % 4
    copies = [
        pltpu.make_async_copy(left_in, left, left_sem),
        pltpu.make_async_copy(prev, prev_stage, prev_sem),
    ]
    places = [pick(OFFSETS[name], kind) + z.hops for name in ("relay", "relay_beside")]
    decodings = []
    for index in range(2):
        decodings.append(decode(
            z, (source_a, source_b)[index].at[z.rows * z.slots], places[index], vector.at[index], scalars.at[index],
            place_sem.at[index],
        ))
    for copy in copies:
        copy.start()
    low = jnp.maximum(0, jnp.minimum(*places) - z.hops)
    high = jnp.minimum(z.chunks, jnp.maximum(*places) + z.hops + 1)

    def chunk(n):
        return pl.ds(aligned(n, z.span), z.span)

    def clear_total(n, carry):
        total[:, chunk(n)] = jnp.zeros((z.span, z.span), jnp.float32)
        return carry

    def clear_right(n, carry):
        right[:, chunk(n)] = jnp.zeros((2 * z.span, z.span), right.dtype)
        return carry

    lax.fori_loop(0, low, clear_total, 0)
    lax.fori_loop(high, z.chunks, clear_total, 0)
    total[:, z.window * z.block:] = jnp.zeros((z.span, z.block), jnp.float32)
    lax.fori_loop(low, high, clear_right, 0)
    for index in range(2):
        decodings[index].wait()
        scatter(z, right, index * z.span, (source_a, source_b)[index], lambda r, u: scalars[index, r, u])
    copies[0].wait()

    def multiply(n, carry):
        total[:, chunk(n)] = jnp.dot(left[...], right[:, chunk(n)], preferred_element_type=jnp.float32)
        return carry

    lax.fori_loop(low, high, multiply, 0)
    copies[1].wait()
    emit(z, total, positions, out_stage, out, out_sems, prev_stage)


ANY = pl.BlockSpec(memory_space=pl.ANY)
SMEM = pl.BlockSpec(memory_space=pltpu.SMEM)
VMEM = pl.BlockSpec(memory_space=pltpu.VMEM)
DMA = pltpu.SemaphoreType.DMA


def call(z, kernel, operands, in_specs, out_shape, out_specs, scratch, pieces, limit=VMEM_LIMIT):
    return pl.pallas_call(
        kernel,
        out_shape=out_shape,
        in_specs=in_specs,
        out_specs=out_specs,
        scratch_shapes=scratch,
        compiler_params=pltpu.CompilerParams(vmem_limit_bytes=limit),
        cost_estimate=pl.CostEstimate(
            flops=2 * z.span * z.span * z.window * z.block * pieces,
            bytes_accessed=2 * z.span * z.slots * z.block * (pieces + 4),
            transcendentals=0,
        ),
    )(*operands)


def shards(tiles, columns):
    devices = lax.axis_size(AXES)
    z = Sizes(tiles.shape, devices)
    assert z.hops == 3 and z.rows == 4 and z.slots % 2 == 0 and devices % 4 == 0 and devices > 8
    dtype = tiles.dtype
    shape = jax.ShapeDtypeStruct
    sums = shape(tiles.shape, jnp.float32)
    line = shape((1, z.span), jnp.float32)
    dense = pltpu.VMEM((z.span, z.wide), dtype)
    total_buffer = pltpu.VMEM((z.span, z.wide), jnp.float32)

    payload_shape = (z.rows * z.slots + 1, z.block, z.block)
    places = [pltpu.VMEM((2, 16, z.block), jnp.int32), pltpu.SMEM((2, 16, z.block), jnp.int32)]

    payload = call(
        z, functools.partial(pack_body, z), [tiles, columns], [ANY, VMEM],
        shape(payload_shape, dtype), ANY,
        [
            pltpu.VMEM((z.rows * z.slots, z.block, z.block), dtype), pltpu.VMEM((16, z.block), jnp.int32),
            pltpu.VMEM((z.block, z.block), dtype), DMA((2 * z.rows,)), DMA((2 * z.rows + 1,)),
        ],
        0, WHOLE_VMEM,
    )
    first = receive(payload, FIRST)
    second = receive(payload, SECOND)
    beside = receive(payload, PARTNER)

    total, left, corner, full, positions, trace = call(
        z, functools.partial(own_body, z), [tiles, columns], [ANY, SMEM],
        [
            sums, shape((z.span, z.wide), dtype), shape((z.span // 2, z.span // 2 + z.block), dtype),
            shape((z.span, z.span), dtype),
            shape((z.rows, z.slots), jnp.int32), line,
        ],
        [ANY, ANY, ANY, ANY, SMEM, VMEM],
        [
            pltpu.VMEM(tiles.shape, dtype), dense, total_buffer, pltpu.VMEM(tiles.shape, jnp.float32),
            DMA, DMA, DMA((4,)), DMA((z.rows,)),
        ],
        1, WHOLE_VMEM,
    )
    corner = receive(corner, PARTNER, (0, 3))
    full = receive(full, PARTNER, (0, 3))

    def near(names, arrays, total, trace, final=False):
        extra = [shape((z.span, 2 * z.span), dtype)] * final
        return call(
            z, functools.partial(near_body, z, names, final),
            [left, positions, total, trace] + arrays,
            [ANY, SMEM, ANY, VMEM] + [ANY] * len(arrays),
            [sums, line] + extra,
            [ANY, VMEM] + [ANY] * final,
            [
                dense, pltpu.VMEM((2,) + payload_shape, dtype),
                pltpu.VMEM((len(names), z.span, z.wide), dtype), total_buffer,
                pltpu.VMEM(tiles.shape, jnp.float32), *places,
                DMA, DMA((2,)), DMA, DMA((2,)), DMA((2,)), DMA((z.rows,)),
            ],
            len(names), VMEM_LIMIT if final else WHOLE_VMEM,
        )

    total, trace = near(("beside",), [beside], total, trace)
    first, second, corner, full, total, trace = lax.optimization_barrier(
        (first, second, corner, full, total, trace)
    )
    relay = receive(first, RELAY_FROM)
    device = lax.axis_index(AXES)
    kind = device % 4

    def nearby(first, second, corner, full, total, trace):
        use_first = (kind == 0) | (kind == 3)
        mixed = receive(jnp.where(use_first, first, second), PARTNER)
        corner = receive(corner, (-1, 0, 0, 1), (0, 3))
        total, trace, relay_left = near(("first", "second", "mixed"), [first, second, mixed], total, trace, True)
        trace = call(
            z, functools.partial(corner_body, z), [full, corner, trace], [ANY, VMEM, VMEM], line, VMEM,
            [
                pltpu.VMEM((z.span // 2, z.span // 2), dtype), pltpu.VMEM((z.span // 2, z.block), dtype),
                pltpu.VMEM((z.span // 2 + z.block, z.span // 2), dtype), DMA((2,)),
            ],
            0,
        )
        return total, trace, relay_left

    def nothing(first, second, corner, full, total, trace):
        return jnp.zeros_like(total), jnp.zeros_like(trace), jnp.zeros((z.span, 2 * z.span), dtype)

    total, trace, relay_left = lax.cond(
        device < devices, nearby, nothing, first, second, corner, full, total, trace
    )
    assert devices & (devices - 1) == 0
    steps = [1 << bit for bit in range(devices.bit_length() - 1)]
    trace = trace + fetch(trace, steps[0])
    for index in range(3, len(steps), 2):
        trace = round_of(trace, steps[index:index + 2])
    relay, total, trace = lax.optimization_barrier((relay, total, trace))
    relay_beside = receive(relay, PARTNER)
    others = [fetch(trace, step) for step in (steps[1], steps[2], steps[1] + steps[2])]
    square = call(
        z, functools.partial(last_body, z), [relay_left, positions, total, relay, relay_beside],
        [ANY, SMEM, ANY, VMEM, VMEM],
        [shape(tiles.shape, dtype)],
        [ANY],
        [
            pltpu.VMEM((z.span, 2 * z.span), dtype),
            pltpu.VMEM((2 * z.span, z.wide), dtype), total_buffer,
            pltpu.VMEM(tiles.shape, dtype), pltpu.VMEM(tiles.shape, jnp.float32), *places,
            DMA, DMA, DMA((2,)), DMA((z.rows,)),
        ],
        2, 44 * 1024 * 1024,
    )[0]
    square, trace, others = lax.optimization_barrier((square, trace, others))
    return square, jnp.sum((trace + others[0]) + (others[1] + others[2])) / (z.all_rows * z.block)


def solution(mesh):
    return jax.shard_map(
        shards,
        mesh=mesh,
        in_specs=(P(AXES, None, None, None), P(AXES, None)),
        out_specs=(P(AXES, None, None, None), P()),
        check_vma=False,
    )
```
